32 devices in a mesh: dp: 8 (over y, x, core), tensor: 4 (over z).
Axes of the slice: x: 2, y: 2, z: 4, core: 2. Of those that a mesh axis runs over, the one named last changes fastest.
Arguments:
- tokens: bfloat16 [8192, 2048], P(('dp', 'tensor')), may hold values from -6 to 6
- segments: int32 [8192], P('dp'), may hold values from 0 to 3, as said below
- gain_attn: float32 [2048], replicated, may hold values from 0.1 to 1.9
- w_query: bfloat16 [2048, 2048], P('dp', 'tensor'), may hold values from -0.125 to 0.125
- w_keyval: bfloat16 [2048, 512], P('dp'), may hold values from -0.125 to 0.125
- w_output: bfloat16 [2048, 2048], P('dp', 'tensor'), may hold values from -1 to 1
- gain_mlp: float32 [2048], replicated, may hold values from 0.1 to 1.9
- w_gate: bfloat16 [2048, 5632], P('dp', 'tensor'), may hold values from -0.125 to 0.125
- w_up: bfloat16 [2048, 5632], P('dp', 'tensor'), may hold values from -0.125 to 0.125
- w_down: bfloat16 [2048, 5632], P('dp', 'tensor'), may hold values from -0.078125 to 0.078125
- cotangent: bfloat16 [8192, 2048], P(('dp', 'tensor')), may hold values from -6 to 6
Outputs:
- layer_out: bfloat16 [8192, 2048], P(('dp', 'tensor'))
- grad_tokens: bfloat16 [8192, 2048], P(('dp', 'tensor'))
- grad_gain_attn: float32 [2048], P(('dp', 'tensor'))
- grad_query: float32 [2048, 2048], P('dp', 'tensor')
- grad_keyval: float32 [2048, 512], P(('dp', 'tensor'))
- grad_output: float32 [2048, 2048], P('dp', 'tensor')
- grad_gain_mlp: float32 [2048], P(('dp', 'tensor'))
- grad_gate: float32 [2048, 5632], P('dp', 'tensor')
- grad_up: float32 [2048, 5632], P('dp', 'tensor')
- grad_down: float32 [2048, 5632], P('dp', 'tensor')
The draws below stay inside these ranges and needn't reach their ends.
Inputs may be any that keep to these rules, and one draw needn't show every extreme that they name: `segments`: each sequence holds exactly four documents numbered 0 to 3 in order; document 2 starts within the first 129 positions and ends within the last 128 positions of its sequence.
All inputs are finite; a program needn't handle non-finite values.
Results may differ from the reference program's by a relative error of at most 0.023.
Values may be sent and summed in bfloat16 or wider, within the bound.
A program may use at most 256 MiB of HBM per device.

```python
import jax
import jax.numpy as jnp
from jax import lax

D = 2048
H = 32
KVH = 4
HD = 64
FF = 5632
L = 1024
REP = 1
TOKENS = 8192
N_DP = 8
N_TENSOR = 4


def draw_segments(key, part):
    key = jax.random.fold_in(key, 7)
    margin = L // (2 * N_TENSOR)
    key_start = jax.random.fold_in(key, 1)
    key_head = jax.random.fold_in(key, 2)
    key_end = jax.random.fold_in(key, 3)
    main_start = jax.random.randint(key_start, (N_DP, 1), 2, 2 + margin)
    head_cut = jax.random.randint(key_head, (N_DP, 1), 0, 1048576) % (main_start - 1) + 1
    main_end = L - jax.random.randint(key_end, (N_DP, 1), 1, margin + 1)
    places = jnp.arange(L, dtype=jnp.int32)[None, :]
    numbers = (places >= head_cut).astype(jnp.int32) + (places >= main_start).astype(jnp.int32) + (places >= main_end).astype(jnp.int32)
    return numbers.reshape(N_DP * L).astype(jnp.int32)


def spiked(array, own_key, source, target, shards_of, factor):
    def block_of(axis_at):
        return (jnp.arange(array.shape[axis_at]) // (array.shape[axis_at] // shards_of)).reshape((-1,) + (1,) * (array.ndim - 1 - axis_at))

    one_side = jax.random.permutation(own_key, shards_of)[block_of(target)]
    second = (block_of(target) + shards_of // 2) % shards_of
    return jnp.where((block_of(source) == one_side) | (block_of(source) == second), factor * array, array)


def steps_of(own_key, dims, split, low, high):
    level = 1.0
    for axis_at, blocks in split:
        draws = jax.random.uniform(jax.random.fold_in(jax.random.fold_in(own_key, 6), axis_at), (blocks,), jnp.float32, low / len(split), high / len(split))
        level = level * jnp.repeat(jnp.exp(draws), dims[axis_at] // blocks).reshape((-1,) + (1,) * (len(dims) - 1 - axis_at))
    return level


def noise(rng, extent, scale, bound, shards=(), kind=jnp.bfloat16):
    result = scale * jax.random.normal(rng, extent, jnp.float32)
    if shards:
        result = result * steps_of(rng, extent, shards, -0.22, 0.18)
    return jnp.clip(result, -bound, bound).astype(kind)


def bell_draw_with(rng, extent, scale, reach, pieces, heavy, kind=jnp.bfloat16):
    entries = scale * jax.random.normal(rng, extent, jnp.float32)
    if pieces:
        entries = entries * steps_of(rng, extent, pieces, -0.22, 0.18)
    return jnp.clip(spiked(entries, jax.random.fold_in(rng, 3), *heavy), -reach, reach).astype(kind)


def setup_inputs(seed: int = 0) -> dict:
    arg_keys = jax.random.split(jax.random.key(seed), 12)
    return {
        "tokens": noise(arg_keys[0], (TOKENS, D), 1.0, 6.0, ((0, 32),)),
        "segments": draw_segments(jax.random.fold_in(arg_keys[11], 71), 0),
        "gain_attn": jnp.clip(1.0 + 0.18 * jax.random.normal(arg_keys[2], (D,), jnp.float32), 0.1, 1.9),
        "w_query": noise(arg_keys[3], (D, H * HD), D ** -0.5, 0.125, ((0, 8), (1, 4))),
        "w_keyval": noise(arg_keys[4], (D, 2 * KVH * HD), D ** -0.5, 0.125, ((0, 8),)),
        "w_output": noise(arg_keys[5], (D, H * HD), (H * HD // 64) ** -0.5, 1.0, ((0, 8), (1, 4))),
        "gain_mlp": jnp.clip(1.0 + 0.18 * jax.random.normal(arg_keys[6], (D,), jnp.float32), 0.1, 1.9),
        "w_gate": noise(arg_keys[7], (D, FF), D ** -0.5, 0.125, ((0, 8), (1, 4))),
        "w_up": noise(arg_keys[8], (D, FF), D ** -0.5, 0.125, ((0, 8), (1, 4))),
        "w_down": noise(arg_keys[9], (D, FF), FF ** -0.5, 0.078125, ((0, 8), (1, 4))),
        "cotangent": bell_draw_with(arg_keys[10], (TOKENS, D), 1.0, 6.0, ((0, 32),), (0, 1, 32, 2.75)),
    }


epsilon = 1e-05
rope_base = 10000.0
highest = lax.Precision.HIGHEST

@jax.custom_vjp
def low(v):
    return lax.optimization_barrier(v.astype(jnp.bfloat16)).astype(jnp.float32)

@jax.custom_vjp
def low_back(v):
    return v

def low_keep(v):
    return (low(v), None)

def low_pass(kept, grad):
    return (grad,)

def back_keep(v):
    return (v, None)

def back_low(kept, grad):
    return (low(grad),)
low.defvjp(low_keep, low_pass)
low_back.defvjp(back_keep, back_low)

def rms_norm(values, gain_vec):
    inverse = lax.rsqrt(lax.optimization_barrier(jnp.mean(values * values, axis=-1, keepdims=True)) + epsilon)
    return values * inverse * gain_vec

def doc_positions(seg_row):
    length = seg_row.shape[0]
    places = jnp.arange(length, dtype=jnp.int32)
    change = jnp.concatenate([jnp.ones((1,), jnp.bool_), seg_row[1:] != seg_row[:-1]])
    starts = lax.cummax(jnp.where(change, places, 0).astype(jnp.int32), axis=0)
    return places - starts

def rope_tables(places, width):
    half_width = width // 2
    frequency = rope_base ** (-(2.0 * jnp.arange(half_width).astype(jnp.float32)) / width)
    angles = places.astype(jnp.float32)[:, None] * frequency[None, :]
    return (jnp.cos(angles), jnp.sin(angles))

def rotate(values, cosine, sine_table):
    half_width = values.shape[-1] // 2
    front_half = values[..., :half_width]
    back_half = values[..., half_width:]
    cos_rows = cosine[:, None, :]
    sin_rows = sine_table[:, None, :]
    return jnp.concatenate([front_half * cos_rows - back_half * sin_rows, back_half * cos_rows + front_half * sin_rows], axis=-1)

def attend(queries, key_heads, value_heads, seg_row):
    length = queries.shape[0]
    block_rows = min(512, length)
    places = jnp.arange(length)
    scale = HD ** (-0.5)

    def one_block(first_row):
        query_block = lax.dynamic_slice_in_dim(queries, first_row, block_rows, 0)
        seg_block = lax.dynamic_slice_in_dim(seg_row, first_row, block_rows, 0)
        rows_pos = first_row + jnp.arange(block_rows)
        scores = low_back(jnp.einsum('qhd,khd->hqk', query_block, key_heads, precision=highest) * scale)
        allowed = (rows_pos[:, None] >= places[None, :]) & (seg_block[:, None] == seg_row[None, :])
        scores = jnp.where(allowed[None], scores, -1e+30)
        soft_low = low(jax.nn.softmax(scores, axis=-1))
        return jnp.einsum('hqk,khd->qhd', soft_low, value_heads, precision=highest)
    starts = (jnp.arange(length // block_rows) * block_rows).astype(jnp.int32)
    blocks_out = lax.map(jax.checkpoint(one_block), starts)
    return blocks_out.reshape(length, queries.shape[1], HD)

def layer(token_rows, seg_row, gain_attn, w_query, w_keyval, w_output, gain_mlp, w_gate, w_up, w_down):
    length = token_rows.shape[0]
    places = doc_positions(seg_row)
    cosine, sine_table = rope_tables(places, HD)
    normed = low(rms_norm(token_rows, gain_attn))
    query_pre = low_back(jnp.dot(normed, w_query, precision=highest)).reshape(length, H, HD)
    keyval_pre = jnp.dot(normed, w_keyval, precision=highest).reshape(length, 2, KVH, HD)
    key_copies = low_back(jnp.repeat(keyval_pre[:, 0], REP, axis=1))
    value_copies = low(low_back(jnp.repeat(keyval_pre[:, 1], REP, axis=1)))
    queries = low(rotate(query_pre, cosine, sine_table))
    key_copies = low(rotate(key_copies, cosine, sine_table))
    group_size = H // (KVH * REP)
    key_heads = jnp.repeat(key_copies, group_size, axis=1)
    value_heads = jnp.repeat(value_copies, group_size, axis=1)
    head_out = low_back(low(attend(queries, key_heads, value_heads, seg_row))).reshape(length, H * HD)
    residual = token_rows + low_back(jnp.dot(head_out, w_output.T, precision=highest))
    normed_mlp = low(rms_norm(residual, gain_mlp))
    gate_act = low_back(jnp.dot(normed_mlp, w_gate, precision=highest))
    up_act = low_back(jnp.dot(normed_mlp, w_up, precision=highest))
    hidden = low(jax.nn.silu(gate_act) * up_act)
    return residual + low_back(jnp.dot(hidden, w_down.T, precision=highest))

def reference(tokens, segments, gain_attn, w_query, w_keyval, w_output, gain_mlp, w_gate, w_up, w_down, cotangent):
    params = (gain_attn.astype(jnp.float32), w_query.astype(jnp.float32), w_keyval.astype(jnp.float32), w_output.astype(jnp.float32), gain_mlp.astype(jnp.float32), w_gate.astype(jnp.float32), w_up.astype(jnp.float32), w_down.astype(jnp.float32))
    seq_tokens = tokens.astype(jnp.float32).reshape(N_DP, L, D)
    seg_rows = segments.reshape(N_DP, L)
    seq_cots = cotangent.astype(jnp.float32).reshape(N_DP, L, D)

    def step(totals, inputs):
        token_rows, seg_row, cot_rows = inputs

        def forward(rows_in, *weights_in):
            return layer(rows_in, seg_row, *weights_in)
        output, pullback = jax.vjp(forward, token_rows, *params)
        gradients = pullback(cot_rows)
        totals = tuple((total + grad_one for total, grad_one in zip(totals, gradients[1:])))
        return (totals, (output.astype(jnp.bfloat16), gradients[0].astype(jnp.bfloat16)))
    initial = tuple((jnp.zeros_like(param) for param in params))
    totals, (outputs, inputs_grad) = lax.scan(step, initial, (seq_tokens, seg_rows, seq_cots))
    return (outputs.reshape(TOKENS, D), inputs_grad.reshape(TOKENS, D), totals[0], totals[1], totals[2], totals[3], totals[4], totals[5], totals[6], totals[7])
```

```python
import functools

import jax
import jax.numpy as jnp
from jax import lax
from jax.experimental import pallas as pl
from jax.experimental.pallas import tpu as pltpu
from jax.sharding import PartitionSpec as P

KVH = 4
HD = 64
PAIR = 2 * HD

epsilon = 1e-05
rope_base = 10000.0
masked = -1e30


def doc_positions(seg_row):
    length = seg_row.shape[0]
    places = jnp.arange(length, dtype=jnp.int32)
    change = jnp.concatenate([jnp.ones((1,), jnp.bool_), seg_row[1:] != seg_row[:-1]])
    starts = lax.cummax(jnp.where(change, places, 0), axis=0)
    return places - starts


def rope_tables(places, width):
    half_width = width // 2
    frequency = rope_base ** (-(2.0 * jnp.arange(half_width).astype(jnp.float32)) / width)
    angles = places.astype(jnp.float32)[:, None] * frequency[None, :]
    return (jnp.cos(angles), jnp.sin(angles))


def rotate(values, cosine, sine_table):
    rows, width = values.shape
    heads = values.reshape(rows, width // HD, HD)
    half_width = HD // 2
    front_half = heads[..., :half_width]
    back_half = heads[..., half_width:]
    cos_rows = cosine[:, None, :]
    sin_rows = sine_table[:, None, :]
    turned = jnp.concatenate(
        [
            front_half * cos_rows - back_half * sin_rows,
            back_half * cos_rows + front_half * sin_rows,
        ],
        axis=-1,
    )
    return turned.reshape(rows, width)


def norm_forward(values, gain_vec):
    inverse = lax.rsqrt(jnp.mean(values * values, axis=-1, keepdims=True) + epsilon)
    unit_rows = values * inverse
    return (unit_rows * gain_vec, unit_rows, inverse)


def norm_backward(d_normed, unit_rows, inverse, gain_vec):
    gain_part = jnp.sum(d_normed * unit_rows, axis=0)
    d_unit = d_normed * gain_vec
    d_values = inverse * (d_unit - unit_rows * jnp.mean(d_unit * unit_rows, axis=-1, keepdims=True))
    return (d_values, gain_part)


def dot_nn(left, right):
    return jnp.dot(left, right, preferred_element_type=jnp.float32)


def dot_nt(left, right):
    return lax.dot_general(
        left, right, (((1,), (1,)), ((), ())), preferred_element_type=jnp.float32
    )


def dot_tn(left, right):
    return lax.dot_general(
        left, right, (((0,), (0,)), ((), ())), preferred_element_type=jnp.float32
    )


def front_lanes(tile):
    lane = lax.broadcasted_iota(jnp.int32, tile.shape, 1)
    return jnp.where(lane < HD, tile, jnp.zeros_like(tile))


def back_lanes(tile):
    lane = lax.broadcasted_iota(jnp.int32, tile.shape, 1)
    return jnp.where(lane < HD, jnp.zeros_like(tile), tile)


def attend_forward_kernel(query_ref, front_ref, back_ref, value_t_ref, bias_ref, out_ref, log_ref):
    pairs = query_ref.shape[1] // PAIR
    value_t = value_t_ref[0]
    for pair in range(pairs):
        query = query_ref[:, pair * PAIR : (pair + 1) * PAIR]
        outs = []
        for side, key_ref in enumerate((front_ref, back_ref)):
            scores = dot_nt(key_ref[0], query) + bias_ref[...]
            top = jnp.max(scores, axis=0, keepdims=True)
            expo = jnp.exp(scores - top)
            total = jnp.sum(expo, axis=0, keepdims=True)
            outs.append(dot_nn(value_t, expo.astype(jnp.bfloat16)) / total)
            log_ref[0, pl.ds(pair * 2 + side, 1), :] = top + jnp.log(total)
        out = jnp.concatenate(outs, axis=0).T
        out_ref[:, pair * PAIR : (pair + 1) * PAIR] = out.astype(jnp.bfloat16)


def attend_backward_kernel(
    query_ref,
    grad_ref,
    kf_ref,
    kb_ref,
    kt_ref,
    vf_ref,
    vb_ref,
    bias_ref,
    log_ref,
    dq_ref,
    dk_ref,
    dv_ref,
):
    pairs = query_ref.shape[1] // PAIR
    key_t = kt_ref[0]
    dk_ref[0] = jnp.zeros(dk_ref.shape[1:], jnp.float32)
    dv_ref[0] = jnp.zeros(dv_ref.shape[1:], jnp.float32)
    for pair in range(pairs):
        columns = slice(pair * PAIR, (pair + 1) * PAIR)
        query = query_ref[:, columns]
        grad = grad_ref[:, columns]
        outs = []
        for side, (key_ref, value_ref, keep) in enumerate(
            ((kf_ref, vf_ref, front_lanes), (kb_ref, vb_ref, back_lanes))
        ):
            log_sum = log_ref[0, pl.ds(pair * 2 + side, 1), :]
            probs = jnp.exp(dot_nt(key_ref[0], query) + bias_ref[...] - log_sum)
            d_probs = dot_nt(value_ref[0], grad)
            row_dot = jnp.sum(probs * d_probs, axis=0, keepdims=True)
            d_scores = (probs * (d_probs - row_dot)).astype(jnp.bfloat16)
            dk_ref[0] += dot_nn(d_scores, keep(query))
            dv_ref[0] += dot_nn(probs.astype(jnp.bfloat16), keep(grad))
            outs.append(dot_nn(key_t, d_scores))
        dq_ref[:, columns] = jnp.concatenate(outs, axis=0).T * (HD**-0.5)


def whole_group(rows, width):
    return pl.BlockSpec((1, rows, width), lambda g: (g, 0, 0))


def columns_of(rows, width):
    return pl.BlockSpec((rows, width), lambda g: (0, g))


def attend_forward(query, key_f, key_b, value_t, bias):
    rows, width = query.shape
    length = bias.shape[0]
    group = width // KVH
    return pl.pallas_call(
        attend_forward_kernel,
        grid=(KVH,),
        in_specs=[
            columns_of(rows, group),
            whole_group(length, PAIR),
            whole_group(length, PAIR),
            whole_group(HD, length),
            pl.BlockSpec((length, rows), lambda g: (0, 0)),
        ],
        out_specs=[columns_of(rows, group), whole_group(group // HD, rows)],
        out_shape=[
            jax.ShapeDtypeStruct((rows, width), jnp.bfloat16),
            jax.ShapeDtypeStruct((KVH, group // HD, rows), jnp.float32),
        ],
        compiler_params=pltpu.CompilerParams(vmem_limit_bytes=48 * 1024 * 1024),
        name="attend_forward",
    )(query, key_f, key_b, value_t, bias)


def attend_backward(query, grad, key_f, key_b, key_t, value_f, value_b, bias, log_sum):
    rows, width = query.shape
    length = bias.shape[0]
    group = width // KVH
    tall = whole_group(length, PAIR)
    return pl.pallas_call(
        attend_backward_kernel,
        grid=(KVH,),
        in_specs=[
            columns_of(rows, group),
            columns_of(rows, group),
            tall,
            tall,
            whole_group(HD, length),
            tall,
            tall,
            pl.BlockSpec((length, rows), lambda g: (0, 0)),
            whole_group(group // HD, rows),
        ],
        out_specs=[columns_of(rows, group), tall, tall],
        out_shape=[
            jax.ShapeDtypeStruct((rows, width), jnp.float32),
            jax.ShapeDtypeStruct((KVH, length, PAIR), jnp.float32),
            jax.ShapeDtypeStruct((KVH, length, PAIR), jnp.float32),
        ],
        compiler_params=pltpu.CompilerParams(vmem_limit_bytes=48 * 1024 * 1024),
        name="attend_backward",
    )(query, grad, key_f, key_b, key_t, value_f, value_b, bias, log_sum)


def by_head(matrix):
    rows = matrix.shape[0]
    return matrix.reshape(rows, KVH, HD).transpose(1, 0, 2)


MESH = pl.DeviceIdType.MESH


def flip(index, bit):
    return index + bit - 2 * bit * ((index // bit) % 2)


def line_order(place):
    nearest = place - 1 + 2 * (1 - (place + 3) // 4)
    farthest = 3 - 3 * (place // 2)
    return (nearest, 6 - place - nearest - farthest, farthest)


def enter(dp, place):
    barrier = pltpu.get_barrier_semaphore()
    for bit in (1, 2, 4):
        pl.semaphore_signal(barrier, inc=1, device_id=(flip(dp, bit), place), device_id_type=MESH)
    for step in (-1, 1):
        there = (place + step >= 0) & (place + step < 4)

        @pl.when(there)
        def _():
            pl.semaphore_signal(
                barrier, inc=1, device_id=(dp, place + step), device_id_type=MESH
            )

    ends = 1 - ((place + 3) // 4) + place // 3
    pl.semaphore_wait(barrier, 5 - ends)


def gather_kernel(
    kv_ref, q_ref, o_ref, d_ref, g_ref, u_ref, c_ref,
    fkv, fq, fo, fd, fg, fu, fc,
    own_sem, z_send, z_recv, p_send, p_recv,
):
    dp, place = lax.axis_index("dp"), lax.axis_index("tensor")
    rows = kv_ref.shape[0]
    half = rows // 2
    width = q_ref.shape[1]
    order = line_order(place)
    enter(dp, place)

    def rows_of(owner):
        return pl.ds(pl.multiple_of(owner * rows, rows), rows)

    def columns_of_rank(rank):
        return pl.ds(pl.multiple_of(rank * width, width), width)

    def remote(src, dst, send, recv, device):
        return pltpu.make_async_remote_copy(
            src_ref=src, dst_ref=dst, send_sem=send, recv_sem=recv,
            device_id=device, device_id_type=MESH,
        )

    own = [
        (kv_ref, fkv.at[rows_of(dp), :]),
        (q_ref, fq.at[rows_of(dp), columns_of_rank(place)]),
        (o_ref, fo.at[rows_of(dp), columns_of_rank(place)]),
        (d_ref, fd.at[rows_of(dp), :]),
        (g_ref, fg.at[rows_of(dp), :]),
        (u_ref, fu.at[rows_of(dp), :]),
        (c_ref, fc.at[rows_of(place), :]),
    ]
    own_copies = [
        pltpu.make_async_copy(src, dst, own_sem.at[i]) for i, (src, dst) in enumerate(own)
    ]
    for copy in own_copies:
        copy.start()

    def line_block(which, rank):
        if which == 2:
            return fc.at[rows_of(rank), :]
        return (fq, fo)[which].at[rows_of(dp), columns_of_rank(rank)]

    def line_copy(which, rank, step):
        src = (q_ref, o_ref, c_ref)[which] if rank is place else line_block(which, rank)
        side = 0 if step < 0 else 1
        return remote(
            src, line_block(which, rank), z_send.at[which, side, rank], z_recv.at[which, rank],
            (dp, place + step),
        )

    def line_send(which, rank, act):
        @pl.when((rank <= place) & (place < 3))
        def _():
            act(line_copy(which, rank, 1))

        @pl.when((rank >= place) & (place > 0))
        def _():
            act(line_copy(which, rank, -1))

    def start(copy):
        copy.start()

    def wait_send(copy):
        copy.wait_send()

    x, y, core = flip(dp, 2), flip(dp, 4), flip(dp, 1)
    far = flip(x, 4)

    blocks = [("kv", None), ("q", place), ("q", order[0]), ("q", order[1]), ("q", order[2])]
    blocks += [("o", place), ("o", order[0]), ("o", order[1]), ("o", order[2])]
    blocks += [("d", None), ("g", None), ("u", None)]

    def block(index, owner, part=None):
        name, rank = blocks[index]
        ref = {"kv": fkv, "q": fq, "o": fo, "d": fd, "g": fg, "u": fu}[name]
        first = owner * rows if part is None else owner * rows + part * half
        size = rows if part is None else half
        window = pl.ds(pl.multiple_of(first, half), size)
        if rank is None:
            return ref.at[window, :]
        return ref.at[window, columns_of_rank(rank)]

    def own_block(index):
        name, rank = blocks[index]
        if rank is None or rank is place:
            return {"kv": kv_ref, "q": q_ref, "o": o_ref, "d": d_ref, "g": g_ref, "u": u_ref}[name]
        return block(index, dp)

    def plane_copy(index, lane):
        send, recv = p_send.at[index, lane], p_recv.at[index, lane]
        if lane == 0:
            return remote(own_block(index), block(index, dp), send, recv, (x, place))
        if lane == 1:
            return remote(own_block(index), block(index, dp), send, recv, (y, place))
        if lane == 2:
            return remote(block(index, x, 0), block(index, x, 0), send, recv, (y, place))
        if lane == 3:
            return remote(block(index, y, 1), block(index, y, 1), send, recv, (x, place))
        owner = (dp, x, y, far)[lane - 4]
        src = own_block(index) if lane == 4 else block(index, owner)
        return remote(src, block(index, owner), send, recv, (core, place))

    def plane_first(index):
        plane_copy(index, 0).start()
        plane_copy(index, 1).start()
        plane_copy(index, 4).start()

    def plane_second(index):
        plane_copy(index, 0).wait_recv()
        plane_copy(index, 2).start()
        plane_copy(index, 5).start()
        plane_copy(index, 1).wait_recv()
        plane_copy(index, 3).start()
        plane_copy(index, 6).start()

    def plane_third(index):
        plane_copy(index, 2).wait_recv()
        plane_copy(index, 3).wait_recv()
        plane_copy(index, 7).start()

    def plane_last(index):
        for lane in range(4, 8):
            plane_copy(index, lane).wait_recv()
        for lane in range(8):
            plane_copy(index, lane).wait_send()

    line_send(0, place, start)
    plane_first(0)
    plane_first(1)
    line_send(1, place, start)
    line_send(2, place, start)
    count = len(blocks)
    line_of = {2: (0, 0), 3: (0, 1), 4: (0, 2), 6: (1, 0), 7: (1, 1), 8: (1, 2)}
    for index in range(count):
        ahead = index + 2
        if ahead < count:
            if ahead in line_of:
                which, step = line_of[ahead]
                line_copy(which, order[step], 1).wait_recv()
                line_send(which, order[step], start)
            plane_first(ahead)
        if ahead in (7, 9, 10):
            step = (7, 9, 10).index(ahead)
            line_copy(2, order[step], 1).wait_recv()
            line_send(2, order[step], start)
        plane_second(index)
        if index >= 1:
            plane_third(index - 1)
    plane_third(count - 1)
    for index in range(count):
        plane_last(index)
    for which in range(3):
        line_send(which, place, wait_send)
        for step in range(3):
            line_send(which, order[step], wait_send)
    for copy in own_copies:
        copy.wait()


def gather_all(w_keyval, w_query, w_output, w_down, w_gate, w_up, cotangent):
    n_dp, n_line = lax.axis_size("dp"), lax.axis_size("tensor")

    def over(array, rows, columns):
        shape = (array.shape[0] * rows, array.shape[1] * columns)
        return jax.ShapeDtypeStruct(shape, array.dtype)

    anywhere = pl.BlockSpec(memory_space=pl.ANY)
    shapes = [
        over(w_keyval, n_dp, 1),
        over(w_query, n_dp, n_line),
        over(w_output, n_dp, n_line),
        over(w_down, n_dp, 1),
        over(w_gate, n_dp, 1),
        over(w_up, n_dp, 1),
        over(cotangent, n_line, 1),
    ]
    return pl.pallas_call(
        gather_kernel,
        out_shape=shapes,
        in_specs=[anywhere] * 7,
        out_specs=[anywhere] * 7,
        scratch_shapes=[
            pltpu.SemaphoreType.DMA((7,)),
            pltpu.SemaphoreType.DMA((3, 2, 4)),
            pltpu.SemaphoreType.DMA((3, 4)),
            pltpu.SemaphoreType.DMA((12, 8)),
            pltpu.SemaphoreType.DMA((12, 8)),
        ],
        compiler_params=pltpu.CompilerParams(collective_id=0, has_side_effects=True),
        name="gather_all",
    )(w_keyval, w_query, w_output, w_down, w_gate, w_up, cotangent)


def local(
    tokens,
    segments,
    gain_attn,
    w_query,
    w_keyval,
    w_output,
    gain_mlp,
    w_gate,
    w_up,
    w_down,
    cotangent,
):
    tensor_rank = lax.axis_index("tensor")
    length = segments.shape[0]
    rows = tokens.shape[0]
    both = ("dp", "tensor")
    low = jnp.bfloat16

    def gather(array, axes, axis=0):
        return lax.all_gather(array, axes, axis=axis, tiled=True)

    def scatter(array, axes, axis=0):
        return lax.psum_scatter(array, axes, scatter_dimension=axis, tiled=True)

    if (lax.axis_size("dp"), lax.axis_size("tensor")) == (8, 4):
        full_keyval, full_query, full_output, full_down, full_gate, full_up, piece = gather_all(
            w_keyval, w_query, w_output, w_down, w_gate, w_up, cotangent
        )
    else:
        full_keyval = gather(w_keyval, "dp")
        full_query = gather(gather(w_query, "tensor", 1), "dp")
        full_output = gather(gather(w_output, "tensor", 1), "dp")
        full_gate, full_up = gather(w_gate, "dp"), gather(w_up, "dp")
        full_down = gather(w_down, "dp")
        piece = gather(cotangent, "tensor")
    places = doc_positions(segments)
    my_places = lax.dynamic_slice_in_dim(places, tensor_rank * rows, rows, 0)
    my_segments = lax.dynamic_slice_in_dim(segments, tensor_rank * rows, rows, 0)
    cosine, sine_table = rope_tables(my_places, HD)
    order = jnp.arange(length, dtype=jnp.int32)
    allowed = (order[:, None] <= tensor_rank * rows + order[None, :rows]) & (
        segments[:, None] == my_segments[None, :]
    )
    bias = jnp.where(allowed, 0.0, masked).astype(jnp.float32)

    token_rows = tokens.astype(jnp.float32)
    normed_attn, unit_attn, inverse_attn = norm_forward(token_rows, gain_attn)
    normed_attn = normed_attn.astype(low)
    keyval_pre = dot_nn(normed_attn, full_keyval)
    wide = KVH * HD
    key_low = rotate(keyval_pre[:, :wide], cosine, sine_table).astype(low)
    keyval = gather(jnp.concatenate([key_low, keyval_pre[:, wide:].astype(low)], axis=1), "tensor")
    key_heads, value_heads = by_head(keyval[:, :wide]), by_head(keyval[:, wide:])
    blank = jnp.zeros_like(key_heads)
    key_f = jnp.concatenate([key_heads, blank], axis=2)
    key_b = jnp.concatenate([blank, key_heads], axis=2)
    value_f = jnp.concatenate([value_heads, blank], axis=2)
    value_b = jnp.concatenate([blank, value_heads], axis=2)
    key_t = key_heads.transpose(0, 2, 1)
    value_t = value_heads.transpose(0, 2, 1)

    query = (rotate(dot_nn(normed_attn, full_query), cosine, sine_table) * (HD**-0.5)).astype(low)
    heads_low, log_sum = attend_forward(query, key_f, key_b, value_t, bias)
    residual = token_rows + dot_nt(heads_low, full_output)

    normed_mlp, unit_mlp, inverse_mlp = norm_forward(residual, gain_mlp)
    gathered_mlp = gather(normed_mlp.astype(low), "tensor")
    gate_act = dot_nn(gathered_mlp, full_gate)
    up_act = dot_nn(gathered_mlp, full_up)
    sigmoid_gate = jax.nn.sigmoid(gate_act)
    silu_gate = gate_act * sigmoid_gate
    hidden_low = (silu_gate * up_act).astype(low)
    d_hidden = dot_nn(piece, full_down)
    d_gate = (d_hidden * up_act * sigmoid_gate * (1.0 + gate_act * (1.0 - sigmoid_gate))).astype(low)
    d_up = (d_hidden * silu_gate).astype(low)
    d_normed_mlp = scatter(
        (dot_nt(d_gate, full_gate) + dot_nt(d_up, full_up)).astype(low), "tensor"
    ).astype(jnp.float32)
    layer_rows = residual + scatter(dot_nt(hidden_low, full_down).astype(low), "tensor").astype(
        jnp.float32
    )
    grad_down = dot_tn(piece, hidden_low)
    grad_gate = dot_tn(gathered_mlp, d_gate)
    grad_up = dot_tn(gathered_mlp, d_up)
    d_norm_mlp, gain_mlp_part = norm_backward(d_normed_mlp, unit_mlp, inverse_mlp, gain_mlp)
    d_residual = cotangent.astype(jnp.float32) + d_norm_mlp

    d_branch = d_residual.astype(low)
    grad_output = dot_tn(d_branch, heads_low)
    d_heads = dot_nn(d_branch, full_output).astype(low)
    d_queries, d_keys, d_values = attend_backward(
        query, d_heads, key_f, key_b, key_t, value_f, value_b, bias, log_sum
    )

    def flat(parts):
        joined = parts[:, :, :HD] + parts[:, :, HD:]
        return joined.transpose(1, 0, 2).reshape(length, wide)

    d_keyval = scatter(
        jnp.concatenate([flat(d_keys), flat(d_values)], axis=1).astype(low), "tensor"
    ).astype(jnp.float32)
    dq_low = rotate(d_queries, cosine, -sine_table).astype(low)
    dkv_low = jnp.concatenate(
        [rotate(d_keyval[:, :wide], cosine, -sine_table), d_keyval[:, wide:]], axis=1
    ).astype(low)
    grad_query = dot_tn(normed_attn, dq_low)
    grad_keyval = dot_tn(normed_attn, dkv_low)
    d_normed_attn = dot_nt(dq_low, full_query) + dot_nt(dkv_low, full_keyval)
    d_norm_attn, gain_attn_part = norm_backward(d_normed_attn, unit_attn, inverse_attn, gain_attn)
    grad_tokens = (d_residual + d_norm_attn).astype(low)

    def shares(grad):
        return scatter(grad.astype(low), "dp").astype(jnp.float32)

    def square_shares(grad):
        return scatter(scatter(grad.astype(low), "dp"), "tensor", 1).astype(jnp.float32)

    gains = scatter(
        jnp.stack([gain_attn_part, gain_mlp_part]).reshape(2, -1, rows_of_gain(gain_attn)), both, 1
    )
    return (
        layer_rows.astype(low),
        grad_tokens,
        gains[0, 0],
        square_shares(grad_query),
        scatter(grad_keyval.astype(low), both).astype(jnp.float32),
        square_shares(grad_output),
        gains[1, 0],
        shares(grad_gate),
        shares(grad_up),
        shares(grad_down),
    )


def rows_of_gain(gain):
    return gain.shape[0] // (lax.axis_size("dp") * lax.axis_size("tensor"))


def solution(mesh):
    return jax.shard_map(
        local,
        mesh=mesh,
        in_specs=(
            P(("dp", "tensor"), None),
            P("dp"),
            P(),
            P("dp", "tensor"),
            P("dp", None),
            P("dp", "tensor"),
            P(),
            P("dp", "tensor"),
            P("dp", "tensor"),
            P("dp", "tensor"),
            P(("dp", "tensor"), None),
        ),
        out_specs=(
            P(("dp", "tensor"), None),
            P(("dp", "tensor"), None),
            P(("dp", "tensor")),
            P("dp", "tensor"),
            P(("dp", "tensor"), None),
            P("dp", "tensor"),
            P(("dp", "tensor")),
            P("dp", "tensor"),
            P("dp", "tensor"),
            P("dp", "tensor"),
        ),
        check_vma=False,
    )
```

```python
import functools

import jax
import jax.numpy as jnp
from jax import lax
from jax.experimental import pallas as pl
from jax.experimental.pallas import tpu as pltpu
from jax.sharding import PartitionSpec as P

KVH = 4
HD = 64
PAIR = 2 * HD

epsilon = 1e-05
rope_base = 10000.0
masked = -1e30


def doc_positions(seg_row):
    length = seg_row.shape[0]
    places = jnp.arange(length, dtype=jnp.int32)
    change = jnp.concatenate([jnp.ones((1,), jnp.bool_), seg_row[1:] != seg_row[:-1]])
    starts = lax.cummax(jnp.where(change, places, 0), axis=0)
    return places - starts


def rope_tables(places, width):
    half_width = width // 2
    frequency = rope_base ** (-(2.0 * jnp.arange(half_width).astype(jnp.float32)) / width)
    angles = places.astype(jnp.float32)[:, None] * frequency[None, :]
    return (jnp.cos(angles), jnp.sin(angles))


def rotate(values, cosine, sine_table):
    rows, width = values.shape
    heads = values.reshape(rows, width // HD, HD)
    half_width = HD // 2
    front_half = heads[..., :half_width]
    back_half = heads[..., half_width:]
    cos_rows = cosine[:, None, :]
    sin_rows = sine_table[:, None, :]
    turned = jnp.concatenate(
        [
            front_half * cos_rows - back_half * sin_rows,
            back_half * cos_rows + front_half * sin_rows,
        ],
        axis=-1,
    )
    return turned.reshape(rows, width)


def norm_forward(values, gain_vec):
    inverse = lax.rsqrt(jnp.mean(values * values, axis=-1, keepdims=True) + epsilon)
    unit_rows = values * inverse
    return (unit_rows * gain_vec, unit_rows, inverse)


def norm_backward(d_normed, unit_rows, inverse, gain_vec):
    gain_part = jnp.sum(d_normed * unit_rows, axis=0)
    d_unit = d_normed * gain_vec
    d_values = inverse * (d_unit - unit_rows * jnp.mean(d_unit * unit_rows, axis=-1, keepdims=True))
    return (d_values, gain_part)


def dot_nn(left, right):
    return jnp.dot(left, right, preferred_element_type=jnp.float32)


def dot_nt(left, right):
    return lax.dot_general(
        left, right, (((1,), (1,)), ((), ())), preferred_element_type=jnp.float32
    )


def dot_tn(left, right):
    return lax.dot_general(
        left, right, (((0,), (0,)), ((), ())), preferred_element_type=jnp.float32
    )


def front_lanes(tile):
    lane = lax.broadcasted_iota(jnp.int32, tile.shape, 1)
    return jnp.where(lane < HD, tile, jnp.zeros_like(tile))


def back_lanes(tile):
    lane = lax.broadcasted_iota(jnp.int32, tile.shape, 1)
    return jnp.where(lane < HD, jnp.zeros_like(tile), tile)


def attend_forward_kernel(query_ref, front_ref, back_ref, value_t_ref, bias_ref, out_ref, log_ref):
    pairs = query_ref.shape[1] // PAIR
    value_t = value_t_ref[0]
    for pair in range(pairs):
        query = query_ref[:, pair * PAIR : (pair + 1) * PAIR]
        outs = []
        for side, key_ref in enumerate((front_ref, back_ref)):
            scores = dot_nt(key_ref[0], query) + bias_ref[...]
            top = jnp.max(scores, axis=0, keepdims=True)
            expo = jnp.exp(scores - top)
            total = jnp.sum(expo, axis=0, keepdims=True)
            outs.append(dot_nn(value_t, expo.astype(jnp.bfloat16)) / total)
            log_ref[0, pl.ds(pair * 2 + side, 1), :] = top + jnp.log(total)
        out = jnp.concatenate(outs, axis=0).T
        out_ref[:, pair * PAIR : (pair + 1) * PAIR] = out.astype(jnp.bfloat16)


def attend_backward_kernel(
    query_ref,
    grad_ref,
    kf_ref,
    kb_ref,
    kt_ref,
    vf_ref,
    vb_ref,
    bias_ref,
    log_ref,
    dq_ref,
    dk_ref,
    dv_ref,
):
    pairs = query_ref.shape[1] // PAIR
    key_t = kt_ref[0]
    dk_ref[0] = jnp.zeros(dk_ref.shape[1:], jnp.float32)
    dv_ref[0] = jnp.zeros(dv_ref.shape[1:], jnp.float32)
    for pair in range(pairs):
        columns = slice(pair * PAIR, (pair + 1) * PAIR)
        query = query_ref[:, columns]
        grad = grad_ref[:, columns]
        outs = []
        for side, (key_ref, value_ref, keep) in enumerate(
            ((kf_ref, vf_ref, front_lanes), (kb_ref, vb_ref, back_lanes))
        ):
            log_sum = log_ref[0, pl.ds(pair * 2 + side, 1), :]
            probs = jnp.exp(dot_nt(key_ref[0], query) + bias_ref[...] - log_sum)
            d_probs = dot_nt(value_ref[0], grad)
            row_dot = jnp.sum(probs * d_probs, axis=0, keepdims=True)
            d_scores = (probs * (d_probs - row_dot)).astype(jnp.bfloat16)
            dk_ref[0] += dot_nn(d_scores, keep(query))
            dv_ref[0] += dot_nn(probs.astype(jnp.bfloat16), keep(grad))
            outs.append(dot_nn(key_t, d_scores))
        dq_ref[:, columns] = jnp.concatenate(outs, axis=0).T * (HD**-0.5)


def whole_group(rows, width):
    return pl.BlockSpec((1, rows, width), lambda g: (g, 0, 0))


def columns_of(rows, width):
    return pl.BlockSpec((rows, width), lambda g: (0, g))


def attend_forward(query, key_f, key_b, value_t, bias):
    rows, width = query.shape
    length = bias.shape[0]
    group = width // KVH
    return pl.pallas_call(
        attend_forward_kernel,
        grid=(KVH,),
        in_specs=[
            columns_of(rows, group),
            whole_group(length, PAIR),
            whole_group(length, PAIR),
            whole_group(HD, length),
            pl.BlockSpec((length, rows), lambda g: (0, 0)),
        ],
        out_specs=[columns_of(rows, group), whole_group(group // HD, rows)],
        out_shape=[
            jax.ShapeDtypeStruct((rows, width), jnp.bfloat16),
            jax.ShapeDtypeStruct((KVH, group // HD, rows), jnp.float32),
        ],
        compiler_params=pltpu.CompilerParams(vmem_limit_bytes=48 * 1024 * 1024),
        name="attend_forward",
    )(query, key_f, key_b, value_t, bias)


def attend_backward(query, grad, key_f, key_b, key_t, value_f, value_b, bias, log_sum):
    rows, width = query.shape
    length = bias.shape[0]
    group = width // KVH
    tall = whole_group(length, PAIR)
    return pl.pallas_call(
        attend_backward_kernel,
        grid=(KVH,),
        in_specs=[
            columns_of(rows, group),
            columns_of(rows, group),
            tall,
            tall,
            whole_group(HD, length),
            tall,
            tall,
            pl.BlockSpec((length, rows), lambda g: (0, 0)),
            whole_group(group // HD, rows),
        ],
        out_specs=[columns_of(rows, group), tall, tall],
        out_shape=[
            jax.ShapeDtypeStruct((rows, width), jnp.float32),
            jax.ShapeDtypeStruct((KVH, length, PAIR), jnp.float32),
            jax.ShapeDtypeStruct((KVH, length, PAIR), jnp.float32),
        ],
        compiler_params=pltpu.CompilerParams(vmem_limit_bytes=48 * 1024 * 1024),
        name="attend_backward",
    )(query, grad, key_f, key_b, key_t, value_f, value_b, bias, log_sum)


def by_head(matrix):
    rows = matrix.shape[0]
    return matrix.reshape(rows, KVH, HD).transpose(1, 0, 2)


MESH = pl.DeviceIdType.MESH


def flip(index, bit):
    return index + bit - 2 * bit * ((index // bit) % 2)


def line_order(place):
    nearest = place - 1 + 2 * (1 - (place + 3) // 4)
    farthest = 3 - 3 * (place // 2)
    return (nearest, 6 - place - nearest - farthest, farthest)


def enter(dp, place):
    barrier = pltpu.get_barrier_semaphore()
    for bit in (1, 2, 4):
        pl.semaphore_signal(barrier, inc=1, device_id=(flip(dp, bit), place), device_id_type=MESH)
    for step in (-1, 1):
        there = (place + step >= 0) & (place + step < 4)

        @pl.when(there)
        def _():
            pl.semaphore_signal(
                barrier, inc=1, device_id=(dp, place + step), device_id_type=MESH
            )

    ends = 1 - ((place + 3) // 4) + place // 3
    pl.semaphore_wait(barrier, 5 - ends)


def gather_kernel(
    kv_ref, q_ref, o_ref, d_ref, g_ref, u_ref, c_ref,
    fkv, fq, fo, fd, fg, fu, fc,
    own_sem, z_send, z_recv, p_send, p_recv,
):
    dp, place = lax.axis_index("dp"), lax.axis_index("tensor")
    rows = kv_ref.shape[0]
    half = rows // 2
    width = q_ref.shape[1]
    order = line_order(place)
    enter(dp, place)

    def rows_of(owner):
        return pl.ds(pl.multiple_of(owner * rows, rows), rows)

    def columns_of_rank(rank):
        return pl.ds(pl.multiple_of(rank * width, width), width)

    def remote(src, dst, send, recv, device):
        return pltpu.make_async_remote_copy(
            src_ref=src, dst_ref=dst, send_sem=send, recv_sem=recv,
            device_id=device, device_id_type=MESH,
        )

    own = [
        (kv_ref, fkv.at[rows_of(dp), :]),
        (q_ref, fq.at[rows_of(dp), columns_of_rank(place)]),
        (o_ref, fo.at[rows_of(dp), columns_of_rank(place)]),
        (d_ref, fd.at[rows_of(dp), :]),
        (g_ref, fg.at[rows_of(dp), :]),
        (u_ref, fu.at[rows_of(dp), :]),
        (c_ref, fc.at[rows_of(place), :]),
    ]
    own_copies = [
        pltpu.make_async_copy(src, dst, own_sem.at[i]) for i, (src, dst) in enumerate(own)
    ]
    for copy in own_copies:
        copy.start()

    def line_block(which, rank):
        if which == 2:
            return fc.at[rows_of(rank), :]
        return (fq, fo)[which].at[rows_of(dp), columns_of_rank(rank)]

    def line_copy(which, rank, step):
        src = (q_ref, o_ref, c_ref)[which] if rank is place else line_block(which, rank)
        side = 0 if step < 0 else 1
        return remote(
            src, line_block(which, rank), z_send.at[which, side, rank], z_recv.at[which, rank],
            (dp, place + step),
        )

    def line_send(which, rank, act):
        @pl.when((rank <= place) & (place < 3))
        def _():
            act(line_copy(which, rank, 1))

        @pl.when((rank >= place) & (place > 0))
        def _():
            act(line_copy(which, rank, -1))

    def start(copy):
        copy.start()

    def wait_send(copy):
        copy.wait_send()

    x, y, core = flip(dp, 2), flip(dp, 4), flip(dp, 1)
    far = flip(x, 4)

    blocks = [("kv", None), ("q", place), ("q", order[0]), ("q", order[1]), ("q", order[2])]
    blocks += [("o", place), ("o", order[0]), ("o", order[1]), ("o", order[2])]
    blocks += [("d", None), ("g", None), ("u", None)]

    def block(index, owner, part=None):
        name, rank = blocks[index]
        ref = {"kv": fkv, "q": fq, "o": fo, "d": fd, "g": fg, "u": fu}[name]
        first = owner * rows if part is None else owner * rows + part * half
        size = rows if part is None else half
        window = pl.ds(pl.multiple_of(first, half), size)
        if rank is None:
            return ref.at[window, :]
        return ref.at[window, columns_of_rank(rank)]

    def own_block(index):
        name, rank = blocks[index]
        if rank is None or rank is place:
            return {"kv": kv_ref, "q": q_ref, "o": o_ref, "d": d_ref, "g": g_ref, "u": u_ref}[name]
        return block(index, dp)

    def plane_copy(index, lane):
        send, recv = p_send.at[index, lane], p_recv.at[index, lane]
        if lane == 0:
            return remote(own_block(index), block(index, dp), send, recv, (x, place))
        if lane == 1:
            return remote(own_block(index), block(index, dp), send, recv, (y, place))
        if lane == 2:
            return remote(block(index, x, 0), block(index, x, 0), send, recv, (y, place))
        if lane == 3:
            return remote(block(index, y, 1), block(index, y, 1), send, recv, (x, place))
        owner = (dp, x, y, far)[lane - 4]
        src = own_block(index) if lane == 4 else block(index, owner)
        return remote(src, block(index, owner), send, recv, (core, place))

    def plane_first(index):
        plane_copy(index, 0).start()
        plane_copy(index, 1).start()
        plane_copy(index, 4).start()

    def plane_second(index):
        plane_copy(index, 0).wait_recv()
        plane_copy(index, 2).start()
        plane_copy(index, 5).start()
        plane_copy(index, 1).wait_recv()
        plane_copy(index, 3).start()
        plane_copy(index, 6).start()

    def plane_third(index):
        plane_copy(index, 2).wait_recv()
        plane_copy(index, 3).wait_recv()
        plane_copy(index, 7).start()

    def plane_last(index):
        for lane in range(4, 8):
            plane_copy(index, lane).wait_recv()
        for lane in range(8):
            plane_copy(index, lane).wait_send()

    line_send(0, place, start)
    plane_first(0)
    plane_first(1)
    line_send(1, place, start)
    line_send(2, place, start)
    count = len(blocks)
    line_of = {2: (0, 0), 3: (0, 1), 4: (0, 2), 6: (1, 0), 7: (1, 1), 8: (1, 2)}
    for index in range(count):
        ahead = index + 2
        if ahead < count:
            if ahead in line_of:
                which, step = line_of[ahead]
                line_copy(which, order[step], 1).wait_recv()
                line_send(which, order[step], start)
            plane_first(ahead)
        if ahead in (7, 9, 10):
            step = (7, 9, 10).index(ahead)
            line_copy(2, order[step], 1).wait_recv()
            line_send(2, order[step], start)
        plane_second(index)
        if index >= 1:
            plane_third(index - 1)
    plane_third(count - 1)
    for index in range(count):
        plane_last(index)
    for which in range(3):
        line_send(which, place, wait_send)
        for step in range(3):
            line_send(which, order[step], wait_send)
    for copy in own_copies:
        copy.wait()


def gather_all(w_keyval, w_query, w_output, w_down, w_gate, w_up, cotangent):
    n_dp, n_line = lax.axis_size("dp"), lax.axis_size("tensor")

    def over(array, rows, columns):
        shape = (array.shape[0] * rows, array.shape[1] * columns)
        return jax.ShapeDtypeStruct(shape, array.dtype)

    anywhere = pl.BlockSpec(memory_space=pl.ANY)
    shapes = [
        over(w_keyval, n_dp, 1),
        over(w_query, n_dp, n_line),
        over(w_output, n_dp, n_line),
        over(w_down, n_dp, 1),
        over(w_gate, n_dp, 1),
        over(w_up, n_dp, 1),
        over(cotangent, n_line, 1),
    ]
    return pl.pallas_call(
        gather_kernel,
        out_shape=shapes,
        in_specs=[anywhere] * 7,
        out_specs=[anywhere] * 7,
        scratch_shapes=[
            pltpu.SemaphoreType.DMA((7,)),
            pltpu.SemaphoreType.DMA((3, 2, 4)),
            pltpu.SemaphoreType.DMA((3, 4)),
            pltpu.SemaphoreType.DMA((12, 8)),
            pltpu.SemaphoreType.DMA((12, 8)),
        ],
        compiler_params=pltpu.CompilerParams(collective_id=0, has_side_effects=True),
        name="gather_all",
    )(w_keyval, w_query, w_output, w_down, w_gate, w_up, cotangent)


def add_rows(target, source, step=32):
    @pl.loop(0, target.shape[0] // step)
    def _(index):
        window = pl.ds(pl.multiple_of(index * step, step), step)
        target[window, :] = target[window, :] + source[window, :]


def scatter_kernel(
    go_ref, gq_ref, kv_ref, gd_ref, gg_ref, gu_ref, branch_ref, residual_ref,
    go_out, gq_out, kv_out, gd_out, gg_out, gu_out, layer_out,
    go_core, gq_core, kv_core, gd_core, gg_core, gu_core,
    go_part, gq_part, kv_part, gd_part, gg_part, gu_part,
    go_side, gq_side, kv_side, gd_side, gg_side, gu_side,
    go_near, gq_near, kv_near, gd_near, gg_near, gu_near,
    go_line, gq_line, kv_line, layer_line,
    go_in, gq_in, kv_in, layer_in,
    held, total_ref,
    load_sem, core_load, core_send, core_recv, p_send, p_recv, l_send, l_recv, layer_load,
):
    dp, place = lax.axis_index("dp"), lax.axis_index("tensor")
    rows = go_part.shape[1]
    half = rows // 2
    enter(dp, place)
    x, y, core = flip(dp, 2), flip(dp, 4), flip(dp, 1)
    far = flip(x, 4)
    mine = (dp, x, y, far)
    theirs = tuple(flip(owner, 1) for owner in mine)
    grads = (go_ref, gq_ref, kv_ref, gd_ref, gg_ref, gu_ref)
    outs = (go_out, gq_out, kv_out, gd_out, gg_out, gu_out)
    cores = (go_core, gq_core, kv_core, gd_core, gg_core, gu_core)
    parts = (go_part, gq_part, kv_part, gd_part, gg_part, gu_part)
    sides = (go_side, gq_side, kv_side, gd_side, gg_side, gu_side)
    nears = (go_near, gq_near, kv_near, gd_near, gg_near, gu_near)
    lines = (go_line, gq_line, kv_line, layer_line)
    arrivals = (go_in, gq_in, kv_in, layer_in)
    count = len(grads)
    front, back = pl.ds(0, half), pl.ds(half, half)

    def rows_of(owner):
        return pl.ds(pl.multiple_of(owner * rows, rows), rows)

    def remote(src, dst, send, recv, device):
        return pltpu.make_async_remote_copy(
            src_ref=src, dst_ref=dst, send_sem=send, recv_sem=recv,
            device_id=device, device_id_type=MESH,
        )

    def core_copy(i, k):
        return remote(
            grads[i].at[rows_of(theirs[k]), :], cores[i].at[k],
            core_send.at[i, k], core_recv.at[i, k], (core, place),
        )

    def own_load(i, k):
        return pltpu.make_async_copy(
            grads[i].at[rows_of(mine[k]), :], parts[i].at[k], load_sem.at[i, k]
        )

    def core_fetch(i, k):
        width = grads[i].shape[1]
        return pltpu.make_async_copy(
            cores[i].at[k], held.at[k, :, pl.ds(0, width)], core_load.at[k]
        )

    def plane_copy(i, lane):
        part = parts[i]
        src, dst, device = (
            (part.at[3, front, :], sides[i].at[0], y),
            (part.at[3, back, :], sides[i].at[1], x),
            (part.at[1, back, :], nears[i].at[0, back, :], x),
            (part.at[2, front, :], nears[i].at[1, front, :], y),
            (part.at[1, front, :], nears[i].at[0, front, :], x),
            (part.at[2, back, :], nears[i].at[1, back, :], y),
        )[lane]
        return remote(src, dst, p_send.at[i, lane], p_recv.at[i, lane], (device, place))

    def stage_core(i):
        width = grads[i].shape[1]
        for k in (3, 1, 2, 0):
            core_copy(i, k).wait_recv()
            core_fetch(i, k).start()
        for k in (3, 1, 2, 0):
            core_fetch(i, k).wait()
            own_load(i, k).wait()
            add_rows(parts[i].at[k], held.at[k, :, pl.ds(0, width)])
            for lane in ((), (2,), (3,), (0, 1))[k]:
                plane_copy(i, lane).start()

    def stage_side(i):
        plane_copy(i, 0).wait_recv()
        add_rows(parts[i].at[1, front, :], sides[i].at[0])
        plane_copy(i, 4).start()
        plane_copy(i, 1).wait_recv()
        add_rows(parts[i].at[2, back, :], sides[i].at[1])
        plane_copy(i, 5).start()

    def stage_near(i):
        for lane in (2, 3, 4, 5):
            plane_copy(i, lane).wait_recv()
        part, near, out = parts[i], nears[i], outs[i]

        @pl.loop(0, rows // 32)
        def _(index):
            window = pl.ds(pl.multiple_of(index * 32, 32), 32)
            total = (
                part[0, window, :].astype(jnp.float32)
                + near[0, window, :].astype(jnp.float32)
                + near[1, window, :].astype(jnp.float32)
            )
            if i >= 3:
                out[window, :] = total
            elif i < 2:
                width = lines[i].shape[2]
                for rank in range(4):
                    lines[i][rank, window, :] = total[:, rank * width : (rank + 1) * width].astype(
                        jnp.bfloat16
                    )
            else:
                per = rows // 4
                lines[i][index * 32 // per, pl.ds(pl.multiple_of(index * 32 % per, 32), 32), :] = (
                    total.astype(jnp.bfloat16)
                )

    def line_copy(i, rank, slot, step):
        return remote(
            lines[i].at[rank], arrivals[i].at[slot], l_send.at[i, rank], l_recv.at[i, slot],
            (dp, place + step),
        )

    def line_step(i, step):
        down, up = place - 3 + step, place + 3 - step

        @pl.when(down >= 0)
        def _():
            @pl.when(place < 3)
            def _():
                line_copy(i, down, down, -1).wait_recv()
                add_rows(lines[i].at[down], arrivals[i].at[down])

            line_copy(i, down, down, -1).start()

        @pl.when(up <= 3)
        def _():
            @pl.when(place > 0)
            def _():
                line_copy(i, up, up, 1).wait_recv()
                add_rows(lines[i].at[up], arrivals[i].at[up])

            line_copy(i, up, 4 if step == 2 else up, 1).start()

    def line_last(i, begin, add, finish):
        begin(lines[i].at[place])

        @pl.when(place < 3)
        def _():
            line_copy(i, place, place, 1).wait_recv()
            add(arrivals[i].at[place])

        @pl.when(place > 0)
        def _():
            line_copy(i, place, 4, 1).wait_recv()
            add(arrivals[i].at[4])

        finish()

    def line_sent(i):
        for rank in range(4):

            @pl.when(rank != place)
            def _():
                line_copy(i, rank, rank, 1).wait_send()

    def by_rows(total_rows, act):
        @pl.loop(0, total_rows // 32)
        def _(index):
            act(pl.ds(pl.multiple_of(index * 32, 32), 32))

    def line_out(i):
        out = outs[i]
        size = out.shape[0]

        def begin(ref):
            def act(window):
                out[window, :] = ref[window, :].astype(jnp.float32)

            by_rows(size, act)

        def add(ref):
            def act(window):
                out[window, :] += ref[window, :].astype(jnp.float32)

            by_rows(size, act)

        line_last(i, begin, add, lambda: None)

    branch_load = pltpu.make_async_copy(branch_ref, layer_line, layer_load)
    branch_load.start()
    for i in range(count):
        for k in (3, 1, 2, 0):
            core_copy(i, k).start()
            own_load(i, k).start()
    branch_load.wait()
    line_step(3, 0)
    for i in range(count + 2):
        if i < count:
            stage_core(i)
        if 1 <= i <= count:
            stage_side(i - 1)
        if i >= 2:
            stage_near(i - 2)
        for j in range(3):
            if 0 <= i - 2 - j < 3:
                line_step(j, i - 2 - j)
        if i in (2, 4):
            line_step(3, i // 2)
    for j in range(3):
        line_out(j)

    def layer_begin(ref):
        def act(window):
            total_ref[window, :] = residual_ref[window, :] + ref[window, :].astype(jnp.float32)

        by_rows(rows, act)

    def layer_add(ref):
        def act(window):
            total_ref[window, :] += ref[window, :].astype(jnp.float32)

        by_rows(rows, act)

    def layer_finish():
        def act(window):
            layer_out[window, :] = total_ref[window, :].astype(jnp.bfloat16)

        by_rows(rows, act)

    line_last(3, layer_begin, layer_add, layer_finish)
    for i in range(count):
        for k in range(4):
            core_copy(i, k).wait_send()
        for lane in range(6):
            plane_copy(i, lane).wait_send()
    for i in range(4):
        line_sent(i)


def scatter_all(grads, branch, residual):
    low = jnp.bfloat16
    n_line = lax.axis_size("tensor")
    rows = grads[0].shape[0] // lax.axis_size("dp")
    half = rows // 2
    widths = [grad.shape[1] for grad in grads]
    square = widths[0] // n_line
    few = rows // n_line
    tokens, width = residual.shape
    anywhere = pl.BlockSpec(memory_space=pl.ANY)
    in_vmem = pl.BlockSpec(memory_space=pltpu.VMEM)
    out_shape = [
        jax.ShapeDtypeStruct((rows, square), jnp.float32),
        jax.ShapeDtypeStruct((rows, square), jnp.float32),
        jax.ShapeDtypeStruct((few, widths[2]), jnp.float32),
    ]
    out_shape += [jax.ShapeDtypeStruct((rows, w), jnp.float32) for w in widths[3:]]
    out_shape += [jax.ShapeDtypeStruct((tokens, width), low)]
    out_shape += [jax.ShapeDtypeStruct((4, rows, w), low) for w in widths]
    scratch = [pltpu.VMEM((4, rows, w), low) for w in widths]
    scratch += [pltpu.VMEM((2, half, w), low) for w in widths]
    scratch += [pltpu.VMEM((2, rows, w), low) for w in widths]
    line_shapes = [(rows, square), (rows, square), (few, widths[2]), (tokens, width)]
    scratch += [pltpu.VMEM((4,) + shape, low) for shape in line_shapes]
    scratch += [pltpu.VMEM((5,) + shape, low) for shape in line_shapes]
    scratch += [pltpu.VMEM((4, rows, max(widths)), low)]
    scratch += [pltpu.VMEM((tokens, width), jnp.float32)]
    dma = pltpu.SemaphoreType.DMA
    scratch += [
        dma((6, 4)), dma((4,)), dma((6, 4)), dma((6, 4)), dma((6, 6)), dma((6, 6)),
        dma((4, 4)), dma((4, 5)), dma,
    ]
    results = pl.pallas_call(
        scatter_kernel,
        out_shape=out_shape,
        in_specs=[anywhere] * 7 + [in_vmem],
        out_specs=[in_vmem] * 7 + [anywhere] * 6,
        scratch_shapes=scratch,
        compiler_params=pltpu.CompilerParams(
            collective_id=1, has_side_effects=True, vmem_limit_bytes=62 * 1024 * 1024
        ),
        name="scatter_all",
    )(*grads, branch.reshape(n_line, tokens, width), residual)
    return results[:7]


def local(
    tokens,
    segments,
    gain_attn,
    w_query,
    w_keyval,
    w_output,
    gain_mlp,
    w_gate,
    w_up,
    w_down,
    cotangent,
):
    tensor_rank = lax.axis_index("tensor")
    length = segments.shape[0]
    rows = tokens.shape[0]
    both = ("dp", "tensor")
    low = jnp.bfloat16

    def gather(array, axes, axis=0):
        return lax.all_gather(array, axes, axis=axis, tiled=True)

    def scatter(array, axes, axis=0):
        return lax.psum_scatter(array, axes, scatter_dimension=axis, tiled=True)

    by_kernels = (lax.axis_size("dp"), lax.axis_size("tensor")) == (8, 4)
    if by_kernels:
        full_keyval, full_query, full_output, full_down, full_gate, full_up, piece = gather_all(
            w_keyval, w_query, w_output, w_down, w_gate, w_up, cotangent
        )
    else:
        full_keyval = gather(w_keyval, "dp")
        full_query = gather(gather(w_query, "tensor", 1), "dp")
        full_output = gather(gather(w_output, "tensor", 1), "dp")
        full_gate, full_up = gather(w_gate, "dp"), gather(w_up, "dp")
        full_down = gather(w_down, "dp")
        piece = gather(cotangent, "tensor")
    places = doc_positions(segments)
    my_places = lax.dynamic_slice_in_dim(places, tensor_rank * rows, rows, 0)
    my_segments = lax.dynamic_slice_in_dim(segments, tensor_rank * rows, rows, 0)
    cosine, sine_table = rope_tables(my_places, HD)
    order = jnp.arange(length, dtype=jnp.int32)
    allowed = (order[:, None] <= tensor_rank * rows + order[None, :rows]) & (
        segments[:, None] == my_segments[None, :]
    )
    bias = jnp.where(allowed, 0.0, masked).astype(jnp.float32)

    token_rows = tokens.astype(jnp.float32)
    normed_attn, unit_attn, inverse_attn = norm_forward(token_rows, gain_attn)
    normed_attn = normed_attn.astype(low)
    keyval_pre = dot_nn(normed_attn, full_keyval)
    wide = KVH * HD
    key_low = rotate(keyval_pre[:, :wide], cosine, sine_table).astype(low)
    keyval = gather(jnp.concatenate([key_low, keyval_pre[:, wide:].astype(low)], axis=1), "tensor")
    key_heads, value_heads = by_head(keyval[:, :wide]), by_head(keyval[:, wide:])
    blank = jnp.zeros_like(key_heads)
    key_f = jnp.concatenate([key_heads, blank], axis=2)
    key_b = jnp.concatenate([blank, key_heads], axis=2)
    value_f = jnp.concatenate([value_heads, blank], axis=2)
    value_b = jnp.concatenate([blank, value_heads], axis=2)
    key_t = key_heads.transpose(0, 2, 1)
    value_t = value_heads.transpose(0, 2, 1)

    query = (rotate(dot_nn(normed_attn, full_query), cosine, sine_table) * (HD**-0.5)).astype(low)
    heads_low, log_sum = attend_forward(query, key_f, key_b, value_t, bias)
    residual = token_rows + dot_nt(heads_low, full_output)

    normed_mlp, unit_mlp, inverse_mlp = norm_forward(residual, gain_mlp)
    gathered_mlp = gather(normed_mlp.astype(low), "tensor")
    gate_act = dot_nn(gathered_mlp, full_gate)
    up_act = dot_nn(gathered_mlp, full_up)
    sigmoid_gate = jax.nn.sigmoid(gate_act)
    silu_gate = gate_act * sigmoid_gate
    hidden_low = (silu_gate * up_act).astype(low)
    d_hidden = dot_nn(piece, full_down)
    d_gate = (d_hidden * up_act * sigmoid_gate * (1.0 + gate_act * (1.0 - sigmoid_gate))).astype(low)
    d_up = (d_hidden * silu_gate).astype(low)
    d_normed_mlp = scatter(
        (dot_nt(d_gate, full_gate) + dot_nt(d_up, full_up)).astype(low), "tensor"
    ).astype(jnp.float32)
    branch = dot_nt(hidden_low, full_down).astype(low)
    grad_down = dot_tn(piece, hidden_low)
    grad_gate = dot_tn(gathered_mlp, d_gate)
    grad_up = dot_tn(gathered_mlp, d_up)
    d_norm_mlp, gain_mlp_part = norm_backward(d_normed_mlp, unit_mlp, inverse_mlp, gain_mlp)
    d_residual = cotangent.astype(jnp.float32) + d_norm_mlp

    d_branch = d_residual.astype(low)
    grad_output = dot_tn(d_branch, heads_low)
    d_heads = dot_nn(d_branch, full_output).astype(low)
    d_queries, d_keys, d_values = attend_backward(
        query, d_heads, key_f, key_b, key_t, value_f, value_b, bias, log_sum
    )

    def flat(parts):
        joined = parts[:, :, :HD] + parts[:, :, HD:]
        return joined.transpose(1, 0, 2).reshape(length, wide)

    d_keyval = scatter(
        jnp.concatenate([flat(d_keys), flat(d_values)], axis=1).astype(low), "tensor"
    ).astype(jnp.float32)
    dq_low = rotate(d_queries, cosine, -sine_table).astype(low)
    dkv_low = jnp.concatenate(
        [rotate(d_keyval[:, :wide], cosine, -sine_table), d_keyval[:, wide:]], axis=1
    ).astype(low)
    grad_query = dot_tn(normed_attn, dq_low)
    grad_keyval = dot_tn(normed_attn, dkv_low)
    d_normed_attn = dot_nt(dq_low, full_query) + dot_nt(dkv_low, full_keyval)
    d_norm_attn, gain_attn_part = norm_backward(d_normed_attn, unit_attn, inverse_attn, gain_attn)
    grad_tokens = (d_residual + d_norm_attn).astype(low)

    if by_kernels:
        gain_columns = jnp.stack([gain_attn_part, gain_mlp_part], axis=1)
        gain_columns = jnp.pad(gain_columns, ((0, 0), (0, 126)))
        grad_narrow = jnp.concatenate([grad_keyval, gain_columns], axis=1)
        grads = (grad_output, grad_query, grad_narrow, grad_down, grad_gate, grad_up)
        to_output, to_query, to_narrow, to_down, to_gate, to_up, layer_out = scatter_all(
            [grad.astype(low) for grad in grads], branch, residual
        )
        wide = grad_keyval.shape[1]
        return (
            layer_out,
            grad_tokens,
            to_narrow[:, wide],
            to_query,
            to_narrow[:, :wide],
            to_output,
            to_narrow[:, wide + 1],
            to_gate,
            to_up,
            to_down,
        )

    layer_rows = residual + scatter(branch, "tensor").astype(jnp.float32)

    def shares(grad):
        return scatter(grad.astype(low), "dp").astype(jnp.float32)

    def square_shares(grad):
        return scatter(scatter(grad.astype(low), "dp"), "tensor", 1).astype(jnp.float32)

    gains = scatter(
        jnp.stack([gain_attn_part, gain_mlp_part]).reshape(2, -1, rows_of_gain(gain_attn)), both, 1
    )
    return (
        layer_rows.astype(low),
        grad_tokens,
        gains[0, 0],
        square_shares(grad_query),
        scatter(grad_keyval.astype(low), both).astype(jnp.float32),
        square_shares(grad_output),
        gains[1, 0],
        shares(grad_gate),
        shares(grad_up),
        shares(grad_down),
    )


def rows_of_gain(gain):
    return gain.shape[0] // (lax.axis_size("dp") * lax.axis_size("tensor"))


def solution(mesh):
    return jax.shard_map(
        local,
        mesh=mesh,
        in_specs=(
            P(("dp", "tensor"), None),
            P("dp"),
            P(),
            P("dp", "tensor"),
            P("dp", None),
            P("dp", "tensor"),
            P(),
            P("dp", "tensor"),
            P("dp", "tensor"),
            P("dp", "tensor"),
            P(("dp", "tensor"), None),
        ),
        out_specs=(
            P(("dp", "tensor"), None),
            P(("dp", "tensor"), None),
            P(("dp", "tensor")),
            P("dp", "tensor"),
            P(("dp", "tensor"), None),
            P("dp", "tensor"),
            P(("dp", "tensor")),
            P("dp", "tensor"),
            P("dp", "tensor"),
            P("dp", "tensor"),
        ),
        check_vma=False,
    )
```

```python
import functools

import jax
import jax.numpy as jnp
from jax import lax
from jax.experimental import pallas as pl
from jax.experimental.pallas import tpu as pltpu
from jax.sharding import PartitionSpec as P

KVH = 4
HD = 64
PAIR = 2 * HD

epsilon = 1e-05
rope_base = 10000.0
masked = -1e30


def doc_positions(seg_row):
    length = seg_row.shape[0]
    places = jnp.arange(length, dtype=jnp.int32)
    change = jnp.concatenate([jnp.ones((1,), jnp.bool_), seg_row[1:] != seg_row[:-1]])
    starts = lax.cummax(jnp.where(change, places, 0), axis=0)
    return places - starts


def rope_tables(places, width):
    half_width = width // 2
    frequency = rope_base ** (-(2.0 * jnp.arange(half_width).astype(jnp.float32)) / width)
    angles = places.astype(jnp.float32)[:, None] * frequency[None, :]
    return (jnp.cos(angles), jnp.sin(angles))


def rotate(values, cosine, sine_table):
    rows, width = values.shape
    heads = values.reshape(rows, width // HD, HD)
    half_width = HD // 2
    front_half = heads[..., :half_width]
    back_half = heads[..., half_width:]
    cos_rows = cosine[:, None, :]
    sin_rows = sine_table[:, None, :]
    turned = jnp.concatenate(
        [
            front_half * cos_rows - back_half * sin_rows,
            back_half * cos_rows + front_half * sin_rows,
        ],
        axis=-1,
    )
    return turned.reshape(rows, width)


def norm_forward(values, gain_vec):
    inverse = lax.rsqrt(jnp.mean(values * values, axis=-1, keepdims=True) + epsilon)
    unit_rows = values * inverse
    return (unit_rows * gain_vec, unit_rows, inverse)


def norm_backward(d_normed, unit_rows, inverse, gain_vec):
    gain_part = jnp.sum(d_normed * unit_rows, axis=0)
    d_unit = d_normed * gain_vec
    d_values = inverse * (d_unit - unit_rows * jnp.mean(d_unit * unit_rows, axis=-1, keepdims=True))
    return (d_values, gain_part)


def dot_nn(left, right):
    return jnp.dot(left, right, preferred_element_type=jnp.float32)


def dot_nt(left, right):
    return lax.dot_general(
        left, right, (((1,), (1,)), ((), ())), preferred_element_type=jnp.float32
    )


def dot_tn(left, right):
    return lax.dot_general(
        left, right, (((0,), (0,)), ((), ())), preferred_element_type=jnp.float32
    )


def front_lanes(tile):
    lane = lax.broadcasted_iota(jnp.int32, tile.shape, 1)
    return jnp.where(lane < HD, tile, jnp.zeros_like(tile))


def back_lanes(tile):
    lane = lax.broadcasted_iota(jnp.int32, tile.shape, 1)
    return jnp.where(lane < HD, jnp.zeros_like(tile), tile)


def attend_forward_kernel(query_ref, front_ref, back_ref, value_t_ref, bias_ref, out_ref, log_ref):
    pairs = query_ref.shape[1] // PAIR
    value_t = value_t_ref[0]
    for pair in range(pairs):
        query = query_ref[:, pair * PAIR : (pair + 1) * PAIR]
        outs = []
        for side, key_ref in enumerate((front_ref, back_ref)):
            scores = dot_nt(key_ref[0], query) + bias_ref[...]
            top = jnp.max(scores, axis=0, keepdims=True)
            expo = jnp.exp(scores - top)
            total = jnp.sum(expo, axis=0, keepdims=True)
            outs.append(dot_nn(value_t, expo.astype(jnp.bfloat16)) / total)
            log_ref[0, pl.ds(pair * 2 + side, 1), :] = top + jnp.log(total)
        out = jnp.concatenate(outs, axis=0).T
        out_ref[:, pair * PAIR : (pair + 1) * PAIR] = out.astype(jnp.bfloat16)


def attend_backward_kernel(
    query_ref,
    grad_ref,
    kf_ref,
    kb_ref,
    kt_ref,
    vf_ref,
    vb_ref,
    bias_ref,
    log_ref,
    dq_ref,
    dk_ref,
    dv_ref,
):
    pairs = query_ref.shape[1] // PAIR
    key_t = kt_ref[0]
    dk_ref[0] = jnp.zeros(dk_ref.shape[1:], jnp.float32)
    dv_ref[0] = jnp.zeros(dv_ref.shape[1:], jnp.float32)
    for pair in range(pairs):
        columns = slice(pair * PAIR, (pair + 1) * PAIR)
        query = query_ref[:, columns]
        grad = grad_ref[:, columns]
        outs = []
        for side, (key_ref, value_ref, keep) in enumerate(
            ((kf_ref, vf_ref, front_lanes), (kb_ref, vb_ref, back_lanes))
        ):
            log_sum = log_ref[0, pl.ds(pair * 2 + side, 1), :]
            probs = jnp.exp(dot_nt(key_ref[0], query) + bias_ref[...] - log_sum)
            d_probs = dot_nt(value_ref[0], grad)
            row_dot = jnp.sum(probs * d_probs, axis=0, keepdims=True)
            d_scores = (probs * (d_probs - row_dot)).astype(jnp.bfloat16)
            dk_ref[0] += dot_nn(d_scores, keep(query))
            dv_ref[0] += dot_nn(probs.astype(jnp.bfloat16), keep(grad))
            outs.append(dot_nn(key_t, d_scores))
        dq_ref[:, columns] = jnp.concatenate(outs, axis=0).T * (HD**-0.5)


def whole_group(rows, width):
    return pl.BlockSpec((1, rows, width), lambda g: (g, 0, 0))


def columns_of(rows, width):
    return pl.BlockSpec((rows, width), lambda g: (0, g))


def attend_forward(query, key_f, key_b, value_t, bias):
    rows, width = query.shape
    length = bias.shape[0]
    group = width // KVH
    return pl.pallas_call(
        attend_forward_kernel,
        grid=(KVH,),
        in_specs=[
            columns_of(rows, group),
            whole_group(length, PAIR),
            whole_group(length, PAIR),
            whole_group(HD, length),
            pl.BlockSpec((length, rows), lambda g: (0, 0)),
        ],
        out_specs=[columns_of(rows, group), whole_group(group // HD, rows)],
        out_shape=[
            jax.ShapeDtypeStruct((rows, width), jnp.bfloat16),
            jax.ShapeDtypeStruct((KVH, group // HD, rows), jnp.float32),
        ],
        compiler_params=pltpu.CompilerParams(vmem_limit_bytes=48 * 1024 * 1024),
        name="attend_forward",
    )(query, key_f, key_b, value_t, bias)


def attend_backward(query, grad, key_f, key_b, key_t, value_f, value_b, bias, log_sum):
    rows, width = query.shape
    length = bias.shape[0]
    group = width // KVH
    tall = whole_group(length, PAIR)
    return pl.pallas_call(
        attend_backward_kernel,
        grid=(KVH,),
        in_specs=[
            columns_of(rows, group),
            columns_of(rows, group),
            tall,
            tall,
            whole_group(HD, length),
            tall,
            tall,
            pl.BlockSpec((length, rows), lambda g: (0, 0)),
            whole_group(group // HD, rows),
        ],
        out_specs=[columns_of(rows, group), tall, tall],
        out_shape=[
            jax.ShapeDtypeStruct((rows, width), jnp.float32),
            jax.ShapeDtypeStruct((KVH, length, PAIR), jnp.float32),
            jax.ShapeDtypeStruct((KVH, length, PAIR), jnp.float32),
        ],
        compiler_params=pltpu.CompilerParams(vmem_limit_bytes=48 * 1024 * 1024),
        name="attend_backward",
    )(query, grad, key_f, key_b, key_t, value_f, value_b, bias, log_sum)


def by_head(matrix):
    rows = matrix.shape[0]
    return matrix.reshape(rows, KVH, HD).transpose(1, 0, 2)


MESH = pl.DeviceIdType.MESH


def flip(index, bit):
    return index + bit - 2 * bit * ((index // bit) % 2)


def line_order(place):
    nearest = place - 1 + 2 * (1 - (place + 3) // 4)
    farthest = 3 - 3 * (place // 2)
    return (nearest, 6 - place - nearest - farthest, farthest)


def enter(dp, place):
    barrier = pltpu.get_barrier_semaphore()
    for bit in (1, 2, 4):
        pl.semaphore_signal(barrier, inc=1, device_id=(flip(dp, bit), place), device_id_type=MESH)
    for step in (-1, 1):
        there = (place + step >= 0) & (place + step < 4)

        @pl.when(there)
        def _():
            pl.semaphore_signal(
                barrier, inc=1, device_id=(dp, place + step), device_id_type=MESH
            )

    ends = 1 - ((place + 3) // 4) + place // 3
    pl.semaphore_wait(barrier, 5 - ends)


def gather_kernel(
    kv_ref, q_ref, o_ref, d_ref, g_ref, u_ref, c_ref,
    fkv, fq, fo, fd, fg, fu, fc,
    own_sem, z_send, z_recv, p_send, p_recv,
):
    dp, place = lax.axis_index("dp"), lax.axis_index("tensor")
    rows = kv_ref.shape[0]
    half = rows // 2
    width = q_ref.shape[1]
    order = line_order(place)
    enter(dp, place)

    def rows_of(owner):
        return pl.ds(pl.multiple_of(owner * rows, rows), rows)

    def columns_of_rank(rank):
        return pl.ds(pl.multiple_of(rank * width, width), width)

    def remote(src, dst, send, recv, device):
        return pltpu.make_async_remote_copy(
            src_ref=src, dst_ref=dst, send_sem=send, recv_sem=recv,
            device_id=device, device_id_type=MESH,
        )

    own = [
        (kv_ref, fkv.at[rows_of(dp), :]),
        (q_ref, fq.at[rows_of(dp), columns_of_rank(place)]),
        (o_ref, fo.at[rows_of(dp), columns_of_rank(place)]),
        (d_ref, fd.at[rows_of(dp), :]),
        (g_ref, fg.at[rows_of(dp), :]),
        (u_ref, fu.at[rows_of(dp), :]),
        (c_ref, fc.at[rows_of(place), :]),
    ]
    own_copies = [
        pltpu.make_async_copy(src, dst, own_sem.at[i]) for i, (src, dst) in enumerate(own)
    ]
    for copy in own_copies:
        copy.start()

    def line_block(which, rank):
        if which == 2:
            return fc.at[rows_of(rank), :]
        return (fq, fo)[which].at[rows_of(dp), columns_of_rank(rank)]

    def line_copy(which, rank, step):
        src = (q_ref, o_ref, c_ref)[which] if rank is place else line_block(which, rank)
        side = 0 if step < 0 else 1
        return remote(
            src, line_block(which, rank), z_send.at[which, side, rank], z_recv.at[which, rank],
            (dp, place + step),
        )

    def line_send(which, rank, act):
        @pl.when((rank <= place) & (place < 3))
        def _():
            act(line_copy(which, rank, 1))

        @pl.when((rank >= place) & (place > 0))
        def _():
            act(line_copy(which, rank, -1))

    def start(copy):
        copy.start()

    def wait_send(copy):
        copy.wait_send()

    x, y, core = flip(dp, 2), flip(dp, 4), flip(dp, 1)
    far = flip(x, 4)

    blocks = [("kv", None), ("q", place), ("q", order[0]), ("q", order[1]), ("q", order[2])]
    blocks += [("o", place), ("o", order[0]), ("o", order[1]), ("o", order[2])]
    blocks += [("d", None), ("g", None), ("u", None)]

    def block(index, owner, part=None):
        name, rank = blocks[index]
        ref = {"kv": fkv, "q": fq, "o": fo, "d": fd, "g": fg, "u": fu}[name]
        first = owner * rows if part is None else owner * rows + part * half
        size = rows if part is None else half
        window = pl.ds(pl.multiple_of(first, half), size)
        if rank is None:
            return ref.at[window, :]
        return ref.at[window, columns_of_rank(rank)]

    def own_block(index):
        name, rank = blocks[index]
        if rank is None or rank is place:
            return {"kv": kv_ref, "q": q_ref, "o": o_ref, "d": d_ref, "g": g_ref, "u": u_ref}[name]
        return block(index, dp)

    def plane_copy(index, lane):
        send, recv = p_send.at[index, lane], p_recv.at[index, lane]
        if lane == 0:
            return remote(own_block(index), block(index, dp), send, recv, (x, place))
        if lane == 1:
            return remote(own_block(index), block(index, dp), send, recv, (y, place))
        if lane == 2:
            return remote(block(index, x, 0), block(index, x, 0), send, recv, (y, place))
        if lane == 3:
            return remote(block(index, y, 1), block(index, y, 1), send, recv, (x, place))
        owner = (dp, x, y, far)[lane - 4]
        src = own_block(index) if lane == 4 else block(index, owner)
        return remote(src, block(index, owner), send, recv, (core, place))

    def plane_first(index):
        plane_copy(index, 0).start()
        plane_copy(index, 1).start()
        plane_copy(index, 4).start()

    def plane_second(index):
        plane_copy(index, 0).wait_recv()
        plane_copy(index, 2).start()
        plane_copy(index, 5).start()
        plane_copy(index, 1).wait_recv()
        plane_copy(index, 3).start()
        plane_copy(index, 6).start()

    def plane_third(index):
        plane_copy(index, 2).wait_recv()
        plane_copy(index, 3).wait_recv()
        plane_copy(index, 7).start()

    def plane_last(index):
        for lane in range(4, 8):
            plane_copy(index, lane).wait_recv()
        for lane in range(8):
            plane_copy(index, lane).wait_send()

    line_send(0, place, start)
    plane_first(0)
    plane_first(1)
    line_send(1, place, start)
    line_send(2, place, start)
    count = len(blocks)
    line_of = {2: (0, 0), 3: (0, 1), 4: (0, 2), 6: (1, 0), 7: (1, 1), 8: (1, 2)}
    for index in range(count):
        ahead = index + 2
        if ahead < count:
            if ahead in line_of:
                which, step = line_of[ahead]
                line_copy(which, order[step], 1).wait_recv()
                line_send(which, order[step], start)
            plane_first(ahead)
        if ahead in (7, 9, 10):
            step = (7, 9, 10).index(ahead)
            line_copy(2, order[step], 1).wait_recv()
            line_send(2, order[step], start)
        plane_second(index)
        if index >= 1:
            plane_third(index - 1)
    plane_third(count - 1)
    for index in range(count):
        plane_last(index)
    for which in range(3):
        line_send(which, place, wait_send)
        for step in range(3):
            line_send(which, order[step], wait_send)
    for copy in own_copies:
        copy.wait()


def gather_all(w_keyval, w_query, w_output, w_down, w_gate, w_up, cotangent):
    n_dp, n_line = lax.axis_size("dp"), lax.axis_size("tensor")

    def over(array, rows, columns):
        shape = (array.shape[0] * rows, array.shape[1] * columns)
        return jax.ShapeDtypeStruct(shape, array.dtype)

    anywhere = pl.BlockSpec(memory_space=pl.ANY)
    shapes = [
        over(w_keyval, n_dp, 1),
        over(w_query, n_dp, n_line),
        over(w_output, n_dp, n_line),
        over(w_down, n_dp, 1),
        over(w_gate, n_dp, 1),
        over(w_up, n_dp, 1),
        over(cotangent, n_line, 1),
    ]
    return pl.pallas_call(
        gather_kernel,
        out_shape=shapes,
        in_specs=[anywhere] * 7,
        out_specs=[anywhere] * 7,
        scratch_shapes=[
            pltpu.SemaphoreType.DMA((7,)),
            pltpu.SemaphoreType.DMA((3, 2, 4)),
            pltpu.SemaphoreType.DMA((3, 4)),
            pltpu.SemaphoreType.DMA((12, 8)),
            pltpu.SemaphoreType.DMA((12, 8)),
        ],
        compiler_params=pltpu.CompilerParams(collective_id=0, has_side_effects=True),
        name="gather_all",
    )(w_keyval, w_query, w_output, w_down, w_gate, w_up, cotangent)


def add_rows(target, source, step=32):
    @pl.loop(0, target.shape[0] // step)
    def _(index):
        window = pl.ds(pl.multiple_of(index * step, step), step)
        target[window, :] = target[window, :] + source[window, :]


def scatter_kernel(
    go_ref, gq_ref, kv_ref, gd_ref, gg_ref, gu_ref, branch_ref, residual_ref,
    go_out, gq_out, kv_out, gd_out, gg_out, gu_out, layer_out,
    go_core, gq_core, kv_core, gd_core, gg_core, gu_core,
    go_part, gq_part, kv_part, gd_part, gg_part, gu_part,
    go_side, gq_side, kv_side, gd_side, gg_side, gu_side,
    go_near, gq_near, kv_near, gd_near, gg_near, gu_near,
    go_line, gq_line, kv_line, layer_line,
    go_in, gq_in, kv_in, layer_in,
    held, total_ref,
    load_sem, core_load, core_send, core_recv, p_send, p_recv, l_send, l_recv, layer_load,
):
    dp, place = lax.axis_index("dp"), lax.axis_index("tensor")
    rows = go_part.shape[1]
    half = rows // 2
    enter(dp, place)
    x, y, core = flip(dp, 2), flip(dp, 4), flip(dp, 1)
    far = flip(x, 4)
    mine = (dp, x, y, far)
    theirs = tuple(flip(owner, 1) for owner in mine)
    grads = (go_ref, gq_ref, kv_ref, gd_ref, gg_ref, gu_ref)
    outs = (go_out, gq_out, kv_out, gd_out, gg_out, gu_out)
    cores = (go_core, gq_core, kv_core, gd_core, gg_core, gu_core)
    parts = (go_part, gq_part, kv_part, gd_part, gg_part, gu_part)
    sides = (go_side, gq_side, kv_side, gd_side, gg_side, gu_side)
    nears = (go_near, gq_near, kv_near, gd_near, gg_near, gu_near)
    lines = (go_line, gq_line, kv_line, layer_line)
    arrivals = (go_in, gq_in, kv_in, layer_in)
    count = len(grads)
    front, back = pl.ds(0, half), pl.ds(half, half)

    def rows_of(owner):
        return pl.ds(pl.multiple_of(owner * rows, rows), rows)

    def remote(src, dst, send, recv, device):
        return pltpu.make_async_remote_copy(
            src_ref=src, dst_ref=dst, send_sem=send, recv_sem=recv,
            device_id=device, device_id_type=MESH,
        )

    def core_copy(i, k):
        return remote(
            grads[i].at[rows_of(theirs[k]), :], cores[i].at[k],
            core_send.at[i, k], core_recv.at[i, k], (core, place),
        )

    def own_load(i, k):
        return pltpu.make_async_copy(
            grads[i].at[rows_of(mine[k]), :], parts[i].at[k], load_sem.at[i, k]
        )

    def core_fetch(i, k):
        width = grads[i].shape[1]
        return pltpu.make_async_copy(
            cores[i].at[k], held.at[k, :, pl.ds(0, width)], core_load.at[k]
        )

    def plane_copy(i, lane):
        part = parts[i]
        src, dst, device = (
            (part.at[3, front, :], sides[i].at[0], y),
            (part.at[3, back, :], sides[i].at[1], x),
            (part.at[1, back, :], nears[i].at[0, back, :], x),
            (part.at[2, front, :], nears[i].at[1, front, :], y),
            (part.at[1, front, :], nears[i].at[0, front, :], x),
            (part.at[2, back, :], nears[i].at[1, back, :], y),
        )[lane]
        return remote(src, dst, p_send.at[i, lane], p_recv.at[i, lane], (device, place))

    def stage_core(i):
        width = grads[i].shape[1]
        for k in (3, 1, 2, 0):
            core_copy(i, k).wait_recv()
            core_fetch(i, k).start()
        for k in (3, 1, 2, 0):
            core_fetch(i, k).wait()
            own_load(i, k).wait()
            add_rows(parts[i].at[k], held.at[k, :, pl.ds(0, width)])
            for lane in ((), (2,), (3,), (0, 1))[k]:
                plane_copy(i, lane).start()

    def stage_side(i):
        plane_copy(i, 0).wait_recv()
        add_rows(parts[i].at[1, front, :], sides[i].at[0])
        plane_copy(i, 4).start()
        plane_copy(i, 1).wait_recv()
        add_rows(parts[i].at[2, back, :], sides[i].at[1])
        plane_copy(i, 5).start()

    def stage_near(i):
        for lane in (2, 3, 4, 5):
            plane_copy(i, lane).wait_recv()
        part, near, out = parts[i], nears[i], outs[i]

        @pl.loop(0, rows // 32)
        def _(index):
            window = pl.ds(pl.multiple_of(index * 32, 32), 32)
            total = (
                part[0, window, :].astype(jnp.float32)
                + near[0, window, :].astype(jnp.float32)
                + near[1, window, :].astype(jnp.float32)
            )
            if i >= 3:
                out[window, :] = total
            elif i < 2:
                width = lines[i].shape[2]
                for rank in range(4):
                    lines[i][rank, window, :] = total[:, rank * width : (rank + 1) * width].astype(
                        jnp.bfloat16
                    )
            else:
                per = rows // 4
                lines[i][index * 32 // per, pl.ds(pl.multiple_of(index * 32 % per, 32), 32), :] = (
                    total.astype(jnp.bfloat16)
                )

    def line_copy(i, rank, slot, step):
        return remote(
            lines[i].at[rank], arrivals[i].at[slot], l_send.at[i, rank], l_recv.at[i, slot],
            (dp, place + step),
        )

    def line_step(i, step):
        down, up = place - 3 + step, place + 3 - step

        @pl.when(down >= 0)
        def _():
            @pl.when(place < 3)
            def _():
                line_copy(i, down, down, -1).wait_recv()
                add_rows(lines[i].at[down], arrivals[i].at[down])

            line_copy(i, down, down, -1).start()

        @pl.when(up <= 3)
        def _():
            @pl.when(place > 0)
            def _():
                line_copy(i, up, up, 1).wait_recv()
                add_rows(lines[i].at[up], arrivals[i].at[up])

            line_copy(i, up, 4 if step == 2 else up, 1).start()

    def line_last(i, begin, add, finish):
        begin(lines[i].at[place])

        @pl.when(place < 3)
        def _():
            line_copy(i, place, place, 1).wait_recv()
            add(arrivals[i].at[place])

        @pl.when(place > 0)
        def _():
            line_copy(i, place, 4, 1).wait_recv()
            add(arrivals[i].at[4])

        finish()

    def line_sent(i):
        for rank in range(4):

            @pl.when(rank != place)
            def _():
                line_copy(i, rank, rank, 1).wait_send()

    def by_rows(total_rows, act):
        @pl.loop(0, total_rows // 32)
        def _(index):
            act(pl.ds(pl.multiple_of(index * 32, 32), 32))

    def line_out(i):
        out = outs[i]
        size = out.shape[0]

        def begin(ref):
            def act(window):
                out[window, :] = ref[window, :].astype(jnp.float32)

            by_rows(size, act)

        def add(ref):
            def act(window):
                out[window, :] += ref[window, :].astype(jnp.float32)

            by_rows(size, act)

        line_last(i, begin, add, lambda: None)

    branch_load = pltpu.make_async_copy(branch_ref, layer_line, layer_load)
    branch_load.start()
    for i in range(count):
        for k in (3, 1, 2, 0):
            core_copy(i, k).start()
            own_load(i, k).start()
    branch_load.wait()
    line_step(3, 0)
    for i in range(count + 2):
        if i < count:
            stage_core(i)
        if 1 <= i <= count:
            stage_side(i - 1)
        if i >= 2:
            stage_near(i - 2)
        for j in range(3):
            if 0 <= i - 2 - j < 3:
                line_step(j, i - 2 - j)
        if i in (2, 4):
            line_step(3, i // 2)
    for j in range(3):
        line_out(j)

    def layer_begin(ref):
        def act(window):
            total_ref[window, :] = residual_ref[window, :] + ref[window, :].astype(jnp.float32)

        by_rows(rows, act)

    def layer_add(ref):
        def act(window):
            total_ref[window, :] += ref[window, :].astype(jnp.float32)

        by_rows(rows, act)

    def layer_finish():
        def act(window):
            layer_out[window, :] = total_ref[window, :].astype(jnp.bfloat16)

        by_rows(rows, act)

    line_last(3, layer_begin, layer_add, layer_finish)
    for i in range(count):
        for k in range(4):
            core_copy(i, k).wait_send()
        for lane in range(6):
            plane_copy(i, lane).wait_send()
    for i in range(4):
        line_sent(i)


def scatter_all(grads, branch, residual):
    low = jnp.bfloat16
    n_line = lax.axis_size("tensor")
    rows = grads[0].shape[0] // lax.axis_size("dp")
    half = rows // 2
    widths = [grad.shape[1] for grad in grads]
    square = widths[0] // n_line
    few = rows // n_line
    tokens, width = residual.shape
    anywhere = pl.BlockSpec(memory_space=pl.ANY)
    in_vmem = pl.BlockSpec(memory_space=pltpu.VMEM)
    out_shape = [
        jax.ShapeDtypeStruct((rows, square), jnp.float32),
        jax.ShapeDtypeStruct((rows, square), jnp.float32),
        jax.ShapeDtypeStruct((few, widths[2]), jnp.float32),
    ]
    out_shape += [jax.ShapeDtypeStruct((rows, w), jnp.float32) for w in widths[3:]]
    out_shape += [jax.ShapeDtypeStruct((tokens, width), low)]
    out_shape += [jax.ShapeDtypeStruct((4, rows, w), low) for w in widths]
    scratch = [pltpu.VMEM((4, rows, w), low) for w in widths]
    scratch += [pltpu.VMEM((2, half, w), low) for w in widths]
    scratch += [pltpu.VMEM((2, rows, w), low) for w in widths]
    line_shapes = [(rows, square), (rows, square), (few, widths[2]), (tokens, width)]
    scratch += [pltpu.VMEM((4,) + shape, low) for shape in line_shapes]
    scratch += [pltpu.VMEM((5,) + shape, low) for shape in line_shapes]
    scratch += [pltpu.VMEM((4, rows, max(widths)), low)]
    scratch += [pltpu.VMEM((tokens, width), jnp.float32)]
    dma = pltpu.SemaphoreType.DMA
    scratch += [
        dma((6, 4)), dma((4,)), dma((6, 4)), dma((6, 4)), dma((6, 6)), dma((6, 6)),
        dma((4, 4)), dma((4, 5)), dma,
    ]
    results = pl.pallas_call(
        scatter_kernel,
        out_shape=out_shape,
        in_specs=[anywhere] * 7 + [in_vmem],
        out_specs=[in_vmem] * 7 + [anywhere] * 6,
        scratch_shapes=scratch,
        compiler_params=pltpu.CompilerParams(
            collective_id=1, has_side_effects=True, vmem_limit_bytes=62 * 1024 * 1024
        ),
        name="scatter_all",
    )(*grads, branch, residual)
    return results[:7]


def by_tiles(total, size, act):
    full = total // size

    @pl.loop(0, full)
    def _(index):
        act(pl.ds(pl.multiple_of(index * size, size), size))

    if total % size:
        act(pl.ds(full * size, total % size))


def feed_forward_kernel(
    normed_ref, gate_w_ref, up_w_ref, down_w_ref, cot_ref,
    gg_out, gu_out, gd_out, branch_out, dn_out,
    wg, wu, wd, cot, normed, hid, dg, du, part, arrival, branch_stage, gate_stage, up_stage,
    load_sem, n_send, n_recv, l_send, l_recv, stage_sem,
):
    dp, place = lax.axis_index("dp"), lax.axis_index("tensor")
    rows, depth = normed_ref.shape
    low = jnp.bfloat16
    order = line_order(place)
    cuts = l_send.shape[1]
    few = rows // cuts
    enter(dp, place)

    def remote(src, dst, send, recv, step):
        return pltpu.make_async_remote_copy(
            src_ref=src, dst_ref=dst, send_sem=send, recv_sem=recv,
            device_id=(dp, place + step), device_id_type=MESH,
        )

    def chunk(rank):
        return pl.ds(pl.multiple_of(rank * rows, rows), rows)

    def own_copy(step):
        return remote(
            normed_ref, normed.at[chunk(place), :], n_send.at[(step + 1) // 2, place],
            n_recv.at[place], step,
        )

    def pass_copy(rank, step):
        ref = normed.at[chunk(rank), :]
        return remote(ref, ref, n_send.at[(step + 1) // 2, rank], n_recv.at[rank], step)

    loads = [
        pltpu.make_async_copy(src, dst, load_sem.at[i])
        for i, (src, dst) in enumerate(
            (
                (normed_ref, normed.at[chunk(place), :]),
                (gate_w_ref, wg),
                (up_w_ref, wu),
                (cot_ref, cot),
                (down_w_ref, wd),
            )
        )
    ]

    @pl.when(place < 3)
    def _():
        own_copy(1).start()

    @pl.when(place > 0)
    def _():
        own_copy(-1).start()

    for load in loads:
        load.start()
    for load in loads:
        load.wait()

    def sums_copy(rank, cut, slot, step):
        window = pl.ds(cut * few, few)
        return remote(
            part.at[rank, window, :], arrival.at[slot, window, :], l_send.at[rank, cut],
            l_recv.at[slot, cut], step,
        )

    def branch_copy(rank):
        return pltpu.make_async_copy(branch_stage, branch_out.at[rank], stage_sem.at[0])

    def compute(rank):
        here = chunk(rank)

        def activate(columns):
            gate = dot_nn(normed[here, :], wg[:, columns])
            up = dot_nn(normed[here, :], wu[:, columns])
            d_hidden = dot_nn(cot[here, :], wd[:, columns])
            sig = 1.0 / (1.0 + jnp.exp(-gate))
            silu = gate * sig
            hid[here, columns] = (silu * up).astype(low)
            dg[here, columns] = (d_hidden * up * sig * (1.0 + gate * (1.0 - sig))).astype(low)
            du[here, columns] = (d_hidden * silu).astype(low)

        by_tiles(wg.shape[1], 256, activate)

        def pull(columns):
            part[rank, :, columns] = (
                dot_nt(dg[here, :], wg[columns, :]) + dot_nt(du[here, :], wu[columns, :])
            ).astype(low)

        by_tiles(depth, 512, pull)

    def branch(rank):
        def push(columns):
            branch_stage[:, columns] = dot_nt(hid[chunk(rank), :], wd[columns, :]).astype(low)

        by_tiles(depth, 512, push)
        branch_copy(rank).start()

    def take(rank):
        pass_copy(rank, 1).wait_recv()

        @pl.when((rank < place) & (place < 3))
        def _():
            pass_copy(rank, 1).start()

        @pl.when((rank > place) & (place > 0))
        def _():
            pass_copy(rank, -1).start()

    @pl.loop(0, 4)
    def _(turn):
        rank = jnp.where(
            turn == 0,
            place,
            jnp.where(turn == 1, order[0], jnp.where(turn == 2, order[1], order[2])),
        )

        inside = (place == 1) | (place == 2)

        @pl.when(turn == 1)
        def _():
            take(order[0])

            @pl.when(inside)
            def _():
                take(order[1])

        @pl.when((turn == 2) & (place != 1) & (place != 2))
        def _():
            take(order[1])

        @pl.when(turn == 3)
        def _():
            take(order[2])

        compute(rank)

        @pl.when((turn > 0) & (place == 3))
        def _():
            for cut in range(cuts):
                sums_copy(rank, cut, rank, -1).start()

        @pl.when((turn > 0) & (place == 0))
        def _():
            slot = jnp.where(rank == 1, 4, rank)
            for cut in range(cuts):
                sums_copy(rank, cut, slot, 1).start()

        @pl.when(turn > 0)
        def _():
            branch_copy(rank).wait()

        branch(rank)

    branch_copy(0).wait()

    def gate_copy(tile):
        return pltpu.make_async_copy(gate_stage, gg_out.at[tile, :], stage_sem.at[1])

    def up_copy(tile):
        return pltpu.make_async_copy(up_stage, gu_out.at[tile, :], stage_sem.at[2])

    def down_copy(tile):
        return pltpu.make_async_copy(gate_stage, gd_out.at[tile, :], stage_sem.at[1])

    size = gate_stage.shape[0]

    @pl.loop(0, depth // size)
    def _(index):
        tile = pl.ds(pl.multiple_of(index * size, size), size)
        left = normed[:, tile]
        gate_grad = dot_tn(left, dg[...]).astype(low)

        @pl.when(index > 0)
        def _():
            gate_copy(tile).wait()
            up_copy(tile).wait()

        gate_stage[...] = gate_grad
        gate_copy(tile).start()
        up_stage[...] = dot_tn(left, du[...]).astype(low)
        up_copy(tile).start()

    last = pl.ds(depth - size, size)
    gate_copy(last).wait()
    up_copy(last).wait()

    def relay(rank, slot, step, cut):
        sums_copy(rank, cut, rank, step).wait_recv()
        window = pl.ds(cut * few, few)
        part[rank, window, :] = part[rank, window, :] + arrival[rank, window, :]
        sums_copy(rank, cut, slot, step).start()

    @pl.when((place == 1) | (place == 2))
    def _():
        outward = 3 - 2 * place
        for cut in range(cuts):
            relay(3 - place, 4 - 3 * (place - 1), outward, cut)
        for cut in range(cuts):
            relay(6 - 3 * place, 6 - 3 * place, outward, cut)
            relay(3 * (place - 1), 4 * (place - 1), -outward, cut)

    @pl.loop(0, depth // size)
    def _(index):
        tile = pl.ds(pl.multiple_of(index * size, size), size)
        down_grad = dot_tn(cot[:, tile], hid[...]).astype(low)

        @pl.when(index > 0)
        def _():
            down_copy(tile).wait()

        gate_stage[...] = down_grad
        down_copy(tile).start()

    down_copy(last).wait()

    for cut in range(cuts):
        window = pl.ds(cut * few, few)
        dn_out[window, :] = part[place, window, :].astype(jnp.float32)

        @pl.when(place < 3)
        def _():
            sums_copy(place, cut, place, 1).wait_recv()
            dn_out[window, :] += arrival[place, window, :].astype(jnp.float32)

        @pl.when(place > 0)
        def _():
            sums_copy(place, cut, 4, 1).wait_recv()
            dn_out[window, :] += arrival[4, window, :].astype(jnp.float32)

    @pl.when(place < 3)
    def _():
        own_copy(1).wait_send()

    @pl.when(place > 0)
    def _():
        own_copy(-1).wait_send()

    for rank in range(4):

        @pl.when((rank < place) & (place < 3))
        def _():
            pass_copy(rank, 1).wait_send()

        @pl.when((rank > place) & (place > 0))
        def _():
            pass_copy(rank, -1).wait_send()

        @pl.when(rank != place)
        def _():
            for cut in range(cuts):
                sums_copy(rank, cut, rank, 1).wait_send()


def feed_forward(normed, w_gate, w_up, w_down, cotangent):
    low = jnp.bfloat16
    rows, depth = normed.shape
    length = cotangent.shape[0]
    units = w_gate.shape[1]
    ranks = length // rows
    cuts = 4
    anywhere = pl.BlockSpec(memory_space=pl.ANY)
    in_vmem = pl.BlockSpec(memory_space=pltpu.VMEM)
    dma = pltpu.SemaphoreType.DMA
    flops = 9 * 2 * length * depth * units
    return pl.pallas_call(
        feed_forward_kernel,
        out_shape=[jax.ShapeDtypeStruct((depth, units), low)] * 3
        + [
            jax.ShapeDtypeStruct((ranks, rows, depth), low),
            jax.ShapeDtypeStruct((rows, depth), jnp.float32),
        ],
        in_specs=[anywhere] * 5,
        out_specs=[anywhere] * 4 + [in_vmem],
        scratch_shapes=[pltpu.VMEM((depth, units), low)] * 3
        + [pltpu.VMEM((length, depth), low)] * 2
        + [pltpu.VMEM((length, units), low)] * 3
        + [
            pltpu.VMEM((ranks, rows, depth), low),
            pltpu.VMEM((ranks + 1, rows, depth), low),
            pltpu.VMEM((rows, depth), low),
            pltpu.VMEM((256, units), low),
            pltpu.VMEM((256, units), low),
            dma((5,)), dma((2, ranks)), dma((ranks,)), dma((ranks, cuts)), dma((ranks + 1, cuts)),
            dma((3,)),
        ],
        compiler_params=pltpu.CompilerParams(
            collective_id=2, has_side_effects=True, vmem_limit_bytes=62 * 1024 * 1024
        ),
        cost_estimate=pl.CostEstimate(flops=flops, bytes_accessed=60 << 20, transcendentals=0),
        name="feed_forward",
    )(normed, w_gate, w_up, w_down, cotangent)


def local(
    tokens,
    segments,
    gain_attn,
    w_query,
    w_keyval,
    w_output,
    gain_mlp,
    w_gate,
    w_up,
    w_down,
    cotangent,
):
    tensor_rank = lax.axis_index("tensor")
    length = segments.shape[0]
    rows = tokens.shape[0]
    both = ("dp", "tensor")
    low = jnp.bfloat16

    def gather(array, axes, axis=0):
        return lax.all_gather(array, axes, axis=axis, tiled=True)

    def scatter(array, axes, axis=0):
        return lax.psum_scatter(array, axes, scatter_dimension=axis, tiled=True)

    by_kernels = (lax.axis_size("dp"), lax.axis_size("tensor")) == (8, 4)
    if by_kernels:
        full_keyval, full_query, full_output, full_down, full_gate, full_up, piece = gather_all(
            w_keyval, w_query, w_output, w_down, w_gate, w_up, cotangent
        )
    else:
        full_keyval = gather(w_keyval, "dp")
        full_query = gather(gather(w_query, "tensor", 1), "dp")
        full_output = gather(gather(w_output, "tensor", 1), "dp")
        full_gate, full_up = gather(w_gate, "dp"), gather(w_up, "dp")
        full_down = gather(w_down, "dp")
        piece = gather(cotangent, "tensor")
    places = doc_positions(segments)
    my_places = lax.dynamic_slice_in_dim(places, tensor_rank * rows, rows, 0)
    my_segments = lax.dynamic_slice_in_dim(segments, tensor_rank * rows, rows, 0)
    cosine, sine_table = rope_tables(my_places, HD)
    order = jnp.arange(length, dtype=jnp.int32)
    allowed = (order[:, None] <= tensor_rank * rows + order[None, :rows]) & (
        segments[:, None] == my_segments[None, :]
    )
    bias = jnp.where(allowed, 0.0, masked).astype(jnp.float32)

    token_rows = tokens.astype(jnp.float32)
    normed_attn, unit_attn, inverse_attn = norm_forward(token_rows, gain_attn)
    normed_attn = normed_attn.astype(low)
    keyval_pre = dot_nn(normed_attn, full_keyval)
    wide = KVH * HD
    key_low = rotate(keyval_pre[:, :wide], cosine, sine_table).astype(low)
    keyval = gather(jnp.concatenate([key_low, keyval_pre[:, wide:].astype(low)], axis=1), "tensor")
    key_heads, value_heads = by_head(keyval[:, :wide]), by_head(keyval[:, wide:])
    blank = jnp.zeros_like(key_heads)
    key_f = jnp.concatenate([key_heads, blank], axis=2)
    key_b = jnp.concatenate([blank, key_heads], axis=2)
    value_f = jnp.concatenate([value_heads, blank], axis=2)
    value_b = jnp.concatenate([blank, value_heads], axis=2)
    key_t = key_heads.transpose(0, 2, 1)
    value_t = value_heads.transpose(0, 2, 1)

    query = (rotate(dot_nn(normed_attn, full_query), cosine, sine_table) * (HD**-0.5)).astype(low)
    heads_low, log_sum = attend_forward(query, key_f, key_b, value_t, bias)
    residual = token_rows + dot_nt(heads_low, full_output)

    normed_mlp, unit_mlp, inverse_mlp = norm_forward(residual, gain_mlp)
    if by_kernels:
        grad_gate, grad_up, grad_down, branch, d_normed_mlp = feed_forward(
            normed_mlp.astype(low), full_gate, full_up, full_down, piece
        )
    else:
        gathered_mlp = gather(normed_mlp.astype(low), "tensor")
        gate_act = dot_nn(gathered_mlp, full_gate)
        up_act = dot_nn(gathered_mlp, full_up)
        sigmoid_gate = jax.nn.sigmoid(gate_act)
        silu_gate = gate_act * sigmoid_gate
        hidden_low = (silu_gate * up_act).astype(low)
        d_hidden = dot_nn(piece, full_down)
        d_gate = (d_hidden * up_act * sigmoid_gate * (1.0 + gate_act * (1.0 - sigmoid_gate))).astype(low)
        d_up = (d_hidden * silu_gate).astype(low)
        d_normed_mlp = scatter(
            (dot_nt(d_gate, full_gate) + dot_nt(d_up, full_up)).astype(low), "tensor"
        ).astype(jnp.float32)
        branch = dot_nt(hidden_low, full_down).astype(low)
        grad_down = dot_tn(piece, hidden_low)
        grad_gate = dot_tn(gathered_mlp, d_gate)
        grad_up = dot_tn(gathered_mlp, d_up)
    d_norm_mlp, gain_mlp_part = norm_backward(d_normed_mlp, unit_mlp, inverse_mlp, gain_mlp)
    d_residual = cotangent.astype(jnp.float32) + d_norm_mlp

    d_branch = d_residual.astype(low)
    grad_output = dot_tn(d_branch, heads_low)
    d_heads = dot_nn(d_branch, full_output).astype(low)
    d_queries, d_keys, d_values = attend_backward(
        query, d_heads, key_f, key_b, key_t, value_f, value_b, bias, log_sum
    )

    def flat(parts):
        joined = parts[:, :, :HD] + parts[:, :, HD:]
        return joined.transpose(1, 0, 2).reshape(length, wide)

    d_keyval = scatter(
        jnp.concatenate([flat(d_keys), flat(d_values)], axis=1).astype(low), "tensor"
    ).astype(jnp.float32)
    dq_low = rotate(d_queries, cosine, -sine_table).astype(low)
    dkv_low = jnp.concatenate(
        [rotate(d_keyval[:, :wide], cosine, -sine_table), d_keyval[:, wide:]], axis=1
    ).astype(low)
    grad_query = dot_tn(normed_attn, dq_low)
    grad_keyval = dot_tn(normed_attn, dkv_low)
    d_normed_attn = dot_nt(dq_low, full_query) + dot_nt(dkv_low, full_keyval)
    d_norm_attn, gain_attn_part = norm_backward(d_normed_attn, unit_attn, inverse_attn, gain_attn)
    grad_tokens = (d_residual + d_norm_attn).astype(low)

    if by_kernels:
        gain_columns = jnp.stack([gain_attn_part, gain_mlp_part], axis=1)
        gain_columns = jnp.pad(gain_columns, ((0, 0), (0, 126)))
        grad_narrow = jnp.concatenate([grad_keyval, gain_columns], axis=1)
        grads = (grad_output, grad_query, grad_narrow, grad_down, grad_gate, grad_up)
        to_output, to_query, to_narrow, to_down, to_gate, to_up, layer_out = scatter_all(
            [grad.astype(low) for grad in grads], branch, residual
        )
        wide = grad_keyval.shape[1]
        return (
            layer_out,
            grad_tokens,
            to_narrow[:, wide],
            to_query,
            to_narrow[:, :wide],
            to_output,
            to_narrow[:, wide + 1],
            to_gate,
            to_up,
            to_down,
        )

    layer_rows = residual + scatter(branch, "tensor").astype(jnp.float32)

    def shares(grad):
        return scatter(grad.astype(low), "dp").astype(jnp.float32)

    def square_shares(grad):
        return scatter(scatter(grad.astype(low), "dp"), "tensor", 1).astype(jnp.float32)

    gains = scatter(
        jnp.stack([gain_attn_part, gain_mlp_part]).reshape(2, -1, rows_of_gain(gain_attn)), both, 1
    )
    return (
        layer_rows.astype(low),
        grad_tokens,
        gains[0, 0],
        square_shares(grad_query),
        scatter(grad_keyval.astype(low), both).astype(jnp.float32),
        square_shares(grad_output),
        gains[1, 0],
        shares(grad_gate),
        shares(grad_up),
        shares(grad_down),
    )


def rows_of_gain(gain):
    return gain.shape[0] // (lax.axis_size("dp") * lax.axis_size("tensor"))


def solution(mesh):
    return jax.shard_map(
        local,
        mesh=mesh,
        in_specs=(
            P(("dp", "tensor"), None),
            P("dp"),
            P(),
            P("dp", "tensor"),
            P("dp", None),
            P("dp", "tensor"),
            P(),
            P("dp", "tensor"),
            P("dp", "tensor"),
            P("dp", "tensor"),
            P(("dp", "tensor"), None),
        ),
        out_specs=(
            P(("dp", "tensor"), None),
            P(("dp", "tensor"), None),
            P(("dp", "tensor")),
            P("dp", "tensor"),
            P(("dp", "tensor"), None),
            P("dp", "tensor"),
            P(("dp", "tensor")),
            P("dp", "tensor"),
            P("dp", "tensor"),
            P("dp", "tensor"),
        ),
        check_vma=False,
    )
```

```python
import functools

import jax
import jax.numpy as jnp
from jax import lax
from jax.experimental import pallas as pl
from jax.experimental.pallas import tpu as pltpu
from jax.sharding import PartitionSpec as P

KVH = 4
HD = 64
PAIR = 2 * HD

epsilon = 1e-05
rope_base = 10000.0
masked = -1e30


def doc_positions(seg_row):
    length = seg_row.shape[0]
    places = jnp.arange(length, dtype=jnp.int32)
    change = jnp.concatenate([jnp.ones((1,), jnp.bool_), seg_row[1:] != seg_row[:-1]])
    starts = lax.cummax(jnp.where(change, places, 0), axis=0)
    return places - starts


def rope_tables(places, width):
    half_width = width // 2
    frequency = rope_base ** (-(2.0 * jnp.arange(half_width).astype(jnp.float32)) / width)
    angles = places.astype(jnp.float32)[:, None] * frequency[None, :]
    return (jnp.cos(angles), jnp.sin(angles))


def rotate(values, cosine, sine_table):
    rows, width = values.shape
    heads = values.reshape(rows, width // HD, HD)
    half_width = HD // 2
    front_half = heads[..., :half_width]
    back_half = heads[..., half_width:]
    cos_rows = cosine[:, None, :]
    sin_rows = sine_table[:, None, :]
    turned = jnp.concatenate(
        [
            front_half * cos_rows - back_half * sin_rows,
            back_half * cos_rows + front_half * sin_rows,
        ],
        axis=-1,
    )
    return turned.reshape(rows, width)


def norm_forward(values, gain_vec):
    inverse = lax.rsqrt(jnp.mean(values * values, axis=-1, keepdims=True) + epsilon)
    unit_rows = values * inverse
    return (unit_rows * gain_vec, unit_rows, inverse)


def norm_backward(d_normed, unit_rows, inverse, gain_vec):
    gain_part = jnp.sum(d_normed * unit_rows, axis=0)
    d_unit = d_normed * gain_vec
    d_values = inverse * (d_unit - unit_rows * jnp.mean(d_unit * unit_rows, axis=-1, keepdims=True))
    return (d_values, gain_part)


def dot_nn(left, right):
    return jnp.dot(left, right, preferred_element_type=jnp.float32)


def dot_nt(left, right):
    return lax.dot_general(
        left, right, (((1,), (1,)), ((), ())), preferred_element_type=jnp.float32
    )


def dot_tn(left, right):
    return lax.dot_general(
        left, right, (((0,), (0,)), ((), ())), preferred_element_type=jnp.float32
    )


def front_lanes(tile):
    lane = lax.broadcasted_iota(jnp.int32, tile.shape, 1)
    return jnp.where(lane < HD, tile, jnp.zeros_like(tile))


def back_lanes(tile):
    lane = lax.broadcasted_iota(jnp.int32, tile.shape, 1)
    return jnp.where(lane < HD, jnp.zeros_like(tile), tile)


def attend_forward_kernel(query_ref, front_ref, back_ref, value_t_ref, bias_ref, out_ref, log_ref):
    pairs = query_ref.shape[1] // PAIR
    value_t = value_t_ref[0]
    for pair in range(pairs):
        query = query_ref[:, pair * PAIR : (pair + 1) * PAIR]
        outs = []
        for side, key_ref in enumerate((front_ref, back_ref)):
            scores = dot_nt(key_ref[0], query) + bias_ref[...]
            top = jnp.max(scores, axis=0, keepdims=True)
            expo = jnp.exp(scores - top)
            total = jnp.sum(expo, axis=0, keepdims=True)
            outs.append(dot_nn(value_t, expo.astype(jnp.bfloat16)) / total)
            log_ref[0, pl.ds(pair * 2 + side, 1), :] = top + jnp.log(total)
        out = jnp.concatenate(outs, axis=0).T
        out_ref[:, pair * PAIR : (pair + 1) * PAIR] = out.astype(jnp.bfloat16)


def attend_backward_kernel(
    query_ref,
    grad_ref,
    kf_ref,
    kb_ref,
    kt_ref,
    vf_ref,
    vb_ref,
    bias_ref,
    log_ref,
    dq_ref,
    dk_ref,
    dv_ref,
):
    pairs = query_ref.shape[1] // PAIR
    key_t = kt_ref[0]
    dk_ref[0] = jnp.zeros(dk_ref.shape[1:], jnp.float32)
    dv_ref[0] = jnp.zeros(dv_ref.shape[1:], jnp.float32)
    for pair in range(pairs):
        columns = slice(pair * PAIR, (pair + 1) * PAIR)
        query = query_ref[:, columns]
        grad = grad_ref[:, columns]
        outs = []
        for side, (key_ref, value_ref, keep) in enumerate(
            ((kf_ref, vf_ref, front_lanes), (kb_ref, vb_ref, back_lanes))
        ):
            log_sum = log_ref[0, pl.ds(pair * 2 + side, 1), :]
            probs = jnp.exp(dot_nt(key_ref[0], query) + bias_ref[...] - log_sum)
            d_probs = dot_nt(value_ref[0], grad)
            row_dot = jnp.sum(probs * d_probs, axis=0, keepdims=True)
            d_scores = (probs * (d_probs - row_dot)).astype(jnp.bfloat16)
            dk_ref[0] += dot_nn(d_scores, keep(query))
            dv_ref[0] += dot_nn(probs.astype(jnp.bfloat16), keep(grad))
            outs.append(dot_nn(key_t, d_scores))
        dq_ref[:, columns] = jnp.concatenate(outs, axis=0).T * (HD**-0.5)


def whole_group(rows, width):
    return pl.BlockSpec((1, rows, width), lambda g: (g, 0, 0))


def columns_of(rows, width):
    return pl.BlockSpec((rows, width), lambda g: (0, g))


def attend_forward(query, key_f, key_b, value_t, bias):
    rows, width = query.shape
    length = bias.shape[0]
    group = width // KVH
    return pl.pallas_call(
        attend_forward_kernel,
        grid=(KVH,),
        in_specs=[
            columns_of(rows, group),
            whole_group(length, PAIR),
            whole_group(length, PAIR),
            whole_group(HD, length),
            pl.BlockSpec((length, rows), lambda g: (0, 0)),
        ],
        out_specs=[columns_of(rows, group), whole_group(group // HD, rows)],
        out_shape=[
            jax.ShapeDtypeStruct((rows, width), jnp.bfloat16),
            jax.ShapeDtypeStruct((KVH, group // HD, rows), jnp.float32),
        ],
        compiler_params=pltpu.CompilerParams(vmem_limit_bytes=48 * 1024 * 1024),
        name="attend_forward",
    )(query, key_f, key_b, value_t, bias)


def attend_backward(query, grad, key_f, key_b, key_t, value_f, value_b, bias, log_sum):
    rows, width = query.shape
    length = bias.shape[0]
    group = width // KVH
    tall = whole_group(length, PAIR)
    return pl.pallas_call(
        attend_backward_kernel,
        grid=(KVH,),
        in_specs=[
            columns_of(rows, group),
            columns_of(rows, group),
            tall,
            tall,
            whole_group(HD, length),
            tall,
            tall,
            pl.BlockSpec((length, rows), lambda g: (0, 0)),
            whole_group(group // HD, rows),
        ],
        out_specs=[columns_of(rows, group), tall, tall],
        out_shape=[
            jax.ShapeDtypeStruct((rows, width), jnp.float32),
            jax.ShapeDtypeStruct((KVH, length, PAIR), jnp.float32),
            jax.ShapeDtypeStruct((KVH, length, PAIR), jnp.float32),
        ],
        compiler_params=pltpu.CompilerParams(vmem_limit_bytes=48 * 1024 * 1024),
        name="attend_backward",
    )(query, grad, key_f, key_b, key_t, value_f, value_b, bias, log_sum)


def by_head(matrix):
    rows = matrix.shape[0]
    return matrix.reshape(rows, KVH, HD).transpose(1, 0, 2)


MESH = pl.DeviceIdType.MESH


def flip(index, bit):
    return index + bit - 2 * bit * ((index // bit) % 2)


def line_order(place):
    nearest = place - 1 + 2 * (1 - (place + 3) // 4)
    farthest = 3 - 3 * (place // 2)
    return (nearest, 6 - place - nearest - farthest, farthest)


def enter(dp, place):
    barrier = pltpu.get_barrier_semaphore()
    for bit in (1, 2, 4):
        pl.semaphore_signal(barrier, inc=1, device_id=(flip(dp, bit), place), device_id_type=MESH)
    for step in (-1, 1):
        there = (place + step >= 0) & (place + step < 4)

        @pl.when(there)
        def _():
            pl.semaphore_signal(
                barrier, inc=1, device_id=(dp, place + step), device_id_type=MESH
            )

    ends = 1 - ((place + 3) // 4) + place // 3
    pl.semaphore_wait(barrier, 5 - ends)


def turn(tile, cos, sin):
    lane = lax.broadcasted_iota(jnp.int32, tile.shape, 1)
    swapped = jnp.where(
        lane % HD < HD // 2, pltpu.roll(tile, PAIR - HD // 2, 1), pltpu.roll(tile, HD // 2, 1)
    )
    return tile * cos + swapped * sin


def head_tiles(keyval, group):
    columns = slice(group // 2 * PAIR, (group // 2 + 1) * PAIR)
    tile = keyval[:, columns]
    values = slice(KVH * HD + columns.start, KVH * HD + columns.stop)
    if group % 2 == 0:
        front = front_lanes(tile)
        keys = (front, pltpu.roll(front, HD, 1))
    else:
        back = back_lanes(tile)
        keys = (pltpu.roll(back, HD, 1), back)
    return keys, keyval[:, values]


def attend_kernel(
    tokens_ref, normed_ref, cos_ref, sin_ref, bias_ref, gain_ref,
    kv_ref, q_ref, o_ref, d_ref, g_ref, u_ref, c_ref,
    query_out, keyval_out, heads_out, log_out, residual_out, mlp_out,
    fkv, fq, fo, fd, fg, fu, fc,
    kv_weight, weight, wide_weight, keyval, key_f, key_b, value_t,
    own_sem, z_send, z_recv, p_send, p_recv, k_send, k_recv, w_sem,
):
    dp, place = lax.axis_index("dp"), lax.axis_index("tensor")
    rows = kv_ref.shape[0]
    half = rows // 2
    width = q_ref.shape[1]
    order = line_order(place)
    enter(dp, place)

    def rows_of(owner):
        return pl.ds(pl.multiple_of(owner * rows, rows), rows)

    def columns_of_rank(rank):
        return pl.ds(pl.multiple_of(rank * width, width), width)

    def remote(src, dst, send, recv, device):
        return pltpu.make_async_remote_copy(
            src_ref=src, dst_ref=dst, send_sem=send, recv_sem=recv,
            device_id=device, device_id_type=MESH,
        )

    own = [
        (kv_ref, fkv.at[rows_of(dp), :]),
        (q_ref, fq.at[rows_of(dp), columns_of_rank(place)]),
        (o_ref, fo.at[rows_of(dp), columns_of_rank(place)]),
        (d_ref, fd.at[rows_of(dp), :]),
        (g_ref, fg.at[rows_of(dp), :]),
        (u_ref, fu.at[rows_of(dp), :]),
        (c_ref, fc.at[rows_of(place), :]),
    ]
    own_copies = [
        pltpu.make_async_copy(src, dst, own_sem.at[i]) for i, (src, dst) in enumerate(own)
    ]
    for copy in own_copies:
        copy.start()

    def line_block(which, rank):
        if which == 2:
            return fc.at[rows_of(rank), :]
        return (fq, fo)[which].at[rows_of(dp), columns_of_rank(rank)]

    def line_copy(which, rank, step):
        src = (q_ref, o_ref, c_ref)[which] if rank is place else line_block(which, rank)
        side = 0 if step < 0 else 1
        return remote(
            src, line_block(which, rank), z_send.at[which, side, rank], z_recv.at[which, rank],
            (dp, place + step),
        )

    def line_send(which, rank, act):
        @pl.when((rank <= place) & (place < 3))
        def _():
            act(line_copy(which, rank, 1))

        @pl.when((rank >= place) & (place > 0))
        def _():
            act(line_copy(which, rank, -1))

    def start(copy):
        copy.start()

    def wait_send(copy):
        copy.wait_send()

    x, y, core = flip(dp, 2), flip(dp, 4), flip(dp, 1)
    far = flip(x, 4)

    blocks = [("kv", None), ("q", place), ("q", order[0]), ("q", order[1]), ("q", order[2])]
    blocks += [("o", place), ("o", order[0]), ("o", order[1]), ("o", order[2])]
    blocks += [("d", None), ("g", None), ("u", None)]

    def block(index, owner, part=None):
        name, rank = blocks[index]
        ref = {"kv": fkv, "q": fq, "o": fo, "d": fd, "g": fg, "u": fu}[name]
        first = owner * rows if part is None else owner * rows + part * half
        size = rows if part is None else half
        window = pl.ds(pl.multiple_of(first, half), size)
        if rank is None:
            return ref.at[window, :]
        return ref.at[window, columns_of_rank(rank)]

    def own_block(index):
        name, rank = blocks[index]
        if rank is None or rank is place:
            return {"kv": kv_ref, "q": q_ref, "o": o_ref, "d": d_ref, "g": g_ref, "u": u_ref}[name]
        return block(index, dp)

    def plane_copy(index, lane):
        send, recv = p_send.at[index, lane], p_recv.at[index, lane]
        if lane == 0:
            return remote(own_block(index), block(index, dp), send, recv, (x, place))
        if lane == 1:
            return remote(own_block(index), block(index, dp), send, recv, (y, place))
        if lane == 2:
            return remote(block(index, x, 0), block(index, x, 0), send, recv, (y, place))
        if lane == 3:
            return remote(block(index, y, 1), block(index, y, 1), send, recv, (x, place))
        owner = (dp, x, y, far)[lane - 4]
        src = own_block(index) if lane == 4 else block(index, owner)
        return remote(src, block(index, owner), send, recv, (core, place))

    def plane_first(index):
        plane_copy(index, 0).start()
        plane_copy(index, 1).start()
        plane_copy(index, 4).start()

    def plane_second(index):
        plane_copy(index, 0).wait_recv()
        plane_copy(index, 2).start()
        plane_copy(index, 5).start()
        plane_copy(index, 1).wait_recv()
        plane_copy(index, 3).start()
        plane_copy(index, 6).start()

    def plane_third(index):
        plane_copy(index, 2).wait_recv()
        plane_copy(index, 3).wait_recv()
        plane_copy(index, 7).start()

    def plane_ready(index):
        for lane in range(4, 8):
            plane_copy(index, lane).wait_recv()

    def plane_sent(index):
        for lane in range(8):
            plane_copy(index, lane).wait_send()

    def keyval_block(rank):
        return keyval.at[rows_of(rank), :]

    def keyval_copy(rank, step):
        side = 0 if step < 0 else 1
        return remote(
            keyval_block(rank), keyval_block(rank), k_send.at[side, rank], k_recv.at[rank],
            (dp, place + step),
        )

    def keyval_send(rank, act):
        @pl.when((rank <= place) & (place < 3))
        def _():
            act(keyval_copy(rank, 1))

        @pl.when((rank >= place) & (place > 0))
        def _():
            act(keyval_copy(rank, -1))

    def keyval_take(step):
        keyval_copy(order[step], 1).wait_recv()
        keyval_send(order[step], start)

    low = jnp.bfloat16
    wide = KVH * HD

    def make_keyval():
        load = pltpu.make_async_copy(fkv, kv_weight, w_sem.at[0])
        load.start()
        load.wait()
        made = dot_nn(normed_ref[...], kv_weight[...])
        for tile in range(wide // PAIR):
            columns = slice(tile * PAIR, (tile + 1) * PAIR)
            keyval[rows_of(place), columns] = turn(
                made[:, columns], cos_ref[...], sin_ref[...]
            ).astype(low)
        keyval[rows_of(place), wide:] = made[:, wide:].astype(low)
        keyval_send(place, start)

    def weight_load(source, rank, by_rows):
        window = pl.ds(pl.multiple_of(rank * width, width), width)
        src = source.at[window, :] if by_rows else source.at[:, window]
        dst = wide_weight.at[rank % 2] if by_rows else weight.at[rank % 2]
        return pltpu.make_async_copy(src, dst, w_sem.at[rank % 2])

    def make_query():
        weight_load(fq, 0, False).start()
        for rank in range(4):
            if rank < 3:
                weight_load(fq, rank + 1, False).start()
            weight_load(fq, rank, False).wait()
            made = dot_nn(normed_ref[...], weight[rank % 2])
            for tile in range(width // PAIR):
                columns = slice(tile * PAIR, (tile + 1) * PAIR)
                query_out[:, rank * width + tile * PAIR : rank * width + (tile + 1) * PAIR] = (
                    turn(made[:, columns], cos_ref[...], sin_ref[...]) * (HD**-0.5)
                ).astype(low)

    def attend(group):
        key_tile, value_tile = head_tiles(keyval, group)
        key_f[...], key_b[...] = key_tile
        side = group % 2
        value_t[...] = value_tile.T[side * HD : (side + 1) * HD, :]
        pairs = query_out.shape[1] // PAIR // KVH

        @pl.loop(0, pairs)
        def _(index):
            pair = group * pairs + index
            columns = pl.ds(pl.multiple_of(pair * PAIR, PAIR), PAIR)
            query = query_out[:, columns]
            outs, logs = [], []
            for key_ref in (key_f, key_b):
                scores = dot_nt(key_ref[...], query) + bias_ref[...]
                top = jnp.max(scores, axis=0, keepdims=True)
                expo = jnp.exp(scores - top)
                total = jnp.sum(expo, axis=0, keepdims=True)
                outs.append(dot_nn(value_t[...], expo.astype(low)) / total)
                logs.append(top + jnp.log(total))
            log_out[pair] = jnp.concatenate(logs, axis=0)
            heads_out[:, columns] = jnp.concatenate(outs, axis=0).T.astype(low)

    def make_residual():
        weight_load(fo, 0, True).start()
        square = jnp.zeros((rows, 1), jnp.float32)
        for rank in range(4):
            if rank < 3:
                weight_load(fo, rank + 1, True).start()
            weight_load(fo, rank, True).wait()
            columns = slice(rank * width, (rank + 1) * width)
            made = tokens_ref[:, columns].astype(jnp.float32) + dot_nt(
                heads_out[...], wide_weight[rank % 2]
            )
            residual_out[:, columns] = made
            square += jnp.sum(made * made, axis=1, keepdims=True)
        inverse = lax.rsqrt(square * (1.0 / (4 * width)) + epsilon)
        for rank in range(4):
            columns = slice(rank * width, (rank + 1) * width)
            mlp_out[:, columns] = (
                residual_out[:, columns] * inverse * gain_ref[:, columns]
            ).astype(low)

    line_send(0, place, start)
    plane_first(0)
    plane_first(1)
    count = len(blocks)
    line_of = {2: (0, 0), 3: (0, 1), 4: (0, 2), 6: (1, 0), 7: (1, 1), 8: (1, 2)}
    for index in range(count):
        ahead = index + 2
        if ahead < count:
            if ahead in line_of:
                which, step = line_of[ahead]
                line_copy(which, order[step], 1).wait_recv()
                line_send(which, order[step], start)
            plane_first(ahead)
        if index == 0:
            line_send(1, place, start)
        if index == 6:
            line_send(2, place, start)
        if index >= 9:
            line_copy(2, order[index - 9], 1).wait_recv()
            line_send(2, order[index - 9], start)
        plane_second(index)
        if index >= 1:
            plane_third(index - 1)
        if index == 1:
            plane_ready(0)
            own_copies[0].wait()
            make_keyval()
        if 2 <= index <= 4:
            keyval_take(index - 2)
        if index == 5:
            for block_index in range(1, 5):
                plane_ready(block_index)
            own_copies[1].wait()
            make_query()
        if 6 <= index <= 9:
            attend(index - 6)
        if index == 10:
            for block_index in range(5, 9):
                plane_ready(block_index)
            own_copies[2].wait()
            make_residual()
    plane_third(count - 1)
    for index in range(9, count):
        plane_ready(index)
    for index in range(count):
        plane_sent(index)
    for which in range(3):
        line_send(which, place, wait_send)
        for step in range(3):
            line_send(which, order[step], wait_send)
    keyval_send(place, wait_send)
    for step in range(3):
        keyval_send(order[step], wait_send)
    for copy in own_copies[3:]:
        copy.wait()
    out_copy = pltpu.make_async_copy(keyval, keyval_out, w_sem.at[0])
    out_copy.start()
    out_copy.wait()


def attend_all(
    tokens, normed, cos, sin, bias, gain, w_keyval, w_query, w_output, w_down, w_gate, w_up,
    cotangent,
):
    n_dp, n_line = lax.axis_size("dp"), lax.axis_size("tensor")
    low = jnp.bfloat16
    rows, depth = tokens.shape
    length = bias.shape[0]
    wide = 2 * KVH * HD
    heads = w_query.shape[1] * n_line // HD

    def over(array, by_rows, by_columns):
        shape = (array.shape[0] * by_rows, array.shape[1] * by_columns)
        return jax.ShapeDtypeStruct(shape, array.dtype)

    anywhere = pl.BlockSpec(memory_space=pl.ANY)
    in_vmem = pl.BlockSpec(memory_space=pltpu.VMEM)
    shapes = [
        jax.ShapeDtypeStruct((rows, heads * HD), low),
        jax.ShapeDtypeStruct((length, wide), low),
        jax.ShapeDtypeStruct((rows, heads * HD), low),
        jax.ShapeDtypeStruct((heads // 2, 2, rows), jnp.float32),
        jax.ShapeDtypeStruct((rows, depth), jnp.float32),
        jax.ShapeDtypeStruct((rows, depth), low),
        over(w_keyval, n_dp, 1),
        over(w_query, n_dp, n_line),
        over(w_output, n_dp, n_line),
        over(w_down, n_dp, 1),
        over(w_gate, n_dp, 1),
        over(w_up, n_dp, 1),
        over(cotangent, n_line, 1),
    ]
    dma = pltpu.SemaphoreType.DMA
    return pl.pallas_call(
        attend_kernel,
        out_shape=shapes,
        in_specs=[in_vmem] * 6 + [anywhere] * 7,
        out_specs=[in_vmem, anywhere] + [in_vmem] * 4 + [anywhere] * 7,
        scratch_shapes=[
            pltpu.VMEM((depth, wide), low),
            pltpu.VMEM((2, depth, w_query.shape[1]), low),
            pltpu.VMEM((2, w_query.shape[1], depth), low),
            pltpu.VMEM((length, wide), low),
            pltpu.VMEM((length, PAIR), low),
            pltpu.VMEM((length, PAIR), low),
            pltpu.VMEM((HD, length), low),
            dma((7,)), dma((3, 2, 4)), dma((3, 4)), dma((12, 8)), dma((12, 8)),
            dma((2, 4)), dma((4,)), dma((2,)),
        ],
        compiler_params=pltpu.CompilerParams(
            collective_id=0, has_side_effects=True, vmem_limit_bytes=62 * 1024 * 1024
        ),
        name="attend_all",
    )(
        tokens, normed, cos, sin, bias, gain, w_keyval, w_query, w_output, w_down, w_gate, w_up,
        cotangent,
    )


def add_rows(target, source, step=32):
    @pl.loop(0, target.shape[0] // step)
    def _(index):
        window = pl.ds(pl.multiple_of(index * step, step), step)
        target[window, :] = target[window, :] + source[window, :]


def over_rows(total_rows, act, step=32):
    @pl.loop(0, total_rows // step)
    def _(index):
        act(pl.ds(pl.multiple_of(index * step, step), step))


def reach_back_kernel(
    gd_ref, gg_ref, gu_ref, branch_ref, fkv, fq, fo, dn_ref, residual_ref,
    cot_ref, tokens_ref, normed_ref, query_ref, heads_ref, keyval_ref, log_ref, bias_ref,
    cos_ref, sin_ref, gain_attn_ref, gain_mlp_ref,
    gd_out, gg_out, gu_out, go_out, gq_out, nar_out, layer_out, tokens_out,
    gd_core, gg_core, gu_core, go_core, gq_core, nar_core,
    gd_side, gg_side, gu_side, go_side, gq_side, nar_side,
    gd_near, gg_near, gu_near, go_near, gq_near, nar_near,
    go_in, gq_in, nar_in, dkv_in, layer_in,
    parts, held, stage, go_line, gq_line, nar_line, dkv_line, layer_line,
    d_residual, total, wide, d_branch, d_heads, dq_low, dkv_low, gains, weight, kv_weight,
    key_f, key_b, key_t, value_f, value_b, dk, dv,
    load_sem, fetch_sem, core_send, core_recv, p_send, p_recv, l_send, l_recv, in_sem, w_sem,
):
    dp, place = lax.axis_index("dp"), lax.axis_index("tensor")
    low = jnp.bfloat16
    rows, depth = d_branch.shape
    half = rows // 2
    enter(dp, place)
    x, y, core = flip(dp, 2), flip(dp, 4), flip(dp, 1)
    far = flip(x, 4)
    mine = (dp, x, y, far)
    theirs = tuple(flip(owner, 1) for owner in mine)
    grads = (gd_ref, gg_ref, gu_ref)
    outs = (gd_out, gg_out, gu_out, go_out, gq_out, nar_out)
    cores = (gd_core, gg_core, gu_core, go_core, gq_core, nar_core)
    sides = (gd_side, gg_side, gu_side, go_side, gq_side, nar_side)
    nears = (gd_near, gg_near, gu_near, go_near, gq_near, nar_near)
    lines = {3: go_line, 4: gq_line, 5: nar_line, 6: dkv_line, 7: layer_line}
    arrivals = {3: go_in, 4: gq_in, 5: nar_in, 6: dkv_in, 7: layer_in}
    front, back = pl.ds(0, half), pl.ds(half, half)
    ranks = dkv_line.shape[0]
    last = ranks - 1
    turns = (3, 1, 2, 0)

    def rows_of(owner):
        return pl.ds(pl.multiple_of(owner * rows, rows), rows)

    def remote(src, dst, send, recv, device):
        return pltpu.make_async_remote_copy(
            src_ref=src, dst_ref=dst, send_sem=send, recv_sem=recv,
            device_id=device, device_id_type=MESH,
        )

    def width_of(i):
        return cores[i].shape[2]

    def part(i, k):
        return parts.at[i % 2, k, :, pl.ds(0, width_of(i))]

    def half_part(i, k, window):
        return parts.at[i % 2, k, window, pl.ds(0, width_of(i))]

    def held_part(slot, count, width):
        return held.at[slot, pl.ds(0, count), pl.ds(0, width)]

    def fetch(src, slot):
        return pltpu.make_async_copy(
            src, held_part(slot, src.shape[0], src.shape[1]), fetch_sem.at[slot]
        )

    def core_copy(i, k):
        if i < 3:
            src = grads[i].at[rows_of(theirs[k]), :]
        else:
            src = stage.at[turns.index(k) % 2, :, pl.ds(0, width_of(i))]
        return remote(
            src, cores[i].at[k], core_send.at[i, k], core_recv.at[i, k], (core, place)
        )

    def own_load(i, k):
        return pltpu.make_async_copy(
            grads[i].at[rows_of(mine[k]), :], part(i, k), load_sem.at[i, k]
        )

    def plane_copy(i, lane):
        src, dst, device = (
            (half_part(i, 3, front), sides[i].at[0], y),
            (half_part(i, 3, back), sides[i].at[1], x),
            (half_part(i, 1, back), nears[i].at[0, back, :], x),
            (half_part(i, 2, front), nears[i].at[1, front, :], y),
            (half_part(i, 1, front), nears[i].at[0, front, :], x),
            (half_part(i, 2, back), nears[i].at[1, back, :], y),
        )[lane]
        return remote(src, dst, p_send.at[i, lane], p_recv.at[i, lane], (device, place))

    def plane_sent(i):
        for lane in range(6):
            plane_copy(i, lane).wait_send()

    def load_own(i):
        for k in turns:
            own_load(i, k).start()

    def stage_core(i):
        def begin(n):
            core_copy(i, turns[n]).wait_recv()
            fetch(cores[i].at[turns[n]], n % 2).start()

        begin(0)
        begin(1)
        for n, k in enumerate(turns):
            fetch(cores[i].at[k], n % 2).wait()
            if i < 3:
                own_load(i, k).wait()
            add_rows(part(i, k), held_part(n % 2, rows, width_of(i)))
            for lane in ((), (2,), (3,), (0, 1))[k]:
                plane_copy(i, lane).start()
            if n + 2 < 4:
                begin(n + 2)

    def stage_side(i):
        for side in range(2):
            plane_copy(i, side).wait_recv()
            fetch(sides[i].at[side], side).start()
        for side, (k, window, lane) in enumerate(((1, front, 4), (2, back, 5))):
            fetch(sides[i].at[side], side).wait()
            add_rows(half_part(i, k, window), held_part(side, half, width_of(i)))
            plane_copy(i, lane).start()

    def stage_near(i):
        for side, lanes in enumerate(((2, 4), (3, 5))):
            for lane in lanes:
                plane_copy(i, lane).wait_recv()
            fetch(nears[i].at[side], side).start()
        for side in range(2):
            fetch(nears[i].at[side], side).wait()
        own, width, out = part(i, 0), width_of(i), outs[i]

        @pl.loop(0, rows // 32)
        def _(index):
            window = pl.ds(pl.multiple_of(index * 32, 32), 32)
            sums = (
                own[window, :].astype(jnp.float32)
                + held[0, window, pl.ds(0, width)].astype(jnp.float32)
                + held[1, window, pl.ds(0, width)].astype(jnp.float32)
            )
            if i < 3:
                out[window, :] = sums
            elif i < 5:
                piece = width // ranks
                for rank in range(ranks):
                    lines[i][rank, window, :] = sums[:, rank * piece : (rank + 1) * piece].astype(
                        low
                    )
            else:
                per = rows // ranks
                lines[i][index * 32 // per, pl.ds(pl.multiple_of(index * 32 % per, 32), 32), :] = (
                    sums.astype(low)
                )

    def line_copy(i, rank, slot, step):
        src = lines[i].at[(step + 1) // 2] if i == 7 else lines[i].at[rank]
        return remote(
            src, arrivals[i].at[slot], l_send.at[i - 3, rank], l_recv.at[i - 3, slot],
            (dp, place + step),
        )

    def line_add(i, ref, slot, step):
        line_copy(i, slot, slot, step).wait_recv()
        copy = fetch(arrivals[i].at[slot], 0)
        copy.start()
        copy.wait()
        add_rows(ref, held_part(0, ref.shape[0], ref.shape[1]))

    def line_own(i, rank, step):
        if i != 7:
            return lines[i].at[rank]
        ref = lines[i].at[(step + 1) // 2]
        copy = pltpu.make_async_copy(branch_ref.at[rank], ref, in_sem.at[0])
        copy.start()
        copy.wait()
        return ref

    def line_step(i, turn):
        down, up = place - last + turn, place + last - turn

        @pl.when(down >= 0)
        def _():
            if i == 7 and turn > 0:

                @pl.when(down > 0)
                def _():
                    line_copy(i, down - 1, down - 1, -1).wait_send()

            ref = line_own(i, down, -1)

            @pl.when(place < last)
            def _():
                line_add(i, ref, down, -1)

            line_copy(i, down, down, -1).start()

        @pl.when(up <= last)
        def _():
            if i == 7 and turn > 0:

                @pl.when(up < last)
                def _():
                    line_copy(i, up + 1, up + 1, 1).wait_send()

            ref = line_own(i, up, 1)

            @pl.when(place > 0)
            def _():
                line_add(i, ref, up, 1)

            line_copy(i, up, ranks if turn == last - 1 else up, 1).start()

    def line_last(i, add):
        @pl.when(place < last)
        def _():
            line_copy(i, place, place, 1).wait_recv()
            copy = fetch(arrivals[i].at[place], 0)
            copy.start()
            copy.wait()
            add()

        @pl.when(place > 0)
        def _():
            line_copy(i, place, ranks, 1).wait_recv()
            copy = fetch(arrivals[i].at[ranks], 0)
            copy.start()
            copy.wait()
            add()

    def line_sent(i):
        for rank in range(ranks):
            if i == 7:

                @pl.when((rank == place - 1) | (rank == place + 1))
                def _():
                    line_copy(i, rank, rank, 1).wait_send()

            else:

                @pl.when(rank != place)
                def _():
                    line_copy(i, rank, rank, 1).wait_send()

    def line_out(i):
        out = outs[i]
        count, width = out.shape

        def begin(window):
            out[window, :] = lines[i][place, window, :].astype(jnp.float32)

        def add():
            def act(window):
                out[window, :] += held[0, window, pl.ds(0, width)].astype(jnp.float32)

            over_rows(count, act)

        over_rows(count, begin)
        line_last(i, add)

    def norm_back(grad_ref, rows_ref, gain_ref, gain_row, act):
        gains[gain_row : gain_row + 1, :] = jnp.zeros((1, depth), jnp.float32)

        def block(window):
            values = rows_ref[window, :].astype(jnp.float32)
            inverse = lax.rsqrt(jnp.mean(values * values, axis=1, keepdims=True) + epsilon)
            unit = values * inverse
            grad = grad_ref[window, :]
            gains[gain_row : gain_row + 1, :] += jnp.sum(grad * unit, axis=0, keepdims=True)
            d_unit = grad * gain_ref[...]
            act(
                window,
                inverse * (d_unit - unit * jnp.mean(d_unit * unit, axis=1, keepdims=True)),
            )

        over_rows(rows, block, 64)

    def after_mlp(window, d_values):
        made = cot_ref[window, :].astype(jnp.float32) + d_values
        d_residual[window, :] = made
        d_branch[window, :] = made.astype(low)

    def after_attn(window, d_values):
        tokens_out[window, :] = (d_residual[window, :] + d_values).astype(low)

    def square_tile(left, right, owner):
        columns = pl.ds(pl.multiple_of(owner * rows, rows), rows)
        return dot_tn(left[:, columns], right[...]).astype(low)

    def narrow_tile(owner):
        columns = pl.ds(pl.multiple_of(owner * rows, rows), rows)
        keys = dot_tn(normed_ref[:, columns], dkv_low[...]).astype(low)
        line = lax.broadcasted_iota(jnp.int32, (PAIR, rows), 0)
        both = jnp.where(
            line == 0, gains[0:1, columns], jnp.where(line == 1, gains[1:2, columns], 0.0)
        )
        return jnp.concatenate([keys, both.T.astype(low)], axis=1)

    def send_theirs(i, tile):
        for n, k in enumerate(turns):
            if n >= 2:
                core_copy(i, turns[n - 2]).wait_send()
            stage[n % 2, :, pl.ds(0, width_of(i))] = tile(theirs[k])
            core_copy(i, k).start()

    def theirs_sent(i):
        for k in turns[2:]:
            core_copy(i, k).wait_send()

    def keep_mine(i, tile):
        for k in turns:
            parts[i % 2, k, :, pl.ds(0, width_of(i))] = tile(mine[k])

    def go_tile(owner):
        return square_tile(d_branch, heads_ref, owner)

    def gq_tile(owner):
        return square_tile(normed_ref, dq_low, owner)

    size = weight.shape[1]
    steps = depth // size

    def weight_load(source, index):
        return pltpu.make_async_copy(
            source.at[pl.ds(index * size, size), :], weight.at[index % 2], w_sem.at[index % 2]
        )

    def make_d_heads():
        weight_load(fo, 0).start()
        for index in range(steps):
            if index + 1 < steps:
                weight_load(fo, index + 1).start()
            weight_load(fo, index).wait()
            made = dot_nn(d_branch[:, index * size : (index + 1) * size], weight[index % 2])
            if index == 0:
                wide[...] = made
            elif index + 1 < steps:
                wide[...] += made
            else:
                d_heads[...] = (wide[...] + made).astype(low)

    def make_d_normed():
        weight_load(fq, 0).start()
        for index in range(steps):
            if index + 1 < steps:
                weight_load(fq, index + 1).start()
            weight_load(fq, index).wait()
            wide[:, index * size : (index + 1) * size] = dot_nt(
                dq_low[...], weight[index % 2]
            ) + dot_nt(dkv_low[...], kv_weight[index * size : (index + 1) * size, :])

    def attend_back(group):
        (key_f[...], key_b[...]), value_tile = head_tiles(keyval_ref, group)
        side = group % 2
        lane_side = slice(side * HD, (side + 1) * HD)
        tile_columns = slice(group // 2 * PAIR, (group // 2 + 1) * PAIR)
        key_t[...] = keyval_ref[:, tile_columns].T[lane_side, :]
        if side == 0:
            kept = front_lanes(value_tile)
            value_f[...], value_b[...] = kept, pltpu.roll(kept, HD, 1)
        else:
            kept = back_lanes(value_tile)
            value_f[...], value_b[...] = pltpu.roll(kept, HD, 1), kept
        dk[...] = jnp.zeros(dk.shape, jnp.float32)
        dv[...] = jnp.zeros(dv.shape, jnp.float32)
        pairs = query_ref.shape[1] // PAIR // KVH

        @pl.loop(0, pairs)
        def _(index):
            pair = group * pairs + index
            columns = pl.ds(pl.multiple_of(pair * PAIR, PAIR), PAIR)
            query, grad = query_ref[:, columns], d_heads[:, columns]
            logs = log_ref[pair]
            made = []
            for number, (key_ref, value_ref, keep) in enumerate(
                ((key_f, value_f, front_lanes), (key_b, value_b, back_lanes))
            ):
                probs = jnp.exp(
                    dot_nt(key_ref[...], query) + bias_ref[...] - logs[number : number + 1, :]
                )
                d_probs = dot_nt(value_ref[...], grad)
                row_dot = jnp.sum(probs * d_probs, axis=0, keepdims=True)
                d_scores = (probs * (d_probs - row_dot)).astype(low)
                dk[...] += dot_nn(d_scores, keep(query))
                dv[...] += dot_nn(probs.astype(low), keep(grad))
                made.append(dot_nn(key_t[...], d_scores))
            dq = jnp.concatenate(made, axis=0).T * (HD**-0.5)
            dq_low[:, columns] = turn(dq, cos_ref[...], -sin_ref[...]).astype(low)

        for sums, first in ((dk, 0), (dv, KVH * HD)):
            joined = (sums[...] + pltpu.roll(sums[...], HD, 1)).astype(low)
            columns = slice(first + tile_columns.start, first + tile_columns.stop)
            for rank in range(ranks):
                block = joined[rank * rows : (rank + 1) * rows, :]
                if side == 1:
                    block = front_lanes(dkv_line[rank, :, columns]) + back_lanes(block)
                dkv_line[rank, :, columns] = block

    def make_dkv():
        wide_columns = dkv_line.shape[2]

        def begin(window):
            wide[window, pl.ds(0, wide_columns)] = dkv_line[place, window, :].astype(jnp.float32)

        def add():
            def act(window):
                wide[window, pl.ds(0, wide_columns)] += held[
                    0, window, pl.ds(0, wide_columns)
                ].astype(jnp.float32)

            over_rows(rows, act)

        over_rows(rows, begin)
        line_last(6, add)
        for tile in range(wide_columns // PAIR):
            columns = slice(tile * PAIR, (tile + 1) * PAIR)
            made = wide[:, columns]
            if tile < KVH * HD // PAIR:
                made = turn(made, cos_ref[...], -sin_ref[...])
            dkv_low[:, columns] = made.astype(low)

    def finish_layer():
        line_sent(7)
        own = line_own(7, place, -1)

        def begin(window):
            total[window, :] += own[window, :].astype(jnp.float32)

        def add():
            def act(window):
                total[window, :] += held[0, window, :].astype(jnp.float32)

            over_rows(rows, act)

        def end(window):
            layer_out[window, :] = total[window, :].astype(low)

        over_rows(rows, begin)
        line_last(7, add)
        over_rows(rows, end)

    dn_load = pltpu.make_async_copy(dn_ref, wide, in_sem.at[1])
    total_load = pltpu.make_async_copy(residual_ref, total, in_sem.at[2])
    kv_load = pltpu.make_async_copy(fkv, kv_weight, in_sem.at[3])
    for i in range(3):
        for k in turns:
            core_copy(i, k).start()
    for load in (dn_load, total_load, kv_load):
        load.start()
    load_own(0)
    load_own(1)
    line_step(7, 0)
    dn_load.wait()
    total_load.wait()
    norm_back(wide, total, gain_mlp_ref, 1, after_mlp)
    stage_core(0)
    send_theirs(3, go_tile)
    stage_core(1)
    make_d_heads()
    stage_side(0)
    line_step(7, 1)
    attend_back(0)
    stage_near(0)
    plane_sent(0)
    load_own(2)
    stage_side(1)
    attend_back(1)
    stage_core(2)
    stage_near(1)
    plane_sent(1)
    keep_mine(3, go_tile)
    stage_core(3)
    line_step(7, 2)
    attend_back(2)
    stage_side(2)
    attend_back(3)
    theirs_sent(3)
    send_theirs(4, gq_tile)
    line_step(6, 0)
    stage_near(2)
    plane_sent(2)
    keep_mine(4, gq_tile)
    stage_side(3)
    stage_core(4)
    line_step(6, 1)
    stage_near(3)
    plane_sent(3)
    line_step(6, 2)
    line_step(3, 0)
    kv_load.wait()
    make_dkv()
    make_d_normed()
    norm_back(wide, tokens_ref, gain_attn_ref, 0, after_attn)
    theirs_sent(4)
    send_theirs(5, narrow_tile)
    keep_mine(5, narrow_tile)
    stage_side(4)
    line_step(3, 1)
    stage_core(5)
    line_step(3, 2)
    stage_near(4)
    line_step(4, 0)
    stage_side(5)
    finish_layer()
    line_step(4, 1)
    stage_near(5)
    line_step(5, 0)
    line_step(4, 2)
    line_step(5, 1)
    line_out(3)
    line_step(5, 2)
    line_out(4)
    line_out(5)
    plane_sent(4)
    plane_sent(5)
    theirs_sent(5)
    for i in range(3):
        for k in turns:
            core_copy(i, k).wait_send()
    for i in range(3, 7):
        line_sent(i)


def reach_back(grads, branch, full, d_normed, residual, others):
    low, wide = jnp.bfloat16, jnp.float32
    n_dp, ranks = lax.axis_size("dp"), lax.axis_size("tensor")
    units = grads[0].shape[1]
    rows, depth = residual.shape
    half = rows // 2
    square = depth // ranks
    few = depth // n_dp // ranks
    length, keyval = others[5].shape
    narrow = keyval + PAIR
    widths = [units] * 3 + [depth, depth, narrow]
    anywhere = pl.BlockSpec(memory_space=pl.ANY)
    in_vmem = pl.BlockSpec(memory_space=pltpu.VMEM)
    lined = [(rows, square), (rows, square), (few, narrow), (rows, keyval), (rows, depth)]
    out_shape = [jax.ShapeDtypeStruct((rows, units), wide)] * 3
    out_shape += [jax.ShapeDtypeStruct((rows, square), wide)] * 2
    out_shape += [jax.ShapeDtypeStruct((few, narrow), wide)]
    out_shape += [jax.ShapeDtypeStruct((rows, depth), low)] * 2
    out_shape += [jax.ShapeDtypeStruct((4, rows, w), low) for w in widths]
    out_shape += [jax.ShapeDtypeStruct((2, half, w), low) for w in widths]
    out_shape += [jax.ShapeDtypeStruct((2, rows, w), low) for w in widths]
    out_shape += [jax.ShapeDtypeStruct((ranks + 1,) + shape, low) for shape in lined]
    dma = pltpu.SemaphoreType.DMA
    scratch = [
        pltpu.VMEM((2, 4, rows, depth), low),
        pltpu.VMEM((2, rows, depth), low),
        pltpu.VMEM((2, rows, depth), low),
    ]
    scratch += [pltpu.VMEM((ranks,) + shape, low) for shape in lined[:4]]
    scratch += [pltpu.VMEM((2, rows, depth), low)]
    scratch += [pltpu.VMEM((rows, depth), wide)] * 3
    scratch += [pltpu.VMEM((rows, depth), low)] * 3
    scratch += [
        pltpu.VMEM((rows, keyval), low),
        pltpu.VMEM((8, depth), wide),
        pltpu.VMEM((2, square, depth), low),
        pltpu.VMEM((depth, keyval), low),
        pltpu.VMEM((length, PAIR), low),
        pltpu.VMEM((length, PAIR), low),
        pltpu.VMEM((HD, length), low),
        pltpu.VMEM((length, PAIR), low),
        pltpu.VMEM((length, PAIR), low),
        pltpu.VMEM((length, PAIR), wide),
        pltpu.VMEM((length, PAIR), wide),
        dma((3, 4)), dma((2,)), dma((6, 4)), dma((6, 4)), dma((6, 6)), dma((6, 6)),
        dma((5, ranks)), dma((5, ranks + 1)), dma((4,)), dma((2,)),
    ]
    results = pl.pallas_call(
        reach_back_kernel,
        out_shape=out_shape,
        in_specs=[anywhere] * 9 + [in_vmem] * 12,
        out_specs=[in_vmem] * 8 + [anywhere] * 23,
        scratch_shapes=scratch,
        compiler_params=pltpu.CompilerParams(
            collective_id=1, has_side_effects=True, vmem_limit_bytes=63 * 1024 * 1024
        ),
        name="reach_back",
    )(*grads, branch, *full, d_normed, residual, *others)
    return results[:8]


def by_tiles(total, size, act):
    full = total // size

    @pl.loop(0, full)
    def _(index):
        act(pl.ds(pl.multiple_of(index * size, size), size))

    if total % size:
        act(pl.ds(full * size, total % size))


def feed_forward_kernel(
    normed_ref, gate_w_ref, up_w_ref, down_w_ref, cot_ref,
    gg_out, gu_out, gd_out, branch_out, dn_out,
    wg, wu, wd, cot, normed, hid, dg, du, part, arrival, branch_stage, gate_stage, up_stage,
    load_sem, n_send, n_recv, l_send, l_recv, stage_sem,
):
    dp, place = lax.axis_index("dp"), lax.axis_index("tensor")
    rows, depth = normed_ref.shape
    low = jnp.bfloat16
    order = line_order(place)
    cuts = l_send.shape[1]
    few = rows // cuts
    enter(dp, place)

    def remote(src, dst, send, recv, step):
        return pltpu.make_async_remote_copy(
            src_ref=src, dst_ref=dst, send_sem=send, recv_sem=recv,
            device_id=(dp, place + step), device_id_type=MESH,
        )

    def chunk(rank):
        return pl.ds(pl.multiple_of(rank * rows, rows), rows)

    def own_copy(step):
        return remote(
            normed_ref, normed.at[chunk(place), :], n_send.at[(step + 1) // 2, place],
            n_recv.at[place], step,
        )

    def pass_copy(rank, step):
        ref = normed.at[chunk(rank), :]
        return remote(ref, ref, n_send.at[(step + 1) // 2, rank], n_recv.at[rank], step)

    loads = [
        pltpu.make_async_copy(src, dst, load_sem.at[i])
        for i, (src, dst) in enumerate(
            (
                (normed_ref, normed.at[chunk(place), :]),
                (gate_w_ref, wg),
                (up_w_ref, wu),
                (cot_ref, cot),
                (down_w_ref, wd),
            )
        )
    ]

    @pl.when(place < 3)
    def _():
        own_copy(1).start()

    @pl.when(place > 0)
    def _():
        own_copy(-1).start()

    for load in loads:
        load.start()
    for load in loads:
        load.wait()

    def sums_copy(rank, cut, slot, step):
        window = pl.ds(cut * few, few)
        return remote(
            part.at[rank, window, :], arrival.at[slot, window, :], l_send.at[rank, cut],
            l_recv.at[slot, cut], step,
        )

    def branch_copy(rank):
        return pltpu.make_async_copy(branch_stage, branch_out.at[rank], stage_sem.at[0])

    def compute(rank):
        here = chunk(rank)

        def activate(columns):
            gate = dot_nn(normed[here, :], wg[:, columns])
            up = dot_nn(normed[here, :], wu[:, columns])
            d_hidden = dot_nn(cot[here, :], wd[:, columns])
            sig = 1.0 / (1.0 + jnp.exp(-gate))
            silu = gate * sig
            hid[here, columns] = (silu * up).astype(low)
            dg[here, columns] = (d_hidden * up * sig * (1.0 + gate * (1.0 - sig))).astype(low)
            du[here, columns] = (d_hidden * silu).astype(low)

        by_tiles(wg.shape[1], 256, activate)

        def pull(columns):
            part[rank, :, columns] = (
                dot_nt(dg[here, :], wg[columns, :]) + dot_nt(du[here, :], wu[columns, :])
            ).astype(low)

        by_tiles(depth, 512, pull)

    def branch(rank):
        def push(columns):
            branch_stage[:, columns] = dot_nt(hid[chunk(rank), :], wd[columns, :]).astype(low)

        by_tiles(depth, 512, push)
        branch_copy(rank).start()

    def take(rank):
        pass_copy(rank, 1).wait_recv()

        @pl.when((rank < place) & (place < 3))
        def _():
            pass_copy(rank, 1).start()

        @pl.when((rank > place) & (place > 0))
        def _():
            pass_copy(rank, -1).start()

    @pl.loop(0, 4)
    def _(turn):
        rank = jnp.where(
            turn == 0,
            place,
            jnp.where(turn == 1, order[0], jnp.where(turn == 2, order[1], order[2])),
        )

        inside = (place == 1) | (place == 2)

        @pl.when(turn == 1)
        def _():
            take(order[0])

            @pl.when(inside)
            def _():
                take(order[1])

        @pl.when((turn == 2) & (place != 1) & (place != 2))
        def _():
            take(order[1])

        @pl.when(turn == 3)
        def _():
            take(order[2])

        compute(rank)

        @pl.when((turn > 0) & (place == 3))
        def _():
            for cut in range(cuts):
                sums_copy(rank, cut, rank, -1).start()

        @pl.when((turn > 0) & (place == 0))
        def _():
            slot = jnp.where(rank == 1, 4, rank)
            for cut in range(cuts):
                sums_copy(rank, cut, slot, 1).start()

        @pl.when(turn > 0)
        def _():
            branch_copy(rank).wait()

        branch(rank)

    branch_copy(0).wait()

    def gate_copy(tile):
        return pltpu.make_async_copy(gate_stage, gg_out.at[tile, :], stage_sem.at[1])

    def up_copy(tile):
        return pltpu.make_async_copy(up_stage, gu_out.at[tile, :], stage_sem.at[2])

    def down_copy(tile):
        return pltpu.make_async_copy(gate_stage, gd_out.at[tile, :], stage_sem.at[1])

    size = gate_stage.shape[0]

    @pl.loop(0, depth // size)
    def _(index):
        tile = pl.ds(pl.multiple_of(index * size, size), size)
        left = normed[:, tile]
        gate_grad = dot_tn(left, dg[...]).astype(low)

        @pl.when(index > 0)
        def _():
            gate_copy(tile).wait()
            up_copy(tile).wait()

        gate_stage[...] = gate_grad
        gate_copy(tile).start()
        up_stage[...] = dot_tn(left, du[...]).astype(low)
        up_copy(tile).start()

    last = pl.ds(depth - size, size)
    gate_copy(last).wait()
    up_copy(last).wait()

    def relay(rank, slot, step, cut):
        sums_copy(rank, cut, rank, step).wait_recv()
        window = pl.ds(cut * few, few)
        part[rank, window, :] = part[rank, window, :] + arrival[rank, window, :]
        sums_copy(rank, cut, slot, step).start()

    @pl.when((place == 1) | (place == 2))
    def _():
        outward = 3 - 2 * place
        for cut in range(cuts):
            relay(3 - place, 4 - 3 * (place - 1), outward, cut)
        for cut in range(cuts):
            relay(6 - 3 * place, 6 - 3 * place, outward, cut)
            relay(3 * (place - 1), 4 * (place - 1), -outward, cut)

    @pl.loop(0, depth // size)
    def _(index):
        tile = pl.ds(pl.multiple_of(index * size, size), size)
        down_grad = dot_tn(cot[:, tile], hid[...]).astype(low)

        @pl.when(index > 0)
        def _():
            down_copy(tile).wait()

        gate_stage[...] = down_grad
        down_copy(tile).start()

    down_copy(last).wait()

    for cut in range(cuts):
        window = pl.ds(cut * few, few)
        dn_out[window, :] = part[place, window, :].astype(jnp.float32)

        @pl.when(place < 3)
        def _():
            sums_copy(place, cut, place, 1).wait_recv()
            dn_out[window, :] += arrival[place, window, :].astype(jnp.float32)

        @pl.when(place > 0)
        def _():
            sums_copy(place, cut, 4, 1).wait_recv()
            dn_out[window, :] += arrival[4, window, :].astype(jnp.float32)

    @pl.when(place < 3)
    def _():
        own_copy(1).wait_send()

    @pl.when(place > 0)
    def _():
        own_copy(-1).wait_send()

    for rank in range(4):

        @pl.when((rank < place) & (place < 3))
        def _():
            pass_copy(rank, 1).wait_send()

        @pl.when((rank > place) & (place > 0))
        def _():
            pass_copy(rank, -1).wait_send()

        @pl.when(rank != place)
        def _():
            for cut in range(cuts):
                sums_copy(rank, cut, rank, 1).wait_send()


def feed_forward(normed, w_gate, w_up, w_down, cotangent):
    low = jnp.bfloat16
    rows, depth = normed.shape
    length = cotangent.shape[0]
    units = w_gate.shape[1]
    ranks = length // rows
    cuts = 4
    anywhere = pl.BlockSpec(memory_space=pl.ANY)
    in_vmem = pl.BlockSpec(memory_space=pltpu.VMEM)
    dma = pltpu.SemaphoreType.DMA
    flops = 9 * 2 * length * depth * units
    return pl.pallas_call(
        feed_forward_kernel,
        out_shape=[jax.ShapeDtypeStruct((depth, units), low)] * 3
        + [
            jax.ShapeDtypeStruct((ranks, rows, depth), low),
            jax.ShapeDtypeStruct((rows, depth), jnp.float32),
        ],
        in_specs=[anywhere] * 5,
        out_specs=[anywhere] * 4 + [in_vmem],
        scratch_shapes=[pltpu.VMEM((depth, units), low)] * 3
        + [pltpu.VMEM((length, depth), low)] * 2
        + [pltpu.VMEM((length, units), low)] * 3
        + [
            pltpu.VMEM((ranks, rows, depth), low),
            pltpu.VMEM((ranks + 1, rows, depth), low),
            pltpu.VMEM((rows, depth), low),
            pltpu.VMEM((256, units), low),
            pltpu.VMEM((256, units), low),
            dma((5,)), dma((2, ranks)), dma((ranks,)), dma((ranks, cuts)), dma((ranks + 1, cuts)),
            dma((3,)),
        ],
        compiler_params=pltpu.CompilerParams(
            collective_id=2, has_side_effects=True, vmem_limit_bytes=62 * 1024 * 1024
        ),
        cost_estimate=pl.CostEstimate(flops=flops, bytes_accessed=60 << 20, transcendentals=0),
        name="feed_forward",
    )(normed, w_gate, w_up, w_down, cotangent)


def local(
    tokens,
    segments,
    gain_attn,
    w_query,
    w_keyval,
    w_output,
    gain_mlp,
    w_gate,
    w_up,
    w_down,
    cotangent,
):
    tensor_rank = lax.axis_index("tensor")
    length = segments.shape[0]
    rows = tokens.shape[0]
    both = ("dp", "tensor")
    low = jnp.bfloat16

    def gather(array, axes, axis=0):
        return lax.all_gather(array, axes, axis=axis, tiled=True)

    def scatter(array, axes, axis=0):
        return lax.psum_scatter(array, axes, scatter_dimension=axis, tiled=True)

    by_kernels = (lax.axis_size("dp"), lax.axis_size("tensor")) == (8, 4)
    places = doc_positions(segments)
    my_places = lax.dynamic_slice_in_dim(places, tensor_rank * rows, rows, 0)
    my_segments = lax.dynamic_slice_in_dim(segments, tensor_rank * rows, rows, 0)
    cosine, sine_table = rope_tables(my_places, HD)
    order = jnp.arange(length, dtype=jnp.int32)
    allowed = (order[:, None] <= tensor_rank * rows + order[None, :rows]) & (
        segments[:, None] == my_segments[None, :]
    )
    bias = jnp.where(allowed, 0.0, masked).astype(jnp.float32)

    token_rows = tokens.astype(jnp.float32)
    normed_attn, unit_attn, inverse_attn = norm_forward(token_rows, gain_attn)
    normed_attn = normed_attn.astype(low)
    wide = KVH * HD
    if by_kernels:
        cos_tile = jnp.tile(cosine, (1, 4))
        sin_tile = jnp.tile(jnp.concatenate([-sine_table, sine_table], axis=1), (1, 2))
        (
            query, keyval, heads_low, log_sum, residual, normed_mlp,
            full_keyval, full_query, full_output, full_down, full_gate, full_up, piece,
        ) = attend_all(
            tokens, normed_attn, cos_tile, sin_tile, bias, gain_mlp[None, :],
            w_keyval, w_query, w_output, w_down, w_gate, w_up, cotangent,
        )
    else:
        full_keyval = gather(w_keyval, "dp")
        keyval_pre = dot_nn(normed_attn, full_keyval)
        key_low = rotate(keyval_pre[:, :wide], cosine, sine_table).astype(low)
        keyval = jnp.concatenate([key_low, keyval_pre[:, wide:].astype(low)], axis=1)
        keyval = gather(keyval, "tensor")
        full_query = gather(gather(w_query, "tensor", 1), "dp")
        query = rotate(dot_nn(normed_attn, full_query), cosine, sine_table) * (HD**-0.5)
        query = query.astype(low)
    if by_kernels:
        grad_gate, grad_up, grad_down, branch, d_normed_mlp = feed_forward(
            normed_mlp, full_gate, full_up, full_down, piece
        )
        to_down, to_gate, to_up, to_output, to_query, to_narrow, layer_out, grad_tokens = (
            reach_back(
                (grad_down, grad_gate, grad_up),
                branch,
                (full_keyval, full_query, full_output),
                d_normed_mlp,
                residual,
                (
                    cotangent, tokens, normed_attn, query, heads_low, keyval, log_sum, bias,
                    cos_tile, sin_tile, gain_attn[None, :], gain_mlp[None, :],
                ),
            )
        )
        wide = 2 * KVH * HD
        return (
            layer_out,
            grad_tokens,
            to_narrow[:, wide],
            to_query,
            to_narrow[:, :wide],
            to_output,
            to_narrow[:, wide + 1],
            to_gate,
            to_up,
            to_down,
        )

    key_heads, value_heads = by_head(keyval[:, :wide]), by_head(keyval[:, wide:])
    blank = jnp.zeros_like(key_heads)
    key_f = jnp.concatenate([key_heads, blank], axis=2)
    key_b = jnp.concatenate([blank, key_heads], axis=2)
    value_f = jnp.concatenate([value_heads, blank], axis=2)
    value_b = jnp.concatenate([blank, value_heads], axis=2)
    key_t = key_heads.transpose(0, 2, 1)
    value_t = value_heads.transpose(0, 2, 1)
    heads_low, log_sum = attend_forward(query, key_f, key_b, value_t, bias)
    full_output = gather(gather(w_output, "tensor", 1), "dp")
    residual = token_rows + dot_nt(heads_low, full_output)
    full_gate, full_up = gather(w_gate, "dp"), gather(w_up, "dp")
    full_down = gather(w_down, "dp")
    piece = gather(cotangent, "tensor")
    normed_mlp_rows, unit_mlp, inverse_mlp = norm_forward(residual, gain_mlp)
    normed_mlp = normed_mlp_rows.astype(low)
    gathered_mlp = gather(normed_mlp, "tensor")
    gate_act = dot_nn(gathered_mlp, full_gate)
    up_act = dot_nn(gathered_mlp, full_up)
    sigmoid_gate = jax.nn.sigmoid(gate_act)
    silu_gate = gate_act * sigmoid_gate
    hidden_low = (silu_gate * up_act).astype(low)
    d_hidden = dot_nn(piece, full_down)
    d_gate = (d_hidden * up_act * sigmoid_gate * (1.0 + gate_act * (1.0 - sigmoid_gate))).astype(low)
    d_up = (d_hidden * silu_gate).astype(low)
    d_normed_mlp = scatter(
        (dot_nt(d_gate, full_gate) + dot_nt(d_up, full_up)).astype(low), "tensor"
    ).astype(jnp.float32)
    branch = dot_nt(hidden_low, full_down).astype(low)
    grad_down = dot_tn(piece, hidden_low)
    grad_gate = dot_tn(gathered_mlp, d_gate)
    grad_up = dot_tn(gathered_mlp, d_up)
    d_norm_mlp, gain_mlp_part = norm_backward(d_normed_mlp, unit_mlp, inverse_mlp, gain_mlp)
    d_residual = cotangent.astype(jnp.float32) + d_norm_mlp

    d_branch = d_residual.astype(low)
    grad_output = dot_tn(d_branch, heads_low)
    d_heads = dot_nn(d_branch, full_output).astype(low)
    d_queries, d_keys, d_values = attend_backward(
        query, d_heads, key_f, key_b, key_t, value_f, value_b, bias, log_sum
    )

    def flat(parts):
        joined = parts[:, :, :HD] + parts[:, :, HD:]
        return joined.transpose(1, 0, 2).reshape(length, wide)

    d_keyval = scatter(
        jnp.concatenate([flat(d_keys), flat(d_values)], axis=1).astype(low), "tensor"
    ).astype(jnp.float32)
    dq_low = rotate(d_queries, cosine, -sine_table).astype(low)
    dkv_low = jnp.concatenate(
        [rotate(d_keyval[:, :wide], cosine, -sine_table), d_keyval[:, wide:]], axis=1
    ).astype(low)
    grad_query = dot_tn(normed_attn, dq_low)
    grad_keyval = dot_tn(normed_attn, dkv_low)
    d_normed_attn = dot_nt(dq_low, full_query) + dot_nt(dkv_low, full_keyval)
    d_norm_attn, gain_attn_part = norm_backward(d_normed_attn, unit_attn, inverse_attn, gain_attn)
    grad_tokens = (d_residual + d_norm_attn).astype(low)

    layer_rows = residual + scatter(branch, "tensor").astype(jnp.float32)

    def shares(grad):
        return scatter(grad.astype(low), "dp").astype(jnp.float32)

    def square_shares(grad):
        return scatter(scatter(grad.astype(low), "dp"), "tensor", 1).astype(jnp.float32)

    gains = scatter(
        jnp.stack([gain_attn_part, gain_mlp_part]).reshape(2, -1, rows_of_gain(gain_attn)), both, 1
    )
    return (
        layer_rows.astype(low),
        grad_tokens,
        gains[0, 0],
        square_shares(grad_query),
        scatter(grad_keyval.astype(low), both).astype(jnp.float32),
        square_shares(grad_output),
        gains[1, 0],
        shares(grad_gate),
        shares(grad_up),
        shares(grad_down),
    )


def rows_of_gain(gain):
    return gain.shape[0] // (lax.axis_size("dp") * lax.axis_size("tensor"))


def solution(mesh):
    return jax.shard_map(
        local,
        mesh=mesh,
        in_specs=(
            P(("dp", "tensor"), None),
            P("dp"),
            P(),
            P("dp", "tensor"),
            P("dp", None),
            P("dp", "tensor"),
            P(),
            P("dp", "tensor"),
            P("dp", "tensor"),
            P("dp", "tensor"),
            P(("dp", "tensor"), None),
        ),
        out_specs=(
            P(("dp", "tensor"), None),
            P(("dp", "tensor"), None),
            P(("dp", "tensor")),
            P("dp", "tensor"),
            P(("dp", "tensor"), None),
            P("dp", "tensor"),
            P(("dp", "tensor")),
            P("dp", "tensor"),
            P("dp", "tensor"),
            P("dp", "tensor"),
        ),
        check_vma=False,
    )
```

```python
import functools

import jax
import jax.numpy as jnp
from jax import lax
from jax.experimental import pallas as pl
from jax.experimental.pallas import tpu as pltpu
from jax.sharding import PartitionSpec as P

KVH = 4
HD = 64
PAIR = 2 * HD

epsilon = 1e-05
rope_base = 10000.0
masked = -1e30


def doc_positions(seg_row):
    length = seg_row.shape[0]
    places = jnp.arange(length, dtype=jnp.int32)
    change = jnp.concatenate([jnp.ones((1,), jnp.bool_), seg_row[1:] != seg_row[:-1]])
    starts = lax.cummax(jnp.where(change, places, 0), axis=0)
    return places - starts


def rope_tables(places, width):
    half_width = width // 2
    frequency = rope_base ** (-(2.0 * jnp.arange(half_width).astype(jnp.float32)) / width)
    angles = places.astype(jnp.float32)[:, None] * frequency[None, :]
    return (jnp.cos(angles), jnp.sin(angles))


def rotate(values, cosine, sine_table):
    rows, width = values.shape
    heads = values.reshape(rows, width // HD, HD)
    half_width = HD // 2
    front_half = heads[..., :half_width]
    back_half = heads[..., half_width:]
    cos_rows = cosine[:, None, :]
    sin_rows = sine_table[:, None, :]
    turned = jnp.concatenate(
        [
            front_half * cos_rows - back_half * sin_rows,
            back_half * cos_rows + front_half * sin_rows,
        ],
        axis=-1,
    )
    return turned.reshape(rows, width)


def norm_forward(values, gain_vec):
    inverse = lax.rsqrt(jnp.mean(values * values, axis=-1, keepdims=True) + epsilon)
    unit_rows = values * inverse
    return (unit_rows * gain_vec, unit_rows, inverse)


def norm_backward(d_normed, unit_rows, inverse, gain_vec):
    gain_part = jnp.sum(d_normed * unit_rows, axis=0)
    d_unit = d_normed * gain_vec
    d_values = inverse * (d_unit - unit_rows * jnp.mean(d_unit * unit_rows, axis=-1, keepdims=True))
    return (d_values, gain_part)


def dot_nn(left, right):
    return jnp.dot(left, right, preferred_element_type=jnp.float32)


def dot_nt(left, right):
    return lax.dot_general(
        left, right, (((1,), (1,)), ((), ())), preferred_element_type=jnp.float32
    )


def dot_tn(left, right):
    return lax.dot_general(
        left, right, (((0,), (0,)), ((), ())), preferred_element_type=jnp.float32
    )


def front_lanes(tile):
    lane = lax.broadcasted_iota(jnp.int32, tile.shape, 1)
    return jnp.where(lane < HD, tile, jnp.zeros_like(tile))


def back_lanes(tile):
    lane = lax.broadcasted_iota(jnp.int32, tile.shape, 1)
    return jnp.where(lane < HD, jnp.zeros_like(tile), tile)


def attend_forward_kernel(query_ref, front_ref, back_ref, value_t_ref, bias_ref, out_ref, log_ref):
    pairs = query_ref.shape[1] // PAIR
    value_t = value_t_ref[0]
    for pair in range(pairs):
        query = query_ref[:, pair * PAIR : (pair + 1) * PAIR]
        outs = []
        for side, key_ref in enumerate((front_ref, back_ref)):
            scores = dot_nt(key_ref[0], query) + bias_ref[...]
            top = jnp.max(scores, axis=0, keepdims=True)
            expo = jnp.exp(scores - top)
            total = jnp.sum(expo, axis=0, keepdims=True)
            outs.append(dot_nn(value_t, expo.astype(jnp.bfloat16)) / total)
            log_ref[0, pl.ds(pair * 2 + side, 1), :] = top + jnp.log(total)
        out = jnp.concatenate(outs, axis=0).T
        out_ref[:, pair * PAIR : (pair + 1) * PAIR] = out.astype(jnp.bfloat16)


def attend_backward_kernel(
    query_ref,
    grad_ref,
    kf_ref,
    kb_ref,
    kt_ref,
    vf_ref,
    vb_ref,
    bias_ref,
    log_ref,
    dq_ref,
    dk_ref,
    dv_ref,
):
    pairs = query_ref.shape[1] // PAIR
    key_t = kt_ref[0]
    dk_ref[0] = jnp.zeros(dk_ref.shape[1:], jnp.float32)
    dv_ref[0] = jnp.zeros(dv_ref.shape[1:], jnp.float32)
    for pair in range(pairs):
        columns = slice(pair * PAIR, (pair + 1) * PAIR)
        query = query_ref[:, columns]
        grad = grad_ref[:, columns]
        outs = []
        for side, (key_ref, value_ref, keep) in enumerate(
            ((kf_ref, vf_ref, front_lanes), (kb_ref, vb_ref, back_lanes))
        ):
            log_sum = log_ref[0, pl.ds(pair * 2 + side, 1), :]
            probs = jnp.exp(dot_nt(key_ref[0], query) + bias_ref[...] - log_sum)
            d_probs = dot_nt(value_ref[0], grad)
            row_dot = jnp.sum(probs * d_probs, axis=0, keepdims=True)
            d_scores = (probs * (d_probs - row_dot)).astype(jnp.bfloat16)
            dk_ref[0] += dot_nn(d_scores, keep(query))
            dv_ref[0] += dot_nn(probs.astype(jnp.bfloat16), keep(grad))
            outs.append(dot_nn(key_t, d_scores))
        dq_ref[:, columns] = jnp.concatenate(outs, axis=0).T * (HD**-0.5)


def whole_group(rows, width):
    return pl.BlockSpec((1, rows, width), lambda g: (g, 0, 0))


def columns_of(rows, width):
    return pl.BlockSpec((rows, width), lambda g: (0, g))


def attend_forward(query, key_f, key_b, value_t, bias):
    rows, width = query.shape
    length = bias.shape[0]
    group = width // KVH
    return pl.pallas_call(
        attend_forward_kernel,
        grid=(KVH,),
        in_specs=[
            columns_of(rows, group),
            whole_group(length, PAIR),
            whole_group(length, PAIR),
            whole_group(HD, length),
            pl.BlockSpec((length, rows), lambda g: (0, 0)),
        ],
        out_specs=[columns_of(rows, group), whole_group(group // HD, rows)],
        out_shape=[
            jax.ShapeDtypeStruct((rows, width), jnp.bfloat16),
            jax.ShapeDtypeStruct((KVH, group // HD, rows), jnp.float32),
        ],
        compiler_params=pltpu.CompilerParams(vmem_limit_bytes=48 * 1024 * 1024),
        name="attend_forward",
    )(query, key_f, key_b, value_t, bias)


def attend_backward(query, grad, key_f, key_b, key_t, value_f, value_b, bias, log_sum):
    rows, width = query.shape
    length = bias.shape[0]
    group = width // KVH
    tall = whole_group(length, PAIR)
    return pl.pallas_call(
        attend_backward_kernel,
        grid=(KVH,),
        in_specs=[
            columns_of(rows, group),
            columns_of(rows, group),
            tall,
            tall,
            whole_group(HD, length),
            tall,
            tall,
            pl.BlockSpec((length, rows), lambda g: (0, 0)),
            whole_group(group // HD, rows),
        ],
        out_specs=[columns_of(rows, group), tall, tall],
        out_shape=[
            jax.ShapeDtypeStruct((rows, width), jnp.float32),
            jax.ShapeDtypeStruct((KVH, length, PAIR), jnp.float32),
            jax.ShapeDtypeStruct((KVH, length, PAIR), jnp.float32),
        ],
        compiler_params=pltpu.CompilerParams(vmem_limit_bytes=48 * 1024 * 1024),
        name="attend_backward",
    )(query, grad, key_f, key_b, key_t, value_f, value_b, bias, log_sum)


def by_head(matrix):
    rows = matrix.shape[0]
    return matrix.reshape(rows, KVH, HD).transpose(1, 0, 2)


MESH = pl.DeviceIdType.MESH


def flip(index, bit):
    return index + bit - 2 * bit * ((index // bit) % 2)


def line_order(place):
    nearest = place - 1 + 2 * (1 - (place + 3) // 4)
    farthest = 3 - 3 * (place // 2)
    return (nearest, 6 - place - nearest - farthest, farthest)


def enter(dp, place):
    barrier = pltpu.get_barrier_semaphore()
    for bit in (1, 2, 4):
        pl.semaphore_signal(barrier, inc=1, device_id=(flip(dp, bit), place), device_id_type=MESH)
    for step in (-1, 1):
        there = (place + step >= 0) & (place + step < 4)

        @pl.when(there)
        def _():
            pl.semaphore_signal(
                barrier, inc=1, device_id=(dp, place + step), device_id_type=MESH
            )

    ends = 1 - ((place + 3) // 4) + place // 3
    pl.semaphore_wait(barrier, 5 - ends)


def turn(tile, cos, sin):
    lane = lax.broadcasted_iota(jnp.int32, tile.shape, 1)
    swapped = jnp.where(
        lane % HD < HD // 2, pltpu.roll(tile, PAIR - HD // 2, 1), pltpu.roll(tile, HD // 2, 1)
    )
    return tile * cos + swapped * sin


def head_tiles(keyval, group):
    columns = slice(group // 2 * PAIR, (group // 2 + 1) * PAIR)
    tile = keyval[:, columns]
    values = slice(KVH * HD + columns.start, KVH * HD + columns.stop)
    if group % 2 == 0:
        front = front_lanes(tile)
        keys = (front, pltpu.roll(front, HD, 1))
    else:
        back = back_lanes(tile)
        keys = (pltpu.roll(back, HD, 1), back)
    return keys, keyval[:, values]


def attend_kernel(
    tokens_ref, normed_ref, cos_ref, sin_ref, bias_ref, gain_ref,
    kv_ref, q_ref, o_ref, g_ref, u_ref, c_ref,
    query_out, keyval_out, heads_out, log_out, residual_out, mlp_out,
    fkv, fq, fo, fg, fu, fc,
    kv_weight, weight, wide_weight, keyval, key_f, key_b, value_t,
    own_sem, z_send, z_recv, p_send, p_recv, k_send, k_recv, w_sem,
):
    dp, place = lax.axis_index("dp"), lax.axis_index("tensor")
    rows = kv_ref.shape[0]
    half = rows // 2
    width = q_ref.shape[1]
    order = line_order(place)
    enter(dp, place)

    def rows_of(owner):
        return pl.ds(pl.multiple_of(owner * rows, rows), rows)

    def columns_of_rank(rank):
        return pl.ds(pl.multiple_of(rank * width, width), width)

    def remote(src, dst, send, recv, device):
        return pltpu.make_async_remote_copy(
            src_ref=src, dst_ref=dst, send_sem=send, recv_sem=recv,
            device_id=device, device_id_type=MESH,
        )

    own = [
        (kv_ref, fkv.at[rows_of(dp), :]),
        (q_ref, fq.at[rows_of(dp), columns_of_rank(place)]),
        (o_ref, fo.at[rows_of(dp), columns_of_rank(place)]),
        (g_ref, fg.at[rows_of(dp), :]),
        (u_ref, fu.at[rows_of(dp), :]),
        (c_ref, fc.at[rows_of(place), :]),
    ]
    own_copies = [
        pltpu.make_async_copy(src, dst, own_sem.at[i]) for i, (src, dst) in enumerate(own)
    ]
    for copy in own_copies:
        copy.start()

    def line_block(which, rank):
        if which == 2:
            return fc.at[rows_of(rank), :]
        return (fq, fo)[which].at[rows_of(dp), columns_of_rank(rank)]

    def line_copy(which, rank, step):
        src = (q_ref, o_ref, c_ref)[which] if rank is place else line_block(which, rank)
        side = 0 if step < 0 else 1
        return remote(
            src, line_block(which, rank), z_send.at[which, side, rank], z_recv.at[which, rank],
            (dp, place + step),
        )

    def line_send(which, rank, act):
        @pl.when((rank <= place) & (place < 3))
        def _():
            act(line_copy(which, rank, 1))

        @pl.when((rank >= place) & (place > 0))
        def _():
            act(line_copy(which, rank, -1))

    def start(copy):
        copy.start()

    def wait_send(copy):
        copy.wait_send()

    x, y, core = flip(dp, 2), flip(dp, 4), flip(dp, 1)
    far = flip(x, 4)

    blocks = [("kv", None), ("q", place), ("g", None)] + [("q", rank) for rank in order]
    blocks += [("o", place)] + [("o", rank) for rank in order] + [("u", None)]

    def block(index, owner, part=None):
        name, rank = blocks[index]
        ref = {"kv": fkv, "q": fq, "o": fo, "g": fg, "u": fu}[name]
        first = owner * rows if part is None else owner * rows + part * half
        size = rows if part is None else half
        window = pl.ds(pl.multiple_of(first, half), size)
        if rank is None:
            return ref.at[window, :]
        return ref.at[window, columns_of_rank(rank)]

    def own_block(index):
        name, rank = blocks[index]
        if rank is None or rank is place:
            return {"kv": kv_ref, "q": q_ref, "o": o_ref, "g": g_ref, "u": u_ref}[name]
        return block(index, dp)

    def plane_copy(index, lane):
        send, recv = p_send.at[index, lane], p_recv.at[index, lane]
        if lane == 0:
            return remote(own_block(index), block(index, dp), send, recv, (x, place))
        if lane == 1:
            return remote(own_block(index), block(index, dp), send, recv, (y, place))
        if lane == 2:
            return remote(block(index, x, 0), block(index, x, 0), send, recv, (y, place))
        if lane == 3:
            return remote(block(index, y, 1), block(index, y, 1), send, recv, (x, place))
        owner = (dp, x, y, far)[lane - 4]
        src = own_block(index) if lane == 4 else block(index, owner)
        return remote(src, block(index, owner), send, recv, (core, place))

    def plane_first(index):
        plane_copy(index, 0).start()
        plane_copy(index, 1).start()
        plane_copy(index, 4).start()

    def plane_second(index):
        plane_copy(index, 0).wait_recv()
        plane_copy(index, 2).start()
        plane_copy(index, 5).start()
        plane_copy(index, 1).wait_recv()
        plane_copy(index, 3).start()
        plane_copy(index, 6).start()

    def plane_third(index):
        plane_copy(index, 2).wait_recv()
        plane_copy(index, 3).wait_recv()
        plane_copy(index, 7).start()

    def plane_ready(index):
        for lane in range(4, 8):
            plane_copy(index, lane).wait_recv()

    def plane_sent(index):
        for lane in range(8):
            plane_copy(index, lane).wait_send()

    def keyval_block(rank):
        return keyval.at[rows_of(rank), :]

    def keyval_copy(rank, step):
        side = 0 if step < 0 else 1
        return remote(
            keyval_block(rank), keyval_block(rank), k_send.at[side, rank], k_recv.at[rank],
            (dp, place + step),
        )

    def keyval_send(rank, act):
        @pl.when((rank <= place) & (place < 3))
        def _():
            act(keyval_copy(rank, 1))

        @pl.when((rank >= place) & (place > 0))
        def _():
            act(keyval_copy(rank, -1))

    def keyval_take(step):
        keyval_copy(order[step], 1).wait_recv()
        keyval_send(order[step], start)

    low = jnp.bfloat16
    wide = KVH * HD

    def make_keyval():
        load = pltpu.make_async_copy(fkv, kv_weight, w_sem.at[0])
        load.start()
        load.wait()
        made = dot_nn(normed_ref[...], kv_weight[...])
        for tile in range(wide // PAIR):
            columns = slice(tile * PAIR, (tile + 1) * PAIR)
            keyval[rows_of(place), columns] = turn(
                made[:, columns], cos_ref[...], sin_ref[...]
            ).astype(low)
        keyval[rows_of(place), wide:] = made[:, wide:].astype(low)
        keyval_send(place, start)

    def weight_load(source, rank, by_rows):
        window = pl.ds(pl.multiple_of(rank * width, width), width)
        src = source.at[window, :] if by_rows else source.at[:, window]
        dst = wide_weight.at[rank % 2] if by_rows else weight.at[rank % 2]
        return pltpu.make_async_copy(src, dst, w_sem.at[rank % 2])

    def make_query():
        weight_load(fq, 0, False).start()
        for rank in range(4):
            if rank < 3:
                weight_load(fq, rank + 1, False).start()
            weight_load(fq, rank, False).wait()
            made = dot_nn(normed_ref[...], weight[rank % 2])
            for tile in range(width // PAIR):
                columns = slice(tile * PAIR, (tile + 1) * PAIR)
                query_out[:, rank * width + tile * PAIR : rank * width + (tile + 1) * PAIR] = (
                    turn(made[:, columns], cos_ref[...], sin_ref[...]) * (HD**-0.5)
                ).astype(low)

    def attend(group):
        key_tile, value_tile = head_tiles(keyval, group)
        key_f[...], key_b[...] = key_tile
        side = group % 2
        value_t[...] = value_tile.T[side * HD : (side + 1) * HD, :]
        pairs = query_out.shape[1] // PAIR // KVH

        @pl.loop(0, pairs)
        def _(index):
            pair = group * pairs + index
            columns = pl.ds(pl.multiple_of(pair * PAIR, PAIR), PAIR)
            query = query_out[:, columns]
            outs, logs = [], []
            for key_ref in (key_f, key_b):
                scores = dot_nt(key_ref[...], query) + bias_ref[...]
                top = jnp.max(scores, axis=0, keepdims=True)
                expo = jnp.exp(scores - top)
                total = jnp.sum(expo, axis=0, keepdims=True)
                outs.append(dot_nn(value_t[...], expo.astype(low)) / total)
                logs.append(top + jnp.log(total))
            log_out[pair] = jnp.concatenate(logs, axis=0)
            heads_out[:, columns] = jnp.concatenate(outs, axis=0).T.astype(low)

    def make_residual():
        weight_load(fo, 0, True).start()
        square = jnp.zeros((rows, 1), jnp.float32)
        for rank in range(4):
            if rank < 3:
                weight_load(fo, rank + 1, True).start()
            weight_load(fo, rank, True).wait()
            columns = slice(rank * width, (rank + 1) * width)
            made = tokens_ref[:, columns].astype(jnp.float32) + dot_nt(
                heads_out[...], wide_weight[rank % 2]
            )
            residual_out[:, columns] = made
            square += jnp.sum(made * made, axis=1, keepdims=True)
        inverse = lax.rsqrt(square * (1.0 / (4 * width)) + epsilon)
        for rank in range(4):
            columns = slice(rank * width, (rank + 1) * width)
            mlp_out[:, columns] = (
                residual_out[:, columns] * inverse * gain_ref[:, columns]
            ).astype(low)

    inside = (place == 1) | (place == 2)

    def cot_take(rank):
        line_copy(2, rank, 1).wait_recv()
        line_send(2, rank, start)

    def line_take(which, step):
        line_copy(which, order[step], 1).wait_recv()
        line_send(which, order[step], start)

    count = len(blocks)
    kv, q_own, gate, o_own, up = 0, 1, 2, 6, 10
    q_far, o_far = (3, 4, 5), (7, 8, 9)
    plane_first(kv)
    line_send(0, place, start)
    plane_first(q_own)
    line_take(0, 0)
    line_send(1, place, start)
    plane_second(kv)
    plane_first(gate)
    plane_second(q_own)
    plane_third(kv)
    plane_ready(kv)
    own_copies[0].wait()
    line_take(0, 1)
    make_keyval()
    plane_first(q_far[0])
    plane_third(q_own)
    line_take(1, 0)
    line_take(0, 2)
    plane_second(gate)
    plane_first(q_far[1])
    keyval_take(0)
    line_take(1, 1)
    plane_second(q_far[0])
    plane_first(q_far[2])
    plane_third(gate)
    keyval_take(1)
    line_take(1, 2)
    plane_second(q_far[1])
    plane_first(o_own)
    plane_third(q_far[0])
    keyval_take(2)
    line_send(2, place, start)
    plane_second(q_far[2])
    plane_first(o_far[0])
    plane_third(q_far[1])
    plane_second(o_own)
    plane_first(o_far[1])
    plane_third(q_far[2])
    for index in (q_own,) + q_far:
        plane_ready(index)
    own_copies[1].wait()
    make_query()
    cot_take(order[0])

    @pl.when(inside)
    def _():
        cot_take(order[1])

    plane_second(o_far[0])
    plane_first(o_far[2])
    plane_third(o_own)
    attend(0)
    plane_second(o_far[1])
    plane_first(up)
    plane_third(o_far[0])
    attend(1)
    plane_second(o_far[2])
    plane_third(o_far[1])
    attend(2)
    plane_third(o_far[2])
    cot_take(jnp.where(inside, order[2], order[1]))
    attend(3)
    plane_second(up)
    for index in (o_own,) + o_far:
        plane_ready(index)
    own_copies[2].wait()
    make_residual()
    plane_third(up)

    @pl.when(jnp.logical_not(inside))
    def _():
        cot_take(order[2])

    plane_ready(gate)
    plane_ready(up)
    for index in range(count):
        plane_sent(index)
    for which in range(3):
        line_send(which, place, wait_send)
        for step in range(3):
            line_send(which, order[step], wait_send)
    keyval_send(place, wait_send)
    for step in range(3):
        keyval_send(order[step], wait_send)
    for copy in own_copies[3:]:
        copy.wait()
    out_copy = pltpu.make_async_copy(keyval, keyval_out, w_sem.at[0])
    out_copy.start()
    out_copy.wait()


def attend_all(
    tokens, normed, cos, sin, bias, gain, w_keyval, w_query, w_output, w_gate, w_up, cotangent
):
    n_dp, n_line = lax.axis_size("dp"), lax.axis_size("tensor")
    low = jnp.bfloat16
    rows, depth = tokens.shape
    length = bias.shape[0]
    wide = 2 * KVH * HD
    heads = w_query.shape[1] * n_line // HD

    def over(array, by_rows, by_columns):
        shape = (array.shape[0] * by_rows, array.shape[1] * by_columns)
        return jax.ShapeDtypeStruct(shape, array.dtype)

    anywhere = pl.BlockSpec(memory_space=pl.ANY)
    in_vmem = pl.BlockSpec(memory_space=pltpu.VMEM)
    shapes = [
        jax.ShapeDtypeStruct((rows, heads * HD), low),
        jax.ShapeDtypeStruct((length, wide), low),
        jax.ShapeDtypeStruct((rows, heads * HD), low),
        jax.ShapeDtypeStruct((heads // 2, 2, rows), jnp.float32),
        jax.ShapeDtypeStruct((rows, depth), jnp.float32),
        jax.ShapeDtypeStruct((rows, depth), low),
        over(w_keyval, n_dp, 1),
        over(w_query, n_dp, n_line),
        over(w_output, n_dp, n_line),
        over(w_gate, n_dp, 1),
        over(w_up, n_dp, 1),
        over(cotangent, n_line, 1),
    ]
    dma = pltpu.SemaphoreType.DMA
    return pl.pallas_call(
        attend_kernel,
        out_shape=shapes,
        in_specs=[in_vmem] * 6 + [anywhere] * 6,
        out_specs=[in_vmem, anywhere] + [in_vmem] * 4 + [anywhere] * 6,
        scratch_shapes=[
            pltpu.VMEM((depth, wide), low),
            pltpu.VMEM((2, depth, w_query.shape[1]), low),
            pltpu.VMEM((2, w_query.shape[1], depth), low),
            pltpu.VMEM((length, wide), low),
            pltpu.VMEM((length, PAIR), low),
            pltpu.VMEM((length, PAIR), low),
            pltpu.VMEM((HD, length), low),
            dma((6,)), dma((3, 2, 4)), dma((3, 4)), dma((11, 8)), dma((11, 8)),
            dma((2, 4)), dma((4,)), dma((2,)),
        ],
        compiler_params=pltpu.CompilerParams(
            collective_id=0, has_side_effects=True, vmem_limit_bytes=62 * 1024 * 1024
        ),
        name="attend_all",
    )(
        tokens, normed, cos, sin, bias, gain, w_keyval, w_query, w_output, w_gate, w_up, cotangent
    )


def add_rows(target, source, step=32):
    @pl.loop(0, target.shape[0] // step)
    def _(index):
        window = pl.ds(pl.multiple_of(index * step, step), step)
        target[window, :] = target[window, :] + source[window, :]


def over_rows(total_rows, act, step=32):
    @pl.loop(0, total_rows // step)
    def _(index):
        act(pl.ds(pl.multiple_of(index * step, step), step))


def enter_wide(dp, place):
    barrier = pltpu.get_barrier_semaphore()
    for bit in (1, 2, 4):
        pl.semaphore_signal(barrier, inc=1, device_id=(flip(dp, bit), place), device_id_type=MESH)
    for step in range(1, 4):
        pl.semaphore_signal(
            barrier, inc=1, device_id=(dp, (place + step) % 4), device_id_type=MESH
        )
    pl.semaphore_wait(barrier, 6)


def reach_back_kernel(
    gd_ref, gg_ref, gu_ref, branch_ref, fkv, fq, fo, dn_ref, residual_ref,
    cot_ref, tokens_ref, normed_ref, query_ref, heads_ref, keyval_ref, log_ref, bias_ref,
    cos_ref, sin_ref, gain_attn_ref, gain_mlp_ref,
    gd_out, gg_out, gu_out, go_out, gq_out, nar_out, layer_out, tokens_out,
    gd_core, gg_core, gu_core, go_core, gq_core, nar_core,
    gd_side, gg_side, gu_side, go_side, gq_side, nar_side,
    gd_near, gg_near, gu_near, go_near, gq_near, nar_near,
    go_in, gq_in, nar_in, dkv_in, layer_in,
    parts, held, stage, go_line, gq_line, nar_line, dkv_line, sums,
    d_residual, total, wide, d_branch, d_heads, dq_low, dkv_low, gains, weight, kv_weight,
    key_f, key_b, key_t, value_f, value_b, dk, dv,
    load_sem, fetch_sem, core_send, core_recv, p_send, p_recv, l_send, l_recv, in_sem, w_sem,
):
    dp, place = lax.axis_index("dp"), lax.axis_index("tensor")
    low = jnp.bfloat16
    rows, depth = d_branch.shape
    half = rows // 2
    enter_wide(dp, place)
    x, y, core = flip(dp, 2), flip(dp, 4), flip(dp, 1)
    far = flip(x, 4)
    mine = (dp, x, y, far)
    theirs = tuple(flip(owner, 1) for owner in mine)
    grads = (gd_ref, gg_ref, gu_ref)
    outs = (gd_out, gg_out, gu_out, go_out, gq_out, nar_out)
    cores = (gd_core, gg_core, gu_core, go_core, gq_core, nar_core)
    sides = (gd_side, gg_side, gu_side, go_side, gq_side, nar_side)
    nears = (gd_near, gg_near, gu_near, go_near, gq_near, nar_near)
    lines = {3: go_line, 4: gq_line, 5: nar_line, 6: dkv_line}
    arrivals = {3: go_in, 4: gq_in, 5: nar_in, 6: dkv_in, 7: layer_in}
    front, back = pl.ds(0, half), pl.ds(half, half)
    ranks = dkv_line.shape[0]
    turns = (3, 1, 2, 0)

    def rows_of(owner):
        return pl.ds(pl.multiple_of(owner * rows, rows), rows)

    def remote(src, dst, send, recv, device):
        return pltpu.make_async_remote_copy(
            src_ref=src, dst_ref=dst, send_sem=send, recv_sem=recv,
            device_id=device, device_id_type=MESH,
        )

    def width_of(i):
        return cores[i].shape[2]

    sets = (0, 1, 0, 0, 1, 1)

    def part(i, k):
        return parts.at[sets[i], k, :, pl.ds(0, width_of(i))]

    def half_part(i, k, window):
        return parts.at[sets[i], k, window, pl.ds(0, width_of(i))]

    def held_part(slot, count, width):
        return held.at[slot, pl.ds(0, count), pl.ds(0, width)]

    def fetch(src, slot):
        return pltpu.make_async_copy(
            src, held_part(slot, src.shape[0], src.shape[1]), fetch_sem.at[slot]
        )

    def core_copy(i, k):
        if i < 3:
            src = grads[i].at[rows_of(theirs[k]), :]
        else:
            src = stage.at[turns.index(k) % 2, :, pl.ds(0, width_of(i))]
        return remote(
            src, cores[i].at[k], core_send.at[i, k], core_recv.at[i, k], (core, place)
        )

    def own_load(i, k):
        return pltpu.make_async_copy(
            grads[i].at[rows_of(mine[k]), :], part(i, k), load_sem.at[i, k]
        )

    def plane_copy(i, lane):
        src, dst, device = (
            (half_part(i, 3, front), sides[i].at[0], y),
            (half_part(i, 3, back), sides[i].at[1], x),
            (half_part(i, 1, back), nears[i].at[0, back, :], x),
            (half_part(i, 2, front), nears[i].at[1, front, :], y),
            (half_part(i, 1, front), nears[i].at[0, front, :], x),
            (half_part(i, 2, back), nears[i].at[1, back, :], y),
        )[lane]
        return remote(src, dst, p_send.at[i, lane], p_recv.at[i, lane], (device, place))

    def plane_sent(i):
        for lane in range(6):
            plane_copy(i, lane).wait_send()

    def load_own(i):
        for k in turns:
            own_load(i, k).start()

    def stage_core(i):
        def begin(n):
            core_copy(i, turns[n]).wait_recv()
            fetch(cores[i].at[turns[n]], n % 2).start()

        begin(0)
        begin(1)
        for n, k in enumerate(turns):
            fetch(cores[i].at[k], n % 2).wait()
            if i < 3:
                own_load(i, k).wait()
            add_rows(part(i, k), held_part(n % 2, rows, width_of(i)))
            for lane in ((), (2,), (3,), (0, 1))[k]:
                plane_copy(i, lane).start()
            if n + 2 < 4:
                begin(n + 2)

    def stage_side(i):
        for side in range(2):
            plane_copy(i, side).wait_recv()
            fetch(sides[i].at[side], side).start()
        for side, (k, window, lane) in enumerate(((1, front, 4), (2, back, 5))):
            fetch(sides[i].at[side], side).wait()
            add_rows(half_part(i, k, window), held_part(side, half, width_of(i)))
            plane_copy(i, lane).start()

    def stage_near(i):
        for side, lanes in enumerate(((2, 4), (3, 5))):
            for lane in lanes:
                plane_copy(i, lane).wait_recv()
            fetch(nears[i].at[side], side).start()
        for side in range(2):
            fetch(nears[i].at[side], side).wait()
        own, width, out = part(i, 0), width_of(i), outs[i]

        @pl.loop(0, rows // 32)
        def _(index):
            window = pl.ds(pl.multiple_of(index * 32, 32), 32)
            sums = (
                own[window, :].astype(jnp.float32)
                + held[0, window, pl.ds(0, width)].astype(jnp.float32)
                + held[1, window, pl.ds(0, width)].astype(jnp.float32)
            )
            if i < 3:
                out[window, :] = sums
            elif i < 5:
                piece = width // ranks
                for rank in range(ranks):
                    lines[i][rank, window, :] = sums[:, rank * piece : (rank + 1) * piece].astype(
                        low
                    )
            else:
                per = rows // ranks
                lines[i][index * 32 // per, pl.ds(pl.multiple_of(index * 32 % per, 32), 32), :] = (
                    sums.astype(low)
                )

    def line_copy(i, step):
        target = (place + step) % ranks
        src = branch_ref.at[target] if i == 7 else lines[i].at[target]
        return remote(
            src, arrivals[i].at[place], l_send.at[i - 3, step], l_recv.at[i - 3, step],
            (dp, target),
        )

    def line_start(i):
        for step in range(1, ranks):
            line_copy(i, step).start()

    def line_last(i, add):
        def begin(step):
            line_copy(i, step).wait_recv()
            fetch(arrivals[i].at[(place + ranks - step) % ranks], step % 2).start()

        begin(1)
        for step in range(1, ranks):
            if step + 1 < ranks:
                begin(step + 1)
            fetch(arrivals[i].at[place], step % 2).wait()
            add(step % 2)

    def line_sent(i):
        for step in range(1, ranks):
            line_copy(i, step).wait_send()

    def line_out(i):
        out = outs[i]
        count, width = out.shape

        def begin(window):
            out[window, :] = lines[i][place, window, :].astype(jnp.float32)

        def add(slot):
            def act(window):
                out[window, :] += held[slot, window, pl.ds(0, width)].astype(jnp.float32)

            over_rows(count, act)

        over_rows(count, begin)
        line_last(i, add)

    def norm_back(grad_ref, rows_ref, gain_ref, gain_row, act):
        gains[gain_row : gain_row + 1, :] = jnp.zeros((1, depth), jnp.float32)

        def block(window):
            values = rows_ref[window, :].astype(jnp.float32)
            inverse = lax.rsqrt(jnp.mean(values * values, axis=1, keepdims=True) + epsilon)
            unit = values * inverse
            grad = grad_ref[window, :]
            gains[gain_row : gain_row + 1, :] += jnp.sum(grad * unit, axis=0, keepdims=True)
            d_unit = grad * gain_ref[...]
            act(
                window,
                inverse * (d_unit - unit * jnp.mean(d_unit * unit, axis=1, keepdims=True)),
            )

        over_rows(rows, block, 64)

    def after_mlp(window, d_values):
        made = cot_ref[window, :].astype(jnp.float32) + d_values
        d_residual[window, :] = made
        d_branch[window, :] = made.astype(low)

    def after_attn(window, d_values):
        tokens_out[window, :] = (d_residual[window, :] + d_values).astype(low)

    def square_tile(left, right, owner):
        columns = pl.ds(pl.multiple_of(owner * rows, rows), rows)
        return dot_tn(left[:, columns], right[...]).astype(low)

    def narrow_tile(owner):
        columns = pl.ds(pl.multiple_of(owner * rows, rows), rows)
        keys = dot_tn(normed_ref[:, columns], dkv_low[...]).astype(low)
        line = lax.broadcasted_iota(jnp.int32, (PAIR, rows), 0)
        both = jnp.where(
            line == 0, gains[0:1, columns], jnp.where(line == 1, gains[1:2, columns], 0.0)
        )
        return jnp.concatenate([keys, both.T.astype(low)], axis=1)

    def send_theirs(i, tile):
        for n, k in enumerate(turns):
            if n >= 2:
                core_copy(i, turns[n - 2]).wait_send()
            stage[n % 2, :, pl.ds(0, width_of(i))] = tile(theirs[k])
            core_copy(i, k).start()

    def theirs_sent(i):
        for k in turns[2:]:
            core_copy(i, k).wait_send()

    def keep_mine(i, tile):
        for k in turns:
            parts[sets[i], k, :, pl.ds(0, width_of(i))] = tile(mine[k])

    def go_tile(owner):
        return square_tile(d_branch, heads_ref, owner)

    def gq_tile(owner):
        return square_tile(normed_ref, dq_low, owner)

    size = weight.shape[1]
    steps = depth // size

    def weight_load(source, index):
        return pltpu.make_async_copy(
            source.at[pl.ds(index * size, size), :], weight.at[index % 2], w_sem.at[index % 2]
        )

    def make_d_heads():
        weight_load(fo, 0).start()
        for index in range(steps):
            if index + 1 < steps:
                weight_load(fo, index + 1).start()
            weight_load(fo, index).wait()
            made = dot_nn(d_branch[:, index * size : (index + 1) * size], weight[index % 2])
            if index == 0:
                wide[...] = made
            elif index + 1 < steps:
                wide[...] += made
            else:
                d_heads[...] = (wide[...] + made).astype(low)

    def make_d_normed():
        weight_load(fq, 0).start()
        for index in range(steps):
            if index + 1 < steps:
                weight_load(fq, index + 1).start()
            weight_load(fq, index).wait()
            wide[:, index * size : (index + 1) * size] = dot_nt(dq_low[...], weight[index % 2])

    def add_d_normed():
        for index in range(steps):
            wide[:, index * size : (index + 1) * size] += dot_nt(
                dkv_low[...], kv_weight[index * size : (index + 1) * size, :]
            )

    def attend_back(group):
        (key_f[...], key_b[...]), value_tile = head_tiles(keyval_ref, group)
        side = group % 2
        lane_side = slice(side * HD, (side + 1) * HD)
        tile_columns = slice(group // 2 * PAIR, (group // 2 + 1) * PAIR)
        key_t[...] = keyval_ref[:, tile_columns].T[lane_side, :]
        if side == 0:
            kept = front_lanes(value_tile)
            value_f[...], value_b[...] = kept, pltpu.roll(kept, HD, 1)
        else:
            kept = back_lanes(value_tile)
            value_f[...], value_b[...] = pltpu.roll(kept, HD, 1), kept
        dk[...] = jnp.zeros(dk.shape, jnp.float32)
        dv[...] = jnp.zeros(dv.shape, jnp.float32)
        pairs = query_ref.shape[1] // PAIR // KVH

        @pl.loop(0, pairs)
        def _(index):
            pair = group * pairs + index
            columns = pl.ds(pl.multiple_of(pair * PAIR, PAIR), PAIR)
            query, grad = query_ref[:, columns], d_heads[:, columns]
            logs = log_ref[pair]
            made = []
            for number, (key_ref, value_ref, keep) in enumerate(
                ((key_f, value_f, front_lanes), (key_b, value_b, back_lanes))
            ):
                probs = jnp.exp(
                    dot_nt(key_ref[...], query) + bias_ref[...] - logs[number : number + 1, :]
                )
                d_probs = dot_nt(value_ref[...], grad)
                row_dot = jnp.sum(probs * d_probs, axis=0, keepdims=True)
                d_scores = (probs * (d_probs - row_dot)).astype(low)
                dk[...] += dot_nn(d_scores, keep(query))
                dv[...] += dot_nn(probs.astype(low), keep(grad))
                made.append(dot_nn(key_t[...], d_scores))
            dq = jnp.concatenate(made, axis=0).T * (HD**-0.5)
            dq_low[:, columns] = turn(dq, cos_ref[...], -sin_ref[...]).astype(low)

        for sums, first in ((dk, 0), (dv, KVH * HD)):
            joined = (sums[...] + pltpu.roll(sums[...], HD, 1)).astype(low)
            columns = slice(first + tile_columns.start, first + tile_columns.stop)
            for rank in range(ranks):
                block = joined[rank * rows : (rank + 1) * rows, :]
                if side == 1:
                    block = front_lanes(dkv_line[rank, :, columns]) + back_lanes(block)
                dkv_line[rank, :, columns] = block

    def make_dkv():
        wide_columns = dkv_line.shape[2]

        def begin(window):
            sums[window, :] = dkv_line[place, window, :].astype(jnp.float32)

        def add(slot):
            def act(window):
                sums[window, :] += held[slot, window, pl.ds(0, wide_columns)].astype(jnp.float32)

            over_rows(rows, act)

        over_rows(rows, begin)
        line_last(6, add)
        for tile in range(wide_columns // PAIR):
            columns = slice(tile * PAIR, (tile + 1) * PAIR)
            made = sums[:, columns]
            if tile < KVH * HD // PAIR:
                made = turn(made, cos_ref[...], -sin_ref[...])
            dkv_low[:, columns] = made.astype(low)

    def finish_layer():
        own = parts.at[0, 0]
        copy = pltpu.make_async_copy(branch_ref.at[place], own, in_sem.at[0])
        copy.start()
        copy.wait()

        def begin(window):
            total[window, :] += own[window, :].astype(jnp.float32)

        def add(slot):
            def act(window):
                total[window, :] += held[slot, window, :].astype(jnp.float32)

            over_rows(rows, act)

        def end(window):
            layer_out[window, :] = total[window, :].astype(low)

        over_rows(rows, begin)
        line_last(7, add)
        over_rows(rows, end)

    dn_load = pltpu.make_async_copy(dn_ref, wide, in_sem.at[1])
    total_load = pltpu.make_async_copy(residual_ref, total, in_sem.at[2])
    kv_load = pltpu.make_async_copy(fkv, kv_weight, in_sem.at[3])

    def send_core(i):
        for k in turns:
            core_copy(i, k).start()

    send_core(0)
    for load in (dn_load, total_load, kv_load):
        load.start()
    load_own(0)
    load_own(1)
    line_start(7)
    dn_load.wait()
    total_load.wait()
    send_core(1)
    norm_back(wide, total, gain_mlp_ref, 1, after_mlp)
    stage_core(0)
    send_theirs(3, go_tile)
    stage_core(1)
    send_core(2)
    make_d_heads()
    stage_side(0)
    attend_back(0)
    stage_side(1)
    stage_near(0)
    plane_sent(0)
    keep_mine(3, go_tile)
    stage_core(3)
    attend_back(1)
    stage_near(1)
    plane_sent(1)
    attend_back(2)
    stage_side(3)
    attend_back(3)
    line_start(6)
    theirs_sent(3)
    send_theirs(4, gq_tile)
    keep_mine(4, gq_tile)
    stage_core(4)
    stage_near(3)
    line_start(3)
    plane_sent(3)
    load_own(2)
    stage_core(2)
    make_d_normed()
    kv_load.wait()
    make_dkv()
    add_d_normed()
    stage_side(4)
    norm_back(wide, tokens_ref, gain_attn_ref, 0, after_attn)
    theirs_sent(4)
    send_theirs(5, narrow_tile)
    stage_near(4)
    line_start(4)
    plane_sent(4)
    keep_mine(5, narrow_tile)
    stage_core(5)
    stage_side(2)
    line_out(3)
    stage_side(5)
    stage_near(5)
    line_start(5)
    stage_near(2)
    plane_sent(2)
    finish_layer()
    line_out(4)
    line_out(5)
    plane_sent(5)
    theirs_sent(5)
    for i in range(3):
        for k in turns:
            core_copy(i, k).wait_send()
    for i in range(3, 8):
        line_sent(i)


def reach_back(grads, branch, full, d_normed, residual, others):
    low, wide = jnp.bfloat16, jnp.float32
    n_dp, ranks = lax.axis_size("dp"), lax.axis_size("tensor")
    units = grads[0].shape[1]
    rows, depth = residual.shape
    half = rows // 2
    square = depth // ranks
    few = depth // n_dp // ranks
    length, keyval = others[5].shape
    narrow = keyval + PAIR
    widths = [units] * 3 + [depth, depth, narrow]
    anywhere = pl.BlockSpec(memory_space=pl.ANY)
    in_vmem = pl.BlockSpec(memory_space=pltpu.VMEM)
    lined = [(rows, square), (rows, square), (few, narrow), (rows, keyval), (rows, depth)]
    out_shape = [jax.ShapeDtypeStruct((rows, units), wide)] * 3
    out_shape += [jax.ShapeDtypeStruct((rows, square), wide)] * 2
    out_shape += [jax.ShapeDtypeStruct((few, narrow), wide)]
    out_shape += [jax.ShapeDtypeStruct((rows, depth), low)] * 2
    out_shape += [jax.ShapeDtypeStruct((4, rows, w), low) for w in widths]
    out_shape += [jax.ShapeDtypeStruct((2, half, w), low) for w in widths]
    out_shape += [jax.ShapeDtypeStruct((2, rows, w), low) for w in widths]
    out_shape += [jax.ShapeDtypeStruct((ranks,) + shape, low) for shape in lined]
    dma = pltpu.SemaphoreType.DMA
    scratch = [
        pltpu.VMEM((2, 4, rows, depth), low),
        pltpu.VMEM((2, rows, depth), low),
        pltpu.VMEM((2, rows, depth), low),
    ]
    scratch += [pltpu.VMEM((ranks,) + shape, low) for shape in lined[:4]]
    scratch += [pltpu.VMEM((rows, keyval), wide)]
    scratch += [pltpu.VMEM((rows, depth), wide)] * 3
    scratch += [pltpu.VMEM((rows, depth), low)] * 3
    scratch += [
        pltpu.VMEM((rows, keyval), low),
        pltpu.VMEM((8, depth), wide),
        pltpu.VMEM((2, square, depth), low),
        pltpu.VMEM((depth, keyval), low),
        pltpu.VMEM((length, PAIR), low),
        pltpu.VMEM((length, PAIR), low),
        pltpu.VMEM((HD, length), low),
        pltpu.VMEM((length, PAIR), low),
        pltpu.VMEM((length, PAIR), low),
        pltpu.VMEM((length, PAIR), wide),
        pltpu.VMEM((length, PAIR), wide),
        dma((3, 4)), dma((2,)), dma((6, 4)), dma((6, 4)), dma((6, 6)), dma((6, 6)),
        dma((5, ranks)), dma((5, ranks)), dma((4,)), dma((2,)),
    ]
    results = pl.pallas_call(
        reach_back_kernel,
        out_shape=out_shape,
        in_specs=[anywhere] * 9 + [in_vmem] * 12,
        out_specs=[in_vmem] * 8 + [anywhere] * 23,
        scratch_shapes=scratch,
        compiler_params=pltpu.CompilerParams(
            collective_id=1, has_side_effects=True, vmem_limit_bytes=63 * 1024 * 1024
        ),
        name="reach_back",
    )(*grads, branch, *full, d_normed, residual, *others)
    return results[:8]


def by_tiles(total, size, act):
    full = total // size

    @pl.loop(0, full)
    def _(index):
        act(pl.ds(pl.multiple_of(index * size, size), size))

    if total % size:
        act(pl.ds(full * size, total % size))


def feed_forward_kernel(
    normed_ref, gate_w_ref, up_w_ref, down_w_ref, cot_ref,
    gg_out, gu_out, gd_out, branch_out, dn_out,
    wg, wu, wd, cot, normed, hid, dg, du, part, arrival, branch_stage, gate_stage, up_stage,
    load_sem, n_send, n_recv, l_send, l_recv, stage_sem, p_send, p_recv,
):
    dp, place = lax.axis_index("dp"), lax.axis_index("tensor")
    rows, depth = normed_ref.shape
    low = jnp.bfloat16
    order = line_order(place)
    cuts = l_send.shape[1]
    few = rows // cuts
    enter(dp, place)

    def remote(src, dst, send, recv, step):
        return pltpu.make_async_remote_copy(
            src_ref=src, dst_ref=dst, send_sem=send, recv_sem=recv,
            device_id=(dp, place + step), device_id_type=MESH,
        )

    def chunk(rank):
        return pl.ds(pl.multiple_of(rank * rows, rows), rows)

    def own_copy(step):
        return remote(
            normed_ref, normed.at[chunk(place), :], n_send.at[(step + 1) // 2, place],
            n_recv.at[place], step,
        )

    def pass_copy(rank, step):
        ref = normed.at[chunk(rank), :]
        return remote(ref, ref, n_send.at[(step + 1) // 2, rank], n_recv.at[rank], step)

    x, y, core = flip(dp, 2), flip(dp, 4), flip(dp, 1)
    far = flip(x, 4)
    shards = (down_w_ref,)
    weights = (wd,)
    depth_rows = down_w_ref.shape[0]
    half = depth_rows // 2

    def weight_rows(i, owner, part=None):
        first = owner * depth_rows if part is None else owner * depth_rows + part * half
        count = depth_rows if part is None else half
        return weights[i].at[pl.ds(pl.multiple_of(first, half), count), :]

    def plane_copy(i, lane):
        if lane < 2:
            src, dst, device = shards[i], weight_rows(i, dp), (x, y)[lane]
        elif lane < 4:
            src = dst = weight_rows(i, (x, y)[lane - 2], lane - 2)
            device = (y, x)[lane - 2]
        else:
            owner = (dp, x, y, far)[lane - 4]
            dst, device = weight_rows(i, owner), core
            src = shards[i] if lane == 4 else dst
        return pltpu.make_async_remote_copy(
            src_ref=src, dst_ref=dst, send_sem=p_send.at[i, lane], recv_sem=p_recv.at[i, lane],
            device_id=(device, place), device_id_type=MESH,
        )

    loads = [
        pltpu.make_async_copy(src, dst, load_sem.at[i])
        for i, (src, dst) in enumerate(
            (
                (normed_ref, normed.at[chunk(place), :]),
                (gate_w_ref, wg),
                (cot_ref, cot),
                (up_w_ref, wu),
                (down_w_ref, weight_rows(0, dp)),
            )
        )
    ]

    @pl.when(place < 3)
    def _():
        own_copy(1).start()

    @pl.when(place > 0)
    def _():
        own_copy(-1).start()

    for lane in (0, 1, 4):
        plane_copy(0, lane).start()
    for load in loads:
        load.start()

    def plane_second(i):
        for lane in range(2):
            plane_copy(i, lane).wait_recv()
            plane_copy(i, lane + 2).start()
            plane_copy(i, lane + 5).start()

    def plane_third(i):
        plane_copy(i, 2).wait_recv()
        plane_copy(i, 3).wait_recv()
        plane_copy(i, 7).start()

    def plane_ready(i):
        for lane in range(4, 8):
            plane_copy(i, lane).wait_recv()

    def sums_copy(rank, cut, slot, step):
        window = pl.ds(pl.multiple_of(cut * few, few), few)
        return remote(
            part.at[rank, window, :], arrival.at[slot, window, :], l_send.at[rank, cut],
            l_recv.at[slot, cut], step,
        )

    def branch_copy(rank):
        return pltpu.make_async_copy(branch_stage, branch_out.at[rank], stage_sem.at[0])

    def compute(rank):
        here = chunk(rank)

        def activate(columns):
            gate = dot_nn(normed[here, :], wg[:, columns])
            up = dot_nn(normed[here, :], wu[:, columns])
            d_hidden = dot_nn(cot[here, :], wd[:, columns])
            sig = 1.0 / (1.0 + jnp.exp(-gate))
            silu = gate * sig
            hid[here, columns] = (silu * up).astype(low)
            dg[here, columns] = (d_hidden * up * sig * (1.0 + gate * (1.0 - sig))).astype(low)
            du[here, columns] = (d_hidden * silu).astype(low)

        by_tiles(wg.shape[1], 256, activate)

        def pull(columns):
            part[rank, :, columns] = (
                dot_nt(dg[here, :], wg[columns, :]) + dot_nt(du[here, :], wu[columns, :])
            ).astype(low)

        by_tiles(depth, 512, pull)

    def branch(rank):
        def push(columns):
            branch_stage[:, columns] = dot_nt(hid[chunk(rank), :], wd[columns, :]).astype(low)

        by_tiles(depth, 512, push)
        branch_copy(rank).start()

    def take(rank):
        pass_copy(rank, 1).wait_recv()

        @pl.when((rank < place) & (place < 3))
        def _():
            pass_copy(rank, 1).start()

        @pl.when((rank > place) & (place > 0))
        def _():
            pass_copy(rank, -1).start()

    inside = (place == 1) | (place == 2)
    plane_second(0)
    take(order[0])

    @pl.when(inside)
    def _():
        take(order[1])

    plane_third(0)
    for load in loads:
        load.wait()
    plane_ready(0)

    @pl.loop(0, 4)
    def _(turn):
        rank = jnp.where(
            turn == 0,
            order[0],
            jnp.where(turn == 1, place, jnp.where(turn == 2, order[1], order[2])),
        )

        @pl.when((turn == 1) & inside)
        def _():
            take(order[2])

        @pl.when((turn == 2) & jnp.logical_not(inside))
        def _():
            take(order[1])

        @pl.when((turn == 3) & jnp.logical_not(inside))
        def _():
            take(order[2])

        compute(rank)

        @pl.when((turn != 1) & (place == 3))
        def _():
            for cut in range(cuts):
                sums_copy(rank, cut, rank, -1).start()

        @pl.when((turn != 1) & (place == 0))
        def _():
            slot = jnp.where(rank == 1, 4, rank)
            for cut in range(cuts):
                sums_copy(rank, cut, slot, 1).start()

    def gate_copy(tile):
        return pltpu.make_async_copy(gate_stage, gg_out.at[tile, :], stage_sem.at[1])

    def up_copy(tile):
        return pltpu.make_async_copy(up_stage, gu_out.at[tile, :], stage_sem.at[2])

    def down_copy(tile):
        return pltpu.make_async_copy(gate_stage, gd_out.at[tile, :], stage_sem.at[1])

    size = gate_stage.shape[0]
    tiles = depth // size

    def gate_up_tile(index):
        tile = pl.ds(pl.multiple_of(index * size, size), size)
        left = normed[:, tile]
        gate_grad = dot_tn(left, dg[...]).astype(low)

        @pl.when(index > 0)
        def _():
            gate_copy(tile).wait()
            up_copy(tile).wait()

        gate_stage[...] = gate_grad
        gate_copy(tile).start()
        up_stage[...] = dot_tn(left, du[...]).astype(low)
        up_copy(tile).start()

    def down_tile(index):
        tile = pl.ds(pl.multiple_of(index * size, size), size)
        down_grad = dot_tn(cot[:, tile], hid[...]).astype(low)

        @pl.when(index > 0)
        def _():
            down_copy(tile).wait()

        gate_stage[...] = down_grad
        down_copy(tile).start()

    last = pl.ds(depth - size, size)

    def relay(rank, slot, step, cut):
        sums_copy(rank, cut, rank, step).wait_recv()
        window = pl.ds(pl.multiple_of(cut * few, few), few)
        part[rank, window, :] = part[rank, window, :] + arrival[rank, window, :]
        sums_copy(rank, cut, slot, step).start()

    outward = 3 - 2 * place

    @pl.loop(0, cuts)
    def _(cut):
        @pl.when(inside)
        def _():
            relay(3 - place, 4 - 3 * (place - 1), outward, cut)

        @pl.loop(0, tiles // cuts)
        def _(index):
            gate_up_tile(cut * (tiles // cuts) + index)

    gate_copy(last).wait()
    up_copy(last).wait()

    @pl.loop(0, cuts)
    def _(cut):
        @pl.when(inside)
        def _():
            relay(6 - 3 * place, 6 - 3 * place, outward, cut)
            relay(3 * (place - 1), 4 * (place - 1), -outward, cut)

        @pl.loop(0, tiles // cuts)
        def _(index):
            down_tile(cut * (tiles // cuts) + index)

    down_copy(last).wait()

    @pl.loop(0, 4)
    def _(rank):
        @pl.when(rank > 0)
        def _():
            branch_copy(rank).wait()

        branch(rank)

    branch_copy(0).wait()

    for cut in range(cuts):
        window = pl.ds(cut * few, few)
        dn_out[window, :] = part[place, window, :].astype(jnp.float32)

        @pl.when(place < 3)
        def _():
            sums_copy(place, cut, place, 1).wait_recv()
            dn_out[window, :] += arrival[place, window, :].astype(jnp.float32)

        @pl.when(place > 0)
        def _():
            sums_copy(place, cut, 4, 1).wait_recv()
            dn_out[window, :] += arrival[4, window, :].astype(jnp.float32)

    @pl.when(place < 3)
    def _():
        own_copy(1).wait_send()

    @pl.when(place > 0)
    def _():
        own_copy(-1).wait_send()

    for rank in range(4):

        @pl.when((rank < place) & (place < 3))
        def _():
            pass_copy(rank, 1).wait_send()

        @pl.when((rank > place) & (place > 0))
        def _():
            pass_copy(rank, -1).wait_send()

        @pl.when(rank != place)
        def _():
            for cut in range(cuts):
                sums_copy(rank, cut, rank, 1).wait_send()

    for lane in range(8):
        plane_copy(0, lane).wait_send()


def feed_forward(normed, w_gate, w_up, w_down, cotangent):
    low = jnp.bfloat16
    rows, depth = normed.shape
    length = cotangent.shape[0]
    units = w_gate.shape[1]
    ranks = length // rows
    cuts = 4
    anywhere = pl.BlockSpec(memory_space=pl.ANY)
    in_vmem = pl.BlockSpec(memory_space=pltpu.VMEM)
    dma = pltpu.SemaphoreType.DMA
    flops = 9 * 2 * length * depth * units
    return pl.pallas_call(
        feed_forward_kernel,
        out_shape=[jax.ShapeDtypeStruct((depth, units), low)] * 3
        + [
            jax.ShapeDtypeStruct((ranks, rows, depth), low),
            jax.ShapeDtypeStruct((rows, depth), jnp.float32),
        ],
        in_specs=[anywhere] * 5,
        out_specs=[anywhere] * 4 + [in_vmem],
        scratch_shapes=[pltpu.VMEM((depth, units), low)] * 3
        + [pltpu.VMEM((length, depth), low)] * 2
        + [pltpu.VMEM((length, units), low)] * 3
        + [
            pltpu.VMEM((ranks, rows, depth), low),
            pltpu.VMEM((ranks + 1, rows, depth), low),
            pltpu.VMEM((rows, depth), low),
            pltpu.VMEM((256, units), low),
            pltpu.VMEM((256, units), low),
            dma((5,)), dma((2, ranks)), dma((ranks,)), dma((ranks, cuts)), dma((ranks + 1, cuts)),
            dma((3,)), dma((1, 8)), dma((1, 8)),
        ],
        compiler_params=pltpu.CompilerParams(
            collective_id=2, has_side_effects=True, vmem_limit_bytes=62 * 1024 * 1024
        ),
        cost_estimate=pl.CostEstimate(flops=flops, bytes_accessed=60 << 20, transcendentals=0),
        name="feed_forward",
    )(normed, w_gate, w_up, w_down, cotangent)


def local(
    tokens,
    segments,
    gain_attn,
    w_query,
    w_keyval,
    w_output,
    gain_mlp,
    w_gate,
    w_up,
    w_down,
    cotangent,
):
    tensor_rank = lax.axis_index("tensor")
    length = segments.shape[0]
    rows = tokens.shape[0]
    both = ("dp", "tensor")
    low = jnp.bfloat16

    def gather(array, axes, axis=0):
        return lax.all_gather(array, axes, axis=axis, tiled=True)

    def scatter(array, axes, axis=0):
        return lax.psum_scatter(array, axes, scatter_dimension=axis, tiled=True)

    by_kernels = (lax.axis_size("dp"), lax.axis_size("tensor")) == (8, 4)
    places = doc_positions(segments)
    my_places = lax.dynamic_slice_in_dim(places, tensor_rank * rows, rows, 0)
    my_segments = lax.dynamic_slice_in_dim(segments, tensor_rank * rows, rows, 0)
    cosine, sine_table = rope_tables(my_places, HD)
    order = jnp.arange(length, dtype=jnp.int32)
    allowed = (order[:, None] <= tensor_rank * rows + order[None, :rows]) & (
        segments[:, None] == my_segments[None, :]
    )
    bias = jnp.where(allowed, 0.0, masked).astype(jnp.float32)

    token_rows = tokens.astype(jnp.float32)
    normed_attn, unit_attn, inverse_attn = norm_forward(token_rows, gain_attn)
    normed_attn = normed_attn.astype(low)
    wide = KVH * HD
    if by_kernels:
        cos_tile = jnp.tile(cosine, (1, 4))
        sin_tile = jnp.tile(jnp.concatenate([-sine_table, sine_table], axis=1), (1, 2))
        (
            query, keyval, heads_low, log_sum, residual, normed_mlp,
            full_keyval, full_query, full_output, full_gate, full_up, piece,
        ) = attend_all(
            tokens, normed_attn, cos_tile, sin_tile, bias, gain_mlp[None, :],
            w_keyval, w_query, w_output, w_gate, w_up, cotangent,
        )
    else:
        full_keyval = gather(w_keyval, "dp")
        keyval_pre = dot_nn(normed_attn, full_keyval)
        key_low = rotate(keyval_pre[:, :wide], cosine, sine_table).astype(low)
        keyval = jnp.concatenate([key_low, keyval_pre[:, wide:].astype(low)], axis=1)
        keyval = gather(keyval, "tensor")
        full_query = gather(gather(w_query, "tensor", 1), "dp")
        query = rotate(dot_nn(normed_attn, full_query), cosine, sine_table) * (HD**-0.5)
        query = query.astype(low)
    if by_kernels:
        grad_gate, grad_up, grad_down, branch, d_normed_mlp = feed_forward(
            normed_mlp, full_gate, full_up, w_down, piece
        )
        to_down, to_gate, to_up, to_output, to_query, to_narrow, layer_out, grad_tokens = (
            reach_back(
                (grad_down, grad_gate, grad_up),
                branch,
                (full_keyval, full_query, full_output),
                d_normed_mlp,
                residual,
                (
                    cotangent, tokens, normed_attn, query, heads_low, keyval, log_sum, bias,
                    cos_tile, sin_tile, gain_attn[None, :], gain_mlp[None, :],
                ),
            )
        )
        wide = 2 * KVH * HD
        return (
            layer_out,
            grad_tokens,
            to_narrow[:, wide],
            to_query,
            to_narrow[:, :wide],
            to_output,
            to_narrow[:, wide + 1],
            to_gate,
            to_up,
            to_down,
        )

    key_heads, value_heads = by_head(keyval[:, :wide]), by_head(keyval[:, wide:])
    blank = jnp.zeros_like(key_heads)
    key_f = jnp.concatenate([key_heads, blank], axis=2)
    key_b = jnp.concatenate([blank, key_heads], axis=2)
    value_f = jnp.concatenate([value_heads, blank], axis=2)
    value_b = jnp.concatenate([blank, value_heads], axis=2)
    key_t = key_heads.transpose(0, 2, 1)
    value_t = value_heads.transpose(0, 2, 1)
    heads_low, log_sum = attend_forward(query, key_f, key_b, value_t, bias)
    full_output = gather(gather(w_output, "tensor", 1), "dp")
    residual = token_rows + dot_nt(heads_low, full_output)
    full_gate, full_up = gather(w_gate, "dp"), gather(w_up, "dp")
    full_down = gather(w_down, "dp")
    piece = gather(cotangent, "tensor")
    normed_mlp_rows, unit_mlp, inverse_mlp = norm_forward(residual, gain_mlp)
    normed_mlp = normed_mlp_rows.astype(low)
    gathered_mlp = gather(normed_mlp, "tensor")
    gate_act = dot_nn(gathered_mlp, full_gate)
    up_act = dot_nn(gathered_mlp, full_up)
    sigmoid_gate = jax.nn.sigmoid(gate_act)
    silu_gate = gate_act * sigmoid_gate
    hidden_low = (silu_gate * up_act).astype(low)
    d_hidden = dot_nn(piece, full_down)
    d_gate = (d_hidden * up_act * sigmoid_gate * (1.0 + gate_act * (1.0 - sigmoid_gate))).astype(low)
    d_up = (d_hidden * silu_gate).astype(low)
    d_normed_mlp = scatter(
        (dot_nt(d_gate, full_gate) + dot_nt(d_up, full_up)).astype(low), "tensor"
    ).astype(jnp.float32)
    branch = dot_nt(hidden_low, full_down).astype(low)
    grad_down = dot_tn(piece, hidden_low)
    grad_gate = dot_tn(gathered_mlp, d_gate)
    grad_up = dot_tn(gathered_mlp, d_up)
    d_norm_mlp, gain_mlp_part = norm_backward(d_normed_mlp, unit_mlp, inverse_mlp, gain_mlp)
    d_residual = cotangent.astype(jnp.float32) + d_norm_mlp

    d_branch = d_residual.astype(low)
    grad_output = dot_tn(d_branch, heads_low)
    d_heads = dot_nn(d_branch, full_output).astype(low)
    d_queries, d_keys, d_values = attend_backward(
        query, d_heads, key_f, key_b, key_t, value_f, value_b, bias, log_sum
    )

    def flat(parts):
        joined = parts[:, :, :HD] + parts[:, :, HD:]
        return joined.transpose(1, 0, 2).reshape(length, wide)

    d_keyval = scatter(
        jnp.concatenate([flat(d_keys), flat(d_values)], axis=1).astype(low), "tensor"
    ).astype(jnp.float32)
    dq_low = rotate(d_queries, cosine, -sine_table).astype(low)
    dkv_low = jnp.concatenate(
        [rotate(d_keyval[:, :wide], cosine, -sine_table), d_keyval[:, wide:]], axis=1
    ).astype(low)
    grad_query = dot_tn(normed_attn, dq_low)
    grad_keyval = dot_tn(normed_attn, dkv_low)
    d_normed_attn = dot_nt(dq_low, full_query) + dot_nt(dkv_low, full_keyval)
    d_norm_attn, gain_attn_part = norm_backward(d_normed_attn, unit_attn, inverse_attn, gain_attn)
    grad_tokens = (d_residual + d_norm_attn).astype(low)

    layer_rows = residual + scatter(branch, "tensor").astype(jnp.float32)

    def shares(grad):
        return scatter(grad.astype(low), "dp").astype(jnp.float32)

    def square_shares(grad):
        return scatter(scatter(grad.astype(low), "dp"), "tensor", 1).astype(jnp.float32)

    gains = scatter(
        jnp.stack([gain_attn_part, gain_mlp_part]).reshape(2, -1, rows_of_gain(gain_attn)), both, 1
    )
    return (
        layer_rows.astype(low),
        grad_tokens,
        gains[0, 0],
        square_shares(grad_query),
        scatter(grad_keyval.astype(low), both).astype(jnp.float32),
        square_shares(grad_output),
        gains[1, 0],
        shares(grad_gate),
        shares(grad_up),
        shares(grad_down),
    )


def rows_of_gain(gain):
    return gain.shape[0] // (lax.axis_size("dp") * lax.axis_size("tensor"))


def solution(mesh):
    return jax.shard_map(
        local,
        mesh=mesh,
        in_specs=(
            P(("dp", "tensor"), None),
            P("dp"),
            P(),
            P("dp", "tensor"),
            P("dp", None),
            P("dp", "tensor"),
            P(),
            P("dp", "tensor"),
            P("dp", "tensor"),
            P("dp", "tensor"),
            P(("dp", "tensor"), None),
        ),
        out_specs=(
            P(("dp", "tensor"), None),
            P(("dp", "tensor"), None),
            P(("dp", "tensor")),
            P("dp", "tensor"),
            P(("dp", "tensor"), None),
            P("dp", "tensor"),
            P(("dp", "tensor")),
            P("dp", "tensor"),
            P("dp", "tensor"),
            P("dp", "tensor"),
        ),
        check_vma=False,
    )
```

```python
import functools

import jax
import jax.numpy as jnp
from jax import lax
from jax.experimental import pallas as pl
from jax.experimental.pallas import tpu as pltpu
from jax.sharding import PartitionSpec as P

KVH = 4
HD = 64
PAIR = 2 * HD

epsilon = 1e-05
rope_base = 10000.0
masked = -1e30


def doc_positions(seg_row):
    length = seg_row.shape[0]
    places = jnp.arange(length, dtype=jnp.int32)
    change = jnp.concatenate([jnp.ones((1,), jnp.bool_), seg_row[1:] != seg_row[:-1]])
    starts = lax.cummax(jnp.where(change, places, 0), axis=0)
    return places - starts


def rope_tables(places, width):
    half_width = width // 2
    frequency = rope_base ** (-(2.0 * jnp.arange(half_width).astype(jnp.float32)) / width)
    angles = places.astype(jnp.float32)[:, None] * frequency[None, :]
    return (jnp.cos(angles), jnp.sin(angles))


def rotate(values, cosine, sine_table):
    rows, width = values.shape
    heads = values.reshape(rows, width // HD, HD)
    half_width = HD // 2
    front_half = heads[..., :half_width]
    back_half = heads[..., half_width:]
    cos_rows = cosine[:, None, :]
    sin_rows = sine_table[:, None, :]
    turned = jnp.concatenate(
        [
            front_half * cos_rows - back_half * sin_rows,
            back_half * cos_rows + front_half * sin_rows,
        ],
        axis=-1,
    )
    return turned.reshape(rows, width)


def norm_forward(values, gain_vec):
    inverse = lax.rsqrt(jnp.mean(values * values, axis=-1, keepdims=True) + epsilon)
    unit_rows = values * inverse
    return (unit_rows * gain_vec, unit_rows, inverse)


def norm_backward(d_normed, unit_rows, inverse, gain_vec):
    gain_part = jnp.sum(d_normed * unit_rows, axis=0)
    d_unit = d_normed * gain_vec
    d_values = inverse * (d_unit - unit_rows * jnp.mean(d_unit * unit_rows, axis=-1, keepdims=True))
    return (d_values, gain_part)


def dot_nn(left, right):
    return jnp.dot(left, right, preferred_element_type=jnp.float32)


def dot_nt(left, right):
    return lax.dot_general(
        left, right, (((1,), (1,)), ((), ())), preferred_element_type=jnp.float32
    )


def dot_tn(left, right):
    return lax.dot_general(
        left, right, (((0,), (0,)), ((), ())), preferred_element_type=jnp.float32
    )


def front_lanes(tile):
    lane = lax.broadcasted_iota(jnp.int32, tile.shape, 1)
    return jnp.where(lane < HD, tile, jnp.zeros_like(tile))


def back_lanes(tile):
    lane = lax.broadcasted_iota(jnp.int32, tile.shape, 1)
    return jnp.where(lane < HD, jnp.zeros_like(tile), tile)


def attend_forward_kernel(query_ref, front_ref, back_ref, value_t_ref, bias_ref, out_ref, log_ref):
    pairs = query_ref.shape[1] // PAIR
    value_t = value_t_ref[0]
    for pair in range(pairs):
        query = query_ref[:, pair * PAIR : (pair + 1) * PAIR]
        outs = []
        for side, key_ref in enumerate((front_ref, back_ref)):
            scores = dot_nt(key_ref[0], query) + bias_ref[...]
            top = jnp.max(scores, axis=0, keepdims=True)
            expo = jnp.exp(scores - top)
            total = jnp.sum(expo, axis=0, keepdims=True)
            outs.append(dot_nn(value_t, expo.astype(jnp.bfloat16)) / total)
            log_ref[0, pl.ds(pair * 2 + side, 1), :] = top + jnp.log(total)
        out = jnp.concatenate(outs, axis=0).T
        out_ref[:, pair * PAIR : (pair + 1) * PAIR] = out.astype(jnp.bfloat16)


def attend_backward_kernel(
    query_ref,
    grad_ref,
    kf_ref,
    kb_ref,
    kt_ref,
    vf_ref,
    vb_ref,
    bias_ref,
    log_ref,
    dq_ref,
    dk_ref,
    dv_ref,
):
    pairs = query_ref.shape[1] // PAIR
    key_t = kt_ref[0]
    dk_ref[0] = jnp.zeros(dk_ref.shape[1:], jnp.float32)
    dv_ref[0] = jnp.zeros(dv_ref.shape[1:], jnp.float32)
    for pair in range(pairs):
        columns = slice(pair * PAIR, (pair + 1) * PAIR)
        query = query_ref[:, columns]
        grad = grad_ref[:, columns]
        outs = []
        for side, (key_ref, value_ref, keep) in enumerate(
            ((kf_ref, vf_ref, front_lanes), (kb_ref, vb_ref, back_lanes))
        ):
            log_sum = log_ref[0, pl.ds(pair * 2 + side, 1), :]
            probs = jnp.exp(dot_nt(key_ref[0], query) + bias_ref[...] - log_sum)
            d_probs = dot_nt(value_ref[0], grad)
            row_dot = jnp.sum(probs * d_probs, axis=0, keepdims=True)
            d_scores = (probs * (d_probs - row_dot)).astype(jnp.bfloat16)
            dk_ref[0] += dot_nn(d_scores, keep(query))
            dv_ref[0] += dot_nn(probs.astype(jnp.bfloat16), keep(grad))
            outs.append(dot_nn(key_t, d_scores))
        dq_ref[:, columns] = jnp.concatenate(outs, axis=0).T * (HD**-0.5)


def whole_group(rows, width):
    return pl.BlockSpec((1, rows, width), lambda g: (g, 0, 0))


def columns_of(rows, width):
    return pl.BlockSpec((rows, width), lambda g: (0, g))


def attend_forward(query, key_f, key_b, value_t, bias):
    rows, width = query.shape
    length = bias.shape[0]
    group = width // KVH
    return pl.pallas_call(
        attend_forward_kernel,
        grid=(KVH,),
        in_specs=[
            columns_of(rows, group),
            whole_group(length, PAIR),
            whole_group(length, PAIR),
            whole_group(HD, length),
            pl.BlockSpec((length, rows), lambda g: (0, 0)),
        ],
        out_specs=[columns_of(rows, group), whole_group(group // HD, rows)],
        out_shape=[
            jax.ShapeDtypeStruct((rows, width), jnp.bfloat16),
            jax.ShapeDtypeStruct((KVH, group // HD, rows), jnp.float32),
        ],
        compiler_params=pltpu.CompilerParams(vmem_limit_bytes=48 * 1024 * 1024),
        name="attend_forward",
    )(query, key_f, key_b, value_t, bias)


def attend_backward(query, grad, key_f, key_b, key_t, value_f, value_b, bias, log_sum):
    rows, width = query.shape
    length = bias.shape[0]
    group = width // KVH
    tall = whole_group(length, PAIR)
    return pl.pallas_call(
        attend_backward_kernel,
        grid=(KVH,),
        in_specs=[
            columns_of(rows, group),
            columns_of(rows, group),
            tall,
            tall,
            whole_group(HD, length),
            tall,
            tall,
            pl.BlockSpec((length, rows), lambda g: (0, 0)),
            whole_group(group // HD, rows),
        ],
        out_specs=[columns_of(rows, group), tall, tall],
        out_shape=[
            jax.ShapeDtypeStruct((rows, width), jnp.float32),
            jax.ShapeDtypeStruct((KVH, length, PAIR), jnp.float32),
            jax.ShapeDtypeStruct((KVH, length, PAIR), jnp.float32),
        ],
        compiler_params=pltpu.CompilerParams(vmem_limit_bytes=48 * 1024 * 1024),
        name="attend_backward",
    )(query, grad, key_f, key_b, key_t, value_f, value_b, bias, log_sum)


def by_head(matrix):
    rows = matrix.shape[0]
    return matrix.reshape(rows, KVH, HD).transpose(1, 0, 2)


MESH = pl.DeviceIdType.MESH


def flip(index, bit):
    return index + bit - 2 * bit * ((index // bit) % 2)


def line_order(place):
    nearest = place - 1 + 2 * (1 - (place + 3) // 4)
    farthest = 3 - 3 * (place // 2)
    return (nearest, 6 - place - nearest - farthest, farthest)


def enter(dp, place):
    barrier = pltpu.get_barrier_semaphore()
    for bit in (1, 2, 4):
        pl.semaphore_signal(barrier, inc=1, device_id=(flip(dp, bit), place), device_id_type=MESH)
    for step in (-1, 1):
        there = (place + step >= 0) & (place + step < 4)

        @pl.when(there)
        def _():
            pl.semaphore_signal(
                barrier, inc=1, device_id=(dp, place + step), device_id_type=MESH
            )

    ends = 1 - ((place + 3) // 4) + place // 3
    pl.semaphore_wait(barrier, 5 - ends)


def turn(tile, cos, sin):
    lane = lax.broadcasted_iota(jnp.int32, tile.shape, 1)
    swapped = jnp.where(
        lane % HD < HD // 2, pltpu.roll(tile, PAIR - HD // 2, 1), pltpu.roll(tile, HD // 2, 1)
    )
    return tile * cos + swapped * sin


def head_tiles(keyval, group):
    columns = slice(group // 2 * PAIR, (group // 2 + 1) * PAIR)
    tile = keyval[:, columns]
    values = slice(KVH * HD + columns.start, KVH * HD + columns.stop)
    if group % 2 == 0:
        front = front_lanes(tile)
        keys = (front, pltpu.roll(front, HD, 1))
    else:
        back = back_lanes(tile)
        keys = (pltpu.roll(back, HD, 1), back)
    return keys, keyval[:, values]


def attend_kernel(
    tokens_ref, normed_ref, cos_ref, sin_ref, bias_ref, gain_ref,
    kv_ref, q_ref, o_ref, g_ref, u_ref, c_ref,
    query_out, keyval_out, heads_out, log_out, residual_out, mlp_out,
    fkv, fq, fo, fg, fu, fc,
    kv_weight, weight, wide_weight, keyval, key_f, key_b, value_t,
    own_sem, z_send, z_recv, p_send, p_recv, k_send, k_recv, w_sem,
):
    dp, place = lax.axis_index("dp"), lax.axis_index("tensor")
    rows = kv_ref.shape[0]
    half = rows // 2
    width = q_ref.shape[1]
    order = line_order(place)
    enter(dp, place)

    def rows_of(owner):
        return pl.ds(pl.multiple_of(owner * rows, rows), rows)

    def columns_of_rank(rank):
        return pl.ds(pl.multiple_of(rank * width, width), width)

    def remote(src, dst, send, recv, device):
        return pltpu.make_async_remote_copy(
            src_ref=src, dst_ref=dst, send_sem=send, recv_sem=recv,
            device_id=device, device_id_type=MESH,
        )

    own = [
        (kv_ref, fkv.at[rows_of(dp), :]),
        (q_ref, fq.at[rows_of(dp), columns_of_rank(place)]),
        (o_ref, fo.at[rows_of(dp), columns_of_rank(place)]),
        (g_ref, fg.at[rows_of(dp), :]),
        (u_ref, fu.at[rows_of(dp), :]),
        (c_ref, fc.at[rows_of(place), :]),
    ]
    own_copies = [
        pltpu.make_async_copy(src, dst, own_sem.at[i]) for i, (src, dst) in enumerate(own)
    ]
    for copy in own_copies:
        copy.start()

    def line_block(which, rank):
        if which == 2:
            return fc.at[rows_of(rank), :]
        return (fq, fo)[which].at[rows_of(dp), columns_of_rank(rank)]

    def line_copy(which, rank, step):
        src = (q_ref, o_ref, c_ref)[which] if rank is place else line_block(which, rank)
        side = 0 if step < 0 else 1
        return remote(
            src, line_block(which, rank), z_send.at[which, side, rank], z_recv.at[which, rank],
            (dp, place + step),
        )

    def line_send(which, rank, act):
        @pl.when((rank <= place) & (place < 3))
        def _():
            act(line_copy(which, rank, 1))

        @pl.when((rank >= place) & (place > 0))
        def _():
            act(line_copy(which, rank, -1))

    def start(copy):
        copy.start()

    def wait_send(copy):
        copy.wait_send()

    x, y, core = flip(dp, 2), flip(dp, 4), flip(dp, 1)
    far = flip(x, 4)

    blocks = [("kv", None), ("q", place), ("g", None)] + [("q", rank) for rank in order]
    blocks += [("o", place)] + [("o", rank) for rank in order] + [("u", None)]

    def block(index, owner, part=None):
        name, rank = blocks[index]
        ref = {"kv": fkv, "q": fq, "o": fo, "g": fg, "u": fu}[name]
        first = owner * rows if part is None else owner * rows + part * half
        size = rows if part is None else half
        window = pl.ds(pl.multiple_of(first, half), size)
        if rank is None:
            return ref.at[window, :]
        return ref.at[window, columns_of_rank(rank)]

    def own_block(index):
        name, rank = blocks[index]
        if rank is None or rank is place:
            return {"kv": kv_ref, "q": q_ref, "o": o_ref, "g": g_ref, "u": u_ref}[name]
        return block(index, dp)

    def plane_copy(index, lane):
        send, recv = p_send.at[index, lane], p_recv.at[index, lane]
        if lane == 0:
            return remote(own_block(index), block(index, dp), send, recv, (x, place))
        if lane == 1:
            return remote(own_block(index), block(index, dp), send, recv, (y, place))
        if lane == 2:
            return remote(block(index, x, 0), block(index, x, 0), send, recv, (y, place))
        if lane == 3:
            return remote(block(index, y, 1), block(index, y, 1), send, recv, (x, place))
        owner = (dp, x, y, far)[lane - 4]
        src = own_block(index) if lane == 4 else block(index, owner)
        return remote(src, block(index, owner), send, recv, (core, place))

    def plane_first(index):
        plane_copy(index, 0).start()
        plane_copy(index, 1).start()
        plane_copy(index, 4).start()

    def plane_second(index):
        plane_copy(index, 0).wait_recv()
        plane_copy(index, 2).start()
        plane_copy(index, 5).start()
        plane_copy(index, 1).wait_recv()
        plane_copy(index, 3).start()
        plane_copy(index, 6).start()

    def plane_third(index):
        plane_copy(index, 2).wait_recv()
        plane_copy(index, 3).wait_recv()
        plane_copy(index, 7).start()

    def plane_ready(index):
        for lane in range(4, 8):
            plane_copy(index, lane).wait_recv()

    def plane_sent(index):
        for lane in range(8):
            plane_copy(index, lane).wait_send()

    def keyval_block(rank):
        return keyval.at[rows_of(rank), :]

    def keyval_copy(rank, step):
        side = 0 if step < 0 else 1
        return remote(
            keyval_block(rank), keyval_block(rank), k_send.at[side, rank], k_recv.at[rank],
            (dp, place + step),
        )

    def keyval_send(rank, act):
        @pl.when((rank <= place) & (place < 3))
        def _():
            act(keyval_copy(rank, 1))

        @pl.when((rank >= place) & (place > 0))
        def _():
            act(keyval_copy(rank, -1))

    def keyval_take(step):
        keyval_copy(order[step], 1).wait_recv()
        keyval_send(order[step], start)

    low = jnp.bfloat16
    wide = KVH * HD

    def make_keyval():
        load = pltpu.make_async_copy(fkv, kv_weight, w_sem.at[0])
        load.start()
        load.wait()
        made = dot_nn(normed_ref[...], kv_weight[...])
        for tile in range(wide // PAIR):
            columns = slice(tile * PAIR, (tile + 1) * PAIR)
            keyval[rows_of(place), columns] = turn(
                made[:, columns], cos_ref[...], sin_ref[...]
            ).astype(low)
        keyval[rows_of(place), wide:] = made[:, wide:].astype(low)
        keyval_send(place, start)

    def weight_load(source, rank, by_rows):
        window = pl.ds(pl.multiple_of(rank * width, width), width)
        src = source.at[window, :] if by_rows else source.at[:, window]
        dst = wide_weight.at[rank % 2] if by_rows else weight.at[rank % 2]
        return pltpu.make_async_copy(src, dst, w_sem.at[rank % 2])

    def make_query():
        weight_load(fq, 0, False).start()
        for rank in range(4):
            if rank < 3:
                weight_load(fq, rank + 1, False).start()
            weight_load(fq, rank, False).wait()
            made = dot_nn(normed_ref[...], weight[rank % 2])
            for tile in range(width // PAIR):
                columns = slice(tile * PAIR, (tile + 1) * PAIR)
                query_out[:, rank * width + tile * PAIR : rank * width + (tile + 1) * PAIR] = (
                    turn(made[:, columns], cos_ref[...], sin_ref[...]) * (HD**-0.5)
                ).astype(low)

    def attend(group):
        key_tile, value_tile = head_tiles(keyval, group)
        key_f[...], key_b[...] = key_tile
        side = group % 2
        value_t[...] = value_tile.T[side * HD : (side + 1) * HD, :]
        pairs = query_out.shape[1] // PAIR // KVH

        @pl.loop(0, pairs)
        def _(index):
            pair = group * pairs + index
            columns = pl.ds(pl.multiple_of(pair * PAIR, PAIR), PAIR)
            query = query_out[:, columns]
            outs, logs = [], []
            for key_ref in (key_f, key_b):
                scores = dot_nt(key_ref[...], query) + bias_ref[...]
                top = jnp.max(scores, axis=0, keepdims=True)
                expo = jnp.exp(scores - top)
                total = jnp.sum(expo, axis=0, keepdims=True)
                outs.append(dot_nn(value_t[...], expo.astype(low)) / total)
                logs.append(top + jnp.log(total))
            log_out[pair] = jnp.concatenate(logs, axis=0)
            heads_out[:, columns] = jnp.concatenate(outs, axis=0).T.astype(low)

    def make_residual():
        weight_load(fo, 0, True).start()
        square = jnp.zeros((rows, 1), jnp.float32)
        for rank in range(4):
            if rank < 3:
                weight_load(fo, rank + 1, True).start()
            weight_load(fo, rank, True).wait()
            columns = slice(rank * width, (rank + 1) * width)
            made = tokens_ref[:, columns].astype(jnp.float32) + dot_nt(
                heads_out[...], wide_weight[rank % 2]
            )
            residual_out[:, columns] = made
            square += jnp.sum(made * made, axis=1, keepdims=True)
        inverse = lax.rsqrt(square * (1.0 / (4 * width)) + epsilon)
        for rank in range(4):
            columns = slice(rank * width, (rank + 1) * width)
            mlp_out[:, columns] = (
                residual_out[:, columns] * inverse * gain_ref[:, columns]
            ).astype(low)

    inside = (place == 1) | (place == 2)

    def cot_take(rank):
        line_copy(2, rank, 1).wait_recv()
        line_send(2, rank, start)

    def line_take(which, step):
        line_copy(which, order[step], 1).wait_recv()
        line_send(which, order[step], start)

    count = len(blocks)
    kv, q_own, gate, o_own, up = 0, 1, 2, 6, 10
    q_far, o_far = (3, 4, 5), (7, 8, 9)
    plane_first(kv)
    line_send(0, place, start)
    plane_first(q_own)
    line_take(0, 0)
    line_send(1, place, start)
    plane_second(kv)
    plane_first(gate)
    plane_second(q_own)
    plane_third(kv)
    plane_ready(kv)
    own_copies[0].wait()
    line_take(0, 1)
    make_keyval()
    plane_first(q_far[0])
    plane_third(q_own)
    line_take(1, 0)
    line_take(0, 2)
    plane_second(gate)
    plane_first(q_far[1])
    keyval_take(0)
    line_take(1, 1)
    plane_second(q_far[0])
    plane_first(q_far[2])
    plane_third(gate)
    keyval_take(1)
    line_take(1, 2)
    plane_second(q_far[1])
    plane_first(o_own)
    plane_third(q_far[0])
    keyval_take(2)
    line_send(2, place, start)
    plane_second(q_far[2])
    plane_first(o_far[0])
    plane_third(q_far[1])
    plane_second(o_own)
    plane_first(o_far[1])
    plane_third(q_far[2])
    for index in (q_own,) + q_far:
        plane_ready(index)
    own_copies[1].wait()
    make_query()
    cot_take(order[0])

    @pl.when(inside)
    def _():
        cot_take(order[1])

    plane_second(o_far[0])
    plane_first(o_far[2])
    plane_third(o_own)
    attend(0)
    plane_second(o_far[1])
    plane_first(up)
    plane_third(o_far[0])
    attend(1)
    plane_second(o_far[2])
    plane_third(o_far[1])
    attend(2)
    plane_third(o_far[2])
    cot_take(jnp.where(inside, order[2], order[1]))
    attend(3)
    plane_second(up)
    for index in (o_own,) + o_far:
        plane_ready(index)
    own_copies[2].wait()
    make_residual()
    plane_third(up)

    @pl.when(jnp.logical_not(inside))
    def _():
        cot_take(order[2])

    plane_ready(gate)
    plane_ready(up)
    for index in range(count):
        plane_sent(index)
    for which in range(3):
        line_send(which, place, wait_send)
        for step in range(3):
            line_send(which, order[step], wait_send)
    keyval_send(place, wait_send)
    for step in range(3):
        keyval_send(order[step], wait_send)
    for copy in own_copies[3:]:
        copy.wait()
    out_copy = pltpu.make_async_copy(keyval, keyval_out, w_sem.at[0])
    out_copy.start()
    out_copy.wait()


def attend_all(
    tokens, normed, cos, sin, bias, gain, w_keyval, w_query, w_output, w_gate, w_up, cotangent
):
    n_dp, n_line = lax.axis_size("dp"), lax.axis_size("tensor")
    low = jnp.bfloat16
    rows, depth = tokens.shape
    length = bias.shape[0]
    wide = 2 * KVH * HD
    heads = w_query.shape[1] * n_line // HD

    def over(array, by_rows, by_columns):
        shape = (array.shape[0] * by_rows, array.shape[1] * by_columns)
        return jax.ShapeDtypeStruct(shape, array.dtype)

    anywhere = pl.BlockSpec(memory_space=pl.ANY)
    in_vmem = pl.BlockSpec(memory_space=pltpu.VMEM)
    shapes = [
        jax.ShapeDtypeStruct((rows, heads * HD), low),
        jax.ShapeDtypeStruct((length, wide), low),
        jax.ShapeDtypeStruct((rows, heads * HD), low),
        jax.ShapeDtypeStruct((heads // 2, 2, rows), jnp.float32),
        jax.ShapeDtypeStruct((rows, depth), jnp.float32),
        jax.ShapeDtypeStruct((rows, depth), low),
        over(w_keyval, n_dp, 1),
        over(w_query, n_dp, n_line),
        over(w_output, n_dp, n_line),
        over(w_gate, n_dp, 1),
        over(w_up, n_dp, 1),
        over(cotangent, n_line, 1),
    ]
    dma = pltpu.SemaphoreType.DMA
    return pl.pallas_call(
        attend_kernel,
        out_shape=shapes,
        in_specs=[in_vmem] * 6 + [anywhere] * 6,
        out_specs=[in_vmem, anywhere] + [in_vmem] * 4 + [anywhere] * 6,
        scratch_shapes=[
            pltpu.VMEM((depth, wide), low),
            pltpu.VMEM((2, depth, w_query.shape[1]), low),
            pltpu.VMEM((2, w_query.shape[1], depth), low),
            pltpu.VMEM((length, wide), low),
            pltpu.VMEM((length, PAIR), low),
            pltpu.VMEM((length, PAIR), low),
            pltpu.VMEM((HD, length), low),
            dma((6,)), dma((3, 2, 4)), dma((3, 4)), dma((11, 8)), dma((11, 8)),
            dma((2, 4)), dma((4,)), dma((2,)),
        ],
        compiler_params=pltpu.CompilerParams(
            collective_id=0, has_side_effects=True, vmem_limit_bytes=62 * 1024 * 1024
        ),
        name="attend_all",
    )(
        tokens, normed, cos, sin, bias, gain, w_keyval, w_query, w_output, w_gate, w_up, cotangent
    )


def add_rows(target, source, step=32):
    @pl.loop(0, target.shape[0] // step)
    def _(index):
        window = pl.ds(pl.multiple_of(index * step, step), step)
        target[window, :] = target[window, :] + source[window, :]


def over_rows(total_rows, act, step=32):
    @pl.loop(0, total_rows // step)
    def _(index):
        act(pl.ds(pl.multiple_of(index * step, step), step))


def enter_wide(dp, place):
    barrier = pltpu.get_barrier_semaphore()
    for bit in (1, 2, 4):
        pl.semaphore_signal(barrier, inc=1, device_id=(flip(dp, bit), place), device_id_type=MESH)
    for step in range(1, 4):
        pl.semaphore_signal(
            barrier, inc=1, device_id=(dp, (place + step) % 4), device_id_type=MESH
        )
    pl.semaphore_wait(barrier, 6)


def reach_back_kernel(
    gd_ref, gg_ref, gu_ref, branch_ref, fkv, fq, fo, dn_ref, residual_ref,
    cot_in, tokens_in, normed_in, query_in, heads_in, keyval_in, log_in, bias_in,
    cos_in, sin_in, gain_attn_in, gain_mlp_in,
    gd_out, gg_out, gu_out, go_out, gq_out, nar_out, layer_out, tokens_out,
    gd_core, gg_core, gu_core, go_core, gq_core, nar_core,
    gd_near, gg_near, gu_near, go_near, gq_near, nar_near,
    go_in, gq_in, nar_in, dkv_in, layer_in,
    gd_side, gg_side, gu_side, go_side, gq_side, nar_side,
    parts, held, early, stage, go_line, gq_line, nar_line, dkv_line, sums,
    d_residual, total, wide, d_branch, d_heads, dq_low, dkv_low, gains, weight, kv_weight,
    key_f, key_b, key_t, value_f, value_b, dk, dv,
    chain, units_made, go_made, gq_made, nar_made, tokens_made,
    cot_ref, tokens_ref, normed_ref, query_ref, heads_ref, keyval_ref, log_ref, bias_ref,
    cos_ref, sin_ref, gain_attn_ref, gain_mlp_ref,
    load_sem, fetch_sem, core_send, core_recv, p_send, p_recv, l_send, l_recv, in_sem, w_sem,
    c_send, c_recv, early_sem, leave_sem, enter_sem,
):
    dp, place = lax.axis_index("dp"), lax.axis_index("tensor")
    low = jnp.bfloat16
    rows, depth = d_branch.shape
    half = rows // 2
    arriving = [
        pltpu.make_async_copy(src, dst, enter_sem.at[number])
        for number, (src, dst) in enumerate(
            (
                (cot_in, cot_ref),
                (gain_mlp_in, gain_mlp_ref),
                (keyval_in, keyval_ref),
                (query_in, query_ref),
                (bias_in, bias_ref),
                (log_in, log_ref),
                (cos_in, cos_ref),
                (sin_in, sin_ref),
                (heads_in, heads_ref),
                (normed_in, normed_ref),
                (tokens_in, tokens_ref),
                (gain_attn_in, gain_attn_ref),
            )
        )
    ]
    dn_load = pltpu.make_async_copy(dn_ref, wide, in_sem.at[1])
    total_load = pltpu.make_async_copy(residual_ref, total, in_sem.at[2])
    kv_load = pltpu.make_async_copy(fkv, kv_weight, in_sem.at[3])
    for load in (dn_load, total_load):
        load.start()
    for load in arriving:
        load.start()
    kv_load.start()
    enter_wide(dp, place)
    x, y, core = flip(dp, 2), flip(dp, 4), flip(dp, 1)
    far = flip(x, 4)
    mine = (dp, x, y, far)
    theirs = tuple(flip(owner, 1) for owner in mine)
    grads = (gd_ref, gg_ref, gu_ref)
    outs = (gd_out, gg_out, gu_out, go_out, gq_out, nar_out)
    cores = (gd_core, gg_core, gu_core, go_core, gq_core, nar_core)
    sides = (gd_side, gg_side, gu_side, go_side, gq_side, nar_side)
    nears = (gd_near, gg_near, gu_near, go_near, gq_near, nar_near)
    lines = {3: go_line, 4: gq_line, 5: nar_line, 6: dkv_line}
    arrivals = {3: go_in, 4: gq_in, 5: nar_in, 6: dkv_in}
    front, back = pl.ds(0, half), pl.ds(half, half)
    ranks = dkv_line.shape[0]
    turns = (3, 1, 2, 0)

    def rows_of(owner):
        return pl.ds(pl.multiple_of(owner * rows, rows), rows)

    def remote(src, dst, send, recv, device):
        return pltpu.make_async_remote_copy(
            src_ref=src, dst_ref=dst, send_sem=send, recv_sem=recv,
            device_id=device, device_id_type=MESH,
        )

    def width_of(i):
        return cores[i].shape[2]

    sets = (0, 1, 0, 0, 1, 1)

    def part(i, k):
        return parts.at[sets[i], k, :, pl.ds(0, width_of(i))]

    def half_part(i, k, window):
        return parts.at[sets[i], k, window, pl.ds(0, width_of(i))]

    def held_part(slot, count, width):
        return held.at[slot, pl.ds(0, count), pl.ds(0, width)]

    def fetch(src, slot):
        return pltpu.make_async_copy(
            src, held_part(slot, src.shape[0], src.shape[1]), fetch_sem.at[slot]
        )

    def core_copy(i, k):
        if i < 3:
            src = grads[i].at[rows_of(theirs[k]), :]
        else:
            src = stage.at[turns.index(k), :, pl.ds(0, width_of(i))]
        return remote(
            src, cores[i].at[k], core_send.at[i, k], core_recv.at[i, k], (core, place)
        )

    def leave(src, dst, number):
        return pltpu.make_async_copy(src, dst, leave_sem.at[number])

    def own_load(i, k):
        return pltpu.make_async_copy(
            grads[i].at[rows_of(mine[k]), :], part(i, k), load_sem.at[i, k]
        )

    def plane_copy(i, lane):
        src, dst, device = (
            (half_part(i, 3, front), sides[i].at[0], y),
            (half_part(i, 3, back), sides[i].at[1], x),
            (half_part(i, 1, back), nears[i].at[0, back, :], x),
            (half_part(i, 2, front), nears[i].at[1, front, :], y),
            (half_part(i, 1, front), nears[i].at[0, front, :], x),
            (half_part(i, 2, back), nears[i].at[1, back, :], y),
        )[lane]
        return remote(src, dst, p_send.at[i, lane], p_recv.at[i, lane], (device, place))

    def plane_sent(i):
        for lane in range(6):
            plane_copy(i, lane).wait_send()

    def load_own(i):
        for k in turns:
            own_load(i, k).start()

    def core_fetch(i, n):
        src = cores[i].at[turns[n]]
        return pltpu.make_async_copy(
            src, early.at[n % 2, :, pl.ds(0, width_of(i))], early_sem.at[n % 2]
        )

    def core_begin(i, n):
        core_copy(i, turns[n]).wait_recv()
        core_fetch(i, n).start()

    def ready_core(i):
        core_begin(i, 0)
        core_begin(i, 1)

    def stage_core(i):
        for n, k in enumerate(turns):
            core_fetch(i, n).wait()
            if i < 3:
                own_load(i, k).wait()
            add_rows(part(i, k), early.at[n % 2, :, pl.ds(0, width_of(i))])
            for lane in ((), (2,), (3,), (0, 1))[k]:
                plane_copy(i, lane).start()
            if n + 2 < 4:
                core_begin(i, n + 2)

    def stage_side(i):
        for side, (k, window, lane) in enumerate(((1, front, 4), (2, back, 5))):
            plane_copy(i, side).wait_recv()
            add_rows(half_part(i, k, window), sides[i].at[side])
            plane_copy(i, lane).start()

    def stage_near(i):
        for side, lanes in enumerate(((2, 4), (3, 5))):
            for lane in lanes:
                plane_copy(i, lane).wait_recv()
            fetch(nears[i].at[side], side).start()
        for side in range(2):
            fetch(nears[i].at[side], side).wait()
        own, width, out = part(i, 0), width_of(i), outs[i]
        if 0 < i < 3:
            leave(units_made, out, i - 1).wait()

        @pl.loop(0, rows // 32)
        def _(index):
            window = pl.ds(pl.multiple_of(index * 32, 32), 32)
            sums = (
                own[window, :].astype(jnp.float32)
                + held[0, window, pl.ds(0, width)].astype(jnp.float32)
                + held[1, window, pl.ds(0, width)].astype(jnp.float32)
            )
            if i < 3:
                units_made[window, :] = sums
            elif i < 5:
                piece = width // ranks
                for rank in range(ranks):
                    lines[i][rank, window, :] = sums[:, rank * piece : (rank + 1) * piece].astype(
                        low
                    )
            else:
                per = rows // ranks
                lines[i][index * 32 // per, pl.ds(pl.multiple_of(index * 32 % per, 32), 32), :] = (
                    sums.astype(low)
                )

        if i < 3:
            leave(units_made, out, i).start()

    def line_copy(i, step):
        target = (place + step) % ranks
        return remote(
            lines[i].at[target], arrivals[i].at[place], l_send.at[i - 3, step], l_recv.at[i - 3, step],
            (dp, target),
        )

    def line_start(i):
        for step in range(1, ranks):
            line_copy(i, step).start()

    def line_last(i, add):
        def begin(step):
            line_copy(i, step).wait_recv()
            fetch(arrivals[i].at[(place + ranks - step) % ranks], step % 2).start()

        begin(1)
        for step in range(1, ranks):
            if step + 1 < ranks:
                begin(step + 1)
            fetch(arrivals[i].at[place], step % 2).wait()
            add(step % 2)

    def line_sent(i):
        for step in range(1, ranks):
            line_copy(i, step).wait_send()

    def chain_copy(rank, slot, step):
        return remote(
            chain.at[(step + 1) // 2], layer_in.at[slot], c_send.at[rank], c_recv.at[slot],
            (dp, place + step),
        )

    def chain_load(rank, step):
        copy = pltpu.make_async_copy(
            branch_ref.at[rank], chain.at[(step + 1) // 2], in_sem.at[0]
        )
        copy.start()
        copy.wait()

    def chain_fetch(slot):
        chain_copy(slot, slot, 1).wait_recv()
        copy = fetch(layer_in.at[slot], 0)
        copy.start()
        copy.wait()

    def chain_step(turn):
        down, up = place - ranks + 1 + turn, place + ranks - 1 - turn

        @pl.when(down >= 0)
        def _():
            @pl.when((down > 0) & (turn > 0))
            def _():
                chain_copy(down - 1, down - 1, -1).wait_send()

            chain_load(down, -1)

            @pl.when(place < ranks - 1)
            def _():
                chain_fetch(down)
                add_rows(chain.at[0], held.at[0])

            chain_copy(down, down, -1).start()

        @pl.when(up < ranks)
        def _():
            @pl.when((up < ranks - 1) & (turn > 0))
            def _():
                chain_copy(up + 1, up + 1, 1).wait_send()

            chain_load(up, 1)

            @pl.when(place > 0)
            def _():
                chain_fetch(up)
                add_rows(chain.at[1], held.at[0])

            chain_copy(up, ranks if turn == ranks - 2 else up, 1).start()

    def line_out(i):
        out = (go_made, gq_made, nar_made)[i - 3]
        count, width = out.shape

        def begin(window):
            out[window, :] = lines[i][place, window, :].astype(jnp.float32)

        def add(slot):
            def act(window):
                out[window, :] += held[slot, window, pl.ds(0, width)].astype(jnp.float32)

            over_rows(count, act)

        over_rows(count, begin)
        line_last(i, add)
        leave(out, outs[i], i).start()

    def norm_back(grad_ref, rows_ref, gain_ref, gain_row, act):
        gains[gain_row : gain_row + 1, :] = jnp.zeros((1, depth), jnp.float32)

        def block(window):
            values = rows_ref[window, :].astype(jnp.float32)
            inverse = lax.rsqrt(jnp.mean(values * values, axis=1, keepdims=True) + epsilon)
            unit = values * inverse
            grad = grad_ref[window, :]
            gains[gain_row : gain_row + 1, :] += jnp.sum(grad * unit, axis=0, keepdims=True)
            d_unit = grad * gain_ref[...]
            act(
                window,
                inverse * (d_unit - unit * jnp.mean(d_unit * unit, axis=1, keepdims=True)),
            )

        over_rows(rows, block, 64)

    def after_mlp(window, d_values):
        made = cot_ref[window, :].astype(jnp.float32) + d_values
        d_residual[window, :] = made
        d_branch[window, :] = made.astype(low)

    def after_attn(window, d_values):
        tokens_made[window, :] = (d_residual[window, :] + d_values).astype(low)

    def square_tile(left, right, owner):
        columns = pl.ds(pl.multiple_of(owner * rows, rows), rows)
        return dot_tn(left[:, columns], right[...]).astype(low)

    def narrow_tile(owner):
        columns = pl.ds(pl.multiple_of(owner * rows, rows), rows)
        keys = dot_tn(normed_ref[:, columns], dkv_low[...]).astype(low)
        line = lax.broadcasted_iota(jnp.int32, (PAIR, rows), 0)
        both = jnp.where(
            line == 0, gains[0:1, columns], jnp.where(line == 1, gains[1:2, columns], 0.0)
        )
        return jnp.concatenate([keys, both.T.astype(low)], axis=1)

    def send_theirs(i, tile):
        for n, k in enumerate(turns):
            stage[n, :, pl.ds(0, width_of(i))] = tile(theirs[k])
            core_copy(i, k).start()

    def theirs_sent(i):
        for k in turns:
            core_copy(i, k).wait_send()

    def keep_mine(i, tile):
        for k in turns:
            parts[sets[i], k, :, pl.ds(0, width_of(i))] = tile(mine[k])

    def go_tile(owner):
        return square_tile(d_branch, heads_ref, owner)

    def gq_tile(owner):
        return square_tile(normed_ref, dq_low, owner)

    size = weight.shape[1]
    steps = depth // size

    def weight_load(source, index):
        return pltpu.make_async_copy(
            source.at[pl.ds(index * size, size), :], weight.at[index % 2], w_sem.at[index % 2]
        )

    def make_d_heads():
        for index in range(steps):
            if index + 1 < steps:
                weight_load(fo, index + 1).start()
            weight_load(fo, index).wait()
            made = dot_nn(d_branch[:, index * size : (index + 1) * size], weight[index % 2])
            if index == 0:
                wide[...] = made
            elif index + 1 < steps:
                wide[...] += made
            else:
                d_heads[...] = (wide[...] + made).astype(low)

    def make_d_normed():
        for index in range(steps):
            if index + 1 < steps:
                weight_load(fq, index + 1).start()
            weight_load(fq, index).wait()
            wide[:, index * size : (index + 1) * size] = dot_nt(dq_low[...], weight[index % 2])

    def add_d_normed():
        for index in range(steps):
            wide[:, index * size : (index + 1) * size] += dot_nt(
                dkv_low[...], kv_weight[index * size : (index + 1) * size, :]
            )

    def attend_back(group):
        (key_f[...], key_b[...]), value_tile = head_tiles(keyval_ref, group)
        side = group % 2
        lane_side = slice(side * HD, (side + 1) * HD)
        tile_columns = slice(group // 2 * PAIR, (group // 2 + 1) * PAIR)
        key_t[...] = keyval_ref[:, tile_columns].T[lane_side, :]
        if side == 0:
            kept = front_lanes(value_tile)
            value_f[...], value_b[...] = kept, pltpu.roll(kept, HD, 1)
        else:
            kept = back_lanes(value_tile)
            value_f[...], value_b[...] = pltpu.roll(kept, HD, 1), kept
        dk[...] = jnp.zeros(dk.shape, jnp.float32)
        dv[...] = jnp.zeros(dv.shape, jnp.float32)
        pairs = query_ref.shape[1] // PAIR // KVH

        @pl.loop(0, pairs)
        def _(index):
            pair = group * pairs + index
            columns = pl.ds(pl.multiple_of(pair * PAIR, PAIR), PAIR)
            query, grad = query_ref[:, columns], d_heads[:, columns]
            logs = log_ref[pair]
            made = []
            for number, (key_ref, value_ref, keep) in enumerate(
                ((key_f, value_f, front_lanes), (key_b, value_b, back_lanes))
            ):
                probs = jnp.exp(
                    dot_nt(key_ref[...], query) + bias_ref[...] - logs[number : number + 1, :]
                )
                d_probs = dot_nt(value_ref[...], grad)
                row_dot = jnp.sum(probs * d_probs, axis=0, keepdims=True)
                d_scores = (probs * (d_probs - row_dot)).astype(low)
                dk[...] += dot_nn(d_scores, keep(query))
                dv[...] += dot_nn(probs.astype(low), keep(grad))
                made.append(dot_nn(key_t[...], d_scores))
            dq = jnp.concatenate(made, axis=0).T * (HD**-0.5)
            dq_low[:, columns] = turn(dq, cos_ref[...], -sin_ref[...]).astype(low)

        for sums, first in ((dk, 0), (dv, KVH * HD)):
            joined = (sums[...] + pltpu.roll(sums[...], HD, 1)).astype(low)
            columns = slice(first + tile_columns.start, first + tile_columns.stop)
            for rank in range(ranks):
                block = joined[rank * rows : (rank + 1) * rows, :]
                if side == 1:
                    block = front_lanes(dkv_line[rank, :, columns]) + back_lanes(block)
                dkv_line[rank, :, columns] = block

    def make_dkv():
        wide_columns = dkv_line.shape[2]

        def begin(window):
            sums[window, :] = dkv_line[place, window, :].astype(jnp.float32)

        def add(slot):
            def act(window):
                sums[window, :] += held[slot, window, pl.ds(0, wide_columns)].astype(jnp.float32)

            over_rows(rows, act)

        over_rows(rows, begin)
        line_last(6, add)
        for tile in range(wide_columns // PAIR):
            columns = slice(tile * PAIR, (tile + 1) * PAIR)
            made = sums[:, columns]
            if tile < KVH * HD // PAIR:
                made = turn(made, cos_ref[...], -sin_ref[...])
            dkv_low[:, columns] = made.astype(low)

    def finish_layer():
        for step in (-1, 1):

            @pl.when((place + step >= 0) & (place + step < ranks))
            def _():
                chain_copy(place + step, place, step).wait_send()

        chain_load(place, -1)

        def begin(window):
            total[window, :] += chain[0, window, :].astype(jnp.float32)

        def add(window):
            total[window, :] += held[0, window, :].astype(jnp.float32)

        def end(window):
            chain[1, window, :] = total[window, :].astype(low)

        over_rows(rows, begin)

        @pl.when(place < ranks - 1)
        def _():
            chain_fetch(place)
            over_rows(rows, add)

        @pl.when(place > 0)
        def _():
            chain_fetch(ranks)
            over_rows(rows, add)

        over_rows(rows, end)
        leave(chain.at[1], layer_out, 6).start()

    def send_core(i):
        for k in turns:
            core_copy(i, k).start()

    send_core(0)
    load_own(0)
    load_own(1)
    chain_step(0)
    dn_load.wait()
    total_load.wait()
    for load in arriving:
        load.wait()
    send_core(1)
    norm_back(wide, total, gain_mlp_ref, 1, after_mlp)
    ready_core(0)
    weight_load(fo, 0).start()
    stage_core(0)
    send_theirs(3, go_tile)
    ready_core(1)
    make_d_heads()
    stage_core(1)
    send_core(2)
    stage_side(0)
    chain_step(1)
    attend_back(0)
    stage_side(1)
    stage_near(0)
    plane_sent(0)
    ready_core(3)
    keep_mine(3, go_tile)
    stage_core(3)
    attend_back(1)
    stage_near(1)
    plane_sent(1)
    chain_step(2)
    attend_back(2)
    stage_side(3)
    attend_back(3)
    line_start(6)
    theirs_sent(3)
    send_theirs(4, gq_tile)
    ready_core(4)
    keep_mine(4, gq_tile)
    stage_core(4)
    stage_near(3)
    line_start(3)
    plane_sent(3)
    load_own(2)
    ready_core(2)
    weight_load(fq, 0).start()
    make_d_normed()
    kv_load.wait()
    make_dkv()
    add_d_normed()
    stage_core(2)
    stage_side(4)
    norm_back(wide, tokens_ref, gain_attn_ref, 0, after_attn)
    leave(tokens_made, tokens_out, 7).start()
    theirs_sent(4)
    send_theirs(5, narrow_tile)
    stage_near(4)
    line_start(4)
    plane_sent(4)
    ready_core(5)
    keep_mine(5, narrow_tile)
    stage_core(5)
    stage_side(2)
    line_out(3)
    stage_side(5)
    stage_near(5)
    line_start(5)
    finish_layer()
    stage_near(2)
    plane_sent(2)
    line_out(4)
    line_out(5)
    for src, dst, number in (
        (units_made, gu_out, 2),
        (go_made, go_out, 3),
        (gq_made, gq_out, 4),
        (nar_made, nar_out, 5),
        (chain.at[1], layer_out, 6),
        (tokens_made, tokens_out, 7),
    ):
        leave(src, dst, number).wait()
    plane_sent(5)
    theirs_sent(5)
    for i in range(3):
        for k in turns:
            core_copy(i, k).wait_send()
    for i in range(3, 7):
        line_sent(i)


def reach_back(grads, branch, full, d_normed, residual, others):
    low, wide = jnp.bfloat16, jnp.float32
    n_dp, ranks = lax.axis_size("dp"), lax.axis_size("tensor")
    units = grads[0].shape[1]
    rows, depth = residual.shape
    half = rows // 2
    square = depth // ranks
    few = depth // n_dp // ranks
    length, keyval = others[5].shape
    narrow = keyval + PAIR
    widths = [units] * 3 + [depth, depth, narrow]
    anywhere = pl.BlockSpec(memory_space=pl.ANY)
    in_vmem = pl.BlockSpec(memory_space=pltpu.VMEM)
    lined = [(rows, square), (rows, square), (few, narrow), (rows, keyval), (rows, depth)]
    out_shape = [jax.ShapeDtypeStruct((rows, units), wide)] * 3
    out_shape += [jax.ShapeDtypeStruct((rows, square), wide)] * 2
    out_shape += [jax.ShapeDtypeStruct((few, narrow), wide)]
    out_shape += [jax.ShapeDtypeStruct((rows, depth), low)] * 2
    out_shape += [jax.ShapeDtypeStruct((4, rows, w), low) for w in widths]
    out_shape += [jax.ShapeDtypeStruct((2, rows, w), low) for w in widths]
    out_shape += [jax.ShapeDtypeStruct((ranks,) + shape, low) for shape in lined[:4]]
    out_shape += [jax.ShapeDtypeStruct((ranks + 1, rows, depth), low)]
    dma = pltpu.SemaphoreType.DMA
    scratch = [pltpu.VMEM((2, half, w), low) for w in widths]
    scratch += [
        pltpu.VMEM((2, 4, rows, depth), low),
        pltpu.VMEM((2, rows, depth), low),
        pltpu.VMEM((2, rows, depth), low),
        pltpu.VMEM((4, rows, depth), low),
    ]
    scratch += [pltpu.VMEM((ranks,) + shape, low) for shape in lined[:4]]
    scratch += [pltpu.VMEM((rows, keyval), wide)]
    scratch += [pltpu.VMEM((rows, depth), wide)] * 3
    scratch += [pltpu.VMEM((rows, depth), low)] * 3
    scratch += [
        pltpu.VMEM((rows, keyval), low),
        pltpu.VMEM((8, depth), wide),
        pltpu.VMEM((2, square, depth), low),
        pltpu.VMEM((depth, keyval), low),
        pltpu.VMEM((length, PAIR), low),
        pltpu.VMEM((length, PAIR), low),
        pltpu.VMEM((HD, length), low),
        pltpu.VMEM((length, PAIR), low),
        pltpu.VMEM((length, PAIR), low),
        pltpu.VMEM((length, PAIR), wide),
        pltpu.VMEM((length, PAIR), wide),
        pltpu.VMEM((2, rows, depth), low),
        pltpu.VMEM((rows, units), wide),
        pltpu.VMEM((rows, square), wide),
        pltpu.VMEM((rows, square), wide),
        pltpu.VMEM((few, narrow), wide),
        pltpu.VMEM((rows, depth), low),
    ]
    scratch += [pltpu.VMEM(array.shape, array.dtype) for array in others]
    scratch += [
        dma((3, 4)), dma((2,)), dma((6, 4)), dma((6, 4)), dma((6, 6)), dma((6, 6)),
        dma((5, ranks)), dma((5, ranks)), dma((4,)), dma((2,)), dma((ranks,)), dma((ranks + 1,)),
        dma((2,)), dma((8,)), dma((12,)),
    ]
    results = pl.pallas_call(
        reach_back_kernel,
        out_shape=out_shape,
        in_specs=[anywhere] * 21,
        out_specs=[anywhere] * len(out_shape),
        scratch_shapes=scratch,
        compiler_params=pltpu.CompilerParams(
            collective_id=1, has_side_effects=True, vmem_limit_bytes=63 * 1024 * 1024
        ),
        name="reach_back",
    )(*grads, branch, *full, d_normed, residual, *others)
    return results[:8]


def by_tiles(total, size, act):
    full = total // size

    @pl.loop(0, full)
    def _(index):
        act(pl.ds(pl.multiple_of(index * size, size), size))

    if total % size:
        act(pl.ds(full * size, total % size))


def feed_forward_kernel(
    normed_ref, gate_w_ref, up_w_ref, down_w_ref, cot_ref,
    gg_out, gu_out, gd_out, branch_out, dn_out,
    wg, wu, wd, cot, normed, hid, dg, du, part, arrival, branch_stage, gate_stage, up_stage,
    load_sem, n_send, n_recv, l_send, l_recv, stage_sem, p_send, p_recv,
):
    dp, place = lax.axis_index("dp"), lax.axis_index("tensor")
    rows, depth = normed_ref.shape
    low = jnp.bfloat16
    order = line_order(place)
    cuts = l_send.shape[1]
    few = rows // cuts
    enter(dp, place)

    def remote(src, dst, send, recv, step):
        return pltpu.make_async_remote_copy(
            src_ref=src, dst_ref=dst, send_sem=send, recv_sem=recv,
            device_id=(dp, place + step), device_id_type=MESH,
        )

    def chunk(rank):
        return pl.ds(pl.multiple_of(rank * rows, rows), rows)

    def own_copy(step):
        return remote(
            normed_ref, normed.at[chunk(place), :], n_send.at[(step + 1) // 2, place],
            n_recv.at[place], step,
        )

    def pass_copy(rank, step):
        ref = normed.at[chunk(rank), :]
        return remote(ref, ref, n_send.at[(step + 1) // 2, rank], n_recv.at[rank], step)

    x, y, core = flip(dp, 2), flip(dp, 4), flip(dp, 1)
    far = flip(x, 4)
    shards = (down_w_ref,)
    weights = (wd,)
    depth_rows = down_w_ref.shape[0]
    half = depth_rows // 2

    def weight_rows(i, owner, part=None):
        first = owner * depth_rows if part is None else owner * depth_rows + part * half
        count = depth_rows if part is None else half
        return weights[i].at[pl.ds(pl.multiple_of(first, half), count), :]

    def plane_copy(i, lane):
        if lane < 2:
            src, dst, device = shards[i], weight_rows(i, dp), (x, y)[lane]
        elif lane < 4:
            src = dst = weight_rows(i, (x, y)[lane - 2], lane - 2)
            device = (y, x)[lane - 2]
        else:
            owner = (dp, x, y, far)[lane - 4]
            dst, device = weight_rows(i, owner), core
            src = shards[i] if lane == 4 else dst
        return pltpu.make_async_remote_copy(
            src_ref=src, dst_ref=dst, send_sem=p_send.at[i, lane], recv_sem=p_recv.at[i, lane],
            device_id=(device, place), device_id_type=MESH,
        )

    loads = [
        pltpu.make_async_copy(src, dst, load_sem.at[i])
        for i, (src, dst) in enumerate(
            (
                (normed_ref, normed.at[chunk(place), :]),
                (gate_w_ref, wg),
                (cot_ref, cot),
                (up_w_ref, wu),
                (down_w_ref, weight_rows(0, dp)),
            )
        )
    ]

    @pl.when(place < 3)
    def _():
        own_copy(1).start()

    @pl.when(place > 0)
    def _():
        own_copy(-1).start()

    for lane in (0, 1, 4):
        plane_copy(0, lane).start()
    for load in loads:
        load.start()

    def plane_second(i):
        for lane in range(2):
            plane_copy(i, lane).wait_recv()
            plane_copy(i, lane + 2).start()
            plane_copy(i, lane + 5).start()

    def plane_third(i):
        plane_copy(i, 2).wait_recv()
        plane_copy(i, 3).wait_recv()
        plane_copy(i, 7).start()

    def plane_ready(i):
        for lane in range(4, 8):
            plane_copy(i, lane).wait_recv()

    def sums_copy(rank, cut, slot, step):
        window = pl.ds(pl.multiple_of(cut * few, few), few)
        return remote(
            part.at[rank, window, :], arrival.at[slot, window, :], l_send.at[rank, cut],
            l_recv.at[slot, cut], step,
        )

    def branch_copy(rank):
        return pltpu.make_async_copy(branch_stage, branch_out.at[rank], stage_sem.at[0])

    def forward(rank):
        here = chunk(rank)

        def activate(columns):
            gate = dot_nn(normed[here, :], wg[:, columns])
            up = dot_nn(normed[here, :], wu[:, columns])
            sig = 1.0 / (1.0 + jnp.exp(-gate))
            silu = gate * sig
            hid[here, columns] = (silu * up).astype(low)
            dg[here, columns] = (up * sig * (1.0 + gate * (1.0 - sig))).astype(low)
            du[here, columns] = silu.astype(low)

        by_tiles(wg.shape[1], 256, activate)

    def backward(rank):
        here = chunk(rank)

        def meet(columns):
            d_hidden = dot_nn(cot[here, :], wd[:, columns])
            dg[here, columns] = (d_hidden * dg[here, columns].astype(jnp.float32)).astype(low)
            du[here, columns] = (d_hidden * du[here, columns].astype(jnp.float32)).astype(low)

        by_tiles(wg.shape[1], 256, meet)

        def pull(columns):
            part[rank, :, columns] = (
                dot_nt(dg[here, :], wg[columns, :]) + dot_nt(du[here, :], wu[columns, :])
            ).astype(low)

        by_tiles(depth, 512, pull)

    def branch(rank):
        def push(columns):
            branch_stage[:, columns] = dot_nt(hid[chunk(rank), :], wd[columns, :]).astype(low)

        by_tiles(depth, 512, push)
        branch_copy(rank).start()

    def take(rank):
        pass_copy(rank, 1).wait_recv()

        @pl.when((rank < place) & (place < 3))
        def _():
            pass_copy(rank, 1).start()

        @pl.when((rank > place) & (place > 0))
        def _():
            pass_copy(rank, -1).start()

    inside = (place == 1) | (place == 2)
    for load in loads:
        load.wait()
    forward(place)
    plane_second(0)
    take(order[0])

    @pl.when(inside)
    def _():
        take(order[1])

    plane_third(0)

    @pl.loop(0, jnp.where(inside, 2, 1))
    def _(index):
        forward(jnp.where(index == 0, order[0], order[1]))

    plane_ready(0)

    @pl.loop(0, 4)
    def _(turn):
        rank = jnp.where(
            turn == 0,
            order[0],
            jnp.where(
                turn == 1,
                jnp.where(inside, order[1], place),
                jnp.where(
                    turn == 2,
                    jnp.where(inside, order[2], order[1]),
                    jnp.where(inside, place, order[2]),
                ),
            ),
        )

        @pl.when((turn == 2) | ((turn == 3) & jnp.logical_not(inside)))
        def _():
            take(rank)
            forward(rank)

        backward(rank)

        @pl.when((turn != 1) & (place == 3))
        def _():
            for cut in range(cuts):
                sums_copy(rank, cut, rank, -1).start()

        @pl.when((turn != 1) & (place == 0))
        def _():
            slot = jnp.where(rank == 1, 4, rank)
            for cut in range(cuts):
                sums_copy(rank, cut, slot, 1).start()

    def gate_copy(tile):
        return pltpu.make_async_copy(gate_stage, gg_out.at[tile, :], stage_sem.at[1])

    def up_copy(tile):
        return pltpu.make_async_copy(up_stage, gu_out.at[tile, :], stage_sem.at[2])

    def down_copy(tile):
        return pltpu.make_async_copy(gate_stage, gd_out.at[tile, :], stage_sem.at[1])

    size = gate_stage.shape[0]
    tiles = depth // size

    def gate_up_tile(index):
        tile = pl.ds(pl.multiple_of(index * size, size), size)
        left = normed[:, tile]
        gate_grad = dot_tn(left, dg[...]).astype(low)

        @pl.when(index > 0)
        def _():
            gate_copy(tile).wait()
            up_copy(tile).wait()

        gate_stage[...] = gate_grad
        gate_copy(tile).start()
        up_stage[...] = dot_tn(left, du[...]).astype(low)
        up_copy(tile).start()

    def down_tile(index):
        tile = pl.ds(pl.multiple_of(index * size, size), size)
        down_grad = dot_tn(cot[:, tile], hid[...]).astype(low)

        @pl.when(index > 0)
        def _():
            down_copy(tile).wait()

        gate_stage[...] = down_grad
        down_copy(tile).start()

    last = pl.ds(depth - size, size)

    def relay(rank, slot, step, cut):
        sums_copy(rank, cut, rank, step).wait_recv()
        window = pl.ds(pl.multiple_of(cut * few, few), few)
        part[rank, window, :] = part[rank, window, :] + arrival[rank, window, :]
        sums_copy(rank, cut, slot, step).start()

    outward = 3 - 2 * place

    @pl.loop(0, cuts)
    def _(cut):
        @pl.when(inside)
        def _():
            relay(3 - place, 4 - 3 * (place - 1), outward, cut)

        @pl.loop(0, tiles // cuts)
        def _(index):
            gate_up_tile(cut * (tiles // cuts) + index)

    gate_copy(last).wait()
    up_copy(last).wait()

    @pl.loop(0, cuts)
    def _(cut):
        @pl.when(inside)
        def _():
            relay(6 - 3 * place, 6 - 3 * place, outward, cut)
            relay(3 * (place - 1), 4 * (place - 1), -outward, cut)

        @pl.loop(0, tiles // cuts)
        def _(index):
            down_tile(cut * (tiles // cuts) + index)

        @pl.when(cut > 0)
        def _():
            branch_copy(cut).wait()

        branch(cut)

    down_copy(last).wait()
    branch_copy(0).wait()

    for cut in range(cuts):
        window = pl.ds(cut * few, few)
        dn_out[window, :] = part[place, window, :].astype(jnp.float32)

        @pl.when(place < 3)
        def _():
            sums_copy(place, cut, place, 1).wait_recv()
            dn_out[window, :] += arrival[place, window, :].astype(jnp.float32)

        @pl.when(place > 0)
        def _():
            sums_copy(place, cut, 4, 1).wait_recv()
            dn_out[window, :] += arrival[4, window, :].astype(jnp.float32)

    @pl.when(place < 3)
    def _():
        own_copy(1).wait_send()

    @pl.when(place > 0)
    def _():
        own_copy(-1).wait_send()

    for rank in range(4):

        @pl.when((rank < place) & (place < 3))
        def _():
            pass_copy(rank, 1).wait_send()

        @pl.when((rank > place) & (place > 0))
        def _():
            pass_copy(rank, -1).wait_send()

        @pl.when(rank != place)
        def _():
            for cut in range(cuts):
                sums_copy(rank, cut, rank, 1).wait_send()

    for lane in range(8):
        plane_copy(0, lane).wait_send()


def feed_forward(normed, w_gate, w_up, w_down, cotangent):
    low = jnp.bfloat16
    rows, depth = normed.shape
    length = cotangent.shape[0]
    units = w_gate.shape[1]
    ranks = length // rows
    cuts = 4
    anywhere = pl.BlockSpec(memory_space=pl.ANY)
    in_vmem = pl.BlockSpec(memory_space=pltpu.VMEM)
    dma = pltpu.SemaphoreType.DMA
    flops = 9 * 2 * length * depth * units
    return pl.pallas_call(
        feed_forward_kernel,
        out_shape=[jax.ShapeDtypeStruct((depth, units), low)] * 3
        + [
            jax.ShapeDtypeStruct((ranks, rows, depth), low),
            jax.ShapeDtypeStruct((rows, depth), jnp.float32),
        ],
        in_specs=[anywhere] * 5,
        out_specs=[anywhere] * 4 + [in_vmem],
        scratch_shapes=[pltpu.VMEM((depth, units), low)] * 3
        + [pltpu.VMEM((length, depth), low)] * 2
        + [pltpu.VMEM((length, units), low)] * 3
        + [
            pltpu.VMEM((ranks, rows, depth), low),
            pltpu.VMEM((ranks + 1, rows, depth), low),
            pltpu.VMEM((rows, depth), low),
            pltpu.VMEM((256, units), low),
            pltpu.VMEM((256, units), low),
            dma((5,)), dma((2, ranks)), dma((ranks,)), dma((ranks, cuts)), dma((ranks + 1, cuts)),
            dma((3,)), dma((1, 8)), dma((1, 8)),
        ],
        compiler_params=pltpu.CompilerParams(
            collective_id=2, has_side_effects=True, vmem_limit_bytes=62 * 1024 * 1024
        ),
        cost_estimate=pl.CostEstimate(flops=flops, bytes_accessed=60 << 20, transcendentals=0),
        name="feed_forward",
    )(normed, w_gate, w_up, w_down, cotangent)


def local(
    tokens,
    segments,
    gain_attn,
    w_query,
    w_keyval,
    w_output,
    gain_mlp,
    w_gate,
    w_up,
    w_down,
    cotangent,
):
    tensor_rank = lax.axis_index("tensor")
    length = segments.shape[0]
    rows = tokens.shape[0]
    both = ("dp", "tensor")
    low = jnp.bfloat16

    def gather(array, axes, axis=0):
        return lax.all_gather(array, axes, axis=axis, tiled=True)

    def scatter(array, axes, axis=0):
        return lax.psum_scatter(array, axes, scatter_dimension=axis, tiled=True)

    by_kernels = (lax.axis_size("dp"), lax.axis_size("tensor")) == (8, 4)
    places = doc_positions(segments)
    my_places = lax.dynamic_slice_in_dim(places, tensor_rank * rows, rows, 0)
    my_segments = lax.dynamic_slice_in_dim(segments, tensor_rank * rows, rows, 0)
    cosine, sine_table = rope_tables(my_places, HD)
    order = jnp.arange(length, dtype=jnp.int32)
    allowed = (order[:, None] <= tensor_rank * rows + order[None, :rows]) & (
        segments[:, None] == my_segments[None, :]
    )
    bias = jnp.where(allowed, 0.0, masked).astype(jnp.float32)

    token_rows = tokens.astype(jnp.float32)
    normed_attn, unit_attn, inverse_attn = norm_forward(token_rows, gain_attn)
    normed_attn = normed_attn.astype(low)
    wide = KVH * HD
    if by_kernels:
        cos_tile = jnp.tile(cosine, (1, 4))
        sin_tile = jnp.tile(jnp.concatenate([-sine_table, sine_table], axis=1), (1, 2))
        (
            query, keyval, heads_low, log_sum, residual, normed_mlp,
            full_keyval, full_query, full_output, full_gate, full_up, piece,
        ) = attend_all(
            tokens, normed_attn, cos_tile, sin_tile, bias, gain_mlp[None, :],
            w_keyval, w_query, w_output, w_gate, w_up, cotangent,
        )
    else:
        full_keyval = gather(w_keyval, "dp")
        keyval_pre = dot_nn(normed_attn, full_keyval)
        key_low = rotate(keyval_pre[:, :wide], cosine, sine_table).astype(low)
        keyval = jnp.concatenate([key_low, keyval_pre[:, wide:].astype(low)], axis=1)
        keyval = gather(keyval, "tensor")
        full_query = gather(gather(w_query, "tensor", 1), "dp")
        query = rotate(dot_nn(normed_attn, full_query), cosine, sine_table) * (HD**-0.5)
        query = query.astype(low)
    if by_kernels:
        grad_gate, grad_up, grad_down, branch, d_normed_mlp = feed_forward(
            normed_mlp, full_gate, full_up, w_down, piece
        )
        to_down, to_gate, to_up, to_output, to_query, to_narrow, layer_out, grad_tokens = (
            reach_back(
                (grad_down, grad_gate, grad_up),
                branch,
                (full_keyval, full_query, full_output),
                d_normed_mlp,
                residual,
                (
                    cotangent, tokens, normed_attn, query, heads_low, keyval, log_sum, bias,
                    cos_tile, sin_tile, gain_attn[None, :], gain_mlp[None, :],
                ),
            )
        )
        wide = 2 * KVH * HD
        return (
            layer_out,
            grad_tokens,
            to_narrow[:, wide],
            to_query,
            to_narrow[:, :wide],
            to_output,
            to_narrow[:, wide + 1],
            to_gate,
            to_up,
            to_down,
        )

    key_heads, value_heads = by_head(keyval[:, :wide]), by_head(keyval[:, wide:])
    blank = jnp.zeros_like(key_heads)
    key_f = jnp.concatenate([key_heads, blank], axis=2)
    key_b = jnp.concatenate([blank, key_heads], axis=2)
    value_f = jnp.concatenate([value_heads, blank], axis=2)
    value_b = jnp.concatenate([blank, value_heads], axis=2)
    key_t = key_heads.transpose(0, 2, 1)
    value_t = value_heads.transpose(0, 2, 1)
    heads_low, log_sum = attend_forward(query, key_f, key_b, value_t, bias)
    full_output = gather(gather(w_output, "tensor", 1), "dp")
    residual = token_rows + dot_nt(heads_low, full_output)
    full_gate, full_up = gather(w_gate, "dp"), gather(w_up, "dp")
    full_down = gather(w_down, "dp")
    piece = gather(cotangent, "tensor")
    normed_mlp_rows, unit_mlp, inverse_mlp = norm_forward(residual, gain_mlp)
    normed_mlp = normed_mlp_rows.astype(low)
    gathered_mlp = gather(normed_mlp, "tensor")
    gate_act = dot_nn(gathered_mlp, full_gate)
    up_act = dot_nn(gathered_mlp, full_up)
    sigmoid_gate = jax.nn.sigmoid(gate_act)
    silu_gate = gate_act * sigmoid_gate
    hidden_low = (silu_gate * up_act).astype(low)
    d_hidden = dot_nn(piece, full_down)
    d_gate = (d_hidden * up_act * sigmoid_gate * (1.0 + gate_act * (1.0 - sigmoid_gate))).astype(low)
    d_up = (d_hidden * silu_gate).astype(low)
    d_normed_mlp = scatter(
        (dot_nt(d_gate, full_gate) + dot_nt(d_up, full_up)).astype(low), "tensor"
    ).astype(jnp.float32)
    branch = dot_nt(hidden_low, full_down).astype(low)
    grad_down = dot_tn(piece, hidden_low)
    grad_gate = dot_tn(gathered_mlp, d_gate)
    grad_up = dot_tn(gathered_mlp, d_up)
    d_norm_mlp, gain_mlp_part = norm_backward(d_normed_mlp, unit_mlp, inverse_mlp, gain_mlp)
    d_residual = cotangent.astype(jnp.float32) + d_norm_mlp

    d_branch = d_residual.astype(low)
    grad_output = dot_tn(d_branch, heads_low)
    d_heads = dot_nn(d_branch, full_output).astype(low)
    d_queries, d_keys, d_values = attend_backward(
        query, d_heads, key_f, key_b, key_t, value_f, value_b, bias, log_sum
    )

    def flat(parts):
        joined = parts[:, :, :HD] + parts[:, :, HD:]
        return joined.transpose(1, 0, 2).reshape(length, wide)

    d_keyval = scatter(
        jnp.concatenate([flat(d_keys), flat(d_values)], axis=1).astype(low), "tensor"
    ).astype(jnp.float32)
    dq_low = rotate(d_queries, cosine, -sine_table).astype(low)
    dkv_low = jnp.concatenate(
        [rotate(d_keyval[:, :wide], cosine, -sine_table), d_keyval[:, wide:]], axis=1
    ).astype(low)
    grad_query = dot_tn(normed_attn, dq_low)
    grad_keyval = dot_tn(normed_attn, dkv_low)
    d_normed_attn = dot_nt(dq_low, full_query) + dot_nt(dkv_low, full_keyval)
    d_norm_attn, gain_attn_part = norm_backward(d_normed_attn, unit_attn, inverse_attn, gain_attn)
    grad_tokens = (d_residual + d_norm_attn).astype(low)

    layer_rows = residual + scatter(branch, "tensor").astype(jnp.float32)

    def shares(grad):
        return scatter(grad.astype(low), "dp").astype(jnp.float32)

    def square_shares(grad):
        return scatter(scatter(grad.astype(low), "dp"), "tensor", 1).astype(jnp.float32)

    gains = scatter(
        jnp.stack([gain_attn_part, gain_mlp_part]).reshape(2, -1, rows_of_gain(gain_attn)), both, 1
    )
    return (
        layer_rows.astype(low),
        grad_tokens,
        gains[0, 0],
        square_shares(grad_query),
        scatter(grad_keyval.astype(low), both).astype(jnp.float32),
        square_shares(grad_output),
        gains[1, 0],
        shares(grad_gate),
        shares(grad_up),
        shares(grad_down),
    )


def rows_of_gain(gain):
    return gain.shape[0] // (lax.axis_size("dp") * lax.axis_size("tensor"))


def solution(mesh):
    return jax.shard_map(
        local,
        mesh=mesh,
        in_specs=(
            P(("dp", "tensor"), None),
            P("dp"),
            P(),
            P("dp", "tensor"),
            P("dp", None),
            P("dp", "tensor"),
            P(),
            P("dp", "tensor"),
            P("dp", "tensor"),
            P("dp", "tensor"),
            P(("dp", "tensor"), None),
        ),
        out_specs=(
            P(("dp", "tensor"), None),
            P(("dp", "tensor"), None),
            P(("dp", "tensor")),
            P("dp", "tensor"),
            P(("dp", "tensor"), None),
            P("dp", "tensor"),
            P(("dp", "tensor")),
            P("dp", "tensor"),
            P("dp", "tensor"),
            P("dp", "tensor"),
        ),
        check_vma=False,
    )
```

```python
import functools

import jax
import jax.numpy as jnp
from jax import lax
from jax.experimental import pallas as pl
from jax.experimental.pallas import tpu as pltpu
from jax.sharding import PartitionSpec as P

KVH = 4
HD = 64
PAIR = 2 * HD

epsilon = 1e-05
rope_base = 10000.0
masked = -1e30


def doc_positions(seg_row):
    length = seg_row.shape[0]
    places = jnp.arange(length, dtype=jnp.int32)
    change = jnp.concatenate([jnp.ones((1,), jnp.bool_), seg_row[1:] != seg_row[:-1]])
    starts = lax.cummax(jnp.where(change, places, 0), axis=0)
    return places - starts


def rope_tables(places, width):
    half_width = width // 2
    frequency = rope_base ** (-(2.0 * jnp.arange(half_width).astype(jnp.float32)) / width)
    angles = places.astype(jnp.float32)[:, None] * frequency[None, :]
    return (jnp.cos(angles), jnp.sin(angles))


def rotate(values, cosine, sine_table):
    rows, width = values.shape
    heads = values.reshape(rows, width // HD, HD)
    half_width = HD // 2
    front_half = heads[..., :half_width]
    back_half = heads[..., half_width:]
    cos_rows = cosine[:, None, :]
    sin_rows = sine_table[:, None, :]
    turned = jnp.concatenate(
        [
            front_half * cos_rows - back_half * sin_rows,
            back_half * cos_rows + front_half * sin_rows,
        ],
        axis=-1,
    )
    return turned.reshape(rows, width)


def norm_forward(values, gain_vec):
    inverse = lax.rsqrt(jnp.mean(values * values, axis=-1, keepdims=True) + epsilon)
    unit_rows = values * inverse
    return (unit_rows * gain_vec, unit_rows, inverse)


def norm_backward(d_normed, unit_rows, inverse, gain_vec):
    gain_part = jnp.sum(d_normed * unit_rows, axis=0)
    d_unit = d_normed * gain_vec
    d_values = inverse * (d_unit - unit_rows * jnp.mean(d_unit * unit_rows, axis=-1, keepdims=True))
    return (d_values, gain_part)


def dot_nn(left, right):
    return jnp.dot(left, right, preferred_element_type=jnp.float32)


def dot_nt(left, right):
    return lax.dot_general(
        left, right, (((1,), (1,)), ((), ())), preferred_element_type=jnp.float32
    )


def dot_tn(left, right):
    return lax.dot_general(
        left, right, (((0,), (0,)), ((), ())), preferred_element_type=jnp.float32
    )


def front_lanes(tile):
    lane = lax.broadcasted_iota(jnp.int32, tile.shape, 1)
    return jnp.where(lane < HD, tile, jnp.zeros_like(tile))


def back_lanes(tile):
    lane = lax.broadcasted_iota(jnp.int32, tile.shape, 1)
    return jnp.where(lane < HD, jnp.zeros_like(tile), tile)


def attend_forward_kernel(query_ref, front_ref, back_ref, value_t_ref, bias_ref, out_ref, log_ref):
    pairs = query_ref.shape[1] // PAIR
    value_t = value_t_ref[0]
    for pair in range(pairs):
        query = query_ref[:, pair * PAIR : (pair + 1) * PAIR]
        outs = []
        for side, key_ref in enumerate((front_ref, back_ref)):
            scores = dot_nt(key_ref[0], query) + bias_ref[...]
            top = jnp.max(scores, axis=0, keepdims=True)
            expo = jnp.exp(scores - top)
            total = jnp.sum(expo, axis=0, keepdims=True)
            outs.append(dot_nn(value_t, expo.astype(jnp.bfloat16)) / total)
            log_ref[0, pl.ds(pair * 2 + side, 1), :] = top + jnp.log(total)
        out = jnp.concatenate(outs, axis=0).T
        out_ref[:, pair * PAIR : (pair + 1) * PAIR] = out.astype(jnp.bfloat16)


def attend_backward_kernel(
    query_ref,
    grad_ref,
    kf_ref,
    kb_ref,
    kt_ref,
    vf_ref,
    vb_ref,
    bias_ref,
    log_ref,
    dq_ref,
    dk_ref,
    dv_ref,
):
    pairs = query_ref.shape[1] // PAIR
    key_t = kt_ref[0]
    dk_ref[0] = jnp.zeros(dk_ref.shape[1:], jnp.float32)
    dv_ref[0] = jnp.zeros(dv_ref.shape[1:], jnp.float32)
    for pair in range(pairs):
        columns = slice(pair * PAIR, (pair + 1) * PAIR)
        query = query_ref[:, columns]
        grad = grad_ref[:, columns]
        outs = []
        for side, (key_ref, value_ref, keep) in enumerate(
            ((kf_ref, vf_ref, front_lanes), (kb_ref, vb_ref, back_lanes))
        ):
            log_sum = log_ref[0, pl.ds(pair * 2 + side, 1), :]
            probs = jnp.exp(dot_nt(key_ref[0], query) + bias_ref[...] - log_sum)
            d_probs = dot_nt(value_ref[0], grad)
            row_dot = jnp.sum(probs * d_probs, axis=0, keepdims=True)
            d_scores = (probs * (d_probs - row_dot)).astype(jnp.bfloat16)
            dk_ref[0] += dot_nn(d_scores, keep(query))
            dv_ref[0] += dot_nn(probs.astype(jnp.bfloat16), keep(grad))
            outs.append(dot_nn(key_t, d_scores))
        dq_ref[:, columns] = jnp.concatenate(outs, axis=0).T * (HD**-0.5)


def whole_group(rows, width):
    return pl.BlockSpec((1, rows, width), lambda g: (g, 0, 0))


def columns_of(rows, width):
    return pl.BlockSpec((rows, width), lambda g: (0, g))


def attend_forward(query, key_f, key_b, value_t, bias):
    rows, width = query.shape
    length = bias.shape[0]
    group = width // KVH
    return pl.pallas_call(
        attend_forward_kernel,
        grid=(KVH,),
        in_specs=[
            columns_of(rows, group),
            whole_group(length, PAIR),
            whole_group(length, PAIR),
            whole_group(HD, length),
            pl.BlockSpec((length, rows), lambda g: (0, 0)),
        ],
        out_specs=[columns_of(rows, group), whole_group(group // HD, rows)],
        out_shape=[
            jax.ShapeDtypeStruct((rows, width), jnp.bfloat16),
            jax.ShapeDtypeStruct((KVH, group // HD, rows), jnp.float32),
        ],
        compiler_params=pltpu.CompilerParams(vmem_limit_bytes=48 * 1024 * 1024),
        name="attend_forward",
    )(query, key_f, key_b, value_t, bias)


def attend_backward(query, grad, key_f, key_b, key_t, value_f, value_b, bias, log_sum):
    rows, width = query.shape
    length = bias.shape[0]
    group = width // KVH
    tall = whole_group(length, PAIR)
    return pl.pallas_call(
        attend_backward_kernel,
        grid=(KVH,),
        in_specs=[
            columns_of(rows, group),
            columns_of(rows, group),
            tall,
            tall,
            whole_group(HD, length),
            tall,
            tall,
            pl.BlockSpec((length, rows), lambda g: (0, 0)),
            whole_group(group // HD, rows),
        ],
        out_specs=[columns_of(rows, group), tall, tall],
        out_shape=[
            jax.ShapeDtypeStruct((rows, width), jnp.float32),
            jax.ShapeDtypeStruct((KVH, length, PAIR), jnp.float32),
            jax.ShapeDtypeStruct((KVH, length, PAIR), jnp.float32),
        ],
        compiler_params=pltpu.CompilerParams(vmem_limit_bytes=48 * 1024 * 1024),
        name="attend_backward",
    )(query, grad, key_f, key_b, key_t, value_f, value_b, bias, log_sum)


def by_head(matrix):
    rows = matrix.shape[0]
    return matrix.reshape(rows, KVH, HD).transpose(1, 0, 2)


MESH = pl.DeviceIdType.MESH


def flip(index, bit):
    return index + bit - 2 * bit * ((index // bit) % 2)


def line_order(place):
    nearest = place - 1 + 2 * (1 - (place + 3) // 4)
    farthest = 3 - 3 * (place // 2)
    return (nearest, 6 - place - nearest - farthest, farthest)


def enter(dp, place):
    barrier = pltpu.get_barrier_semaphore()
    for bit in (1, 2, 4):
        pl.semaphore_signal(barrier, inc=1, device_id=(flip(dp, bit), place), device_id_type=MESH)
    for step in (-1, 1):
        there = (place + step >= 0) & (place + step < 4)

        @pl.when(there)
        def _():
            pl.semaphore_signal(
                barrier, inc=1, device_id=(dp, place + step), device_id_type=MESH
            )

    ends = 1 - ((place + 3) // 4) + place // 3
    pl.semaphore_wait(barrier, 5 - ends)


def turn(tile, cos, sin):
    lane = lax.broadcasted_iota(jnp.int32, tile.shape, 1)
    swapped = jnp.where(
        lane % HD < HD // 2, pltpu.roll(tile, PAIR - HD // 2, 1), pltpu.roll(tile, HD // 2, 1)
    )
    return tile * cos + swapped * sin


def head_tiles(keyval, group):
    columns = slice(group // 2 * PAIR, (group // 2 + 1) * PAIR)
    tile = keyval[:, columns]
    values = slice(KVH * HD + columns.start, KVH * HD + columns.stop)
    if group % 2 == 0:
        front = front_lanes(tile)
        keys = (front, pltpu.roll(front, HD, 1))
    else:
        back = back_lanes(tile)
        keys = (pltpu.roll(back, HD, 1), back)
    return keys, keyval[:, values]


def attend_kernel(
    tokens_in, gain_attn_in, cos_in, sin_in, bias_in, gain_in,
    kv_ref, q_ref, o_ref, g_ref, u_ref, c_ref,
    normed_to, query_to, keyval_out, heads_to, log_to, residual_to, mlp_to,
    fkv, fq, fo, fg, fu, fc,
    tokens_ref, gain_attn_ref, cos_ref, sin_ref, bias_ref, gain_ref,
    normed_ref, query_out, heads_out, log_out, residual_out, mlp_out,
    kv_weight, weight, wide_weight, keyval, key_f, key_b, value_t,
    own_sem, z_send, z_recv, p_send, p_recv, k_send, k_recv, w_sem, enter_sem, leave_sem,
):
    dp, place = lax.axis_index("dp"), lax.axis_index("tensor")
    rows = kv_ref.shape[0]
    half = rows // 2
    width = q_ref.shape[1]
    order = line_order(place)
    arriving = [
        pltpu.make_async_copy(src, dst, enter_sem.at[number])
        for number, (src, dst) in enumerate(
            (
                (tokens_in, tokens_ref),
                (gain_attn_in, gain_attn_ref),
                (cos_in, cos_ref),
                (sin_in, sin_ref),
                (bias_in, bias_ref),
                (gain_in, gain_ref),
            )
        )
    ]
    leaving = [
        pltpu.make_async_copy(src, dst, leave_sem.at[number])
        for number, (src, dst) in enumerate(
            (
                (normed_ref, normed_to),
                (query_out, query_to),
                (heads_out, heads_to),
                (log_out, log_to),
                (residual_out, residual_to),
                (mlp_out, mlp_to),
            )
        )
    ]
    for copy in arriving:
        copy.start()
    enter(dp, place)

    def rows_of(owner):
        return pl.ds(pl.multiple_of(owner * rows, rows), rows)

    def columns_of_rank(rank):
        return pl.ds(pl.multiple_of(rank * width, width), width)

    def remote(src, dst, send, recv, device):
        return pltpu.make_async_remote_copy(
            src_ref=src, dst_ref=dst, send_sem=send, recv_sem=recv,
            device_id=device, device_id_type=MESH,
        )

    own = [
        (kv_ref, fkv.at[rows_of(dp), :]),
        (q_ref, fq.at[rows_of(dp), columns_of_rank(place)]),
        (o_ref, fo.at[rows_of(dp), columns_of_rank(place)]),
        (g_ref, fg.at[rows_of(dp), :]),
        (u_ref, fu.at[rows_of(dp), :]),
        (c_ref, fc.at[rows_of(place), :]),
    ]
    own_copies = [
        pltpu.make_async_copy(src, dst, own_sem.at[i]) for i, (src, dst) in enumerate(own)
    ]
    for copy in own_copies:
        copy.start()

    def line_block(which, rank):
        if which == 2:
            return fc.at[rows_of(rank), :]
        return (fq, fo)[which].at[rows_of(dp), columns_of_rank(rank)]

    def line_copy(which, rank, step):
        src = (q_ref, o_ref, c_ref)[which] if rank is place else line_block(which, rank)
        side = 0 if step < 0 else 1
        return remote(
            src, line_block(which, rank), z_send.at[which, side, rank], z_recv.at[which, rank],
            (dp, place + step),
        )

    def line_send(which, rank, act):
        @pl.when((rank <= place) & (place < 3))
        def _():
            act(line_copy(which, rank, 1))

        @pl.when((rank >= place) & (place > 0))
        def _():
            act(line_copy(which, rank, -1))

    def start(copy):
        copy.start()

    def wait_send(copy):
        copy.wait_send()

    x, y, core = flip(dp, 2), flip(dp, 4), flip(dp, 1)
    far = flip(x, 4)

    blocks = [("kv", None), ("q", place), ("g", None)] + [("q", rank) for rank in order]
    blocks += [("o", place)] + [("o", rank) for rank in order] + [("u", None)]

    def block(index, owner, part=None):
        name, rank = blocks[index]
        ref = {"kv": fkv, "q": fq, "o": fo, "g": fg, "u": fu}[name]
        first = owner * rows if part is None else owner * rows + part * half
        size = rows if part is None else half
        window = pl.ds(pl.multiple_of(first, half), size)
        if rank is None:
            return ref.at[window, :]
        return ref.at[window, columns_of_rank(rank)]

    def own_block(index):
        name, rank = blocks[index]
        if rank is None or rank is place:
            return {"kv": kv_ref, "q": q_ref, "o": o_ref, "g": g_ref, "u": u_ref}[name]
        return block(index, dp)

    def plane_copy(index, lane):
        send, recv = p_send.at[index, lane], p_recv.at[index, lane]
        if lane == 0:
            return remote(own_block(index), block(index, dp), send, recv, (x, place))
        if lane == 1:
            return remote(own_block(index), block(index, dp), send, recv, (y, place))
        if lane == 2:
            return remote(block(index, x, 0), block(index, x, 0), send, recv, (y, place))
        if lane == 3:
            return remote(block(index, y, 1), block(index, y, 1), send, recv, (x, place))
        owner = (dp, x, y, far)[lane - 4]
        src = own_block(index) if lane == 4 else block(index, owner)
        return remote(src, block(index, owner), send, recv, (core, place))

    def plane_first(index):
        plane_copy(index, 0).start()
        plane_copy(index, 1).start()
        plane_copy(index, 4).start()

    def plane_second(index):
        plane_copy(index, 0).wait_recv()
        plane_copy(index, 2).start()
        plane_copy(index, 5).start()
        plane_copy(index, 1).wait_recv()
        plane_copy(index, 3).start()
        plane_copy(index, 6).start()

    def plane_third(index):
        plane_copy(index, 2).wait_recv()
        plane_copy(index, 3).wait_recv()
        plane_copy(index, 7).start()

    def plane_ready(index):
        for lane in range(4, 8):
            plane_copy(index, lane).wait_recv()

    def plane_sent(index):
        for lane in range(8):
            plane_copy(index, lane).wait_send()

    def keyval_block(rank):
        return keyval.at[rows_of(rank), :]

    def keyval_copy(rank, step):
        side = 0 if step < 0 else 1
        return remote(
            keyval_block(rank), keyval_block(rank), k_send.at[side, rank], k_recv.at[rank],
            (dp, place + step),
        )

    def keyval_send(rank, act):
        @pl.when((rank <= place) & (place < 3))
        def _():
            act(keyval_copy(rank, 1))

        @pl.when((rank >= place) & (place > 0))
        def _():
            act(keyval_copy(rank, -1))

    def keyval_take(step):
        keyval_copy(order[step], 1).wait_recv()
        keyval_send(order[step], start)

    low = jnp.bfloat16
    wide = KVH * HD

    def make_normed():
        for copy in arriving:
            copy.wait()

        @pl.loop(0, rows // 64)
        def _(index):
            window = pl.ds(pl.multiple_of(index * 64, 64), 64)
            values = tokens_ref[window, :].astype(jnp.float32)
            inverse = lax.rsqrt(jnp.mean(values * values, axis=1, keepdims=True) + epsilon)
            normed_ref[window, :] = (values * inverse * gain_attn_ref[...]).astype(low)

        leaving[0].start()

    def make_keyval():
        load = pltpu.make_async_copy(fkv, kv_weight, w_sem.at[0])
        load.start()
        load.wait()
        made = dot_nn(normed_ref[...], kv_weight[...])
        for tile in range(wide // PAIR):
            columns = slice(tile * PAIR, (tile + 1) * PAIR)
            keyval[rows_of(place), columns] = turn(
                made[:, columns], cos_ref[...], sin_ref[...]
            ).astype(low)
        keyval[rows_of(place), wide:] = made[:, wide:].astype(low)
        keyval_send(place, start)

    def weight_load(source, rank, by_rows):
        window = pl.ds(pl.multiple_of(rank * width, width), width)
        src = source.at[window, :] if by_rows else source.at[:, window]
        dst = wide_weight.at[rank % 2] if by_rows else weight.at[rank % 2]
        return pltpu.make_async_copy(src, dst, w_sem.at[rank % 2])

    def make_query():
        weight_load(fq, 0, False).start()
        for rank in range(4):
            if rank < 3:
                weight_load(fq, rank + 1, False).start()
            weight_load(fq, rank, False).wait()
            made = dot_nn(normed_ref[...], weight[rank % 2])
            for tile in range(width // PAIR):
                columns = slice(tile * PAIR, (tile + 1) * PAIR)
                query_out[:, rank * width + tile * PAIR : rank * width + (tile + 1) * PAIR] = (
                    turn(made[:, columns], cos_ref[...], sin_ref[...]) * (HD**-0.5)
                ).astype(low)

    def attend(group):
        key_tile, value_tile = head_tiles(keyval, group)
        key_f[...], key_b[...] = key_tile
        side = group % 2
        value_t[...] = value_tile.T[side * HD : (side + 1) * HD, :]
        pairs = query_out.shape[1] // PAIR // KVH

        @pl.loop(0, pairs)
        def _(index):
            pair = group * pairs + index
            columns = pl.ds(pl.multiple_of(pair * PAIR, PAIR), PAIR)
            query = query_out[:, columns]
            outs, logs = [], []
            for key_ref in (key_f, key_b):
                scores = dot_nt(key_ref[...], query) + bias_ref[...]
                top = jnp.max(scores, axis=0, keepdims=True)
                expo = jnp.exp(scores - top)
                total = jnp.sum(expo, axis=0, keepdims=True)
                outs.append(dot_nn(value_t[...], expo.astype(low)) / total)
                logs.append(top + jnp.log(total))
            log_out[pair] = jnp.concatenate(logs, axis=0)
            heads_out[:, columns] = jnp.concatenate(outs, axis=0).T.astype(low)

    def make_residual():
        weight_load(fo, 0, True).start()
        square = jnp.zeros((rows, 1), jnp.float32)
        for rank in range(4):
            if rank < 3:
                weight_load(fo, rank + 1, True).start()
            weight_load(fo, rank, True).wait()
            columns = slice(rank * width, (rank + 1) * width)
            made = tokens_ref[:, columns].astype(jnp.float32) + dot_nt(
                heads_out[...], wide_weight[rank % 2]
            )
            residual_out[:, columns] = made
            square += jnp.sum(made * made, axis=1, keepdims=True)
        inverse = lax.rsqrt(square * (1.0 / (4 * width)) + epsilon)
        for rank in range(4):
            columns = slice(rank * width, (rank + 1) * width)
            mlp_out[:, columns] = (
                residual_out[:, columns] * inverse * gain_ref[:, columns]
            ).astype(low)

    inside = (place == 1) | (place == 2)

    def cot_take(rank):
        line_copy(2, rank, 1).wait_recv()
        line_send(2, rank, start)

    def line_take(which, step):
        line_copy(which, order[step], 1).wait_recv()
        line_send(which, order[step], start)

    count = len(blocks)
    kv, q_own, gate, o_own, up = 0, 1, 2, 6, 10
    q_far, o_far = (3, 4, 5), (7, 8, 9)
    plane_first(kv)
    line_send(0, place, start)
    plane_first(q_own)
    make_normed()
    line_take(0, 0)
    line_send(1, place, start)
    plane_second(kv)
    plane_first(gate)
    plane_second(q_own)
    plane_third(kv)
    plane_ready(kv)
    own_copies[0].wait()
    line_take(0, 1)
    make_keyval()
    plane_first(q_far[0])
    plane_third(q_own)
    line_take(1, 0)
    line_take(0, 2)
    plane_second(gate)
    plane_first(q_far[1])
    keyval_take(0)
    line_take(1, 1)
    plane_second(q_far[0])
    plane_first(q_far[2])
    plane_third(gate)
    keyval_take(1)
    line_take(1, 2)
    plane_second(q_far[1])
    plane_first(o_own)
    plane_third(q_far[0])
    keyval_take(2)
    line_send(2, place, start)
    plane_second(q_far[2])
    plane_first(o_far[0])
    plane_third(q_far[1])
    plane_second(o_own)
    plane_first(o_far[1])
    plane_third(q_far[2])
    for index in (q_own,) + q_far:
        plane_ready(index)
    own_copies[1].wait()
    make_query()
    leaving[1].start()
    cot_take(order[0])

    @pl.when(inside)
    def _():
        cot_take(order[1])

    plane_second(o_far[0])
    plane_first(o_far[2])
    plane_third(o_own)
    attend(0)
    plane_second(o_far[1])
    plane_first(up)
    plane_third(o_far[0])
    attend(1)
    plane_second(o_far[2])
    plane_third(o_far[1])
    attend(2)
    plane_third(o_far[2])
    cot_take(jnp.where(inside, order[2], order[1]))
    attend(3)
    leaving[2].start()
    leaving[3].start()
    plane_second(up)
    for index in (o_own,) + o_far:
        plane_ready(index)
    own_copies[2].wait()
    make_residual()
    leaving[4].start()
    leaving[5].start()
    plane_third(up)

    @pl.when(jnp.logical_not(inside))
    def _():
        cot_take(order[2])

    plane_ready(gate)
    plane_ready(up)
    for index in range(count):
        plane_sent(index)
    for which in range(3):
        line_send(which, place, wait_send)
        for step in range(3):
            line_send(which, order[step], wait_send)
    keyval_send(place, wait_send)
    for step in range(3):
        keyval_send(order[step], wait_send)
    for copy in own_copies[3:]:
        copy.wait()
    out_copy = pltpu.make_async_copy(keyval, keyval_out, w_sem.at[0])
    out_copy.start()
    for copy in leaving:
        copy.wait()
    out_copy.wait()


def attend_all(
    tokens, gain_attn, cos, sin, bias, gain, w_keyval, w_query, w_output, w_gate, w_up, cotangent
):
    n_dp, n_line = lax.axis_size("dp"), lax.axis_size("tensor")
    low = jnp.bfloat16
    rows, depth = tokens.shape
    length = bias.shape[0]
    wide = 2 * KVH * HD
    heads = w_query.shape[1] * n_line // HD

    def over(array, by_rows, by_columns):
        shape = (array.shape[0] * by_rows, array.shape[1] * by_columns)
        return jax.ShapeDtypeStruct(shape, array.dtype)

    anywhere = pl.BlockSpec(memory_space=pl.ANY)
    shapes = [
        jax.ShapeDtypeStruct((rows, depth), low),
        jax.ShapeDtypeStruct((rows, heads * HD), low),
        jax.ShapeDtypeStruct((length, wide), low),
        jax.ShapeDtypeStruct((rows, heads * HD), low),
        jax.ShapeDtypeStruct((heads // 2, 2, rows), jnp.float32),
        jax.ShapeDtypeStruct((rows, depth), jnp.float32),
        jax.ShapeDtypeStruct((rows, depth), low),
        over(w_keyval, n_dp, 1),
        over(w_query, n_dp, n_line),
        over(w_output, n_dp, n_line),
        over(w_gate, n_dp, 1),
        over(w_up, n_dp, 1),
        over(cotangent, n_line, 1),
    ]
    dma = pltpu.SemaphoreType.DMA
    return pl.pallas_call(
        attend_kernel,
        out_shape=shapes,
        in_specs=[anywhere] * 12,
        out_specs=[anywhere] * len(shapes),
        scratch_shapes=[
            pltpu.VMEM(array.shape, array.dtype) for array in (tokens, gain_attn, cos, sin, bias, gain)
        ]
        + [
            pltpu.VMEM(shapes[number].shape, shapes[number].dtype)
            for number in (0, 1, 3, 4, 5, 6)
        ]
        + [
            pltpu.VMEM((depth, wide), low),
            pltpu.VMEM((2, depth, w_query.shape[1]), low),
            pltpu.VMEM((2, w_query.shape[1], depth), low),
            pltpu.VMEM((length, wide), low),
            pltpu.VMEM((length, PAIR), low),
            pltpu.VMEM((length, PAIR), low),
            pltpu.VMEM((HD, length), low),
            dma((6,)), dma((3, 2, 4)), dma((3, 4)), dma((11, 8)), dma((11, 8)),
            dma((2, 4)), dma((4,)), dma((2,)), dma((6,)), dma((6,)),
        ],
        compiler_params=pltpu.CompilerParams(
            collective_id=0, has_side_effects=True, vmem_limit_bytes=62 * 1024 * 1024
        ),
        name="attend_all",
    )(
        tokens, gain_attn, cos, sin, bias, gain, w_keyval, w_query, w_output, w_gate, w_up, cotangent
    )


def add_rows(target, source, step=32):
    @pl.loop(0, target.shape[0] // step)
    def _(index):
        window = pl.ds(pl.multiple_of(index * step, step), step)
        target[window, :] = target[window, :] + source[window, :]


def over_rows(total_rows, act, step=32):
    @pl.loop(0, total_rows // step)
    def _(index):
        act(pl.ds(pl.multiple_of(index * step, step), step))


def enter_wide(dp, place):
    barrier = pltpu.get_barrier_semaphore()
    for bit in (1, 2, 4):
        pl.semaphore_signal(barrier, inc=1, device_id=(flip(dp, bit), place), device_id_type=MESH)
    for step in range(1, 4):
        pl.semaphore_signal(
            barrier, inc=1, device_id=(dp, (place + step) % 4), device_id_type=MESH
        )
    pl.semaphore_wait(barrier, 6)


def reach_back_kernel(
    gd_ref, gg_ref, gu_ref, branch_ref, fkv, fq, fo, dn_ref, residual_ref,
    cot_in, tokens_in, normed_in, query_in, heads_in, keyval_in, log_in, bias_in,
    cos_in, sin_in, gain_attn_in, gain_mlp_in,
    gd_out, gg_out, gu_out, go_out, gq_out, nar_out, layer_out, tokens_out, gains_out,
    gd_core, gg_core, gu_core, go_core, gq_core, nar_core,
    gd_near, gg_near, gu_near, go_near, gq_near, nar_near,
    go_in, gq_in, nar_in, dkv_in, layer_in,
    gd_side, gg_side, gu_side, go_side, gq_side, nar_side,
    parts, nar_part, held, early, stage, go_line, gq_line, nar_line, dkv_line, sums,
    d_residual, total, wide, d_branch, d_heads, dq_low, dkv_low, gains, weight, kv_weight,
    key_f, key_b, key_t, value_f, value_b, dk, dv,
    chain, units_made, go_made, gq_made, nar_made, gains_made,
    cot_ref, tokens_ref, normed_ref, query_ref, heads_ref, keyval_ref, log_ref, bias_ref,
    cos_ref, sin_ref, gain_attn_ref, gain_mlp_ref,
    load_sem, fetch_sem, core_send, core_recv, p_send, p_recv, l_send, l_recv, in_sem, w_sem,
    c_send, c_recv, early_sem, leave_sem, enter_sem,
):
    dp, place = lax.axis_index("dp"), lax.axis_index("tensor")
    low = jnp.bfloat16
    rows, depth = d_branch.shape
    half = rows // 2
    arriving = [
        pltpu.make_async_copy(src, dst, enter_sem.at[number])
        for number, (src, dst) in enumerate(
            (
                (cot_in, cot_ref),
                (gain_mlp_in, gain_mlp_ref),
                (keyval_in, keyval_ref),
                (query_in, query_ref),
                (bias_in, bias_ref),
                (log_in, log_ref),
                (cos_in, cos_ref),
                (sin_in, sin_ref),
                (heads_in, heads_ref),
                (normed_in, normed_ref),
                (tokens_in, tokens_ref),
                (gain_attn_in, gain_attn_ref),
            )
        )
    ]
    dn_load = pltpu.make_async_copy(dn_ref, wide, in_sem.at[1])
    total_load = pltpu.make_async_copy(residual_ref, total, in_sem.at[2])
    kv_load = pltpu.make_async_copy(fkv, kv_weight, in_sem.at[3])
    for load in (dn_load, total_load):
        load.start()
    for load in arriving:
        load.start()
    kv_load.start()
    enter_wide(dp, place)
    x, y, core = flip(dp, 2), flip(dp, 4), flip(dp, 1)
    far = flip(x, 4)
    mine = (dp, x, y, far)
    theirs = tuple(flip(owner, 1) for owner in mine)
    grads = (gd_ref, gg_ref, gu_ref)
    outs = (gd_out, gg_out, gu_out, go_out, gq_out, nar_out)
    cores = (gd_core, gg_core, gu_core, go_core, gq_core, nar_core)
    sides = (gd_side, gg_side, gu_side, go_side, gq_side, nar_side)
    nears = (gd_near, gg_near, gu_near, go_near, gq_near, nar_near)
    lines = {3: go_line, 4: gq_line, 5: nar_line, 6: dkv_line}
    arrivals = {3: go_in, 4: gq_in, 5: nar_in, 6: dkv_in}
    front, back = pl.ds(0, half), pl.ds(half, half)
    ranks = dkv_line.shape[0]
    narrow_width = nar_out.shape[1]
    turns = (3, 1, 2, 0)

    def rows_of(owner):
        return pl.ds(pl.multiple_of(owner * rows, rows), rows)

    def remote(src, dst, send, recv, device):
        return pltpu.make_async_remote_copy(
            src_ref=src, dst_ref=dst, send_sem=send, recv_sem=recv,
            device_id=device, device_id_type=MESH,
        )

    def width_of(i):
        return cores[i].shape[2]

    sets = (0, 1, 0, 0, 1, 1)

    def part(i, k):
        if i == 5:
            return nar_part.at[k]
        return parts.at[sets[i], k, :, pl.ds(0, width_of(i))]

    def half_part(i, k, window):
        if i == 5:
            return nar_part.at[k, window, :]
        return parts.at[sets[i], k, window, pl.ds(0, width_of(i))]

    def held_part(slot, count, width):
        return held.at[slot, pl.ds(0, count), pl.ds(0, width)]

    def fetch(src, slot):
        return pltpu.make_async_copy(
            src, held_part(slot, src.shape[0], src.shape[1]), fetch_sem.at[slot]
        )

    def core_copy(i, k):
        if i < 3:
            src = grads[i].at[rows_of(theirs[k]), :]
        else:
            src = stage.at[turns.index(k), :, pl.ds(0, width_of(i))]
        return remote(
            src, cores[i].at[k], core_send.at[i, k], core_recv.at[i, k], (core, place)
        )

    def leave(src, dst, number):
        return pltpu.make_async_copy(src, dst, leave_sem.at[number])

    def own_load(i, k):
        return pltpu.make_async_copy(
            grads[i].at[rows_of(mine[k]), :], part(i, k), load_sem.at[i, k]
        )

    def plane_copy(i, lane):
        src, dst, device = (
            (half_part(i, 3, front), sides[i].at[0], y),
            (half_part(i, 3, back), sides[i].at[1], x),
            (half_part(i, 1, back), nears[i].at[0, back, :], x),
            (half_part(i, 2, front), nears[i].at[1, front, :], y),
            (half_part(i, 1, front), nears[i].at[0, front, :], x),
            (half_part(i, 2, back), nears[i].at[1, back, :], y),
        )[lane]
        return remote(src, dst, p_send.at[i, lane], p_recv.at[i, lane], (device, place))

    def plane_sent(i):
        for lane in range(6):
            plane_copy(i, lane).wait_send()

    def load_own(i):
        for k in turns:
            own_load(i, k).start()

    def core_fetch(i, n):
        src = cores[i].at[turns[n]]
        return pltpu.make_async_copy(
            src, early.at[n % 2, :, pl.ds(0, width_of(i))], early_sem.at[n % 2]
        )

    def core_begin(i, n):
        core_copy(i, turns[n]).wait_recv()
        core_fetch(i, n).start()

    def ready_core(i):
        core_begin(i, 0)
        core_begin(i, 1)

    def stage_core(i):
        for n, k in enumerate(turns):
            core_fetch(i, n).wait()
            if i < 3:
                own_load(i, k).wait()
            add_rows(part(i, k), early.at[n % 2, :, pl.ds(0, width_of(i))])
            for lane in ((), (2,), (3,), (0, 1))[k]:
                plane_copy(i, lane).start()
            if n + 2 < 4:
                core_begin(i, n + 2)

    def stage_side(i):
        for side, (k, window, lane) in enumerate(((1, front, 4), (2, back, 5))):
            plane_copy(i, side).wait_recv()
            add_rows(half_part(i, k, window), sides[i].at[side])
            plane_copy(i, lane).start()

    def stage_near(i):
        for side, lanes in enumerate(((2, 4), (3, 5))):
            for lane in lanes:
                plane_copy(i, lane).wait_recv()
            fetch(nears[i].at[side], side).start()
        for side in range(2):
            fetch(nears[i].at[side], side).wait()
        own, width, out = part(i, 0), width_of(i), outs[i]
        if 0 < i < 3:
            leave(units_made, out, i - 1).wait()

        @pl.loop(0, rows // 32)
        def _(index):
            window = pl.ds(pl.multiple_of(index * 32, 32), 32)
            sums = (
                own[window, :].astype(jnp.float32)
                + held[0, window, pl.ds(0, width)].astype(jnp.float32)
                + held[1, window, pl.ds(0, width)].astype(jnp.float32)
            )
            if i < 3:
                units_made[window, :] = sums
            elif i < 5:
                piece = width // ranks
                for rank in range(ranks):
                    lines[i][rank, window, :] = sums[:, rank * piece : (rank + 1) * piece].astype(
                        low
                    )
            else:
                per = rows // ranks
                lines[i][index * 32 // per, pl.ds(pl.multiple_of(index * 32 % per, 32), 32), :] = (
                    sums.astype(low)
                )

        if i < 3:
            leave(units_made, out, i).start()

    def line_copy(i, step):
        target = (place + step) % ranks
        return remote(
            lines[i].at[target], arrivals[i].at[place], l_send.at[i - 3, step], l_recv.at[i - 3, step],
            (dp, target),
        )

    def line_start(i):
        for step in range(1, ranks):
            line_copy(i, step).start()

    def line_last(i, add):
        def begin(step):
            line_copy(i, step).wait_recv()
            fetch(arrivals[i].at[(place + ranks - step) % ranks], step % 2).start()

        begin(1)
        for step in range(1, ranks):
            if step + 1 < ranks:
                begin(step + 1)
            fetch(arrivals[i].at[place], step % 2).wait()
            add(step % 2)

    def line_sent(i):
        for step in range(1, ranks):
            line_copy(i, step).wait_send()

    def chain_copy(rank, slot, step):
        return remote(
            chain.at[(step + 1) // 2], layer_in.at[slot], c_send.at[rank], c_recv.at[slot],
            (dp, place + step),
        )

    def chain_load(rank, step):
        copy = pltpu.make_async_copy(
            branch_ref.at[rank], chain.at[(step + 1) // 2], in_sem.at[0]
        )
        copy.start()
        copy.wait()

    def chain_fetch(slot):
        chain_copy(slot, slot, 1).wait_recv()
        copy = fetch(layer_in.at[slot], 0)
        copy.start()
        copy.wait()

    def chain_step(turn):
        down, up = place - ranks + 1 + turn, place + ranks - 1 - turn

        @pl.when(down >= 0)
        def _():
            @pl.when((down > 0) & (turn > 0))
            def _():
                chain_copy(down - 1, down - 1, -1).wait_send()

            chain_load(down, -1)

            @pl.when(place < ranks - 1)
            def _():
                chain_fetch(down)
                add_rows(chain.at[0], held.at[0])

            chain_copy(down, down, -1).start()

        @pl.when(up < ranks)
        def _():
            @pl.when((up < ranks - 1) & (turn > 0))
            def _():
                chain_copy(up + 1, up + 1, 1).wait_send()

            chain_load(up, 1)

            @pl.when(place > 0)
            def _():
                chain_fetch(up)
                add_rows(chain.at[1], held.at[0])

            chain_copy(up, ranks if turn == ranks - 2 else up, 1).start()

    def line_out(i):
        out = (go_made, gq_made, nar_made)[i - 3]
        count, width = out.shape

        def begin(window):
            out[window, :] = lines[i][place, window, :].astype(jnp.float32)

        def add(slot):
            def act(window):
                out[window, :] += held[slot, window, pl.ds(0, width)].astype(jnp.float32)

            over_rows(count, act)

        over_rows(count, begin)
        line_last(i, add)
        if i == 5:
            gains_made[...] = out[:, narrow_width:].T
            leave(gains_made, gains_out, 8).start()
            leave(out.at[:, pl.ds(0, narrow_width)], nar_out, 5).start()
        else:
            leave(out, outs[i], i).start()

    def norm_back(grad_ref, rows_ref, gain_ref, gain_row, act):
        gains[gain_row : gain_row + 1, :] = jnp.zeros((1, depth), jnp.float32)

        def block(window):
            values = rows_ref[window, :].astype(jnp.float32)
            inverse = lax.rsqrt(jnp.mean(values * values, axis=1, keepdims=True) + epsilon)
            unit = values * inverse
            grad = grad_ref[window, :]
            gains[gain_row : gain_row + 1, :] += jnp.sum(grad * unit, axis=0, keepdims=True)
            d_unit = grad * gain_ref[...]
            act(
                window,
                inverse * (d_unit - unit * jnp.mean(d_unit * unit, axis=1, keepdims=True)),
            )

        over_rows(rows, block, 64)

    def after_mlp(window, d_values):
        made = cot_ref[window, :].astype(jnp.float32) + d_values
        d_residual[window, :] = made
        d_branch[window, :] = made.astype(low)

    def after_attn(window, d_values):
        d_residual[window, :] += d_values

    def square_tile(left, right, owner):
        columns = pl.ds(pl.multiple_of(owner * rows, rows), rows)
        return dot_tn(left[:, columns], right[...]).astype(low)

    def narrow_tile(owner):
        columns = pl.ds(pl.multiple_of(owner * rows, rows), rows)
        keys = dot_tn(normed_ref[:, columns], dkv_low[...]).astype(low)
        line = lax.broadcasted_iota(jnp.int32, (PAIR, rows), 0)
        both = jnp.where(
            line == 0, gains[0:1, columns], jnp.where(line == 1, gains[1:2, columns], 0.0)
        )
        return jnp.concatenate([keys, both.T.astype(low)], axis=1)

    def send_theirs(i, tile):
        for n, k in enumerate(turns):
            stage[n, :, pl.ds(0, width_of(i))] = tile(theirs[k])
            core_copy(i, k).start()

    def theirs_sent(i):
        for k in turns:
            core_copy(i, k).wait_send()

    def keep_mine(i, tile):
        for k in turns:
            part(i, k)[...] = tile(mine[k])

    def go_tile(owner):
        return square_tile(d_branch, heads_ref, owner)

    def gq_tile(owner):
        return square_tile(normed_ref, dq_low, owner)

    size = weight.shape[1]
    steps = depth // size

    def weight_load(source, index):
        return pltpu.make_async_copy(
            source.at[pl.ds(index * size, size), :], weight.at[index % 2], w_sem.at[index % 2]
        )

    def make_d_heads():
        for index in range(steps):
            if index + 1 < steps:
                weight_load(fo, index + 1).start()
            weight_load(fo, index).wait()
            made = dot_nn(d_branch[:, index * size : (index + 1) * size], weight[index % 2])
            if index == 0:
                wide[...] = made
            elif index + 1 < steps:
                wide[...] += made
            else:
                d_heads[...] = (wide[...] + made).astype(low)

    def make_d_normed():
        for index in range(steps):
            if index + 1 < steps:
                weight_load(fq, index + 1).start()
            weight_load(fq, index).wait()
            wide[:, index * size : (index + 1) * size] = dot_nt(dq_low[...], weight[index % 2])

    def add_d_normed():
        for index in range(steps):
            wide[:, index * size : (index + 1) * size] += dot_nt(
                dkv_low[...], kv_weight[index * size : (index + 1) * size, :]
            )

    def attend_back(group):
        (key_f[...], key_b[...]), value_tile = head_tiles(keyval_ref, group)
        side = group % 2
        lane_side = slice(side * HD, (side + 1) * HD)
        tile_columns = slice(group // 2 * PAIR, (group // 2 + 1) * PAIR)
        key_t[...] = keyval_ref[:, tile_columns].T[lane_side, :]
        if side == 0:
            kept = front_lanes(value_tile)
            value_f[...], value_b[...] = kept, pltpu.roll(kept, HD, 1)
        else:
            kept = back_lanes(value_tile)
            value_f[...], value_b[...] = pltpu.roll(kept, HD, 1), kept
        dk[...] = jnp.zeros(dk.shape, jnp.float32)
        dv[...] = jnp.zeros(dv.shape, jnp.float32)
        pairs = query_ref.shape[1] // PAIR // KVH

        @pl.loop(0, pairs)
        def _(index):
            pair = group * pairs + index
            columns = pl.ds(pl.multiple_of(pair * PAIR, PAIR), PAIR)
            query, grad = query_ref[:, columns], d_heads[:, columns]
            logs = log_ref[pair]
            made = []
            for number, (key_ref, value_ref, keep) in enumerate(
                ((key_f, value_f, front_lanes), (key_b, value_b, back_lanes))
            ):
                probs = jnp.exp(
                    dot_nt(key_ref[...], query) + bias_ref[...] - logs[number : number + 1, :]
                )
                d_probs = dot_nt(value_ref[...], grad)
                row_dot = jnp.sum(probs * d_probs, axis=0, keepdims=True)
                d_scores = (probs * (d_probs - row_dot)).astype(low)
                dk[...] += dot_nn(d_scores, keep(query))
                dv[...] += dot_nn(probs.astype(low), keep(grad))
                made.append(dot_nn(key_t[...], d_scores))
            dq = jnp.concatenate(made, axis=0).T * (HD**-0.5)
            dq_low[:, columns] = turn(dq, cos_ref[...], -sin_ref[...]).astype(low)

        for sums, first in ((dk, 0), (dv, KVH * HD)):
            joined = (sums[...] + pltpu.roll(sums[...], HD, 1)).astype(low)
            columns = slice(first + tile_columns.start, first + tile_columns.stop)
            for rank in range(ranks):
                block = joined[rank * rows : (rank + 1) * rows, :]
                if side == 1:
                    block = front_lanes(dkv_line[rank, :, columns]) + back_lanes(block)
                dkv_line[rank, :, columns] = block

    def make_dkv():
        wide_columns = dkv_line.shape[2]

        def begin(window):
            sums[window, :] = dkv_line[place, window, :].astype(jnp.float32)

        def add(slot):
            def act(window):
                sums[window, :] += held[slot, window, pl.ds(0, wide_columns)].astype(jnp.float32)

            over_rows(rows, act)

        over_rows(rows, begin)
        line_last(6, add)
        for tile in range(wide_columns // PAIR):
            columns = slice(tile * PAIR, (tile + 1) * PAIR)
            made = sums[:, columns]
            if tile < KVH * HD // PAIR:
                made = turn(made, cos_ref[...], -sin_ref[...])
            dkv_low[:, columns] = made.astype(low)

    def finish_layer():
        for step in (-1, 1):

            @pl.when((place + step >= 0) & (place + step < ranks))
            def _():
                chain_copy(place + step, place, step).wait_send()

        chain_load(place, -1)

        def begin(window):
            total[window, :] += chain[0, window, :].astype(jnp.float32)

        def add(window):
            total[window, :] += held[0, window, :].astype(jnp.float32)

        over_rows(rows, begin)

        @pl.when(place < ranks - 1)
        def _():
            chain_fetch(place)
            over_rows(rows, add)

        @pl.when(place > 0)
        def _():
            chain_fetch(ranks)
            over_rows(rows, add)

        leave(total, layer_out, 6).start()

    def send_core(i):
        for k in turns:
            core_copy(i, k).start()

    send_core(0)
    load_own(0)
    load_own(1)
    chain_step(0)
    dn_load.wait()
    total_load.wait()
    for load in arriving:
        load.wait()
    send_core(1)
    norm_back(wide, total, gain_mlp_ref, 1, after_mlp)
    ready_core(0)
    weight_load(fo, 0).start()
    stage_core(0)
    send_theirs(3, go_tile)
    ready_core(1)
    make_d_heads()
    stage_core(1)
    send_core(2)
    stage_side(0)
    chain_step(1)
    attend_back(0)
    stage_side(1)
    stage_near(0)
    plane_sent(0)
    ready_core(3)
    keep_mine(3, go_tile)
    stage_core(3)
    attend_back(1)
    stage_near(1)
    plane_sent(1)
    chain_step(2)
    attend_back(2)
    stage_side(3)
    attend_back(3)
    line_start(6)
    theirs_sent(3)
    send_theirs(4, gq_tile)
    ready_core(4)
    keep_mine(4, gq_tile)
    stage_core(4)
    stage_near(3)
    line_start(3)
    plane_sent(3)
    load_own(2)
    ready_core(2)
    weight_load(fq, 0).start()
    make_d_normed()
    kv_load.wait()
    make_dkv()
    add_d_normed()
    stage_core(2)
    stage_side(4)
    norm_back(wide, tokens_ref, gain_attn_ref, 0, after_attn)
    leave(d_residual, tokens_out, 7).start()
    theirs_sent(4)
    send_theirs(5, narrow_tile)
    ready_core(5)
    keep_mine(5, narrow_tile)
    stage_core(5)
    stage_near(4)
    line_start(4)
    stage_side(5)
    stage_side(2)
    line_out(3)
    stage_near(5)
    line_start(5)
    finish_layer()
    stage_near(2)
    line_out(4)
    line_out(5)
    plane_sent(2)
    plane_sent(4)
    for src, dst, number in (
        (units_made, gu_out, 2),
        (go_made, go_out, 3),
        (gq_made, gq_out, 4),
        (nar_made.at[:, pl.ds(0, narrow_width)], nar_out, 5),
        (gains_made, gains_out, 8),
        (total, layer_out, 6),
        (d_residual, tokens_out, 7),
    ):
        leave(src, dst, number).wait()
    plane_sent(5)
    theirs_sent(5)
    for i in range(3):
        for k in turns:
            core_copy(i, k).wait_send()
    for i in range(3, 7):
        line_sent(i)


def reach_back(grads, branch, full, d_normed, residual, others):
    low, wide = jnp.bfloat16, jnp.float32
    n_dp, ranks = lax.axis_size("dp"), lax.axis_size("tensor")
    units = grads[0].shape[1]
    rows, depth = residual.shape
    half = rows // 2
    square = depth // ranks
    few = depth // n_dp // ranks
    length, keyval = others[5].shape
    narrow = keyval + PAIR
    widths = [units] * 3 + [depth, depth, narrow]
    anywhere = pl.BlockSpec(memory_space=pl.ANY)
    in_vmem = pl.BlockSpec(memory_space=pltpu.VMEM)
    lined = [(rows, square), (rows, square), (few, narrow), (rows, keyval), (rows, depth)]
    out_shape = [jax.ShapeDtypeStruct((rows, units), wide)] * 3
    out_shape += [jax.ShapeDtypeStruct((rows, square), wide)] * 2
    out_shape += [jax.ShapeDtypeStruct((few, keyval), wide)]
    out_shape += [jax.ShapeDtypeStruct((rows, depth), wide)] * 2
    out_shape += [jax.ShapeDtypeStruct((PAIR, few), wide)]
    out_shape += [jax.ShapeDtypeStruct((4, rows, w), low) for w in widths]
    out_shape += [jax.ShapeDtypeStruct((2, rows, w), low) for w in widths]
    out_shape += [jax.ShapeDtypeStruct((ranks,) + shape, low) for shape in lined[:4]]
    out_shape += [jax.ShapeDtypeStruct((ranks + 1, rows, depth), low)]
    dma = pltpu.SemaphoreType.DMA
    scratch = [pltpu.VMEM((2, half, w), low) for w in widths]
    scratch += [
        pltpu.VMEM((2, 4, rows, depth), low),
        pltpu.VMEM((4, rows, narrow), low),
        pltpu.VMEM((2, rows, depth), low),
        pltpu.VMEM((2, rows, depth), low),
        pltpu.VMEM((4, rows, depth), low),
    ]
    scratch += [pltpu.VMEM((ranks,) + shape, low) for shape in lined[:4]]
    scratch += [pltpu.VMEM((rows, keyval), wide)]
    scratch += [pltpu.VMEM((rows, depth), wide)] * 3
    scratch += [pltpu.VMEM((rows, depth), low)] * 3
    scratch += [
        pltpu.VMEM((rows, keyval), low),
        pltpu.VMEM((8, depth), wide),
        pltpu.VMEM((2, square, depth), low),
        pltpu.VMEM((depth, keyval), low),
        pltpu.VMEM((length, PAIR), low),
        pltpu.VMEM((length, PAIR), low),
        pltpu.VMEM((HD, length), low),
        pltpu.VMEM((length, PAIR), low),
        pltpu.VMEM((length, PAIR), low),
        pltpu.VMEM((length, PAIR), wide),
        pltpu.VMEM((length, PAIR), wide),
        pltpu.VMEM((2, rows, depth), low),
        pltpu.VMEM((rows, units), wide),
        pltpu.VMEM((rows, square), wide),
        pltpu.VMEM((rows, square), wide),
        pltpu.VMEM((few, narrow), wide),
        pltpu.VMEM((PAIR, few), wide),
    ]
    scratch += [pltpu.VMEM(array.shape, array.dtype) for array in others]
    scratch += [
        dma((3, 4)), dma((2,)), dma((6, 4)), dma((6, 4)), dma((6, 6)), dma((6, 6)),
        dma((5, ranks)), dma((5, ranks)), dma((4,)), dma((2,)), dma((ranks,)), dma((ranks + 1,)),
        dma((2,)), dma((9,)), dma((12,)),
    ]
    results = pl.pallas_call(
        reach_back_kernel,
        out_shape=out_shape,
        in_specs=[anywhere] * 21,
        out_specs=[anywhere] * len(out_shape),
        scratch_shapes=scratch,
        compiler_params=pltpu.CompilerParams(
            collective_id=1, has_side_effects=True, vmem_limit_bytes=63 * 1024 * 1024
        ),
        name="reach_back",
    )(*grads, branch, *full, d_normed, residual, *others)
    return results[:9]


def by_tiles(total, size, act):
    full = total // size

    @pl.loop(0, full)
    def _(index):
        act(pl.ds(pl.multiple_of(index * size, size), size))

    if total % size:
        act(pl.ds(full * size, total % size))


def feed_forward_kernel(
    normed_ref, gate_w_ref, up_w_ref, down_w_ref, cot_ref,
    gg_out, gu_out, gd_out, branch_out, dn_out,
    wg, wu, wd, cot, normed, hid, dg, du, part, arrival, branch_stage, gate_stage, up_stage,
    load_sem, n_send, n_recv, l_send, l_recv, stage_sem, p_send, p_recv,
):
    dp, place = lax.axis_index("dp"), lax.axis_index("tensor")
    rows, depth = normed_ref.shape
    low = jnp.bfloat16
    order = line_order(place)
    cuts = l_send.shape[1]
    few = rows // cuts
    enter(dp, place)

    def remote(src, dst, send, recv, step):
        return pltpu.make_async_remote_copy(
            src_ref=src, dst_ref=dst, send_sem=send, recv_sem=recv,
            device_id=(dp, place + step), device_id_type=MESH,
        )

    def chunk(rank):
        return pl.ds(pl.multiple_of(rank * rows, rows), rows)

    def own_copy(step):
        return remote(
            normed_ref, normed.at[chunk(place), :], n_send.at[(step + 1) // 2, place],
            n_recv.at[place], step,
        )

    def pass_copy(rank, step):
        ref = normed.at[chunk(rank), :]
        return remote(ref, ref, n_send.at[(step + 1) // 2, rank], n_recv.at[rank], step)

    x, y, core = flip(dp, 2), flip(dp, 4), flip(dp, 1)
    far = flip(x, 4)
    shards = (down_w_ref,)
    weights = (wd,)
    depth_rows = down_w_ref.shape[0]
    half = depth_rows // 2

    def weight_rows(i, owner, part=None):
        first = owner * depth_rows if part is None else owner * depth_rows + part * half
        count = depth_rows if part is None else half
        return weights[i].at[pl.ds(pl.multiple_of(first, half), count), :]

    def plane_copy(i, lane):
        if lane < 2:
            src, dst, device = shards[i], weight_rows(i, dp), (x, y)[lane]
        elif lane < 4:
            src = dst = weight_rows(i, (x, y)[lane - 2], lane - 2)
            device = (y, x)[lane - 2]
        else:
            owner = (dp, x, y, far)[lane - 4]
            dst, device = weight_rows(i, owner), core
            src = shards[i] if lane == 4 else dst
        return pltpu.make_async_remote_copy(
            src_ref=src, dst_ref=dst, send_sem=p_send.at[i, lane], recv_sem=p_recv.at[i, lane],
            device_id=(device, place), device_id_type=MESH,
        )

    loads = [
        pltpu.make_async_copy(src, dst, load_sem.at[i])
        for i, (src, dst) in enumerate(
            (
                (normed_ref, normed.at[chunk(place), :]),
                (gate_w_ref, wg),
                (cot_ref, cot),
                (up_w_ref, wu),
                (down_w_ref, weight_rows(0, dp)),
            )
        )
    ]

    @pl.when(place < 3)
    def _():
        own_copy(1).start()

    @pl.when(place > 0)
    def _():
        own_copy(-1).start()

    for lane in (0, 1, 4):
        plane_copy(0, lane).start()
    for load in loads:
        load.start()

    def plane_second(i):
        for lane in range(2):
            plane_copy(i, lane).wait_recv()
            plane_copy(i, lane + 2).start()
            plane_copy(i, lane + 5).start()

    def plane_third(i):
        plane_copy(i, 2).wait_recv()
        plane_copy(i, 3).wait_recv()
        plane_copy(i, 7).start()

    def plane_ready(i):
        for lane in range(4, 8):
            plane_copy(i, lane).wait_recv()

    def sums_copy(rank, cut, slot, step):
        window = pl.ds(pl.multiple_of(cut * few, few), few)
        return remote(
            part.at[rank, window, :], arrival.at[slot, window, :], l_send.at[rank, cut],
            l_recv.at[slot, cut], step,
        )

    def branch_copy(rank):
        return pltpu.make_async_copy(branch_stage, branch_out.at[rank], stage_sem.at[0])

    def forward(rank):
        here = chunk(rank)

        def activate(columns):
            gate = dot_nn(normed[here, :], wg[:, columns])
            up = dot_nn(normed[here, :], wu[:, columns])
            sig = 1.0 / (1.0 + jnp.exp(-gate))
            silu = gate * sig
            hid[here, columns] = (silu * up).astype(low)
            dg[here, columns] = (up * sig * (1.0 + gate * (1.0 - sig))).astype(low)
            du[here, columns] = silu.astype(low)

        by_tiles(wg.shape[1], 256, activate)

    def backward(rank):
        here = chunk(rank)

        def meet(columns):
            d_hidden = dot_nn(cot[here, :], wd[:, columns])
            dg[here, columns] = (d_hidden * dg[here, columns].astype(jnp.float32)).astype(low)
            du[here, columns] = (d_hidden * du[here, columns].astype(jnp.float32)).astype(low)

        by_tiles(wg.shape[1], 256, meet)

        def pull(columns):
            part[rank, :, columns] = (
                dot_nt(dg[here, :], wg[columns, :]) + dot_nt(du[here, :], wu[columns, :])
            ).astype(low)

        by_tiles(depth, 512, pull)

    def branch(rank):
        def push(columns):
            branch_stage[:, columns] = dot_nt(hid[chunk(rank), :], wd[columns, :]).astype(low)

        by_tiles(depth, 512, push)
        branch_copy(rank).start()

    def take(rank):
        pass_copy(rank, 1).wait_recv()

        @pl.when((rank < place) & (place < 3))
        def _():
            pass_copy(rank, 1).start()

        @pl.when((rank > place) & (place > 0))
        def _():
            pass_copy(rank, -1).start()

    inside = (place == 1) | (place == 2)
    for load in loads:
        load.wait()
    forward(place)
    plane_second(0)
    take(order[0])

    @pl.when(inside)
    def _():
        take(order[1])

    plane_third(0)

    @pl.loop(0, jnp.where(inside, 2, 1))
    def _(index):
        forward(jnp.where(index == 0, order[0], order[1]))

    plane_ready(0)

    @pl.loop(0, 4)
    def _(turn):
        rank = jnp.where(
            turn == 0,
            order[0],
            jnp.where(
                turn == 1,
                jnp.where(inside, order[1], place),
                jnp.where(
                    turn == 2,
                    jnp.where(inside, order[2], order[1]),
                    jnp.where(inside, place, order[2]),
                ),
            ),
        )

        @pl.when((turn == 2) | ((turn == 3) & jnp.logical_not(inside)))
        def _():
            take(rank)
            forward(rank)

        backward(rank)

        @pl.when((turn != 1) & (place == 3))
        def _():
            for cut in range(cuts):
                sums_copy(rank, cut, rank, -1).start()

        @pl.when((turn != 1) & (place == 0))
        def _():
            slot = jnp.where(rank == 1, 4, rank)
            for cut in range(cuts):
                sums_copy(rank, cut, slot, 1).start()

    def gate_copy(tile):
        return pltpu.make_async_copy(gate_stage, gg_out.at[tile, :], stage_sem.at[1])

    def up_copy(tile):
        return pltpu.make_async_copy(up_stage, gu_out.at[tile, :], stage_sem.at[2])

    def down_copy(tile):
        return pltpu.make_async_copy(gate_stage, gd_out.at[tile, :], stage_sem.at[1])

    size = gate_stage.shape[0]
    tiles = depth // size

    def gate_up_tile(index):
        tile = pl.ds(pl.multiple_of(index * size, size), size)
        left = normed[:, tile]
        gate_grad = dot_tn(left, dg[...]).astype(low)

        @pl.when(index > 0)
        def _():
            gate_copy(tile).wait()
            up_copy(tile).wait()

        gate_stage[...] = gate_grad
        gate_copy(tile).start()
        up_stage[...] = dot_tn(left, du[...]).astype(low)
        up_copy(tile).start()

    def down_tile(index):
        tile = pl.ds(pl.multiple_of(index * size, size), size)
        down_grad = dot_tn(cot[:, tile], hid[...]).astype(low)

        @pl.when(index > 0)
        def _():
            down_copy(tile).wait()

        gate_stage[...] = down_grad
        down_copy(tile).start()

    last = pl.ds(depth - size, size)

    def relay(rank, slot, step, cut):
        sums_copy(rank, cut, rank, step).wait_recv()
        window = pl.ds(pl.multiple_of(cut * few, few), few)
        part[rank, window, :] = part[rank, window, :] + arrival[rank, window, :]
        sums_copy(rank, cut, slot, step).start()

    outward = 3 - 2 * place

    @pl.loop(0, cuts)
    def _(cut):
        @pl.when(inside)
        def _():
            relay(3 - place, 4 - 3 * (place - 1), outward, cut)

        @pl.loop(0, tiles // cuts)
        def _(index):
            gate_up_tile(cut * (tiles // cuts) + index)

    gate_copy(last).wait()
    up_copy(last).wait()

    @pl.loop(0, cuts)
    def _(cut):
        @pl.when(inside)
        def _():
            relay(6 - 3 * place, 6 - 3 * place, outward, cut)
            relay(3 * (place - 1), 4 * (place - 1), -outward, cut)

        @pl.loop(0, tiles // cuts)
        def _(index):
            down_tile(cut * (tiles // cuts) + index)

        @pl.when(cut > 0)
        def _():
            branch_copy(cut).wait()

        branch(cut)

    down_copy(last).wait()
    branch_copy(0).wait()

    for cut in range(cuts):
        window = pl.ds(cut * few, few)
        dn_out[window, :] = part[place, window, :].astype(jnp.float32)

        @pl.when(place < 3)
        def _():
            sums_copy(place, cut, place, 1).wait_recv()
            dn_out[window, :] += arrival[place, window, :].astype(jnp.float32)

        @pl.when(place > 0)
        def _():
            sums_copy(place, cut, 4, 1).wait_recv()
            dn_out[window, :] += arrival[4, window, :].astype(jnp.float32)

    @pl.when(place < 3)
    def _():
        own_copy(1).wait_send()

    @pl.when(place > 0)
    def _():
        own_copy(-1).wait_send()

    for rank in range(4):

        @pl.when((rank < place) & (place < 3))
        def _():
            pass_copy(rank, 1).wait_send()

        @pl.when((rank > place) & (place > 0))
        def _():
            pass_copy(rank, -1).wait_send()

        @pl.when(rank != place)
        def _():
            for cut in range(cuts):
                sums_copy(rank, cut, rank, 1).wait_send()

    for lane in range(8):
        plane_copy(0, lane).wait_send()


def feed_forward(normed, w_gate, w_up, w_down, cotangent):
    low = jnp.bfloat16
    rows, depth = normed.shape
    length = cotangent.shape[0]
    units = w_gate.shape[1]
    ranks = length // rows
    cuts = 4
    anywhere = pl.BlockSpec(memory_space=pl.ANY)
    in_vmem = pl.BlockSpec(memory_space=pltpu.VMEM)
    dma = pltpu.SemaphoreType.DMA
    flops = 9 * 2 * length * depth * units
    return pl.pallas_call(
        feed_forward_kernel,
        out_shape=[jax.ShapeDtypeStruct((depth, units), low)] * 3
        + [
            jax.ShapeDtypeStruct((ranks, rows, depth), low),
            jax.ShapeDtypeStruct((rows, depth), jnp.float32),
        ],
        in_specs=[anywhere] * 5,
        out_specs=[anywhere] * 4 + [in_vmem],
        scratch_shapes=[pltpu.VMEM((depth, units), low)] * 3
        + [pltpu.VMEM((length, depth), low)] * 2
        + [pltpu.VMEM((length, units), low)] * 3
        + [
            pltpu.VMEM((ranks, rows, depth), low),
            pltpu.VMEM((ranks + 1, rows, depth), low),
            pltpu.VMEM((rows, depth), low),
            pltpu.VMEM((256, units), low),
            pltpu.VMEM((256, units), low),
            dma((5,)), dma((2, ranks)), dma((ranks,)), dma((ranks, cuts)), dma((ranks + 1, cuts)),
            dma((3,)), dma((1, 8)), dma((1, 8)),
        ],
        compiler_params=pltpu.CompilerParams(
            collective_id=2, has_side_effects=True, vmem_limit_bytes=62 * 1024 * 1024
        ),
        cost_estimate=pl.CostEstimate(flops=flops, bytes_accessed=60 << 20, transcendentals=0),
        name="feed_forward",
    )(normed, w_gate, w_up, w_down, cotangent)


def local(
    tokens,
    segments,
    gain_attn,
    w_query,
    w_keyval,
    w_output,
    gain_mlp,
    w_gate,
    w_up,
    w_down,
    cotangent,
):
    tensor_rank = lax.axis_index("tensor")
    length = segments.shape[0]
    rows = tokens.shape[0]
    both = ("dp", "tensor")
    low = jnp.bfloat16

    def gather(array, axes, axis=0):
        return lax.all_gather(array, axes, axis=axis, tiled=True)

    def scatter(array, axes, axis=0):
        return lax.psum_scatter(array, axes, scatter_dimension=axis, tiled=True)

    by_kernels = (lax.axis_size("dp"), lax.axis_size("tensor")) == (8, 4)
    places = doc_positions(segments)
    my_places = lax.dynamic_slice_in_dim(places, tensor_rank * rows, rows, 0)
    my_segments = lax.dynamic_slice_in_dim(segments, tensor_rank * rows, rows, 0)
    cosine, sine_table = rope_tables(my_places, HD)
    order = jnp.arange(length, dtype=jnp.int32)
    allowed = (order[:, None] <= tensor_rank * rows + order[None, :rows]) & (
        segments[:, None] == my_segments[None, :]
    )
    bias = jnp.where(allowed, 0.0, masked).astype(jnp.float32)

    token_rows = tokens.astype(jnp.float32)
    normed_attn, unit_attn, inverse_attn = norm_forward(token_rows, gain_attn)
    normed_attn = normed_attn.astype(low)
    wide = KVH * HD
    if by_kernels:
        before = jnp.sum(segments[None, :] < my_segments[:, None], axis=1, dtype=jnp.int32)
        my_order = tensor_rank * rows + jnp.arange(rows, dtype=jnp.int32)
        lane = jnp.arange(PAIR, dtype=jnp.int32)
        spin = rope_base ** (-(2.0 * (lane % (HD // 2)).astype(jnp.float32)) / HD)
        angles = (my_order - before).astype(jnp.float32)[:, None] * spin[None, :]
        cos_tile = jnp.cos(angles)
        sin_tile = jnp.where((lane % HD < HD // 2)[None, :], -jnp.sin(angles), jnp.sin(angles))
        (
            normed_attn, query, keyval, heads_low, log_sum, residual, normed_mlp,
            full_keyval, full_query, full_output, full_gate, full_up, piece,
        ) = attend_all(
            tokens, gain_attn[None, :], cos_tile, sin_tile, bias, gain_mlp[None, :],
            w_keyval, w_query, w_output, w_gate, w_up, cotangent,
        )
    else:
        full_keyval = gather(w_keyval, "dp")
        keyval_pre = dot_nn(normed_attn, full_keyval)
        key_low = rotate(keyval_pre[:, :wide], cosine, sine_table).astype(low)
        keyval = jnp.concatenate([key_low, keyval_pre[:, wide:].astype(low)], axis=1)
        keyval = gather(keyval, "tensor")
        full_query = gather(gather(w_query, "tensor", 1), "dp")
        query = rotate(dot_nn(normed_attn, full_query), cosine, sine_table) * (HD**-0.5)
        query = query.astype(low)
    if by_kernels:
        grad_gate, grad_up, grad_down, branch, d_normed_mlp = feed_forward(
            normed_mlp, full_gate, full_up, w_down, piece
        )
        to_down, to_gate, to_up, to_output, to_query, to_keyval, layer_out, grad_tokens, to_gains = (
            reach_back(
                (grad_down, grad_gate, grad_up),
                branch,
                (full_keyval, full_query, full_output),
                d_normed_mlp,
                residual,
                (
                    cotangent, tokens, normed_attn, query, heads_low, keyval, log_sum, bias,
                    cos_tile, sin_tile, gain_attn[None, :], gain_mlp[None, :],
                ),
            )
        )
        return (
            layer_out.astype(low),
            grad_tokens.astype(low),
            to_gains[0],
            to_query,
            to_keyval,
            to_output,
            to_gains[1],
            to_gate,
            to_up,
            to_down,
        )

    key_heads, value_heads = by_head(keyval[:, :wide]), by_head(keyval[:, wide:])
    blank = jnp.zeros_like(key_heads)
    key_f = jnp.concatenate([key_heads, blank], axis=2)
    key_b = jnp.concatenate([blank, key_heads], axis=2)
    value_f = jnp.concatenate([value_heads, blank], axis=2)
    value_b = jnp.concatenate([blank, value_heads], axis=2)
    key_t = key_heads.transpose(0, 2, 1)
    value_t = value_heads.transpose(0, 2, 1)
    heads_low, log_sum = attend_forward(query, key_f, key_b, value_t, bias)
    full_output = gather(gather(w_output, "tensor", 1), "dp")
    residual = token_rows + dot_nt(heads_low, full_output)
    full_gate, full_up = gather(w_gate, "dp"), gather(w_up, "dp")
    full_down = gather(w_down, "dp")
    piece = gather(cotangent, "tensor")
    normed_mlp_rows, unit_mlp, inverse_mlp = norm_forward(residual, gain_mlp)
    normed_mlp = normed_mlp_rows.astype(low)
    gathered_mlp = gather(normed_mlp, "tensor")
    gate_act = dot_nn(gathered_mlp, full_gate)
    up_act = dot_nn(gathered_mlp, full_up)
    sigmoid_gate = jax.nn.sigmoid(gate_act)
    silu_gate = gate_act * sigmoid_gate
    hidden_low = (silu_gate * up_act).astype(low)
    d_hidden = dot_nn(piece, full_down)
    d_gate = (d_hidden * up_act * sigmoid_gate * (1.0 + gate_act * (1.0 - sigmoid_gate))).astype(low)
    d_up = (d_hidden * silu_gate).astype(low)
    d_normed_mlp = scatter(
        (dot_nt(d_gate, full_gate) + dot_nt(d_up, full_up)).astype(low), "tensor"
    ).astype(jnp.float32)
    branch = dot_nt(hidden_low, full_down).astype(low)
    grad_down = dot_tn(piece, hidden_low)
    grad_gate = dot_tn(gathered_mlp, d_gate)
    grad_up = dot_tn(gathered_mlp, d_up)
    d_norm_mlp, gain_mlp_part = norm_backward(d_normed_mlp, unit_mlp, inverse_mlp, gain_mlp)
    d_residual = cotangent.astype(jnp.float32) + d_norm_mlp

    d_branch = d_residual.astype(low)
    grad_output = dot_tn(d_branch, heads_low)
    d_heads = dot_nn(d_branch, full_output).astype(low)
    d_queries, d_keys, d_values = attend_backward(
        query, d_heads, key_f, key_b, key_t, value_f, value_b, bias, log_sum
    )

    def flat(parts):
        joined = parts[:, :, :HD] + parts[:, :, HD:]
        return joined.transpose(1, 0, 2).reshape(length, wide)

    d_keyval = scatter(
        jnp.concatenate([flat(d_keys), flat(d_values)], axis=1).astype(low), "tensor"
    ).astype(jnp.float32)
    dq_low = rotate(d_queries, cosine, -sine_table).astype(low)
    dkv_low = jnp.concatenate(
        [rotate(d_keyval[:, :wide], cosine, -sine_table), d_keyval[:, wide:]], axis=1
    ).astype(low)
    grad_query = dot_tn(normed_attn, dq_low)
    grad_keyval = dot_tn(normed_attn, dkv_low)
    d_normed_attn = dot_nt(dq_low, full_query) + dot_nt(dkv_low, full_keyval)
    d_norm_attn, gain_attn_part = norm_backward(d_normed_attn, unit_attn, inverse_attn, gain_attn)
    grad_tokens = (d_residual + d_norm_attn).astype(low)

    layer_rows = residual + scatter(branch, "tensor").astype(jnp.float32)

    def shares(grad):
        return scatter(grad.astype(low), "dp").astype(jnp.float32)

    def square_shares(grad):
        return scatter(scatter(grad.astype(low), "dp"), "tensor", 1).astype(jnp.float32)

    gains = scatter(
        jnp.stack([gain_attn_part, gain_mlp_part]).reshape(2, -1, rows_of_gain(gain_attn)), both, 1
    )
    return (
        layer_rows.astype(low),
        grad_tokens,
        gains[0, 0],
        square_shares(grad_query),
        scatter(grad_keyval.astype(low), both).astype(jnp.float32),
        square_shares(grad_output),
        gains[1, 0],
        shares(grad_gate),
        shares(grad_up),
        shares(grad_down),
    )


def rows_of_gain(gain):
    return gain.shape[0] // (lax.axis_size("dp") * lax.axis_size("tensor"))


def solution(mesh):
    return jax.shard_map(
        local,
        mesh=mesh,
        in_specs=(
            P(("dp", "tensor"), None),
            P("dp"),
            P(),
            P("dp", "tensor"),
            P("dp", None),
            P("dp", "tensor"),
            P(),
            P("dp", "tensor"),
            P("dp", "tensor"),
            P("dp", "tensor"),
            P(("dp", "tensor"), None),
        ),
        out_specs=(
            P(("dp", "tensor"), None),
            P(("dp", "tensor"), None),
            P(("dp", "tensor")),
            P("dp", "tensor"),
            P(("dp", "tensor"), None),
            P("dp", "tensor"),
            P(("dp", "tensor")),
            P("dp", "tensor"),
            P("dp", "tensor"),
            P("dp", "tensor"),
        ),
        check_vma=False,
    )
```

```python
import functools

import jax
import jax.numpy as jnp
from jax import lax
from jax.experimental import pallas as pl
from jax.experimental.pallas import tpu as pltpu
from jax.sharding import PartitionSpec as P

KVH = 4
HD = 64
PAIR = 2 * HD

epsilon = 1e-05
rope_base = 10000.0
masked = -1e30


def doc_positions(seg_row):
    length = seg_row.shape[0]
    places = jnp.arange(length, dtype=jnp.int32)
    change = jnp.concatenate([jnp.ones((1,), jnp.bool_), seg_row[1:] != seg_row[:-1]])
    starts = lax.cummax(jnp.where(change, places, 0), axis=0)
    return places - starts


def rope_tables(places, width):
    half_width = width // 2
    frequency = rope_base ** (-(2.0 * jnp.arange(half_width).astype(jnp.float32)) / width)
    angles = places.astype(jnp.float32)[:, None] * frequency[None, :]
    return (jnp.cos(angles), jnp.sin(angles))


def rotate(values, cosine, sine_table):
    rows, width = values.shape
    heads = values.reshape(rows, width // HD, HD)
    half_width = HD // 2
    front_half = heads[..., :half_width]
    back_half = heads[..., half_width:]
    cos_rows = cosine[:, None, :]
    sin_rows = sine_table[:, None, :]
    turned = jnp.concatenate(
        [
            front_half * cos_rows - back_half * sin_rows,
            back_half * cos_rows + front_half * sin_rows,
        ],
        axis=-1,
    )
    return turned.reshape(rows, width)


def norm_forward(values, gain_vec):
    inverse = lax.rsqrt(jnp.mean(values * values, axis=-1, keepdims=True) + epsilon)
    unit_rows = values * inverse
    return (unit_rows * gain_vec, unit_rows, inverse)


def norm_backward(d_normed, unit_rows, inverse, gain_vec):
    gain_part = jnp.sum(d_normed * unit_rows, axis=0)
    d_unit = d_normed * gain_vec
    d_values = inverse * (d_unit - unit_rows * jnp.mean(d_unit * unit_rows, axis=-1, keepdims=True))
    return (d_values, gain_part)


def dot_nn(left, right):
    return jnp.dot(left, right, preferred_element_type=jnp.float32)


def dot_nt(left, right):
    return lax.dot_general(
        left, right, (((1,), (1,)), ((), ())), preferred_element_type=jnp.float32
    )


def dot_tn(left, right):
    return lax.dot_general(
        left, right, (((0,), (0,)), ((), ())), preferred_element_type=jnp.float32
    )


def front_lanes(tile):
    lane = lax.broadcasted_iota(jnp.int32, tile.shape, 1)
    return jnp.where(lane < HD, tile, jnp.zeros_like(tile))


def back_lanes(tile):
    lane = lax.broadcasted_iota(jnp.int32, tile.shape, 1)
    return jnp.where(lane < HD, jnp.zeros_like(tile), tile)


def attend_forward_kernel(query_ref, front_ref, back_ref, value_t_ref, bias_ref, out_ref, log_ref):
    pairs = query_ref.shape[1] // PAIR
    value_t = value_t_ref[0]
    for pair in range(pairs):
        query = query_ref[:, pair * PAIR : (pair + 1) * PAIR]
        outs = []
        for side, key_ref in enumerate((front_ref, back_ref)):
            scores = dot_nt(key_ref[0], query) + bias_ref[...]
            top = jnp.max(scores, axis=0, keepdims=True)
            expo = jnp.exp(scores - top)
            total = jnp.sum(expo, axis=0, keepdims=True)
            outs.append(dot_nn(value_t, expo.astype(jnp.bfloat16)) / total)
            log_ref[0, pl.ds(pair * 2 + side, 1), :] = top + jnp.log(total)
        out = jnp.concatenate(outs, axis=0).T
        out_ref[:, pair * PAIR : (pair + 1) * PAIR] = out.astype(jnp.bfloat16)


def attend_backward_kernel(
    query_ref,
    grad_ref,
    kf_ref,
    kb_ref,
    kt_ref,
    vf_ref,
    vb_ref,
    bias_ref,
    log_ref,
    dq_ref,
    dk_ref,
    dv_ref,
):
    pairs = query_ref.shape[1] // PAIR
    key_t = kt_ref[0]
    dk_ref[0] = jnp.zeros(dk_ref.shape[1:], jnp.float32)
    dv_ref[0] = jnp.zeros(dv_ref.shape[1:], jnp.float32)
    for pair in range(pairs):
        columns = slice(pair * PAIR, (pair + 1) * PAIR)
        query = query_ref[:, columns]
        grad = grad_ref[:, columns]
        outs = []
        for side, (key_ref, value_ref, keep) in enumerate(
            ((kf_ref, vf_ref, front_lanes), (kb_ref, vb_ref, back_lanes))
        ):
            log_sum = log_ref[0, pl.ds(pair * 2 + side, 1), :]
            probs = jnp.exp(dot_nt(key_ref[0], query) + bias_ref[...] - log_sum)
            d_probs = dot_nt(value_ref[0], grad)
            row_dot = jnp.sum(probs * d_probs, axis=0, keepdims=True)
            d_scores = (probs * (d_probs - row_dot)).astype(jnp.bfloat16)
            dk_ref[0] += dot_nn(d_scores, keep(query))
            dv_ref[0] += dot_nn(probs.astype(jnp.bfloat16), keep(grad))
            outs.append(dot_nn(key_t, d_scores))
        dq_ref[:, columns] = jnp.concatenate(outs, axis=0).T * (HD**-0.5)


def whole_group(rows, width):
    return pl.BlockSpec((1, rows, width), lambda g: (g, 0, 0))


def columns_of(rows, width):
    return pl.BlockSpec((rows, width), lambda g: (0, g))


def attend_forward(query, key_f, key_b, value_t, bias):
    rows, width = query.shape
    length = bias.shape[0]
    group = width // KVH
    return pl.pallas_call(
        attend_forward_kernel,
        grid=(KVH,),
        in_specs=[
            columns_of(rows, group),
            whole_group(length, PAIR),
            whole_group(length, PAIR),
            whole_group(HD, length),
            pl.BlockSpec((length, rows), lambda g: (0, 0)),
        ],
        out_specs=[columns_of(rows, group), whole_group(group // HD, rows)],
        out_shape=[
            jax.ShapeDtypeStruct((rows, width), jnp.bfloat16),
            jax.ShapeDtypeStruct((KVH, group // HD, rows), jnp.float32),
        ],
        compiler_params=pltpu.CompilerParams(vmem_limit_bytes=48 * 1024 * 1024),
        name="attend_forward",
    )(query, key_f, key_b, value_t, bias)


def attend_backward(query, grad, key_f, key_b, key_t, value_f, value_b, bias, log_sum):
    rows, width = query.shape
    length = bias.shape[0]
    group = width // KVH
    tall = whole_group(length, PAIR)
    return pl.pallas_call(
        attend_backward_kernel,
        grid=(KVH,),
        in_specs=[
            columns_of(rows, group),
            columns_of(rows, group),
            tall,
            tall,
            whole_group(HD, length),
            tall,
            tall,
            pl.BlockSpec((length, rows), lambda g: (0, 0)),
            whole_group(group // HD, rows),
        ],
        out_specs=[columns_of(rows, group), tall, tall],
        out_shape=[
            jax.ShapeDtypeStruct((rows, width), jnp.float32),
            jax.ShapeDtypeStruct((KVH, length, PAIR), jnp.float32),
            jax.ShapeDtypeStruct((KVH, length, PAIR), jnp.float32),
        ],
        compiler_params=pltpu.CompilerParams(vmem_limit_bytes=48 * 1024 * 1024),
        name="attend_backward",
    )(query, grad, key_f, key_b, key_t, value_f, value_b, bias, log_sum)


def by_head(matrix):
    rows = matrix.shape[0]
    return matrix.reshape(rows, KVH, HD).transpose(1, 0, 2)


MESH = pl.DeviceIdType.MESH


def flip(index, bit):
    return index + bit - 2 * bit * ((index // bit) % 2)


def line_order(place):
    nearest = place - 1 + 2 * (1 - (place + 3) // 4)
    farthest = 3 - 3 * (place // 2)
    return (nearest, 6 - place - nearest - farthest, farthest)


def enter(dp, place):
    barrier = pltpu.get_barrier_semaphore()
    for bit in (1, 2, 4):
        pl.semaphore_signal(barrier, inc=1, device_id=(flip(dp, bit), place), device_id_type=MESH)
    for step in (-1, 1):
        there = (place + step >= 0) & (place + step < 4)

        @pl.when(there)
        def _():
            pl.semaphore_signal(
                barrier, inc=1, device_id=(dp, place + step), device_id_type=MESH
            )

    ends = 1 - ((place + 3) // 4) + place // 3
    pl.semaphore_wait(barrier, 5 - ends)


def turn(tile, cos, sin):
    lane = lax.broadcasted_iota(jnp.int32, tile.shape, 1)
    swapped = jnp.where(
        lane % HD < HD // 2, pltpu.roll(tile, PAIR - HD // 2, 1), pltpu.roll(tile, HD // 2, 1)
    )
    return tile * cos + swapped * sin


def head_tiles(keyval, group):
    columns = slice(group // 2 * PAIR, (group // 2 + 1) * PAIR)
    tile = keyval[:, columns]
    values = slice(KVH * HD + columns.start, KVH * HD + columns.stop)
    if group % 2 == 0:
        front = front_lanes(tile)
        keys = (front, pltpu.roll(front, HD, 1))
    else:
        back = back_lanes(tile)
        keys = (pltpu.roll(back, HD, 1), back)
    return keys, keyval[:, values]


def attend_kernel(
    tokens_in, gain_attn_in, cos_in, sin_in, bias_in, gain_in,
    kv_ref, q_ref, o_ref, g_ref, u_ref, c_ref,
    normed_to, query_to, keyval_out, heads_to, log_to, residual_to, mlp_to,
    fkv, fq, fo, fg, fu, fc,
    tokens_ref, gain_attn_ref, cos_ref, sin_ref, bias_ref, gain_ref,
    normed_ref, query_out, heads_out, log_out, residual_out, mlp_out,
    kv_weight, weight, wide_weight, keyval, key_f, key_b, value_t,
    own_sem, z_send, z_recv, p_send, p_recv, k_send, k_recv, w_sem, enter_sem, leave_sem,
):
    dp, place = lax.axis_index("dp"), lax.axis_index("tensor")
    rows = kv_ref.shape[0]
    half = rows // 2
    width = q_ref.shape[1]
    order = line_order(place)
    arriving = [
        pltpu.make_async_copy(src, dst, enter_sem.at[number])
        for number, (src, dst) in enumerate(
            (
                (tokens_in, tokens_ref),
                (gain_attn_in, gain_attn_ref),
                (cos_in, cos_ref),
                (sin_in, sin_ref),
                (bias_in, bias_ref),
                (gain_in, gain_ref),
            )
        )
    ]
    leaving = [
        pltpu.make_async_copy(src, dst, leave_sem.at[number])
        for number, (src, dst) in enumerate(
            (
                (normed_ref, normed_to),
                (query_out, query_to),
                (heads_out, heads_to),
                (log_out, log_to),
                (residual_out, residual_to),
                (mlp_out, mlp_to),
            )
        )
    ]
    for copy in arriving:
        copy.start()
    enter(dp, place)

    def rows_of(owner):
        return pl.ds(pl.multiple_of(owner * rows, rows), rows)

    def columns_of_rank(rank):
        return pl.ds(pl.multiple_of(rank * width, width), width)

    def remote(src, dst, send, recv, device):
        return pltpu.make_async_remote_copy(
            src_ref=src, dst_ref=dst, send_sem=send, recv_sem=recv,
            device_id=device, device_id_type=MESH,
        )

    own = [
        (kv_ref, fkv.at[rows_of(dp), :]),
        (q_ref, fq.at[rows_of(dp), columns_of_rank(place)]),
        (o_ref, fo.at[rows_of(dp), columns_of_rank(place)]),
        (g_ref, fg.at[rows_of(dp), :]),
        (u_ref, fu.at[rows_of(dp), :]),
        (c_ref, fc.at[rows_of(place), :]),
    ]
    own_copies = [
        pltpu.make_async_copy(src, dst, own_sem.at[i]) for i, (src, dst) in enumerate(own)
    ]
    for copy in own_copies:
        copy.start()

    def line_block(which, rank):
        if which == 2:
            return fc.at[rows_of(rank), :]
        return (fq, fo)[which].at[rows_of(dp), columns_of_rank(rank)]

    def line_copy(which, rank, step):
        src = (q_ref, o_ref, c_ref)[which] if rank is place else line_block(which, rank)
        side = 0 if step < 0 else 1
        return remote(
            src, line_block(which, rank), z_send.at[which, side, rank], z_recv.at[which, rank],
            (dp, place + step),
        )

    def line_send(which, rank, act):
        @pl.when((rank <= place) & (place < 3))
        def _():
            act(line_copy(which, rank, 1))

        @pl.when((rank >= place) & (place > 0))
        def _():
            act(line_copy(which, rank, -1))

    def start(copy):
        copy.start()

    def wait_send(copy):
        copy.wait_send()

    x, y, core = flip(dp, 2), flip(dp, 4), flip(dp, 1)
    far = flip(x, 4)

    blocks = [("kv", None), ("q", place), ("g", None)] + [("q", rank) for rank in order]
    blocks += [("o", place)] + [("o", rank) for rank in order] + [("u0", None), ("u1", None)]

    def block(index, owner, part=None):
        name, rank = blocks[index]
        ref = {"kv": fkv, "q": fq, "o": fo, "g": fg, "u0": fu, "u1": fu}[name]
        span = half if name in ("u0", "u1") else rows
        first = owner * rows + (span if name == "u1" else 0)
        size = span
        if part is not None:
            size = span // 2
            first = first + part * size
        window = pl.ds(pl.multiple_of(first, span // 2), size)
        if rank is None:
            return ref.at[window, :]
        return ref.at[window, columns_of_rank(rank)]

    def own_block(index):
        name, rank = blocks[index]
        if rank is None or rank is place:
            return {
                "kv": kv_ref, "q": q_ref, "o": o_ref, "g": g_ref,
                "u0": u_ref.at[pl.ds(0, half), :], "u1": u_ref.at[pl.ds(half, half), :],
            }[name]
        return block(index, dp)

    def plane_copy(index, lane):
        send, recv = p_send.at[index, lane], p_recv.at[index, lane]
        if lane == 0:
            return remote(own_block(index), block(index, dp), send, recv, (x, place))
        if lane == 1:
            return remote(own_block(index), block(index, dp), send, recv, (y, place))
        if lane == 2:
            return remote(block(index, x, 0), block(index, x, 0), send, recv, (y, place))
        if lane == 3:
            return remote(block(index, y, 1), block(index, y, 1), send, recv, (x, place))
        owner = (dp, x, y, far)[lane - 4]
        src = own_block(index) if lane == 4 else block(index, owner)
        return remote(src, block(index, owner), send, recv, (core, place))

    def plane_first(index):
        plane_copy(index, 0).start()
        plane_copy(index, 1).start()
        plane_copy(index, 4).start()

    def plane_second(index):
        plane_copy(index, 0).wait_recv()
        plane_copy(index, 2).start()
        plane_copy(index, 5).start()
        plane_copy(index, 1).wait_recv()
        plane_copy(index, 3).start()
        plane_copy(index, 6).start()

    def plane_third(index):
        plane_copy(index, 2).wait_recv()
        plane_copy(index, 3).wait_recv()
        plane_copy(index, 7).start()

    def plane_ready(index):
        for lane in range(4, 8):
            plane_copy(index, lane).wait_recv()

    def plane_sent(index):
        for lane in range(8):
            plane_copy(index, lane).wait_send()

    def keyval_block(rank):
        return keyval.at[rows_of(rank), :]

    def keyval_copy(rank, step):
        side = 0 if step < 0 else 1
        return remote(
            keyval_block(rank), keyval_block(rank), k_send.at[side, rank], k_recv.at[rank],
            (dp, place + step),
        )

    def keyval_send(rank, act):
        @pl.when((rank <= place) & (place < 3))
        def _():
            act(keyval_copy(rank, 1))

        @pl.when((rank >= place) & (place > 0))
        def _():
            act(keyval_copy(rank, -1))

    def keyval_take(step):
        keyval_copy(order[step], 1).wait_recv()
        keyval_send(order[step], start)

    low = jnp.bfloat16
    wide = KVH * HD

    def make_normed():
        for copy in arriving:
            copy.wait()

        @pl.loop(0, rows // 64)
        def _(index):
            window = pl.ds(pl.multiple_of(index * 64, 64), 64)
            values = tokens_ref[window, :].astype(jnp.float32)
            inverse = lax.rsqrt(jnp.mean(values * values, axis=1, keepdims=True) + epsilon)
            normed_ref[window, :] = (values * inverse * gain_attn_ref[...]).astype(low)

        leaving[0].start()

    def make_keyval():
        load = pltpu.make_async_copy(fkv, kv_weight, w_sem.at[0])
        load.start()
        load.wait()
        made = dot_nn(normed_ref[...], kv_weight[...])
        for tile in range(wide // PAIR):
            columns = slice(tile * PAIR, (tile + 1) * PAIR)
            keyval[rows_of(place), columns] = turn(
                made[:, columns], cos_ref[...], sin_ref[...]
            ).astype(low)
        keyval[rows_of(place), wide:] = made[:, wide:].astype(low)
        keyval_send(place, start)

    def weight_load(source, rank, by_rows):
        window = pl.ds(pl.multiple_of(rank * width, width), width)
        src = source.at[window, :] if by_rows else source.at[:, window]
        dst = wide_weight.at[rank % 2] if by_rows else weight.at[rank % 2]
        return pltpu.make_async_copy(src, dst, w_sem.at[rank % 2])

    def make_query():
        weight_load(fq, 0, False).start()
        for rank in range(4):
            if rank < 3:
                weight_load(fq, rank + 1, False).start()
            weight_load(fq, rank, False).wait()
            made = dot_nn(normed_ref[...], weight[rank % 2])
            for tile in range(width // PAIR):
                columns = slice(tile * PAIR, (tile + 1) * PAIR)
                query_out[:, rank * width + tile * PAIR : rank * width + (tile + 1) * PAIR] = (
                    turn(made[:, columns], cos_ref[...], sin_ref[...]) * (HD**-0.5)
                ).astype(low)

    def attend(group):
        key_tile, value_tile = head_tiles(keyval, group)
        key_f[...], key_b[...] = key_tile
        side = group % 2
        value_t[...] = value_tile.T[side * HD : (side + 1) * HD, :]
        pairs = query_out.shape[1] // PAIR // KVH

        @pl.loop(0, pairs)
        def _(index):
            pair = group * pairs + index
            columns = pl.ds(pl.multiple_of(pair * PAIR, PAIR), PAIR)
            query = query_out[:, columns]
            outs, logs = [], []
            for key_ref in (key_f, key_b):
                scores = dot_nt(key_ref[...], query) + bias_ref[...]
                top = jnp.max(scores, axis=0, keepdims=True)
                expo = jnp.exp(scores - top)
                total = jnp.sum(expo, axis=0, keepdims=True)
                outs.append(dot_nn(value_t[...], expo.astype(low)) / total)
                logs.append(top + jnp.log(total))
            log_out[pair] = jnp.concatenate(logs, axis=0)
            heads_out[:, columns] = jnp.concatenate(outs, axis=0).T.astype(low)

    def make_residual():
        weight_load(fo, 0, True).start()
        square = jnp.zeros((rows, 1), jnp.float32)
        for rank in range(4):
            if rank < 3:
                weight_load(fo, rank + 1, True).start()
            weight_load(fo, rank, True).wait()
            columns = slice(rank * width, (rank + 1) * width)
            made = tokens_ref[:, columns].astype(jnp.float32) + dot_nt(
                heads_out[...], wide_weight[rank % 2]
            )
            residual_out[:, columns] = made
            square += jnp.sum(made * made, axis=1, keepdims=True)
        inverse = lax.rsqrt(square * (1.0 / (4 * width)) + epsilon)
        for rank in range(4):
            columns = slice(rank * width, (rank + 1) * width)
            mlp_out[:, columns] = (
                residual_out[:, columns] * inverse * gain_ref[:, columns]
            ).astype(low)

    inside = (place == 1) | (place == 2)

    def cot_take(rank):
        line_copy(2, rank, 1).wait_recv()
        line_send(2, rank, start)

    def line_take(which, step):
        line_copy(which, order[step], 1).wait_recv()
        line_send(which, order[step], start)

    count = len(blocks)
    kv, q_own, gate, o_own, up, up_back = 0, 1, 2, 6, 10, 11
    q_far, o_far = (3, 4, 5), (7, 8, 9)
    plane_first(kv)
    line_send(0, place, start)
    plane_first(q_own)
    make_normed()
    line_take(0, 0)
    line_send(1, place, start)
    plane_second(kv)
    plane_first(gate)
    plane_second(q_own)
    plane_third(kv)
    plane_ready(kv)
    own_copies[0].wait()
    line_take(0, 1)
    make_keyval()
    plane_first(q_far[0])
    plane_third(q_own)
    line_take(1, 0)
    line_take(0, 2)
    plane_second(gate)
    plane_first(q_far[1])
    keyval_take(0)
    line_take(1, 1)
    plane_second(q_far[0])
    plane_first(q_far[2])
    plane_third(gate)
    keyval_take(1)
    line_take(1, 2)
    plane_second(q_far[1])
    plane_first(o_own)
    plane_third(q_far[0])
    keyval_take(2)
    line_send(2, place, start)
    plane_second(q_far[2])
    plane_first(o_far[0])
    plane_third(q_far[1])
    plane_second(o_own)
    plane_first(o_far[1])
    plane_third(q_far[2])
    for index in (q_own,) + q_far:
        plane_ready(index)
    own_copies[1].wait()
    make_query()
    leaving[1].start()
    cot_take(order[0])

    @pl.when(inside)
    def _():
        cot_take(order[1])

    plane_second(o_far[0])
    plane_first(o_far[2])
    plane_third(o_own)
    attend(0)
    plane_second(o_far[1])
    plane_first(up)
    plane_first(up_back)
    plane_third(o_far[0])
    attend(1)
    plane_second(o_far[2])
    plane_third(o_far[1])
    attend(2)
    plane_third(o_far[2])
    cot_take(jnp.where(inside, order[2], order[1]))
    attend(3)
    leaving[2].start()
    leaving[3].start()
    plane_second(up)
    plane_second(up_back)
    for index in (o_own,) + o_far:
        plane_ready(index)
    own_copies[2].wait()
    make_residual()
    leaving[4].start()
    leaving[5].start()
    plane_third(up)
    plane_third(up_back)

    @pl.when(jnp.logical_not(inside))
    def _():
        cot_take(order[2])

    plane_ready(gate)
    plane_ready(up)
    plane_ready(up_back)
    for index in range(count):
        plane_sent(index)
    for which in range(3):
        line_send(which, place, wait_send)
        for step in range(3):
            line_send(which, order[step], wait_send)
    keyval_send(place, wait_send)
    for step in range(3):
        keyval_send(order[step], wait_send)
    for copy in own_copies[3:]:
        copy.wait()
    out_copy = pltpu.make_async_copy(keyval, keyval_out, w_sem.at[0])
    out_copy.start()
    for copy in leaving:
        copy.wait()
    out_copy.wait()


def attend_all(
    tokens, gain_attn, cos, sin, bias, gain, w_keyval, w_query, w_output, w_gate, w_up, cotangent
):
    n_dp, n_line = lax.axis_size("dp"), lax.axis_size("tensor")
    low = jnp.bfloat16
    rows, depth = tokens.shape
    length = bias.shape[0]
    wide = 2 * KVH * HD
    heads = w_query.shape[1] * n_line // HD

    def over(array, by_rows, by_columns):
        shape = (array.shape[0] * by_rows, array.shape[1] * by_columns)
        return jax.ShapeDtypeStruct(shape, array.dtype)

    anywhere = pl.BlockSpec(memory_space=pl.ANY)
    shapes = [
        jax.ShapeDtypeStruct((rows, depth), low),
        jax.ShapeDtypeStruct((rows, heads * HD), low),
        jax.ShapeDtypeStruct((length, wide), low),
        jax.ShapeDtypeStruct((rows, heads * HD), low),
        jax.ShapeDtypeStruct((heads // 2, 2, rows), jnp.float32),
        jax.ShapeDtypeStruct((rows, depth), jnp.float32),
        jax.ShapeDtypeStruct((rows, depth), low),
        over(w_keyval, n_dp, 1),
        over(w_query, n_dp, n_line),
        over(w_output, n_dp, n_line),
        over(w_gate, n_dp, 1),
        over(w_up, n_dp, 1),
        over(cotangent, n_line, 1),
    ]
    dma = pltpu.SemaphoreType.DMA
    return pl.pallas_call(
        attend_kernel,
        out_shape=shapes,
        in_specs=[anywhere] * 12,
        out_specs=[anywhere] * len(shapes),
        scratch_shapes=[
            pltpu.VMEM(array.shape, array.dtype) for array in (tokens, gain_attn, cos, sin, bias, gain)
        ]
        + [
            pltpu.VMEM(shapes[number].shape, shapes[number].dtype)
            for number in (0, 1, 3, 4, 5, 6)
        ]
        + [
            pltpu.VMEM((depth, wide), low),
            pltpu.VMEM((2, depth, w_query.shape[1]), low),
            pltpu.VMEM((2, w_query.shape[1], depth), low),
            pltpu.VMEM((length, wide), low),
            pltpu.VMEM((length, PAIR), low),
            pltpu.VMEM((length, PAIR), low),
            pltpu.VMEM((HD, length), low),
            dma((6,)), dma((3, 2, 4)), dma((3, 4)), dma((12, 8)), dma((12, 8)),
            dma((2, 4)), dma((4,)), dma((2,)), dma((6,)), dma((6,)),
        ],
        compiler_params=pltpu.CompilerParams(
            collective_id=0, has_side_effects=True, vmem_limit_bytes=62 * 1024 * 1024
        ),
        name="attend_all",
    )(
        tokens, gain_attn, cos, sin, bias, gain, w_keyval, w_query, w_output, w_gate, w_up, cotangent
    )


def add_rows(target, source, step=32):
    @pl.loop(0, target.shape[0] // step)
    def _(index):
        window = pl.ds(pl.multiple_of(index * step, step), step)
        target[window, :] = target[window, :] + source[window, :]


def over_rows(total_rows, act, step=32):
    @pl.loop(0, total_rows // step)
    def _(index):
        act(pl.ds(pl.multiple_of(index * step, step), step))


def enter_wide(dp, place):
    barrier = pltpu.get_barrier_semaphore()
    for bit in (1, 2, 4):
        pl.semaphore_signal(barrier, inc=1, device_id=(flip(dp, bit), place), device_id_type=MESH)
    for step in range(1, 4):
        pl.semaphore_signal(
            barrier, inc=1, device_id=(dp, (place + step) % 4), device_id_type=MESH
        )
    pl.semaphore_wait(barrier, 6)


def reach_back_kernel(
    gd_ref, gg_ref, gu_ref, branch_ref, fkv, fq, fo, dn_ref, residual_ref,
    cot_in, tokens_in, normed_in, query_in, heads_in, keyval_in, log_in, bias_in,
    cos_in, sin_in, gain_attn_in, gain_mlp_in,
    gd_out, gg_out, gu_out, go_out, gq_out, nar_out, layer_out, tokens_out, gains_out,
    gd_core, gg_core, gu_core, go_core, gq_core, nar_core,
    gd_near, gg_near, gu_near, go_near, gq_near, nar_near,
    go_in, gq_in, nar_in, dkv_in, layer_in,
    gd_side, gg_side, gu_side, go_side, gq_side, nar_side,
    parts, nar_part, held, early, stage, go_line, gq_line, nar_line, dkv_line, sums,
    d_residual, total, wide, d_branch, d_heads, dq_low, dkv_low, gains, weight, kv_weight,
    key_f, key_b, key_t, value_f, value_b, dk, dv,
    chain, units_made, go_made, gq_made, nar_made, gains_made,
    cot_ref, tokens_ref, normed_ref, query_ref, heads_ref, keyval_ref, log_ref, bias_ref,
    cos_ref, sin_ref, gain_attn_ref, gain_mlp_ref,
    load_sem, fetch_sem, core_send, core_recv, p_send, p_recv, l_send, l_recv, in_sem, w_sem,
    c_send, c_recv, early_sem, leave_sem, enter_sem,
):
    dp, place = lax.axis_index("dp"), lax.axis_index("tensor")
    low = jnp.bfloat16
    rows, depth = d_branch.shape
    half = rows // 2
    arriving = [
        pltpu.make_async_copy(src, dst, enter_sem.at[number])
        for number, (src, dst) in enumerate(
            (
                (cot_in, cot_ref),
                (gain_mlp_in, gain_mlp_ref),
                (keyval_in, keyval_ref),
                (query_in, query_ref),
                (bias_in, bias_ref),
                (log_in, log_ref),
                (cos_in, cos_ref),
                (sin_in, sin_ref),
                (heads_in, heads_ref),
                (normed_in, normed_ref),
                (tokens_in, tokens_ref),
                (gain_attn_in, gain_attn_ref),
            )
        )
    ]
    dn_load = pltpu.make_async_copy(dn_ref, wide, in_sem.at[1])
    total_load = pltpu.make_async_copy(residual_ref, total, in_sem.at[2])
    kv_load = pltpu.make_async_copy(fkv, kv_weight, in_sem.at[3])
    for load in (dn_load, total_load):
        load.start()
    for load in arriving:
        load.start()
    kv_load.start()
    enter_wide(dp, place)
    x, y, core = flip(dp, 2), flip(dp, 4), flip(dp, 1)
    far = flip(x, 4)
    mine = (dp, x, y, far)
    theirs = tuple(flip(owner, 1) for owner in mine)
    grads = (gd_ref, gg_ref, gu_ref)
    outs = (gd_out, gg_out, gu_out, go_out, gq_out, nar_out)
    cores = (gd_core, gg_core, gu_core, go_core, gq_core, nar_core)
    sides = (gd_side, gg_side, gu_side, go_side, gq_side, nar_side)
    nears = (gd_near, gg_near, gu_near, go_near, gq_near, nar_near)
    lines = {3: go_line, 4: gq_line, 5: nar_line, 6: dkv_line}
    arrivals = {3: go_in, 4: gq_in, 5: nar_in, 6: dkv_in}
    front, back = pl.ds(0, half), pl.ds(half, half)
    ranks = dkv_line.shape[0]
    narrow_width = nar_out.shape[1]
    turns = (3, 1, 2, 0)

    def rows_of(owner):
        return pl.ds(pl.multiple_of(owner * rows, rows), rows)

    def remote(src, dst, send, recv, device):
        return pltpu.make_async_remote_copy(
            src_ref=src, dst_ref=dst, send_sem=send, recv_sem=recv,
            device_id=device, device_id_type=MESH,
        )

    def width_of(i):
        return cores[i].shape[2]

    sets = (0, 1, 0, 0, 1, 1)

    def part(i, k):
        if i == 5:
            return nar_part.at[k]
        return parts.at[sets[i], k, :, pl.ds(0, width_of(i))]

    def half_part(i, k, window):
        if i == 5:
            return nar_part.at[k, window, :]
        return parts.at[sets[i], k, window, pl.ds(0, width_of(i))]

    def held_part(slot, count, width):
        return held.at[slot, pl.ds(0, count), pl.ds(0, width)]

    def fetch(src, slot):
        return pltpu.make_async_copy(
            src, held_part(slot, src.shape[0], src.shape[1]), fetch_sem.at[slot]
        )

    def core_copy(i, k):
        if i < 3:
            src = grads[i].at[rows_of(theirs[k]), :]
        else:
            src = stage.at[turns.index(k), :, pl.ds(0, width_of(i))]
        return remote(
            src, cores[i].at[k], core_send.at[i, k], core_recv.at[i, k], (core, place)
        )

    def leave(src, dst, number):
        return pltpu.make_async_copy(src, dst, leave_sem.at[number])

    def own_load(i, k):
        return pltpu.make_async_copy(
            grads[i].at[rows_of(mine[k]), :], part(i, k), load_sem.at[i, k]
        )

    def plane_copy(i, lane):
        src, dst, device = (
            (half_part(i, 3, front), sides[i].at[0], y),
            (half_part(i, 3, back), sides[i].at[1], x),
            (half_part(i, 1, back), nears[i].at[0, back, :], x),
            (half_part(i, 2, front), nears[i].at[1, front, :], y),
            (half_part(i, 1, front), nears[i].at[0, front, :], x),
            (half_part(i, 2, back), nears[i].at[1, back, :], y),
        )[lane]
        return remote(src, dst, p_send.at[i, lane], p_recv.at[i, lane], (device, place))

    def plane_sent(i):
        for lane in range(6):
            plane_copy(i, lane).wait_send()

    def load_own(i):
        for k in turns:
            own_load(i, k).start()

    def core_fetch(i, n):
        src = cores[i].at[turns[n]]
        return pltpu.make_async_copy(
            src, early.at[n % 2, :, pl.ds(0, width_of(i))], early_sem.at[n % 2]
        )

    def core_begin(i, n):
        core_copy(i, turns[n]).wait_recv()
        core_fetch(i, n).start()

    def ready_core(i):
        core_begin(i, 0)
        core_begin(i, 1)

    def stage_core(i):
        for n, k in enumerate(turns):
            core_fetch(i, n).wait()
            if i < 3:
                own_load(i, k).wait()
            add_rows(part(i, k), early.at[n % 2, :, pl.ds(0, width_of(i))])
            for lane in ((), (2,), (3,), (0, 1))[k]:
                plane_copy(i, lane).start()
            if n + 2 < 4:
                core_begin(i, n + 2)

    def stage_side(i):
        for side, (k, window, lane) in enumerate(((1, front, 4), (2, back, 5))):
            plane_copy(i, side).wait_recv()
            add_rows(half_part(i, k, window), sides[i].at[side])
            plane_copy(i, lane).start()

    def stage_near(i):
        for side, lanes in enumerate(((2, 4), (3, 5))):
            for lane in lanes:
                plane_copy(i, lane).wait_recv()
            fetch(nears[i].at[side], side).start()
        for side in range(2):
            fetch(nears[i].at[side], side).wait()
        own, width, out = part(i, 0), width_of(i), outs[i]
        if 0 < i < 3:
            leave(units_made, out, i - 1).wait()

        @pl.loop(0, rows // 32)
        def _(index):
            window = pl.ds(pl.multiple_of(index * 32, 32), 32)
            sums = (
                own[window, :].astype(jnp.float32)
                + held[0, window, pl.ds(0, width)].astype(jnp.float32)
                + held[1, window, pl.ds(0, width)].astype(jnp.float32)
            )
            if i < 3:
                units_made[window, :] = sums
            elif i < 5:
                piece = width // ranks
                for rank in range(ranks):
                    lines[i][rank, window, :] = sums[:, rank * piece : (rank + 1) * piece].astype(
                        low
                    )
            else:
                per = rows // ranks
                lines[i][index * 32 // per, pl.ds(pl.multiple_of(index * 32 % per, 32), 32), :] = (
                    sums.astype(low)
                )

        if i < 3:
            leave(units_made, out, i).start()

    def line_copy(i, step):
        target = (place + step) % ranks
        return remote(
            lines[i].at[target], arrivals[i].at[place], l_send.at[i - 3, step], l_recv.at[i - 3, step],
            (dp, target),
        )

    def line_start(i):
        for step in range(1, ranks):
            line_copy(i, step).start()

    def line_last(i, add):
        def begin(step):
            line_copy(i, step).wait_recv()
            fetch(arrivals[i].at[(place + ranks - step) % ranks], step % 2).start()

        begin(1)
        for step in range(1, ranks):
            if step + 1 < ranks:
                begin(step + 1)
            fetch(arrivals[i].at[place], step % 2).wait()
            add(step % 2)

    def line_sent(i):
        for step in range(1, ranks):
            line_copy(i, step).wait_send()

    def chain_copy(rank, slot, step):
        return remote(
            chain.at[(step + 1) // 2], layer_in.at[slot], c_send.at[rank], c_recv.at[slot],
            (dp, place + step),
        )

    def chain_load(rank, step):
        copy = pltpu.make_async_copy(
            branch_ref.at[rank], chain.at[(step + 1) // 2], in_sem.at[0]
        )
        copy.start()
        copy.wait()

    def chain_fetch(slot):
        chain_copy(slot, slot, 1).wait_recv()
        copy = fetch(layer_in.at[slot], 0)
        copy.start()
        copy.wait()

    def chain_step(turn):
        down, up = place - ranks + 1 + turn, place + ranks - 1 - turn

        @pl.when(down >= 0)
        def _():
            @pl.when((down > 0) & (turn > 0))
            def _():
                chain_copy(down - 1, down - 1, -1).wait_send()

            chain_load(down, -1)

            @pl.when(place < ranks - 1)
            def _():
                chain_fetch(down)
                add_rows(chain.at[0], held.at[0])

            chain_copy(down, down, -1).start()

        @pl.when(up < ranks)
        def _():
            @pl.when((up < ranks - 1) & (turn > 0))
            def _():
                chain_copy(up + 1, up + 1, 1).wait_send()

            chain_load(up, 1)

            @pl.when(place > 0)
            def _():
                chain_fetch(up)
                add_rows(chain.at[1], held.at[0])

            chain_copy(up, ranks if turn == ranks - 2 else up, 1).start()

    def line_out(i):
        out = (go_made, gq_made, nar_made)[i - 3]
        count, width = out.shape

        def begin(window):
            out[window, :] = lines[i][place, window, :].astype(jnp.float32)

        def add(slot):
            def act(window):
                out[window, :] += held[slot, window, pl.ds(0, width)].astype(jnp.float32)

            over_rows(count, act)

        over_rows(count, begin)
        line_last(i, add)
        if i == 5:
            gains_made[...] = out[:, narrow_width:].T
            leave(gains_made, gains_out, 8).start()
            leave(out.at[:, pl.ds(0, narrow_width)], nar_out, 5).start()
        else:
            leave(out, outs[i], i).start()

    def norm_back(grad_ref, rows_ref, gain_ref, gain_row, act):
        gains[gain_row : gain_row + 1, :] = jnp.zeros((1, depth), jnp.float32)

        def block(window):
            values = rows_ref[window, :].astype(jnp.float32)
            inverse = lax.rsqrt(jnp.mean(values * values, axis=1, keepdims=True) + epsilon)
            unit = values * inverse
            grad = grad_ref[window, :]
            gains[gain_row : gain_row + 1, :] += jnp.sum(grad * unit, axis=0, keepdims=True)
            d_unit = grad * gain_ref[...]
            act(
                window,
                inverse * (d_unit - unit * jnp.mean(d_unit * unit, axis=1, keepdims=True)),
            )

        over_rows(rows, block, 64)

    def after_mlp(window, d_values):
        made = cot_ref[window, :].astype(jnp.float32) + d_values
        d_residual[window, :] = made
        d_branch[window, :] = made.astype(low)

    def after_attn(window, d_values):
        d_residual[window, :] += d_values

    def square_tile(left, right, owner):
        columns = pl.ds(pl.multiple_of(owner * rows, rows), rows)
        return dot_tn(left[:, columns], right[...]).astype(low)

    def narrow_tile(owner):
        columns = pl.ds(pl.multiple_of(owner * rows, rows), rows)
        keys = dot_tn(normed_ref[:, columns], dkv_low[...]).astype(low)
        line = lax.broadcasted_iota(jnp.int32, (PAIR, rows), 0)
        both = jnp.where(
            line == 0, gains[0:1, columns], jnp.where(line == 1, gains[1:2, columns], 0.0)
        )
        return jnp.concatenate([keys, both.T.astype(low)], axis=1)

    def send_theirs(i, tile):
        for n, k in enumerate(turns):
            stage[n, :, pl.ds(0, width_of(i))] = tile(theirs[k])
            core_copy(i, k).start()

    def theirs_sent(i):
        for k in turns:
            core_copy(i, k).wait_send()

    def keep_mine(i, tile):
        for k in turns:
            part(i, k)[...] = tile(mine[k])

    def go_tile(owner):
        return square_tile(d_branch, heads_ref, owner)

    def gq_tile(owner):
        return square_tile(normed_ref, dq_low, owner)

    size = weight.shape[1]
    steps = depth // size

    def weight_load(source, index):
        return pltpu.make_async_copy(
            source.at[pl.ds(index * size, size), :], weight.at[index % 2], w_sem.at[index % 2]
        )

    def make_d_heads():
        for index in range(steps):
            if index + 1 < steps:
                weight_load(fo, index + 1).start()
            weight_load(fo, index).wait()
            made = dot_nn(d_branch[:, index * size : (index + 1) * size], weight[index % 2])
            if index == 0:
                wide[...] = made
            elif index + 1 < steps:
                wide[...] += made
            else:
                d_heads[...] = (wide[...] + made).astype(low)

    def make_d_normed():
        for index in range(steps):
            if index + 1 < steps:
                weight_load(fq, index + 1).start()
            weight_load(fq, index).wait()
            wide[:, index * size : (index + 1) * size] = dot_nt(dq_low[...], weight[index % 2])

    def add_d_normed():
        for index in range(steps):
            wide[:, index * size : (index + 1) * size] += dot_nt(
                dkv_low[...], kv_weight[index * size : (index + 1) * size, :]
            )

    def attend_back(group):
        (key_f[...], key_b[...]), value_tile = head_tiles(keyval_ref, group)
        side = group % 2
        lane_side = slice(side * HD, (side + 1) * HD)
        tile_columns = slice(group // 2 * PAIR, (group // 2 + 1) * PAIR)
        key_t[...] = keyval_ref[:, tile_columns].T[lane_side, :]
        if side == 0:
            kept = front_lanes(value_tile)
            value_f[...], value_b[...] = kept, pltpu.roll(kept, HD, 1)
        else:
            kept = back_lanes(value_tile)
            value_f[...], value_b[...] = pltpu.roll(kept, HD, 1), kept
        dk[...] = jnp.zeros(dk.shape, jnp.float32)
        dv[...] = jnp.zeros(dv.shape, jnp.float32)
        pairs = query_ref.shape[1] // PAIR // KVH

        @pl.loop(0, pairs)
        def _(index):
            pair = group * pairs + index
            columns = pl.ds(pl.multiple_of(pair * PAIR, PAIR), PAIR)
            query, grad = query_ref[:, columns], d_heads[:, columns]
            logs = log_ref[pair]
            made = []
            for number, (key_ref, value_ref, keep) in enumerate(
                ((key_f, value_f, front_lanes), (key_b, value_b, back_lanes))
            ):
                probs = jnp.exp(
                    dot_nt(key_ref[...], query) + bias_ref[...] - logs[number : number + 1, :]
                )
                d_probs = dot_nt(value_ref[...], grad)
                row_dot = jnp.sum(probs * d_probs, axis=0, keepdims=True)
                d_scores = (probs * (d_probs - row_dot)).astype(low)
                dk[...] += dot_nn(d_scores, keep(query))
                dv[...] += dot_nn(probs.astype(low), keep(grad))
                made.append(dot_nn(key_t[...], d_scores))
            dq = jnp.concatenate(made, axis=0).T * (HD**-0.5)
            dq_low[:, columns] = turn(dq, cos_ref[...], -sin_ref[...]).astype(low)

        for sums, first in ((dk, 0), (dv, KVH * HD)):
            joined = (sums[...] + pltpu.roll(sums[...], HD, 1)).astype(low)
            columns = slice(first + tile_columns.start, first + tile_columns.stop)
            for rank in range(ranks):
                block = joined[rank * rows : (rank + 1) * rows, :]
                if side == 1:
                    block = front_lanes(dkv_line[rank, :, columns]) + back_lanes(block)
                dkv_line[rank, :, columns] = block

    def make_dkv():
        wide_columns = dkv_line.shape[2]

        def begin(window):
            sums[window, :] = dkv_line[place, window, :].astype(jnp.float32)

        def add(slot):
            def act(window):
                sums[window, :] += held[slot, window, pl.ds(0, wide_columns)].astype(jnp.float32)

            over_rows(rows, act)

        over_rows(rows, begin)
        line_last(6, add)
        for tile in range(wide_columns // PAIR):
            columns = slice(tile * PAIR, (tile + 1) * PAIR)
            made = sums[:, columns]
            if tile < KVH * HD // PAIR:
                made = turn(made, cos_ref[...], -sin_ref[...])
            dkv_low[:, columns] = made.astype(low)

    def finish_layer():
        for step in (-1, 1):

            @pl.when((place + step >= 0) & (place + step < ranks))
            def _():
                chain_copy(place + step, place, step).wait_send()

        chain_load(place, -1)

        def begin(window):
            total[window, :] += chain[0, window, :].astype(jnp.float32)

        def add(window):
            total[window, :] += held[0, window, :].astype(jnp.float32)

        over_rows(rows, begin)

        @pl.when(place < ranks - 1)
        def _():
            chain_fetch(place)
            over_rows(rows, add)

        @pl.when(place > 0)
        def _():
            chain_fetch(ranks)
            over_rows(rows, add)

        leave(total, layer_out, 6).start()

    def send_core(i):
        for k in turns:
            core_copy(i, k).start()

    send_core(0)
    load_own(0)
    load_own(1)
    chain_step(0)
    dn_load.wait()
    total_load.wait()
    for load in arriving:
        load.wait()
    send_core(1)
    norm_back(wide, total, gain_mlp_ref, 1, after_mlp)
    ready_core(0)
    weight_load(fo, 0).start()
    stage_core(0)
    send_theirs(3, go_tile)
    ready_core(1)
    make_d_heads()
    stage_core(1)
    send_core(2)
    stage_side(0)
    chain_step(1)
    attend_back(0)
    stage_side(1)
    stage_near(0)
    plane_sent(0)
    ready_core(3)
    keep_mine(3, go_tile)
    stage_core(3)
    attend_back(1)
    stage_near(1)
    plane_sent(1)
    chain_step(2)
    attend_back(2)
    stage_side(3)
    attend_back(3)
    line_start(6)
    theirs_sent(3)
    send_theirs(4, gq_tile)
    ready_core(4)
    keep_mine(4, gq_tile)
    stage_core(4)
    stage_near(3)
    line_start(3)
    plane_sent(3)
    load_own(2)
    ready_core(2)
    weight_load(fq, 0).start()
    make_d_normed()
    kv_load.wait()
    make_dkv()
    add_d_normed()
    stage_core(2)
    stage_side(4)
    norm_back(wide, tokens_ref, gain_attn_ref, 0, after_attn)
    leave(d_residual, tokens_out, 7).start()
    theirs_sent(4)
    send_theirs(5, narrow_tile)
    ready_core(5)
    keep_mine(5, narrow_tile)
    stage_core(5)
    stage_near(4)
    line_start(4)
    stage_side(5)
    stage_side(2)
    line_out(3)
    stage_near(5)
    line_start(5)
    finish_layer()
    stage_near(2)
    line_out(4)
    line_out(5)
    plane_sent(2)
    plane_sent(4)
    for src, dst, number in (
        (units_made, gu_out, 2),
        (go_made, go_out, 3),
        (gq_made, gq_out, 4),
        (nar_made.at[:, pl.ds(0, narrow_width)], nar_out, 5),
        (gains_made, gains_out, 8),
        (total, layer_out, 6),
        (d_residual, tokens_out, 7),
    ):
        leave(src, dst, number).wait()
    plane_sent(5)
    theirs_sent(5)
    for i in range(3):
        for k in turns:
            core_copy(i, k).wait_send()
    for i in range(3, 7):
        line_sent(i)


def reach_back(grads, branch, full, d_normed, residual, others):
    low, wide = jnp.bfloat16, jnp.float32
    n_dp, ranks = lax.axis_size("dp"), lax.axis_size("tensor")
    units = grads[0].shape[1]
    rows, depth = residual.shape
    half = rows // 2
    square = depth // ranks
    few = depth // n_dp // ranks
    length, keyval = others[5].shape
    narrow = keyval + PAIR
    widths = [units] * 3 + [depth, depth, narrow]
    anywhere = pl.BlockSpec(memory_space=pl.ANY)
    in_vmem = pl.BlockSpec(memory_space=pltpu.VMEM)
    lined = [(rows, square), (rows, square), (few, narrow), (rows, keyval), (rows, depth)]
    out_shape = [jax.ShapeDtypeStruct((rows, units), wide)] * 3
    out_shape += [jax.ShapeDtypeStruct((rows, square), wide)] * 2
    out_shape += [jax.ShapeDtypeStruct((few, keyval), wide)]
    out_shape += [jax.ShapeDtypeStruct((rows, depth), wide)] * 2
    out_shape += [jax.ShapeDtypeStruct((PAIR, few), wide)]
    out_shape += [jax.ShapeDtypeStruct((4, rows, w), low) for w in widths]
    out_shape += [jax.ShapeDtypeStruct((2, rows, w), low) for w in widths]
    out_shape += [jax.ShapeDtypeStruct((ranks,) + shape, low) for shape in lined[:4]]
    out_shape += [jax.ShapeDtypeStruct((ranks + 1, rows, depth), low)]
    dma = pltpu.SemaphoreType.DMA
    scratch = [pltpu.VMEM((2, half, w), low) for w in widths]
    scratch += [
        pltpu.VMEM((2, 4, rows, depth), low),
        pltpu.VMEM((4, rows, narrow), low),
        pltpu.VMEM((2, rows, depth), low),
        pltpu.VMEM((2, rows, depth), low),
        pltpu.VMEM((4, rows, depth), low),
    ]
    scratch += [pltpu.VMEM((ranks,) + shape, low) for shape in lined[:4]]
    scratch += [pltpu.VMEM((rows, keyval), wide)]
    scratch += [pltpu.VMEM((rows, depth), wide)] * 3
    scratch += [pltpu.VMEM((rows, depth), low)] * 3
    scratch += [
        pltpu.VMEM((rows, keyval), low),
        pltpu.VMEM((8, depth), wide),
        pltpu.VMEM((2, square, depth), low),
        pltpu.VMEM((depth, keyval), low),
        pltpu.VMEM((length, PAIR), low),
        pltpu.VMEM((length, PAIR), low),
        pltpu.VMEM((HD, length), low),
        pltpu.VMEM((length, PAIR), low),
        pltpu.VMEM((length, PAIR), low),
        pltpu.VMEM((length, PAIR), wide),
        pltpu.VMEM((length, PAIR), wide),
        pltpu.VMEM((2, rows, depth), low),
        pltpu.VMEM((rows, units), wide),
        pltpu.VMEM((rows, square), wide),
        pltpu.VMEM((rows, square), wide),
        pltpu.VMEM((few, narrow), wide),
        pltpu.VMEM((PAIR, few), wide),
    ]
    scratch += [pltpu.VMEM(array.shape, array.dtype) for array in others]
    scratch += [
        dma((3, 4)), dma((2,)), dma((6, 4)), dma((6, 4)), dma((6, 6)), dma((6, 6)),
        dma((5, ranks)), dma((5, ranks)), dma((4,)), dma((2,)), dma((ranks,)), dma((ranks + 1,)),
        dma((2,)), dma((9,)), dma((12,)),
    ]
    results = pl.pallas_call(
        reach_back_kernel,
        out_shape=out_shape,
        in_specs=[anywhere] * 21,
        out_specs=[anywhere] * len(out_shape),
        scratch_shapes=scratch,
        compiler_params=pltpu.CompilerParams(
            collective_id=1, has_side_effects=True, vmem_limit_bytes=63 * 1024 * 1024
        ),
        name="reach_back",
    )(*grads, branch, *full, d_normed, residual, *others)
    return results[:9]


def by_tiles(total, size, act):
    full = total // size

    @pl.loop(0, full)
    def _(index):
        act(pl.ds(pl.multiple_of(index * size, size), size))

    if total % size:
        act(pl.ds(full * size, total % size))


def feed_forward_kernel(
    normed_ref, gate_w_ref, up_w_ref, down_w_ref, cot_ref,
    gg_out, gu_out, gd_out, branch_out, dn_out,
    wg, wu, wd, cot, normed, hid, dg, du, part, arrival, branch_stage, gate_stage, up_stage,
    load_sem, n_send, n_recv, l_send, l_recv, stage_sem, p_send, p_recv,
):
    dp, place = lax.axis_index("dp"), lax.axis_index("tensor")
    rows, depth = normed_ref.shape
    low = jnp.bfloat16
    order = line_order(place)
    cuts = l_send.shape[1]
    few = rows // cuts
    enter(dp, place)

    def remote(src, dst, send, recv, step):
        return pltpu.make_async_remote_copy(
            src_ref=src, dst_ref=dst, send_sem=send, recv_sem=recv,
            device_id=(dp, place + step), device_id_type=MESH,
        )

    def chunk(rank):
        return pl.ds(pl.multiple_of(rank * rows, rows), rows)

    def own_copy(step):
        return remote(
            normed_ref, normed.at[chunk(place), :], n_send.at[(step + 1) // 2, place],
            n_recv.at[place], step,
        )

    def pass_copy(rank, step):
        ref = normed.at[chunk(rank), :]
        return remote(ref, ref, n_send.at[(step + 1) // 2, rank], n_recv.at[rank], step)

    x, y, core = flip(dp, 2), flip(dp, 4), flip(dp, 1)
    far = flip(x, 4)
    depth_rows = down_w_ref.shape[0]
    span = depth_rows // 2
    half = span // 2
    shards = (down_w_ref.at[pl.ds(0, span), :], down_w_ref.at[pl.ds(span, span), :])

    def weight_rows(i, owner, part=None):
        first = owner * depth_rows + i * span + (0 if part is None else part * half)
        count = span if part is None else half
        return wd.at[pl.ds(pl.multiple_of(first, half), count), :]

    def plane_copy(i, lane):
        if lane < 2:
            src, dst, device = shards[i], weight_rows(i, dp), (x, y)[lane]
        elif lane < 4:
            src = dst = weight_rows(i, (x, y)[lane - 2], lane - 2)
            device = (y, x)[lane - 2]
        else:
            owner = (dp, x, y, far)[lane - 4]
            dst, device = weight_rows(i, owner), core
            src = shards[i] if lane == 4 else dst
        return pltpu.make_async_remote_copy(
            src_ref=src, dst_ref=dst, send_sem=p_send.at[i, lane], recv_sem=p_recv.at[i, lane],
            device_id=(device, place), device_id_type=MESH,
        )

    loads = [
        pltpu.make_async_copy(src, dst, load_sem.at[i])
        for i, (src, dst) in enumerate(
            (
                (normed_ref, normed.at[chunk(place), :]),
                (gate_w_ref, wg),
                (cot_ref, cot),
                (up_w_ref, wu),
                (down_w_ref, wd.at[pl.ds(pl.multiple_of(dp * depth_rows, span), depth_rows), :]),
            )
        )
    ]

    @pl.when(place < 3)
    def _():
        own_copy(1).start()

    @pl.when(place > 0)
    def _():
        own_copy(-1).start()

    for i in range(2):
        for lane in (0, 1, 4):
            plane_copy(i, lane).start()
    for load in loads:
        load.start()

    def plane_second(i):
        for lane in range(2):
            plane_copy(i, lane).wait_recv()
            plane_copy(i, lane + 2).start()
            plane_copy(i, lane + 5).start()

    def plane_third(i):
        plane_copy(i, 2).wait_recv()
        plane_copy(i, 3).wait_recv()
        plane_copy(i, 7).start()

    def plane_ready(i):
        for lane in range(4, 8):
            plane_copy(i, lane).wait_recv()

    def sums_copy(rank, cut, slot, step):
        window = pl.ds(pl.multiple_of(cut * few, few), few)
        return remote(
            part.at[rank, window, :], arrival.at[slot, window, :], l_send.at[rank, cut],
            l_recv.at[slot, cut], step,
        )

    def branch_copy(rank):
        return pltpu.make_async_copy(branch_stage, branch_out.at[rank], stage_sem.at[0])

    def forward(rank):
        here = chunk(rank)

        def activate(columns):
            gate = dot_nn(normed[here, :], wg[:, columns])
            up = dot_nn(normed[here, :], wu[:, columns])
            sig = 1.0 / (1.0 + jnp.exp(-gate))
            silu = gate * sig
            hid[here, columns] = (silu * up).astype(low)
            dg[here, columns] = (up * sig * (1.0 + gate * (1.0 - sig))).astype(low)
            du[here, columns] = silu.astype(low)

        by_tiles(wg.shape[1], 256, activate)

    def backward(rank):
        here = chunk(rank)

        def meet(columns):
            d_hidden = dot_nn(cot[here, :], wd[:, columns])
            dg[here, columns] = (d_hidden * dg[here, columns].astype(jnp.float32)).astype(low)
            du[here, columns] = (d_hidden * du[here, columns].astype(jnp.float32)).astype(low)

        by_tiles(wg.shape[1], 256, meet)

        def pull(columns):
            part[rank, :, columns] = (
                dot_nt(dg[here, :], wg[columns, :]) + dot_nt(du[here, :], wu[columns, :])
            ).astype(low)

        by_tiles(depth, 512, pull)

    def branch(rank):
        def push(columns):
            branch_stage[:, columns] = dot_nt(hid[chunk(rank), :], wd[columns, :]).astype(low)

        by_tiles(depth, 512, push)
        branch_copy(rank).start()

    def take(rank):
        pass_copy(rank, 1).wait_recv()

        @pl.when((rank < place) & (place < 3))
        def _():
            pass_copy(rank, 1).start()

        @pl.when((rank > place) & (place > 0))
        def _():
            pass_copy(rank, -1).start()

    inside = (place == 1) | (place == 2)
    for load in loads:
        load.wait()
    forward(place)
    plane_second(0)
    plane_second(1)
    take(order[0])

    @pl.when(inside)
    def _():
        take(order[1])

    plane_third(0)
    plane_third(1)

    @pl.loop(0, jnp.where(inside, 2, 1))
    def _(index):
        forward(jnp.where(index == 0, order[0], order[1]))

    plane_ready(0)
    plane_ready(1)

    @pl.loop(0, 4)
    def _(turn):
        rank = jnp.where(
            turn == 0,
            order[0],
            jnp.where(
                turn == 1,
                jnp.where(inside, order[1], place),
                jnp.where(
                    turn == 2,
                    jnp.where(inside, order[2], order[1]),
                    jnp.where(inside, place, order[2]),
                ),
            ),
        )

        @pl.when((turn == 2) | ((turn == 3) & jnp.logical_not(inside)))
        def _():
            take(rank)
            forward(rank)

        backward(rank)

        @pl.when((turn != 1) & (place == 3))
        def _():
            for cut in range(cuts):
                sums_copy(rank, cut, rank, -1).start()

        @pl.when((turn != 1) & (place == 0))
        def _():
            slot = jnp.where(rank == 1, 4, rank)
            for cut in range(cuts):
                sums_copy(rank, cut, slot, 1).start()

    def gate_copy(tile):
        return pltpu.make_async_copy(gate_stage, gg_out.at[tile, :], stage_sem.at[1])

    def up_copy(tile):
        return pltpu.make_async_copy(up_stage, gu_out.at[tile, :], stage_sem.at[2])

    def down_copy(tile):
        return pltpu.make_async_copy(gate_stage, gd_out.at[tile, :], stage_sem.at[1])

    size = gate_stage.shape[0]
    tiles = depth // size

    def gate_up_tile(index):
        tile = pl.ds(pl.multiple_of(index * size, size), size)
        left = normed[:, tile]
        gate_grad = dot_tn(left, dg[...]).astype(low)

        @pl.when(index > 0)
        def _():
            gate_copy(tile).wait()
            up_copy(tile).wait()

        gate_stage[...] = gate_grad
        gate_copy(tile).start()
        up_stage[...] = dot_tn(left, du[...]).astype(low)
        up_copy(tile).start()

    def down_tile(index):
        tile = pl.ds(pl.multiple_of(index * size, size), size)
        down_grad = dot_tn(cot[:, tile], hid[...]).astype(low)

        @pl.when(index > 0)
        def _():
            down_copy(tile).wait()

        gate_stage[...] = down_grad
        down_copy(tile).start()

    last = pl.ds(depth - size, size)

    def relay(rank, slot, step, cut):
        sums_copy(rank, cut, rank, step).wait_recv()
        window = pl.ds(pl.multiple_of(cut * few, few), few)
        part[rank, window, :] = part[rank, window, :] + arrival[rank, window, :]
        sums_copy(rank, cut, slot, step).start()

    outward = 3 - 2 * place

    @pl.loop(0, cuts)
    def _(cut):
        @pl.when(inside)
        def _():
            relay(3 - place, 4 - 3 * (place - 1), outward, cut)

        @pl.loop(0, tiles // cuts)
        def _(index):
            gate_up_tile(cut * (tiles // cuts) + index)

    gate_copy(last).wait()
    up_copy(last).wait()

    @pl.loop(0, cuts)
    def _(cut):
        @pl.when(inside)
        def _():
            relay(6 - 3 * place, 6 - 3 * place, outward, cut)
            relay(3 * (place - 1), 4 * (place - 1), -outward, cut)

        @pl.loop(0, tiles // cuts)
        def _(index):
            down_tile(cut * (tiles // cuts) + index)

        @pl.when(cut > 0)
        def _():
            branch_copy(cut).wait()

        branch(cut)

    down_copy(last).wait()
    branch_copy(0).wait()

    for cut in range(cuts):
        window = pl.ds(cut * few, few)
        dn_out[window, :] = part[place, window, :].astype(jnp.float32)

        @pl.when(place < 3)
        def _():
            sums_copy(place, cut, place, 1).wait_recv()
            dn_out[window, :] += arrival[place, window, :].astype(jnp.float32)

        @pl.when(place > 0)
        def _():
            sums_copy(place, cut, 4, 1).wait_recv()
            dn_out[window, :] += arrival[4, window, :].astype(jnp.float32)

    @pl.when(place < 3)
    def _():
        own_copy(1).wait_send()

    @pl.when(place > 0)
    def _():
        own_copy(-1).wait_send()

    for rank in range(4):

        @pl.when((rank < place) & (place < 3))
        def _():
            pass_copy(rank, 1).wait_send()

        @pl.when((rank > place) & (place > 0))
        def _():
            pass_copy(rank, -1).wait_send()

        @pl.when(rank != place)
        def _():
            for cut in range(cuts):
                sums_copy(rank, cut, rank, 1).wait_send()

    for i in range(2):
        for lane in range(8):
            plane_copy(i, lane).wait_send()


def feed_forward(normed, w_gate, w_up, w_down, cotangent):
    low = jnp.bfloat16
    rows, depth = normed.shape
    length = cotangent.shape[0]
    units = w_gate.shape[1]
    ranks = length // rows
    cuts = 4
    anywhere = pl.BlockSpec(memory_space=pl.ANY)
    in_vmem = pl.BlockSpec(memory_space=pltpu.VMEM)
    dma = pltpu.SemaphoreType.DMA
    flops = 9 * 2 * length * depth * units
    return pl.pallas_call(
        feed_forward_kernel,
        out_shape=[jax.ShapeDtypeStruct((depth, units), low)] * 3
        + [
            jax.ShapeDtypeStruct((ranks, rows, depth), low),
            jax.ShapeDtypeStruct((rows, depth), jnp.float32),
        ],
        in_specs=[anywhere] * 5,
        out_specs=[anywhere] * 4 + [in_vmem],
        scratch_shapes=[pltpu.VMEM((depth, units), low)] * 3
        + [pltpu.VMEM((length, depth), low)] * 2
        + [pltpu.VMEM((length, units), low)] * 3
        + [
            pltpu.VMEM((ranks, rows, depth), low),
            pltpu.VMEM((ranks + 1, rows, depth), low),
            pltpu.VMEM((rows, depth), low),
            pltpu.VMEM((256, units), low),
            pltpu.VMEM((256, units), low),
            dma((5,)), dma((2, ranks)), dma((ranks,)), dma((ranks, cuts)), dma((ranks + 1, cuts)),
            dma((3,)), dma((2, 8)), dma((2, 8)),
        ],
        compiler_params=pltpu.CompilerParams(
            collective_id=2, has_side_effects=True, vmem_limit_bytes=62 * 1024 * 1024
        ),
        cost_estimate=pl.CostEstimate(flops=flops, bytes_accessed=60 << 20, transcendentals=0),
        name="feed_forward",
    )(normed, w_gate, w_up, w_down, cotangent)


def local(
    tokens,
    segments,
    gain_attn,
    w_query,
    w_keyval,
    w_output,
    gain_mlp,
    w_gate,
    w_up,
    w_down,
    cotangent,
):
    tensor_rank = lax.axis_index("tensor")
    length = segments.shape[0]
    rows = tokens.shape[0]
    both = ("dp", "tensor")
    low = jnp.bfloat16

    def gather(array, axes, axis=0):
        return lax.all_gather(array, axes, axis=axis, tiled=True)

    def scatter(array, axes, axis=0):
        return lax.psum_scatter(array, axes, scatter_dimension=axis, tiled=True)

    by_kernels = (lax.axis_size("dp"), lax.axis_size("tensor")) == (8, 4)
    places = doc_positions(segments)
    my_places = lax.dynamic_slice_in_dim(places, tensor_rank * rows, rows, 0)
    my_segments = lax.dynamic_slice_in_dim(segments, tensor_rank * rows, rows, 0)
    cosine, sine_table = rope_tables(my_places, HD)
    order = jnp.arange(length, dtype=jnp.int32)
    allowed = (order[:, None] <= tensor_rank * rows + order[None, :rows]) & (
        segments[:, None] == my_segments[None, :]
    )
    bias = jnp.where(allowed, 0.0, masked).astype(jnp.float32)

    token_rows = tokens.astype(jnp.float32)
    normed_attn, unit_attn, inverse_attn = norm_forward(token_rows, gain_attn)
    normed_attn = normed_attn.astype(low)
    wide = KVH * HD
    if by_kernels:
        before = jnp.sum(segments[None, :] < my_segments[:, None], axis=1, dtype=jnp.int32)
        my_order = tensor_rank * rows + jnp.arange(rows, dtype=jnp.int32)
        lane = jnp.arange(PAIR, dtype=jnp.int32)
        spin = rope_base ** (-(2.0 * (lane % (HD // 2)).astype(jnp.float32)) / HD)
        angles = (my_order - before).astype(jnp.float32)[:, None] * spin[None, :]
        cos_tile = jnp.cos(angles)
        sin_tile = jnp.where((lane % HD < HD // 2)[None, :], -jnp.sin(angles), jnp.sin(angles))
        (
            normed_attn, query, keyval, heads_low, log_sum, residual, normed_mlp,
            full_keyval, full_query, full_output, full_gate, full_up, piece,
        ) = attend_all(
            tokens, gain_attn[None, :], cos_tile, sin_tile, bias, gain_mlp[None, :],
            w_keyval, w_query, w_output, w_gate, w_up, cotangent,
        )
    else:
        full_keyval = gather(w_keyval, "dp")
        keyval_pre = dot_nn(normed_attn, full_keyval)
        key_low = rotate(keyval_pre[:, :wide], cosine, sine_table).astype(low)
        keyval = jnp.concatenate([key_low, keyval_pre[:, wide:].astype(low)], axis=1)
        keyval = gather(keyval, "tensor")
        full_query = gather(gather(w_query, "tensor", 1), "dp")
        query = rotate(dot_nn(normed_attn, full_query), cosine, sine_table) * (HD**-0.5)
        query = query.astype(low)
    if by_kernels:
        grad_gate, grad_up, grad_down, branch, d_normed_mlp = feed_forward(
            normed_mlp, full_gate, full_up, w_down, piece
        )
        to_down, to_gate, to_up, to_output, to_query, to_keyval, layer_out, grad_tokens, to_gains = (
            reach_back(
                (grad_down, grad_gate, grad_up),
                branch,
                (full_keyval, full_query, full_output),
                d_normed_mlp,
                residual,
                (
                    cotangent, tokens, normed_attn, query, heads_low, keyval, log_sum, bias,
                    cos_tile, sin_tile, gain_attn[None, :], gain_mlp[None, :],
                ),
            )
        )
        return (
            layer_out.astype(low),
            grad_tokens.astype(low),
            to_gains[0],
            to_query,
            to_keyval,
            to_output,
            to_gains[1],
            to_gate,
            to_up,
            to_down,
        )

    key_heads, value_heads = by_head(keyval[:, :wide]), by_head(keyval[:, wide:])
    blank = jnp.zeros_like(key_heads)
    key_f = jnp.concatenate([key_heads, blank], axis=2)
    key_b = jnp.concatenate([blank, key_heads], axis=2)
    value_f = jnp.concatenate([value_heads, blank], axis=2)
    value_b = jnp.concatenate([blank, value_heads], axis=2)
    key_t = key_heads.transpose(0, 2, 1)
    value_t = value_heads.transpose(0, 2, 1)
    heads_low, log_sum = attend_forward(query, key_f, key_b, value_t, bias)
    full_output = gather(gather(w_output, "tensor", 1), "dp")
    residual = token_rows + dot_nt(heads_low, full_output)
    full_gate, full_up = gather(w_gate, "dp"), gather(w_up, "dp")
    full_down = gather(w_down, "dp")
    piece = gather(cotangent, "tensor")
    normed_mlp_rows, unit_mlp, inverse_mlp = norm_forward(residual, gain_mlp)
    normed_mlp = normed_mlp_rows.astype(low)
    gathered_mlp = gather(normed_mlp, "tensor")
    gate_act = dot_nn(gathered_mlp, full_gate)
    up_act = dot_nn(gathered_mlp, full_up)
    sigmoid_gate = jax.nn.sigmoid(gate_act)
    silu_gate = gate_act * sigmoid_gate
    hidden_low = (silu_gate * up_act).astype(low)
    d_hidden = dot_nn(piece, full_down)
    d_gate = (d_hidden * up_act * sigmoid_gate * (1.0 + gate_act * (1.0 - sigmoid_gate))).astype(low)
    d_up = (d_hidden * silu_gate).astype(low)
    d_normed_mlp = scatter(
        (dot_nt(d_gate, full_gate) + dot_nt(d_up, full_up)).astype(low), "tensor"
    ).astype(jnp.float32)
    branch = dot_nt(hidden_low, full_down).astype(low)
    grad_down = dot_tn(piece, hidden_low)
    grad_gate = dot_tn(gathered_mlp, d_gate)
    grad_up = dot_tn(gathered_mlp, d_up)
    d_norm_mlp, gain_mlp_part = norm_backward(d_normed_mlp, unit_mlp, inverse_mlp, gain_mlp)
    d_residual = cotangent.astype(jnp.float32) + d_norm_mlp

    d_branch = d_residual.astype(low)
    grad_output = dot_tn(d_branch, heads_low)
    d_heads = dot_nn(d_branch, full_output).astype(low)
    d_queries, d_keys, d_values = attend_backward(
        query, d_heads, key_f, key_b, key_t, value_f, value_b, bias, log_sum
    )

    def flat(parts):
        joined = parts[:, :, :HD] + parts[:, :, HD:]
        return joined.transpose(1, 0, 2).reshape(length, wide)

    d_keyval = scatter(
        jnp.concatenate([flat(d_keys), flat(d_values)], axis=1).astype(low), "tensor"
    ).astype(jnp.float32)
    dq_low = rotate(d_queries, cosine, -sine_table).astype(low)
    dkv_low = jnp.concatenate(
        [rotate(d_keyval[:, :wide], cosine, -sine_table), d_keyval[:, wide:]], axis=1
    ).astype(low)
    grad_query = dot_tn(normed_attn, dq_low)
    grad_keyval = dot_tn(normed_attn, dkv_low)
    d_normed_attn = dot_nt(dq_low, full_query) + dot_nt(dkv_low, full_keyval)
    d_norm_attn, gain_attn_part = norm_backward(d_normed_attn, unit_attn, inverse_attn, gain_attn)
    grad_tokens = (d_residual + d_norm_attn).astype(low)

    layer_rows = residual + scatter(branch, "tensor").astype(jnp.float32)

    def shares(grad):
        return scatter(grad.astype(low), "dp").astype(jnp.float32)

    def square_shares(grad):
        return scatter(scatter(grad.astype(low), "dp"), "tensor", 1).astype(jnp.float32)

    gains = scatter(
        jnp.stack([gain_attn_part, gain_mlp_part]).reshape(2, -1, rows_of_gain(gain_attn)), both, 1
    )
    return (
        layer_rows.astype(low),
        grad_tokens,
        gains[0, 0],
        square_shares(grad_query),
        scatter(grad_keyval.astype(low), both).astype(jnp.float32),
        square_shares(grad_output),
        gains[1, 0],
        shares(grad_gate),
        shares(grad_up),
        shares(grad_down),
    )


def rows_of_gain(gain):
    return gain.shape[0] // (lax.axis_size("dp") * lax.axis_size("tensor"))


def solution(mesh):
    return jax.shard_map(
        local,
        mesh=mesh,
        in_specs=(
            P(("dp", "tensor"), None),
            P("dp"),
            P(),
            P("dp", "tensor"),
            P("dp", None),
            P("dp", "tensor"),
            P(),
            P("dp", "tensor"),
            P("dp", "tensor"),
            P("dp", "tensor"),
            P(("dp", "tensor"), None),
        ),
        out_specs=(
            P(("dp", "tensor"), None),
            P(("dp", "tensor"), None),
            P(("dp", "tensor")),
            P("dp", "tensor"),
            P(("dp", "tensor"), None),
            P("dp", "tensor"),
            P(("dp", "tensor")),
            P("dp", "tensor"),
            P("dp", "tensor"),
            P("dp", "tensor"),
        ),
        check_vma=False,
    )
```
